32 devices in a mesh: seq: 8 (over z, y), mem: 4 (over x, core).
Axes of the slice: x: 2, y: 2, z: 4, core: 2. Of those that a mesh axis runs over, the one named last changes fastest.
Arguments:
- tokens: bfloat16 [32768, 1024], P(('seq', 'mem')), may hold values from -6 to 6
- memory: bfloat16 [32, 588, 1024], P('seq', 'mem'), may hold values from -6 to 6
- page_lengths: int32 [32], P(('seq', 'mem')), may hold values from 256 to 1024, as said below
- slot_masks: int32 [32, 588], P('seq'), may hold values from 0 to 1, as said below
- upstream: bfloat16 [32768, 1024], P(('seq', 'mem')), may hold values from -6 to 6
- weights: float32 [1024, 16384], P(None, ('seq', 'mem'))
- weight_average: float32 [1024, 16384], P(None, ('seq', 'mem'))
- weight_moment1: float32 [1024, 16384], P(None, ('seq', 'mem'))
- weight_moment2: float32 [1024, 16384], P(None, ('seq', 'mem')), as said below
- stats: float32 [128, 128, 128], P(('seq', 'mem')), as said below
- bases: float32 [128, 128, 128], P(('seq', 'mem'))
- vectors: float32 [17, 1024], P(None, ('seq', 'mem'))
- vector_average: float32 [17, 1024], P(None, ('seq', 'mem'))
- vector_moment1: float32 [17, 1024], P(None, ('seq', 'mem'))
- vector_moment2: float32 [17, 1024], P(None, ('seq', 'mem')), as said below
Outputs:
- mixed: bfloat16 [32768, 1024], P(('seq', 'mem'))
- input_grad: float32 [32768, 1024], P(('seq', 'mem'))
- memory_grad: float32 [32, 588, 1024], P('seq', 'mem')
- weight_grad: float32 [1024, 16384], P(None, ('seq', 'mem'))
- weight_first: float32 [1024, 16384], P(None, ('seq', 'mem'))
- weight_second: float32 [1024, 16384], P(None, ('seq', 'mem'))
- new_weights: float32 [1024, 16384], P(None, ('seq', 'mem'))
- new_average: float32 [1024, 16384], P(None, ('seq', 'mem'))
- weights_copy: bfloat16 [1024, 16384], P(None, ('seq', 'mem'))
- new_stats: float32 [128, 128, 128], P(('seq', 'mem'))
- new_bases: float32 [128, 128, 128], P(('seq', 'mem'))
- vector_grad: float32 [17, 1024], P(None, ('seq', 'mem'))
- vector_first: float32 [17, 1024], P(None, ('seq', 'mem'))
- vector_second: float32 [17, 1024], P(None, ('seq', 'mem'))
- new_vectors: float32 [17, 1024], P(None, ('seq', 'mem'))
- new_vector_average: float32 [17, 1024], P(None, ('seq', 'mem'))
- vectors_copy: bfloat16 [17, 1024], P(None, ('seq', 'mem'))
- down_bias_grad: float32 [1024], P(('seq', 'mem'))
The draws below stay inside these ranges and needn't reach their ends.
Inputs may be any that keep to these rules, and one draw needn't show every extreme that they name: `page_lengths`: in every aligned group of 4 pages one page has length 1024. `slot_masks`: A page's memory is either full, all 588 slots real, or half, exactly 154 real slots among its first 196 and none after; every aligned group of 4 pages has a full one. `weight_moment2`: every entry is positive. `vector_moment2`: every entry is positive. `stats`: each block is symmetric positive definite.
All inputs are finite; a program needn't handle non-finite values.
Results may differ from the reference program's by a relative error of at most 0.024.
The reference program's roundings to bfloat16 on the way count: a program that leaves them out, or rounds other values in their place, can miss the bound.
Values may be sent and summed in bfloat16 or wider, within the bound.
No kernel may reach another device: no remote copies, remote signals or barrier semaphores. Data moves between devices by JAX's collectives and lax.ppermute only.
A program may use at most 384 MiB of HBM per device.

```python
import math
import jax
import jax.numpy as jnp
import numpy as np
from jax import lax

D = 1024
HEADS = 16
HEAD = 64
FF = 4096
PAGE = 1024
MEMS = 588
HALF_SLOTS = 196
REAL_HALF = 154
BLK = 128
VROWS = 17
STEP = 10
PAGES = 32
GROUP_PAGES = 4
TOKENS = 32768
MQ = 147
NBLK = 128
N_MEM = 4


WEIGHT_SPREAD = np.array([1.2, 1.2, 1.0, 6.0, 1.2, 1.2, 1.0, 6.0, 1.0, 1.0, 1.0, 1.0, 0.8, 0.8, 0.8, 0.8], np.float32)


GRADIENT_SPREAD = np.array([0.5, 0.5, 1.5, 0.15, 0.5, 0.5, 1.5, 0.15, 1.0, 1.0, 1.0, 1.0, 0.6, 0.6, 0.6, 0.6], np.float32)


FIRST_SHARE = 0.111


SECOND_SHARE = 0.0526


VECTOR_SPREAD = 0.7


AVERAGE_SHARE = 0.001


def gradient_size():
    return jnp.sqrt(jnp.float32(0.625 * TOKENS))


def column_gradient():
    return jnp.asarray(GRADIENT_SPREAD)[jnp.arange(16 * D) // D] * gradient_size()


def group_choice(key):
    chosen = jax.random.randint(key, (PAGES // GROUP_PAGES,), 0, GROUP_PAGES)
    return jnp.arange(PAGES) % GROUP_PAGES == jnp.repeat(chosen, GROUP_PAGES)


def draw_page_lengths(key, part):
    key = jax.random.fold_in(key, 1)
    first_key, second_key = jax.random.split(key)
    lengths = jax.random.randint(first_key, (PAGES,), PAGE // 4, PAGE + 1)
    return jnp.where(group_choice(second_key), PAGE, lengths).astype(jnp.int32)


def draw_slot_masks(key, part):
    key = jax.random.fold_in(key, 2)
    first_key, second_key, third_key = jax.random.split(key, 3)
    halves = (jax.random.randint(first_key, (PAGES,), 0, 2) > 0) & jnp.logical_not(group_choice(second_key))
    ranks = jax.vmap(lambda page_key: jax.random.permutation(page_key, HALF_SLOTS))(jax.random.split(third_key, PAGES))
    picked = jnp.concatenate([ranks < REAL_HALF, jnp.zeros((PAGES, MEMS - HALF_SLOTS), jnp.bool_)], axis=1)
    return jnp.where(halves[:, None], picked, True).astype(jnp.int32)


def draw_weights(key, part):
    key = jax.random.fold_in(key, 3)
    spread = jnp.asarray(WEIGHT_SPREAD)[jnp.arange(16 * D) // D] / jnp.sqrt(jnp.float32(D))
    sample = jax.random.normal(key, (D, 16 * D), jnp.float32)
    return sample * spread[None, :]


def draw_weight_average(key, part):
    key = jax.random.fold_in(key, 4)
    spread = AVERAGE_SHARE * jnp.asarray(WEIGHT_SPREAD)[jnp.arange(16 * D) // D] / jnp.sqrt(jnp.float32(D))
    sample = jax.random.normal(key, (D, 16 * D), jnp.float32)
    return sample * spread[None, :]


def draw_weight_moment1(key, part):
    key = jax.random.fold_in(key, 5)
    sample = jnp.clip(jax.random.normal(key, (D, 16 * D), jnp.float32), -5.0, 5.0)
    return sample * FIRST_SHARE * column_gradient()[None, :]


def draw_weight_moment2(key, part):
    key = jax.random.fold_in(key, 6)
    factor = jnp.exp(jax.random.uniform(key, (D, 16 * D), jnp.float32, 0.0, math.log(4.0)))
    return factor * SECOND_SHARE * (column_gradient() ** 2)[None, :]


def draw_stats(key, part):
    key = jax.random.fold_in(key, 7)
    first_key, second_key = jax.random.split(key)
    block_index = jnp.arange(NBLK) * BLK // D
    level = SECOND_SHARE * D * (jnp.asarray(GRADIENT_SPREAD)[block_index] * gradient_size()) ** 2
    diagonal = jnp.exp(jax.random.uniform(first_key, (NBLK, BLK), jnp.float32, 0.0, math.log(4.0)))
    identity = jnp.eye(BLK, dtype=jnp.float32)
    noise = jnp.clip(jax.random.normal(second_key, (NBLK, BLK, BLK), jnp.float32), -3.0, 3.0) * 0.03
    noise = (noise + jnp.swapaxes(noise, 1, 2)) * 0.70710678 * (1.0 - identity)
    return level[:, None, None] * (diagonal[:, :, None] * identity + noise)


def unit_rows(key):
    sample = jax.random.uniform(key, (NBLK, BLK), jnp.float32, 0.5, 2.0)
    signs = jnp.where(jax.random.randint(jax.random.fold_in(key, 1), (NBLK, BLK), 0, 2) > 0, 1.0, -1.0)
    vector_rows = sample * signs
    return vector_rows * lax.rsqrt(jnp.sum(vector_rows * vector_rows, axis=1, keepdims=True))


def draw_bases(key, part):
    key = jax.random.fold_in(key, 8)
    first_key, second_key = jax.random.split(key)
    first_unit = unit_rows(first_key)
    second_unit = unit_rows(second_key)
    inner = jnp.sum(first_unit * second_unit, axis=1)
    identity = jnp.eye(BLK, dtype=jnp.float32)
    outer_first = first_unit[:, :, None] * first_unit[:, None, :]
    outer_second = second_unit[:, :, None] * second_unit[:, None, :]
    outer_mixed = first_unit[:, :, None] * second_unit[:, None, :]
    return identity[None] - 2.0 * outer_first - 2.0 * outer_second + 4.0 * inner[:, None, None] * outer_mixed


def gain_rows():
    rows_index = jnp.arange(VROWS)
    return ((rows_index < 6) & (rows_index % 2 == 0))[:, None]


def draw_vectors(key, part):
    key = jax.random.fold_in(key, 9)
    sample = jnp.clip(jax.random.normal(key, (VROWS, D), jnp.float32), -4.0, 4.0)
    return jnp.where(gain_rows(), 1.0 + 0.1 * sample, 0.1 * sample)


def draw_vector_average(key, part):
    key = jax.random.fold_in(key, 10)
    sample = jnp.clip(jax.random.normal(key, (VROWS, D), jnp.float32), -4.0, 4.0)
    return AVERAGE_SHARE * jnp.where(gain_rows(), 1.0 + 0.1 * sample, 0.1 * sample)


def draw_vector_moment1(key, part):
    key = jax.random.fold_in(key, 11)
    sample = jnp.clip(jax.random.normal(key, (VROWS, D), jnp.float32), -5.0, 5.0)
    return sample * FIRST_SHARE * VECTOR_SPREAD * gradient_size()


def draw_vector_moment2(key, part):
    key = jax.random.fold_in(key, 12)
    factor = jnp.exp(jax.random.uniform(key, (VROWS, D), jnp.float32, 0.0, math.log(4.0)))
    return factor * SECOND_SHARE * (VECTOR_SPREAD * gradient_size()) ** 2


def block_scale(own_key, extent, pieces, smallest, high):
    level, own = 1.0, jax.random.fold_in(own_key, 6)
    for dim, blocks in pieces:
        steps = jnp.exp(jax.random.uniform(jax.random.fold_in(own, dim), (blocks,), jnp.float32, smallest / len(pieces), high / len(pieces)))
        level = level * jnp.repeat(steps, extent[dim] // blocks).reshape([-1 if axis == dim else 1 for axis in range(len(extent))])
    return level


def gaussian(stream_key, dims, scale, bound, pieces=(), held_as=jnp.bfloat16):
    level = block_scale(stream_key, dims, pieces, -0.22, 0.18) if pieces else 1.0
    values = jax.random.normal(stream_key, dims, jnp.float32) * scale * level
    return jnp.minimum(jnp.maximum(values, -bound), bound).astype(held_as)


def setup_inputs(seed: int = 0) -> dict:
    splits = jax.random.split(jax.random.key(seed), 16)
    return {
        "tokens": gaussian(splits[0], (TOKENS, D), 1.0, 6.0, ((0, 32),)),
        "memory": gaussian(splits[1], (PAGES, MEMS, D), 1.0, 6.0, ((0, 8), (1, 4))),
        "page_lengths": draw_page_lengths(jax.random.fold_in(splits[15], 71), 0),
        "slot_masks": draw_slot_masks(jax.random.fold_in(splits[15], 71), 0),
        "upstream": gaussian(splits[4], (TOKENS, D), 1.0, 6.0, ((0, 32),)),
        "weights": draw_weights(jax.random.fold_in(splits[15], 71), 0),
        "weight_average": draw_weight_average(jax.random.fold_in(splits[15], 71), 0),
        "weight_moment1": draw_weight_moment1(jax.random.fold_in(splits[15], 71), 0),
        "weight_moment2": draw_weight_moment2(jax.random.fold_in(splits[15], 71), 0),
        "stats": draw_stats(jax.random.fold_in(splits[15], 71), 0),
        "bases": draw_bases(jax.random.fold_in(splits[15], 71), 0),
        "vectors": draw_vectors(jax.random.fold_in(splits[15], 71), 0),
        "vector_average": draw_vector_average(jax.random.fold_in(splits[15], 71), 0),
        "vector_moment1": draw_vector_moment1(jax.random.fold_in(splits[15], 71), 0),
        "vector_moment2": draw_vector_moment2(jax.random.fold_in(splits[15], 71), 0),
    }


@jax.custom_vjp
def low(v):
    return lax.optimization_barrier(v.astype(jnp.bfloat16)).astype(jnp.float32)

@jax.custom_vjp
def low_back(v):
    return v

def low_keep(v):
    return (low(v), None)

def low_pass(kept, grad):
    return (grad,)

def back_keep(v):
    return (v, None)

def back_low(kept, grad):
    return (low(grad),)
low.defvjp(low_keep, low_pass)
low_back.defvjp(back_keep, back_low)
HIGHEST = lax.Precision.HIGHEST
NORM_EPS = 1e-05
ADAM_EPS = 1e-08
BETA_ONE = 0.9
BETA_TWO = 0.95
RATE = 0.04
VECTOR_RATE = 0.4
DECAY = 0.01
AVERAGE = 0.999
MASKED = -1e+30

def matmul(left, right):
    return jnp.dot(left.astype(jnp.float32), right.astype(jnp.float32), precision=HIGHEST, preferred_element_type=jnp.float32)

def normalize(values, scale_gain, offset):
    centre = lax.optimization_barrier(jnp.mean(values, axis=-1, keepdims=True))
    centred = values - centre
    variance = lax.optimization_barrier(jnp.mean(centred * centred, axis=-1, keepdims=True))
    return centred * lax.rsqrt(variance + NORM_EPS) * scale_gain + offset

def softmax_rows(scores):
    largest = lax.optimization_barrier(jnp.max(scores, axis=-1, keepdims=True))
    raised = jnp.exp(scores - largest)
    summed = lax.optimization_barrier(jnp.sum(raised, axis=-1, keepdims=True))
    return (raised / summed, largest[..., 0] + jnp.log(summed[..., 0]))

def split_heads(values):
    return values.reshape(values.shape[:-1] + (HEADS, HEAD))

def page_layer(inputs, memory_page, slot_live, live_rows, weights_low, vectors_low):
    scale_q = HEAD ** (-0.5)

    def block_columns(first, count):
        return weights_low[:, first * D:(first + count) * D]
    normed_one = low(normalize(inputs, vectors_low[0], vectors_low[1]))
    queries = low(low_back((matmul(normed_one, block_columns(0, 1)) + vectors_low[6]) * scale_q))
    keys_in = low(low_back(matmul(normed_one, block_columns(1, 1))))
    values_in = low(low_back(matmul(normed_one, block_columns(2, 1)) + vectors_low[7]))
    scores = jnp.einsum('qhd,khd->hqk', split_heads(queries), split_heads(keys_in), precision=HIGHEST)
    position = jnp.arange(inputs.shape[0])
    causal = position[None, :] <= position[:, None]
    scores = low_back(jnp.where(causal[None], scores, MASKED))
    chance = softmax_rows(scores)[0]
    attended = jnp.einsum('hqk,khd->qhd', low(chance), split_heads(values_in), precision=HIGHEST)
    attended = low(low_back(attended.reshape(inputs.shape)))
    after_self = inputs + low_back(matmul(attended, block_columns(3, 1)) + vectors_low[8])
    normed_two = low(normalize(after_self, vectors_low[2], vectors_low[3]))
    queries_cross = low(low_back((matmul(normed_two, block_columns(4, 1)) + vectors_low[9]) * scale_q))
    keys_cross = low(low_back(matmul(memory_page, block_columns(5, 1))))
    values_cross = low(low_back(matmul(memory_page, block_columns(6, 1)) + vectors_low[10]))
    keys_quarter = split_heads(keys_cross).reshape(N_MEM, MQ, HEADS, HEAD)
    values_quarter = split_heads(values_cross).reshape(N_MEM, MQ, HEADS, HEAD)
    live_quarter = slot_live.reshape(N_MEM, MQ)
    scores_cross = jnp.einsum('qhd,rkhd->rhqk', split_heads(queries_cross), keys_quarter, precision=HIGHEST)
    scores_cross = low_back(jnp.where(live_quarter[:, None, None, :] > 0, scores_cross, MASKED))
    chance_cross, log_part = softmax_rows(scores_cross)
    partials = jnp.einsum('rhqk,rkhd->rqhd', low(chance_cross), values_quarter, precision=HIGHEST)
    largest = lax.optimization_barrier(jnp.max(log_part, axis=0))
    log_all = largest + jnp.log(lax.optimization_barrier(jnp.sum(jnp.exp(log_part - largest), axis=0)))
    shares = jnp.exp(log_part - log_all)
    merged = lax.optimization_barrier(jnp.sum(jnp.transpose(shares, (0, 2, 1))[..., None] * partials, axis=0))
    merged = low(low_back(merged.reshape(inputs.shape)))
    after_cross = after_self + low_back(matmul(merged, block_columns(7, 1)) + vectors_low[11])
    normed_three = low(normalize(after_cross, vectors_low[4], vectors_low[5]))
    bias_up = vectors_low[13:17].reshape(FF)
    hidden = low_back(matmul(normed_three, block_columns(8, 4)) + bias_up)
    activated = low(jax.nn.gelu(hidden, approximate=True))
    result = after_cross + low_back(matmul(activated, block_columns(12, 4).T) + vectors_low[12])
    return result * live_rows[:, None]

def rotated_update(grad, weights, moment1, moment2, stats, bases):
    block_count = stats.shape[0]
    grads_three = grad.reshape(grad.shape[0], block_count, BLK)
    turned = jnp.einsum('dnb,nbc->dnc', grads_three, bases, precision=HIGHEST)
    first_moment = BETA_ONE * moment1.reshape(grads_three.shape) + (1.0 - BETA_ONE) * turned
    second_moment = BETA_TWO * moment2.reshape(grads_three.shape) + (1.0 - BETA_TWO) * turned * turned
    direction = first_moment / (1.0 - BETA_ONE ** STEP) / (jnp.sqrt(second_moment / (1.0 - BETA_TWO ** STEP)) + ADAM_EPS)
    returned = jnp.einsum('dnc,nbc->dnb', direction, bases, precision=HIGHEST).reshape(grad.shape)
    updated = weights - RATE * (returned + DECAY * weights)
    renewed = BETA_TWO * stats + (1.0 - BETA_TWO) * jnp.einsum('dnb,dnc->nbc', grads_three, grads_three, precision=HIGHEST)
    product = jnp.einsum('nbc,ncd->nbd', renewed, bases, precision=HIGHEST)
    gram_matrix = jnp.einsum('nbc,nbd->ncd', product, product, precision=HIGHEST)
    factor = jnp.linalg.cholesky(gram_matrix)
    solved = jax.scipy.linalg.solve_triangular(factor, jnp.swapaxes(product, 1, 2), lower=True)
    return (first_moment.reshape(grad.shape), second_moment.reshape(grad.shape), updated, renewed, jnp.swapaxes(solved, 1, 2))

def adam_update(grad, values, moment1, moment2):
    first_moment = BETA_ONE * moment1 + (1.0 - BETA_ONE) * grad
    second_moment = BETA_TWO * moment2 + (1.0 - BETA_TWO) * grad * grad
    updated = values - VECTOR_RATE * (first_moment / (1.0 - BETA_ONE ** STEP)) / (jnp.sqrt(second_moment / (1.0 - BETA_TWO ** STEP)) + ADAM_EPS)
    return (first_moment, second_moment, updated)

def reference(tokens, memory, page_lengths, slot_masks, upstream, weights, weight_average, weight_moment1, weight_moment2, stats, bases, vectors, vector_average, vector_moment1, vector_moment2):
    group_count = PAGES // N_MEM
    inputs = tokens.astype(jnp.float32).reshape(group_count, N_MEM, PAGE, D)
    memories = memory.astype(jnp.float32).reshape(group_count, N_MEM, MEMS, D)
    live_slots = slot_masks.reshape(group_count, N_MEM, MEMS)
    live_rows = (jnp.arange(PAGE)[None, :] < page_lengths[:, None]).astype(jnp.float32).reshape(group_count, N_MEM, PAGE)

    def forward(inputs, memories, weights, vectors):
        weights_low = low(weights)
        vectors_low = low(vectors)

        def group_step(running, item_tuple):
            outputs = jax.vmap(page_layer, in_axes=(0, 0, 0, 0, None, None))(item_tuple[0], item_tuple[1], item_tuple[2], item_tuple[3], weights_low, vectors_low)
            return (running, outputs)
        finished, outputs = lax.scan(jax.checkpoint(group_step), jnp.zeros((), jnp.float32), (inputs, memories, live_slots, live_rows))
        return outputs
    outputs, pullback = jax.vjp(forward, inputs, memories, weights, vectors)
    grad_inputs, grad_memory, grad_weights, grad_vectors = pullback(upstream.astype(jnp.float32).reshape(inputs.shape))
    weight_first, weight_second, new_weights, new_stats, new_bases = rotated_update(grad_weights, weights, weight_moment1, weight_moment2, stats, bases)
    new_average = AVERAGE * weight_average + (1.0 - AVERAGE) * new_weights
    vector_first, vector_second, new_vectors = adam_update(grad_vectors, vectors, vector_moment1, vector_moment2)
    new_vector_average = AVERAGE * vector_average + (1.0 - AVERAGE) * new_vectors
    return (outputs.reshape(TOKENS, D).astype(jnp.bfloat16), grad_inputs.reshape(TOKENS, D), grad_memory.reshape(PAGES, MEMS, D), grad_weights, weight_first, weight_second, new_weights, new_average, new_weights.astype(jnp.bfloat16), new_stats, new_bases, grad_vectors, vector_first, vector_second, new_vectors, new_vector_average, new_vectors.astype(jnp.bfloat16), grad_vectors[12])
```

```python
import functools

import jax
import jax.numpy as jnp
from jax import lax
from jax.experimental import pallas as pl
from jax.experimental.pallas import tpu as pltpu
from jax.sharding import PartitionSpec as P

HEADS = 16
HEAD = 64
BLK = 128
STEP = 10
LANES = 128
QUERY_ROWS = 256
SLOT_PAD = 160
VECTOR_PAD = 16
GROUPS = 4
AXES = ("seq", "mem")

F32 = jnp.float32
BF16 = jnp.bfloat16
HIGHEST = lax.Precision.HIGHEST
NORM_EPS = 1e-05
ADAM_EPS = 1e-08
BETA_ONE = 0.9
BETA_TWO = 0.95
RATE = 0.04
VECTOR_RATE = 0.4
DECAY = 0.01
AVERAGE = 0.999
MASKED = -1e30
CONTRACT_ROWS = (((0,), (0,)), ((), ()))
CONTRACT_LAST = (((1,), (1,)), ((), ()))


def dot(left, right):
    return jnp.dot(left, right, preferred_element_type=F32)


def dot_last(left, right):
    return lax.dot_general(left, right, CONTRACT_LAST, preferred_element_type=F32)


def dot_rows(left, right):
    return lax.dot_general(left, right, CONTRACT_ROWS, preferred_element_type=F32)


def normalize(values, scale_gain, offset):
    centre = jnp.mean(values, axis=-1, keepdims=True)
    centred = values - centre
    variance = jnp.mean(centred * centred, axis=-1, keepdims=True)
    return centred * lax.rsqrt(variance + NORM_EPS) * scale_gain + offset


def column_total(values):
    return jnp.sum(values.astype(F32), axis=0)


def causal_mask(scores):
    key_pos = lax.broadcasted_iota(jnp.int32, scores.shape, 0)
    query_pos = lax.broadcasted_iota(jnp.int32, scores.shape, 1)
    return jnp.where(key_pos <= query_pos, scores, MASKED)


def head_of_lane(shape):
    return lax.broadcasted_iota(jnp.int32, shape, 1) // HEAD


def one_head(values, lane_head, head):
    return jnp.where(lane_head == head, values, jnp.zeros_like(values))


def widen(bias, columns):
    return jnp.concatenate([bias] * (columns // LANES), axis=1)


def attention_forward_kernel(*refs, causal):
    if causal:
        q_ref, k_ref, v_ref, out_ref, log_ref = refs
    else:
        q_ref, k_ref, v_ref, bias_ref, out_ref, log_ref = refs
    keys = k_ref[...]
    key_count = keys.shape[0]
    row_count = q_ref.shape[0]
    values_turned = v_ref[...].T
    lane_head = head_of_lane(keys.shape)
    for block in range(row_count // QUERY_ROWS):
        rows = slice(block * QUERY_ROWS, (block + 1) * QUERY_ROWS)
        seen = (block + 1) * QUERY_ROWS if causal else key_count
        queries = q_ref[rows, :]
        outs = []
        for head in range(2):
            scores = dot_last(one_head(keys[:seen], lane_head[:seen], head), queries)
            if causal:
                last = causal_mask(scores[seen - QUERY_ROWS :])
                if seen > QUERY_ROWS:
                    last = jnp.concatenate([scores[: seen - QUERY_ROWS], last], axis=0)
                scores = last
            else:
                scores = scores + widen(bias_ref[...], QUERY_ROWS)
            largest = jnp.max(scores, axis=0, keepdims=True)
            raised = jnp.exp(scores - largest)
            summed = jnp.sum(raised, axis=0, keepdims=True)
            turned = values_turned[head * HEAD : (head + 1) * HEAD, :seen]
            outs.append(dot(turned, raised.astype(BF16)) / summed)
            log_ref[0, head : head + 1, rows] = largest + jnp.log(summed)
        out_ref[rows, :] = jnp.concatenate(outs, axis=0).T.astype(BF16)


def attention_backward_kernel(*refs, causal):
    if causal:
        q_ref, k_ref, v_ref, grad_ref, out_ref, log_ref = refs[:6]
    else:
        q_ref, k_ref, v_ref, grad_ref, out_ref, log_ref, bias_ref = refs[:7]
    dq_ref, dk_ref, dv_ref, chance_ref, score_ref = refs[-5:]
    keys = k_ref[...]
    values = v_ref[...]
    queries = q_ref[...]
    grads = grad_ref[...]
    key_count = keys.shape[0]
    row_count = queries.shape[0]
    keys_turned = keys.T
    product = (grads.astype(F32) * out_ref[...].astype(F32)).T
    inner = [
        jnp.sum(product[head * HEAD : (head + 1) * HEAD], axis=0, keepdims=True)
        for head in range(2)
    ]
    key_rows = chance_ref.shape[1]
    lane_head = head_of_lane((key_rows, LANES))
    for piece in range(key_count // key_rows):
        slots = slice(piece * key_rows, (piece + 1) * key_rows)
        first = piece * key_rows if causal else 0
        grad_keys = []
        grad_values = []
        for head in range(2):
            key_part = one_head(keys[slots], lane_head, head)
            value_part = one_head(values[slots], lane_head, head)
            for block in range(first // QUERY_ROWS, row_count // QUERY_ROWS):
                rows = slice(block * QUERY_ROWS, (block + 1) * QUERY_ROWS)
                scores = dot_last(key_part, queries[rows])
                if causal and block == piece:
                    scores = causal_mask(scores)
                if not causal:
                    scores = scores + widen(bias_ref[slots, :], QUERY_ROWS)
                chance = jnp.exp(scores - log_ref[0, head : head + 1, rows])
                chance_ref[head, :, rows] = chance.astype(BF16)
                grad_chance = dot_last(value_part, grads[rows])
                score_ref[head, slots, rows] = (
                    chance * (grad_chance - inner[head][:, rows])
                ).astype(BF16)
            grad_values.append(dot(chance_ref[head, :, first:], grads[first:]))
            grad_keys.append(dot(score_ref[head, slots, first:], queries[first:]))
        dk_ref[slots, :] = jnp.where(lane_head == 0, grad_keys[0], grad_keys[1]).astype(BF16)
        dv_ref[slots, :] = jnp.where(lane_head == 0, grad_values[0], grad_values[1]).astype(BF16)
    for block in range(row_count // QUERY_ROWS):
        rows = slice(block * QUERY_ROWS, (block + 1) * QUERY_ROWS)
        seen = (block + 1) * QUERY_ROWS if causal else key_count
        parts = [
            dot(
                keys_turned[head * HEAD : (head + 1) * HEAD, :seen],
                score_ref[head, :seen, rows],
            )
            for head in range(2)
        ]
        grad_query = jnp.concatenate(parts, axis=0).T.astype(BF16)
        dq_ref[rows, :] = (grad_query.astype(F32) * HEAD ** (-0.5)).astype(BF16)


def head_pair(row_count, first):
    return pl.BlockSpec((row_count, LANES), lambda pair: (0, first + pair))


def attention_forward(queries, keys, values, firsts, bias=None):
    causal = bias is None
    row_count = queries.shape[0]
    key_count = keys.shape[0]
    pairs = HEADS // 2
    in_specs = [
        head_pair(row_count, firsts[0]),
        head_pair(key_count, firsts[1]),
        head_pair(key_count, firsts[2]),
    ]
    operands = [queries, keys, values]
    if not causal:
        in_specs.append(pl.BlockSpec((key_count, LANES), lambda pair: (0, 0)))
        operands.append(bias)
    return pl.pallas_call(
        functools.partial(attention_forward_kernel, causal=causal),
        grid=(pairs,),
        in_specs=in_specs,
        out_specs=[
            head_pair(row_count, 0),
            pl.BlockSpec((1, 8, row_count), lambda pair: (pair, 0, 0)),
        ],
        out_shape=[
            jax.ShapeDtypeStruct((row_count, pairs * LANES), BF16),
            jax.ShapeDtypeStruct((pairs, 8, row_count), F32),
        ],
        compiler_params=pltpu.CompilerParams(vmem_limit_bytes=40 << 20),
        cost_estimate=pl.CostEstimate(
            flops=16 * row_count * key_count * HEADS * HEAD,
            bytes_accessed=8 << 20,
            transcendentals=row_count * key_count * HEADS,
        ),
    )(*operands)


def attention_backward(queries, keys, values, firsts, grads, outs, log_total, bias=None):
    causal = bias is None
    row_count = queries.shape[0]
    key_count = keys.shape[0]
    pairs = HEADS // 2
    key_rows = QUERY_ROWS if causal else LANES
    in_specs = [
        head_pair(row_count, firsts[0]),
        head_pair(key_count, firsts[1]),
        head_pair(key_count, firsts[2]),
        head_pair(row_count, 0),
        head_pair(row_count, 0),
        pl.BlockSpec((1, 8, row_count), lambda pair: (pair, 0, 0)),
    ]
    operands = [queries, keys, values, grads, outs, log_total]
    if not causal:
        in_specs.append(pl.BlockSpec((key_count, LANES), lambda pair: (0, 0)))
        operands.append(bias)
    return pl.pallas_call(
        functools.partial(attention_backward_kernel, causal=causal),
        grid=(pairs,),
        in_specs=in_specs,
        out_specs=[
            head_pair(row_count, 0),
            head_pair(key_count, 0),
            head_pair(key_count, 0),
        ],
        out_shape=[
            jax.ShapeDtypeStruct((row_count, pairs * LANES), BF16),
            jax.ShapeDtypeStruct((key_count, pairs * LANES), BF16),
            jax.ShapeDtypeStruct((key_count, pairs * LANES), BF16),
        ],
        scratch_shapes=[
            pltpu.VMEM((2, key_rows, row_count), BF16),
            pltpu.VMEM((2, key_count, row_count), BF16),
        ],
        compiler_params=pltpu.CompilerParams(vmem_limit_bytes=40 << 20),
        cost_estimate=pl.CostEstimate(
            flops=20 * row_count * key_count * HEADS * HEAD,
            bytes_accessed=16 << 20,
            transcendentals=row_count * key_count * HEADS,
        ),
    )(*operands)


def gelu_parts(values):
    slope = 0.7978845608028654
    square = values * values
    turned = jnp.tanh(slope * values * (1.0 + 0.044715 * square))
    weight = 0.5 * (1.0 + turned)
    derivative = weight + 0.5 * values * (1.0 - turned * turned) * (
        slope + (3.0 * 0.044715 * slope) * square
    )
    return values * weight, derivative


def feed_kernel(
    half_ref,
    low_ref,
    grad_ref,
    up_ref,
    down_ref,
    bias_ref,
    out_ref,
    back_ref,
    grad_up_ref,
    grad_down_ref,
    grad_bias_ref,
    low_turned,
    grad_turned,
    active_ref,
    hidden_ref,
):
    @pl.when(pl.program_id(0) == 0)
    def _():
        low_turned[...] = low_ref[...].T
        grad_turned[...] = grad_ref[...].T
        out_ref[...] = jnp.zeros_like(out_ref)
        back_ref[...] = jnp.zeros_like(back_ref)

    up = up_ref[...]
    down = down_ref[...]
    total = jnp.zeros((1, up.shape[1]), F32)
    pieces = low_ref.shape[0] // QUERY_ROWS
    for piece in range(pieces):
        rows = slice(piece * QUERY_ROWS, (piece + 1) * QUERY_ROWS)
        active, derivative = gelu_parts(dot(low_ref[rows, :], up) + bias_ref[0])
        active_low = active.astype(BF16)
        hidden_low = (derivative * dot(grad_ref[rows, :], down)).astype(BF16)
        active_ref[rows, :] = active_low
        hidden_ref[rows, :] = hidden_low
        total = total + jnp.sum(hidden_low.astype(F32), axis=0, keepdims=True)
        out_ref[rows, :] += dot_last(active_low, down)
        back_ref[rows, :] += dot_last(hidden_low, up)
    grad_bias_ref[0] = total
    for piece in range(low_turned.shape[0] // QUERY_ROWS):
        rows = slice(piece * QUERY_ROWS, (piece + 1) * QUERY_ROWS)
        grad_down_ref[0, rows, :] = dot(grad_turned[rows, :], active_ref[...]).astype(BF16)
        grad_up_ref[0, rows, :] = dot(low_turned[rows, :], hidden_ref[...]).astype(BF16)


def feed_half(half, low, grad, full_weights, bias, width):
    row_count, model = low.shape
    hidden = bias.shape[0]
    steps = hidden // (2 * width)
    up_first = 2 * hidden // width
    down_first = 3 * hidden // width
    whole = pl.BlockSpec(
        (row_count, model), lambda step, side: (0, 0), pipeline_mode=pl.Buffered(1)
    )
    total = pl.BlockSpec((row_count, model), lambda step, side: (0, 0))
    terms = pl.BlockSpec((1, model, width), lambda step, side: (step, 0, 0))
    return pl.pallas_call(
        feed_kernel,
        grid_spec=pltpu.PrefetchScalarGridSpec(
            num_scalar_prefetch=1,
            grid=(steps,),
            in_specs=[
                whole,
                whole,
                pl.BlockSpec((model, width), lambda step, side: (0, up_first + 2 * step + side[0])),
                pl.BlockSpec(
                    (model, width), lambda step, side: (0, down_first + 2 * step + side[0])
                ),
                pl.BlockSpec((1, 1, width), lambda step, side: (2 * step + side[0], 0, 0)),
            ],
            out_specs=[
                total,
                total,
                terms,
                terms,
                pl.BlockSpec((1, 1, width), lambda step, side: (step, 0, 0)),
            ],
            scratch_shapes=[
                pltpu.VMEM((model, row_count), BF16),
                pltpu.VMEM((model, row_count), BF16),
                pltpu.VMEM((row_count, width), BF16),
                pltpu.VMEM((row_count, width), BF16),
            ],
        ),
        out_shape=[
            jax.ShapeDtypeStruct((row_count, model), F32),
            jax.ShapeDtypeStruct((row_count, model), F32),
            jax.ShapeDtypeStruct((steps, model, width), BF16),
            jax.ShapeDtypeStruct((steps, model, width), BF16),
            jax.ShapeDtypeStruct((steps, 1, width), F32),
        ],
        compiler_params=pltpu.CompilerParams(vmem_limit_bytes=56 << 20),
        cost_estimate=pl.CostEstimate(
            flops=6 * row_count * model * hidden,
            bytes_accessed=40 << 20,
            transcendentals=row_count * hidden // 2,
        ),
    )(half, low, grad, full_weights, full_weights, bias.reshape(-1, 1, width))


def swap_bit(values, device_count, bit):
    return lax.ppermute(values, AXES, [(item, item ^ bit) for item in range(device_count)])


def total_of(terms):
    result = terms[0].astype(F32)
    for term in terms[1:]:
        result = result + term.astype(F32)
    return result


def halve(terms, own_bits, position, device, device_count):
    bit = own_bits[position]
    mine = (device // bit) % 2
    sent = total_of(
        [lax.dynamic_index_in_dim(term, 1 - mine, position, keepdims=False) for term in terms]
    ).astype(BF16)
    got = swap_bit(sent, device_count, bit)
    kept = [lax.dynamic_index_in_dim(term, mine, position, keepdims=False) for term in terms]
    return kept + [got], own_bits[:position] + own_bits[position + 1 :]


def fold_planes(terms, group, plane_size):
    near = []
    for inner in range(plane_size):
        for plane in range(GROUPS):
            if (plane ^ group) & 1:
                near.append((plane * plane_size + inner, (plane ^ 1) * plane_size + inner))
    got = lax.ppermute(total_of(terms).astype(BF16), AXES, near)
    terms = terms + [got]
    other = group ^ 2
    far = [
        (other * plane_size + inner, group * plane_size + inner) for inner in range(plane_size)
    ]
    got = lax.ppermute(total_of(terms).astype(BF16), AXES, far)
    return terms + [got]


def sum_to_plane(sent, kept, group, device, device_count):
    plane_size = device_count // GROUPS
    got = swap_bit(sent, device_count, 1)
    bits = []
    bit = plane_size // 2
    while bit > 1:
        bits.append(bit)
        bit //= 2
    rows = kept.shape[1]
    parts = []
    for part in range(2):
        first = part * (rows // 2)
        terms = [
            term[:, first : first + rows // 2].reshape((2,) * len(bits) + (rows // 2, -1))
            for term in (kept, got)
        ]
        left = list(bits)
        while left:
            position = 0 if part == 0 else len(left) - 1
            terms, left = halve(terms, left, position, device, device_count)
        parts.append(total_of(fold_planes(terms, group, plane_size)))
    return jnp.concatenate(parts, axis=0)


def column_half(values, half, width):
    rows = values.shape[0]
    pieces = values.reshape(rows, -1, 2, width)
    return lax.dynamic_index_in_dim(pieces, half, 2, keepdims=False).reshape(rows, -1)


def weight_half(pairs, half, width):
    terms = []
    for left, right in pairs:
        product = dot_rows(left, column_half(right, half, width)).astype(BF16)
        terms.append(jnp.swapaxes(product.reshape(product.shape[0], -1, width), 0, 1))
    return jnp.concatenate(terms, axis=0)


def rotated_update(grad, weights, moment1, moment2, stats, bases):
    block_count = stats.shape[0]
    grads_three = grad.reshape(grad.shape[0], block_count, BLK)
    turned = jnp.einsum("dnb,nbc->dnc", grads_three, bases, precision=HIGHEST)
    first_moment = BETA_ONE * moment1.reshape(grads_three.shape) + (1.0 - BETA_ONE) * turned
    second_moment = (
        BETA_TWO * moment2.reshape(grads_three.shape) + (1.0 - BETA_TWO) * turned * turned
    )
    direction = (
        first_moment
        / (1.0 - BETA_ONE**STEP)
        / (jnp.sqrt(second_moment / (1.0 - BETA_TWO**STEP)) + ADAM_EPS)
    )
    returned = jnp.einsum("dnc,nbc->dnb", direction, bases, precision=HIGHEST).reshape(grad.shape)
    updated = weights - RATE * (returned + DECAY * weights)
    renewed = BETA_TWO * stats + (1.0 - BETA_TWO) * jnp.einsum(
        "dnb,dnc->nbc", grads_three, grads_three, precision=HIGHEST
    )
    product = jnp.einsum("nbc,ncd->nbd", renewed, bases, precision=HIGHEST)
    gram_matrix = jnp.einsum("nbc,nbd->ncd", product, product, precision=HIGHEST)
    factor = jnp.linalg.cholesky(gram_matrix)
    solved = jax.scipy.linalg.solve_triangular(factor, jnp.swapaxes(product, 1, 2), lower=True)
    return (
        first_moment.reshape(grad.shape),
        second_moment.reshape(grad.shape),
        updated,
        renewed,
        jnp.swapaxes(solved, 1, 2),
    )


def adam_update(grad, values, moment1, moment2):
    first_moment = BETA_ONE * moment1 + (1.0 - BETA_ONE) * grad
    second_moment = BETA_TWO * moment2 + (1.0 - BETA_TWO) * grad * grad
    updated = values - VECTOR_RATE * (first_moment / (1.0 - BETA_ONE**STEP)) / (
        jnp.sqrt(second_moment / (1.0 - BETA_TWO**STEP)) + ADAM_EPS
    )
    return (first_moment, second_moment, updated)


def gather_parameters(weights, vectors, device_count):
    model, width = weights.shape
    vector_rows, vector_width = vectors.shape
    flat = vectors.astype(BF16).reshape(-1)
    flat = jnp.pad(flat, (0, VECTOR_PAD * width - flat.shape[0]))
    packed = jnp.concatenate([weights.astype(BF16), flat.reshape(VECTOR_PAD, width)], axis=0)
    full = lax.all_gather(packed, AXES, axis=1, tiled=True)
    tail = full[model:].reshape(VECTOR_PAD, device_count, width)
    tail = jnp.swapaxes(tail, 0, 1).reshape(device_count, -1)[:, : vector_rows * vector_width]
    tail = jnp.swapaxes(tail.reshape(device_count, vector_rows, vector_width), 0, 1)
    return full, tail.reshape(vector_rows, -1).astype(F32)


def local(
    tokens,
    memory,
    page_lengths,
    slot_masks,
    upstream,
    weights,
    weight_average,
    weight_moment1,
    weight_moment2,
    stats,
    bases,
    vectors,
    vector_average,
    vector_moment1,
    vector_moment2,
):
    row_count, model = tokens.shape
    width = weights.shape[1]
    group_size = lax.axis_size("mem")
    device_count = lax.axis_size("seq") * group_size
    device = lax.axis_index(AXES)
    member = lax.axis_index("mem")
    core = device % 2
    quarter = memory.shape[1]
    scale_q = HEAD ** (-0.5)
    pairs = HEADS // 2

    memory_padded = jnp.pad(memory, ((0, 0), (0, SLOT_PAD - quarter), (0, 0)))
    memory_here = lax.all_to_all(memory_padded, "mem", split_axis=0, concat_axis=0, tiled=True)
    memory_here = memory_here.reshape(group_size * SLOT_PAD, model)
    full_weights, vector_rows = gather_parameters(weights, vectors, device_count)

    def block_columns(first, count):
        return full_weights[:model, first * model : (first + count) * model]

    inputs = tokens.astype(F32)
    live_rows = (jnp.arange(row_count) < page_lengths[0]).astype(F32)[:, None]
    slots_here = lax.dynamic_slice_in_dim(slot_masks, member, 1, 0).reshape(group_size, quarter)
    slots_here = jnp.pad(slots_here, ((0, 0), (0, SLOT_PAD - quarter))).reshape(-1, 1)
    slot_bias = jnp.broadcast_to(
        jnp.where(slots_here > 0, 0.0, MASKED).astype(F32), (group_size * SLOT_PAD, LANES)
    )

    normed_one, pull_one = jax.vjp(normalize, inputs, vector_rows[0], vector_rows[1])
    low_one = normed_one.astype(BF16)
    queries_self = ((dot(low_one, block_columns(0, 1)) + vector_rows[6]) * scale_q).astype(BF16)
    keys_self = dot(low_one, block_columns(1, 1)).astype(BF16)
    values_self = (dot(low_one, block_columns(2, 1)) + vector_rows[7]).astype(BF16)
    attended, self_log = attention_forward(queries_self, keys_self, values_self, (0, 0, 0))
    after_self = inputs + dot(attended, block_columns(3, 1)) + vector_rows[8]
    normed_two, pull_two = jax.vjp(normalize, after_self, vector_rows[2], vector_rows[3])
    low_two = normed_two.astype(BF16)
    queries_cross = ((dot(low_two, block_columns(4, 1)) + vector_rows[9]) * scale_q).astype(BF16)
    keys_cross = dot(memory_here, block_columns(5, 1)).astype(BF16)
    values_cross = (dot(memory_here, block_columns(6, 1)) + vector_rows[10]).astype(BF16)
    merged, cross_log = attention_forward(
        queries_cross, keys_cross, values_cross, (0, 0, 0), slot_bias
    )
    after_cross = after_self + dot(merged, block_columns(7, 1)) + vector_rows[11]
    normed_three, pull_three = jax.vjp(normalize, after_cross, vector_rows[4], vector_rows[5])
    low_three = normed_three.astype(BF16)
    bias_up = vector_rows[13:17].reshape(-1)

    grad_result = upstream.astype(F32) * live_rows
    grad_low_three = grad_result.astype(BF16)
    away = (1 - core).reshape(1).astype(jnp.int32)
    here = core.reshape(1).astype(jnp.int32)
    out_a, back_a, up_sent, down_sent, bias_sent = feed_half(
        away, low_three, grad_low_three, full_weights, bias_up, width
    )
    out_b, back_b, up_kept, down_kept, bias_kept = feed_half(
        here, low_three, grad_low_three, full_weights, bias_up, width
    )
    group_two = sum_to_plane(up_sent, up_kept, 2, device, device_count)
    group_three = sum_to_plane(down_sent, down_kept, 3, device, device_count)
    result = (after_cross + (out_a + out_b) + vector_rows[12]) * live_rows
    mixed = result.astype(BF16)
    bias_even = jnp.where(core == 0, bias_kept, bias_sent)
    bias_odd = jnp.where(core == 0, bias_sent, bias_kept)
    grad_bias_up = jnp.concatenate([bias_even, bias_odd], axis=1).reshape(4, model)
    back_three, gain_three, shift_three = pull_three(back_a + back_b)

    grad_two = grad_result + back_three
    grad_low_two = grad_two.astype(BF16)
    grad_merged = dot_last(grad_low_two, block_columns(7, 1)).astype(BF16)
    grad_queries_cross, grad_keys_cross, grad_values_cross = attention_backward(
        queries_cross,
        keys_cross,
        values_cross,
        (0, 0, 0),
        grad_merged,
        merged,
        cross_log,
        slot_bias,
    )
    cross_pairs = (
        (low_two, grad_queries_cross),
        (memory_here, grad_keys_cross),
        (memory_here, grad_values_cross),
        (merged, grad_low_two),
    )
    group_one = sum_to_plane(
        weight_half(cross_pairs, 1 - core, width),
        weight_half(cross_pairs, core, width),
        1,
        device,
        device_count,
    )
    grad_normed_two = dot_last(grad_queries_cross, block_columns(4, 1))
    back_two, gain_two, shift_two = pull_two(grad_normed_two)

    grad_one = grad_two + back_two
    grad_low_one = grad_one.astype(BF16)
    grad_attended = dot_last(grad_low_one, block_columns(3, 1)).astype(BF16)
    grad_queries_self, grad_keys_self, grad_values_self = attention_backward(
        queries_self,
        keys_self,
        values_self,
        (0, 0, 0),
        grad_attended,
        attended,
        self_log,
    )
    self_pairs = (
        (low_one, grad_queries_self),
        (low_one, grad_keys_self),
        (low_one, grad_values_self),
        (attended, grad_low_one),
    )
    group_zero = sum_to_plane(
        weight_half(self_pairs, 1 - core, width),
        weight_half(self_pairs, core, width),
        0,
        device,
        device_count,
    )
    grad_normed_one = (
        dot_last(grad_queries_self, block_columns(0, 1))
        + dot_last(grad_keys_self, block_columns(1, 1))
        + dot_last(grad_values_self, block_columns(2, 1))
    )
    back_one, gain_one, shift_one = pull_one(grad_normed_one)
    input_grad = grad_one + back_one
    memory_back = dot_last(grad_keys_cross, block_columns(5, 1)) + dot_last(
        grad_values_cross, block_columns(6, 1)
    )
    memory_back = lax.all_to_all(
        memory_back.astype(BF16).reshape(group_size, SLOT_PAD, model),
        "mem",
        split_axis=0,
        concat_axis=0,
        tiled=True,
    )
    memory_back = memory_back[:, :quarter].astype(F32)

    vector_head = jnp.stack(
        [
            gain_one,
            shift_one,
            gain_two,
            shift_two,
            gain_three,
            shift_three,
            column_total(grad_queries_self),
            column_total(grad_values_self),
            column_total(grad_low_one),
            column_total(grad_queries_cross),
            column_total(grad_values_cross),
            column_total(grad_low_two),
            column_total(grad_low_three),
        ],
        axis=0,
    )
    vector_terms = jnp.concatenate([vector_head, grad_bias_up], axis=0)
    vector_grad = lax.psum_scatter(vector_terms, AXES, scatter_dimension=1, tiled=True)

    plane = device // (device_count // GROUPS)
    weight_grad = jnp.where(
        plane < 2,
        jnp.where(plane == 0, group_zero, group_one),
        jnp.where(plane == 2, group_two, group_three),
    )
    weight_first, weight_second, new_weights, new_stats, new_bases = rotated_update(
        weight_grad, weights, weight_moment1, weight_moment2, stats, bases
    )
    new_average = AVERAGE * weight_average + (1.0 - AVERAGE) * new_weights
    vector_first, vector_second, new_vectors = adam_update(
        vector_grad, vectors, vector_moment1, vector_moment2
    )
    new_vector_average = AVERAGE * vector_average + (1.0 - AVERAGE) * new_vectors
    return (
        mixed,
        input_grad,
        memory_back,
        weight_grad,
        weight_first,
        weight_second,
        new_weights,
        new_average,
        new_weights.astype(BF16),
        new_stats,
        new_bases,
        vector_grad,
        vector_first,
        vector_second,
        new_vectors,
        new_vector_average,
        new_vectors.astype(BF16),
        vector_grad[12],
    )


def solution(mesh):
    return jax.shard_map(
        local,
        mesh=mesh,
        in_specs=(
            P(("seq", "mem"), None),
            P("seq", "mem", None),
            P(("seq", "mem")),
            P("seq", None),
            P(("seq", "mem"), None),
            P(None, ("seq", "mem")),
            P(None, ("seq", "mem")),
            P(None, ("seq", "mem")),
            P(None, ("seq", "mem")),
            P(("seq", "mem"), None, None),
            P(("seq", "mem"), None, None),
            P(None, ("seq", "mem")),
            P(None, ("seq", "mem")),
            P(None, ("seq", "mem")),
            P(None, ("seq", "mem")),
        ),
        out_specs=(
            P(("seq", "mem"), None),
            P(("seq", "mem"), None),
            P("seq", "mem", None),
            P(None, ("seq", "mem")),
            P(None, ("seq", "mem")),
            P(None, ("seq", "mem")),
            P(None, ("seq", "mem")),
            P(None, ("seq", "mem")),
            P(None, ("seq", "mem")),
            P(("seq", "mem"), None, None),
            P(("seq", "mem"), None, None),
            P(None, ("seq", "mem")),
            P(None, ("seq", "mem")),
            P(None, ("seq", "mem")),
            P(None, ("seq", "mem")),
            P(None, ("seq", "mem")),
            P(None, ("seq", "mem")),
            P(("seq", "mem")),
        ),
        check_vma=False,
    )
```

```python
import functools

import jax
import jax.numpy as jnp
from jax import lax
from jax.experimental import pallas as pl
from jax.experimental.pallas import tpu as pltpu
from jax.sharding import PartitionSpec as P

HEADS = 16
HEAD = 64
BLK = 128
STEP = 10
LANES = 128
QUERY_ROWS = 256
SLOT_PAD = 160
VECTOR_PAD = 16
PANEL = 8
GROUPS = 4
AXES = ("seq", "mem")

F32 = jnp.float32
BF16 = jnp.bfloat16
HIGHEST = lax.Precision.HIGHEST
NORM_EPS = 1e-05
ADAM_EPS = 1e-08
BETA_ONE = 0.9
BETA_TWO = 0.95
RATE = 0.04
VECTOR_RATE = 0.4
DECAY = 0.01
AVERAGE = 0.999
MASKED = -1e30
CONTRACT_ROWS = (((0,), (0,)), ((), ()))
CONTRACT_LAST = (((1,), (1,)), ((), ()))


def dot(left, right):
    return jnp.dot(left, right, preferred_element_type=F32)


def dot_last(left, right):
    return lax.dot_general(left, right, CONTRACT_LAST, preferred_element_type=F32)


def dot_rows(left, right):
    return lax.dot_general(left, right, CONTRACT_ROWS, preferred_element_type=F32)


def normalize(values, scale_gain, offset):
    centre = jnp.mean(values, axis=-1, keepdims=True)
    centred = values - centre
    variance = jnp.mean(centred * centred, axis=-1, keepdims=True)
    return centred * lax.rsqrt(variance + NORM_EPS) * scale_gain + offset


def column_total(values):
    return jnp.sum(values.astype(F32), axis=0)


def causal_mask(scores):
    key_pos = lax.broadcasted_iota(jnp.int32, scores.shape, 0)
    query_pos = lax.broadcasted_iota(jnp.int32, scores.shape, 1)
    return jnp.where(key_pos <= query_pos, scores, MASKED)


def head_of_lane(shape):
    return lax.broadcasted_iota(jnp.int32, shape, 1) // HEAD


def one_head(values, lane_head, head):
    return jnp.where(lane_head == head, values, jnp.zeros_like(values))


def widen(bias, columns):
    return jnp.concatenate([bias] * (columns // LANES), axis=1)


def attention_forward_kernel(*refs, causal):
    if causal:
        q_ref, k_ref, v_ref, out_ref, log_ref = refs
    else:
        q_ref, k_ref, v_ref, bias_ref, out_ref, log_ref = refs
    keys = k_ref[...]
    key_count = keys.shape[0]
    row_count = q_ref.shape[0]
    values_turned = v_ref[...].T
    lane_head = head_of_lane(keys.shape)
    for block in range(row_count // QUERY_ROWS):
        rows = slice(block * QUERY_ROWS, (block + 1) * QUERY_ROWS)
        seen = (block + 1) * QUERY_ROWS if causal else key_count
        queries = q_ref[rows, :]
        outs = []
        for head in range(2):
            scores = dot_last(one_head(keys[:seen], lane_head[:seen], head), queries)
            if causal:
                last = causal_mask(scores[seen - QUERY_ROWS :])
                if seen > QUERY_ROWS:
                    last = jnp.concatenate([scores[: seen - QUERY_ROWS], last], axis=0)
                scores = last
            else:
                scores = scores + widen(bias_ref[...], QUERY_ROWS)
            largest = jnp.max(scores, axis=0, keepdims=True)
            raised = jnp.exp(scores - largest)
            summed = jnp.sum(raised, axis=0, keepdims=True)
            turned = values_turned[head * HEAD : (head + 1) * HEAD, :seen]
            outs.append(dot(turned, raised.astype(BF16)) / summed)
            log_ref[0, head : head + 1, rows] = largest + jnp.log(summed)
        out_ref[rows, :] = jnp.concatenate(outs, axis=0).T.astype(BF16)


def attention_backward_kernel(*refs, causal):
    _, q_ref, k_ref, v_ref, grad_ref, out_ref, log_ref = refs[:7]
    bias_ref = None if causal else refs[7]
    dq_ref, dk_ref, dv_ref, dq_half, dk_half, dv_half, chance_ref, score_ref = refs[-8:]
    keys = k_ref[...]
    values = v_ref[...]
    queries = q_ref[...]
    grads = grad_ref[...]
    key_count = keys.shape[0]
    row_count = queries.shape[0]
    keys_turned = keys.T
    product = (grads.astype(F32) * out_ref[...].astype(F32)).T
    inner = [
        jnp.sum(product[head * HEAD : (head + 1) * HEAD], axis=0, keepdims=True)
        for head in range(2)
    ]
    key_rows = chance_ref.shape[1]
    lane_head = head_of_lane((key_rows, LANES))
    for piece in range(key_count // key_rows):
        slots = slice(piece * key_rows, (piece + 1) * key_rows)
        first = piece * key_rows if causal else 0
        grad_keys = []
        grad_values = []
        for head in range(2):
            key_part = one_head(keys[slots], lane_head, head)
            value_part = one_head(values[slots], lane_head, head)
            for block in range(first // QUERY_ROWS, row_count // QUERY_ROWS):
                rows = slice(block * QUERY_ROWS, (block + 1) * QUERY_ROWS)
                scores = dot_last(key_part, queries[rows])
                if causal and block == piece:
                    scores = causal_mask(scores)
                if not causal:
                    scores = scores + widen(bias_ref[slots, :], QUERY_ROWS)
                chance = jnp.exp(scores - log_ref[0, head : head + 1, rows])
                chance_ref[head, :, rows] = chance.astype(BF16)
                grad_chance = dot_last(value_part, grads[rows])
                score_ref[head, slots, rows] = (
                    chance * (grad_chance - inner[head][:, rows])
                ).astype(BF16)
            grad_values.append(dot(chance_ref[head, :, first:], grads[first:]))
            grad_keys.append(dot(score_ref[head, slots, first:], queries[first:]))
        grad_key = jnp.where(lane_head == 0, grad_keys[0], grad_keys[1]).astype(BF16)
        grad_value = jnp.where(lane_head == 0, grad_values[0], grad_values[1]).astype(BF16)
        dk_ref[slots, :] = grad_key
        dk_half[slots, :] = grad_key
        dv_ref[slots, :] = grad_value
        dv_half[slots, :] = grad_value
    for block in range(row_count // QUERY_ROWS):
        rows = slice(block * QUERY_ROWS, (block + 1) * QUERY_ROWS)
        seen = (block + 1) * QUERY_ROWS if causal else key_count
        parts = [
            dot(
                keys_turned[head * HEAD : (head + 1) * HEAD, :seen],
                score_ref[head, :seen, rows],
            )
            for head in range(2)
        ]
        grad_query = jnp.concatenate(parts, axis=0).T.astype(BF16)
        grad_query = (grad_query.astype(F32) * HEAD ** (-0.5)).astype(BF16)
        dq_ref[rows, :] = grad_query
        dq_half[rows, :] = grad_query


def head_pair(row_count, first):
    return pl.BlockSpec((row_count, LANES), lambda pair: (0, first + pair))


def attention_forward(queries, keys, values, bias=None):
    causal = bias is None
    row_count = queries.shape[0]
    key_count = keys.shape[0]
    pairs = HEADS // 2
    in_specs = [
        head_pair(row_count, 0),
        head_pair(key_count, 0),
        head_pair(key_count, 0),
    ]
    operands = [queries, keys, values]
    if not causal:
        in_specs.append(pl.BlockSpec((key_count, LANES), lambda pair: (0, 0)))
        operands.append(bias)
    return pl.pallas_call(
        functools.partial(attention_forward_kernel, causal=causal),
        grid=(pairs,),
        in_specs=in_specs,
        out_specs=[
            head_pair(row_count, 0),
            pl.BlockSpec((1, 8, row_count), lambda pair: (pair, 0, 0)),
        ],
        out_shape=[
            jax.ShapeDtypeStruct((row_count, pairs * LANES), BF16),
            jax.ShapeDtypeStruct((pairs, 8, row_count), F32),
        ],
        compiler_params=pltpu.CompilerParams(vmem_limit_bytes=40 << 20),
        cost_estimate=pl.CostEstimate(
            flops=16 * row_count * key_count * HEADS * HEAD,
            bytes_accessed=8 << 20,
            transcendentals=row_count * key_count * HEADS,
        ),
    )(*operands)


def attention_backward(half, width, queries, keys, values, grads, outs, log_total, bias, whole):
    causal = bias is None
    row_count, model = queries.shape
    key_count = keys.shape[0]
    key_rows = QUERY_ROWS if causal else LANES
    per_unit = width // LANES
    steps = HEADS // 4

    def chosen(step, side):
        return (2 * (step // per_unit) + side[0]) * per_unit + step % per_unit

    def in_whole(count):
        return pl.BlockSpec((count, LANES), lambda step, side: (0, chosen(step, side)))

    def alone(count):
        return pl.BlockSpec((count, LANES), lambda step, side: (0, step))

    in_specs = [
        in_whole(row_count),
        in_whole(key_count),
        in_whole(key_count),
        in_whole(row_count),
        in_whole(row_count),
        pl.BlockSpec((1, 8, row_count), lambda step, side: (chosen(step, side), 0, 0)),
    ]
    operands = [queries, keys, values, grads, outs, log_total]
    if not causal:
        in_specs.append(pl.BlockSpec((key_count, LANES), lambda step, side: (0, 0)))
        operands.append(bias)
    aliases = {}
    if whole is not None:
        for item, array in enumerate(whole):
            aliases[1 + len(operands)] = item
            in_specs.append(pl.BlockSpec(memory_space=pl.ANY))
            operands.append(array)
    counts = (row_count, key_count, key_count)
    results = pl.pallas_call(
        functools.partial(attention_backward_kernel, causal=causal),
        grid_spec=pltpu.PrefetchScalarGridSpec(
            num_scalar_prefetch=1,
            grid=(steps,),
            in_specs=in_specs,
            out_specs=[in_whole(count) for count in counts] + [alone(count) for count in counts],
            scratch_shapes=[
                pltpu.VMEM((2, key_rows, row_count), BF16),
                pltpu.VMEM((2, key_count, row_count), BF16),
            ],
        ),
        out_shape=[jax.ShapeDtypeStruct((count, model), BF16) for count in counts]
        + [jax.ShapeDtypeStruct((count, model // 2), BF16) for count in counts],
        input_output_aliases=aliases,
        compiler_params=pltpu.CompilerParams(vmem_limit_bytes=40 << 20),
        cost_estimate=pl.CostEstimate(
            flops=10 * row_count * key_count * HEADS * HEAD,
            bytes_accessed=12 << 20,
            transcendentals=row_count * key_count * HEADS // 2,
        ),
    )(half, *operands)
    return results[:3], results[3:]


def gelu_parts(values):
    slope = 0.7978845608028654
    square = values * values
    turned = jnp.tanh(slope * values * (1.0 + 0.044715 * square))
    weight = 0.5 * (1.0 + turned)
    derivative = weight + 0.5 * values * (1.0 - turned * turned) * (
        slope + (3.0 * 0.044715 * slope) * square
    )
    return values * weight, derivative


def feed_kernel(
    half_ref,
    low_ref,
    grad_ref,
    up_ref,
    down_ref,
    bias_ref,
    out_ref,
    back_ref,
    grad_up_ref,
    grad_down_ref,
    grad_bias_ref,
    low_turned,
    grad_turned,
    active_ref,
    hidden_ref,
):
    @pl.when(pl.program_id(0) == 0)
    def _():
        low_turned[...] = low_ref[...].T
        grad_turned[...] = grad_ref[...].T
        out_ref[...] = jnp.zeros_like(out_ref)
        back_ref[...] = jnp.zeros_like(back_ref)

    up = up_ref[...]
    down = down_ref[...]
    total = jnp.zeros((1, up.shape[1]), F32)
    pieces = low_ref.shape[0] // QUERY_ROWS
    for piece in range(pieces):
        rows = slice(piece * QUERY_ROWS, (piece + 1) * QUERY_ROWS)
        active, derivative = gelu_parts(dot(low_ref[rows, :], up) + bias_ref[0])
        active_low = active.astype(BF16)
        hidden_low = (derivative * dot(grad_ref[rows, :], down)).astype(BF16)
        active_ref[rows, :] = active_low
        hidden_ref[rows, :] = hidden_low
        total = total + jnp.sum(hidden_low.astype(F32), axis=0, keepdims=True)
        out_ref[rows, :] += dot_last(active_low, down)
        back_ref[rows, :] += dot_last(hidden_low, up)
    grad_bias_ref[0] = total
    for piece in range(low_turned.shape[0] // QUERY_ROWS):
        rows = slice(piece * QUERY_ROWS, (piece + 1) * QUERY_ROWS)
        grad_down_ref[0, rows, :] = dot(grad_turned[rows, :], active_ref[...]).astype(BF16)
        grad_up_ref[0, rows, :] = dot(low_turned[rows, :], hidden_ref[...]).astype(BF16)


def feed_half(half, low, grad, full_weights, bias, width):
    row_count, model = low.shape
    hidden = bias.shape[0]
    steps = hidden // (2 * width)
    up_first = 2 * hidden // width
    down_first = 3 * hidden // width
    whole = pl.BlockSpec(
        (row_count, model), lambda step, side: (0, 0), pipeline_mode=pl.Buffered(1)
    )
    total = pl.BlockSpec((row_count, model), lambda step, side: (0, 0))
    terms = pl.BlockSpec((1, model, width), lambda step, side: (step, 0, 0))
    return pl.pallas_call(
        feed_kernel,
        grid_spec=pltpu.PrefetchScalarGridSpec(
            num_scalar_prefetch=1,
            grid=(steps,),
            in_specs=[
                whole,
                whole,
                pl.BlockSpec((model, width), lambda step, side: (0, up_first + 2 * step + side[0])),
                pl.BlockSpec(
                    (model, width), lambda step, side: (0, down_first + 2 * step + side[0])
                ),
                pl.BlockSpec((1, 1, width), lambda step, side: (2 * step + side[0], 0, 0)),
            ],
            out_specs=[
                total,
                total,
                terms,
                terms,
                pl.BlockSpec((1, 1, width), lambda step, side: (step, 0, 0)),
            ],
            scratch_shapes=[
                pltpu.VMEM((model, row_count), BF16),
                pltpu.VMEM((model, row_count), BF16),
                pltpu.VMEM((row_count, width), BF16),
                pltpu.VMEM((row_count, width), BF16),
            ],
        ),
        out_shape=[
            jax.ShapeDtypeStruct((row_count, model), F32),
            jax.ShapeDtypeStruct((row_count, model), F32),
            jax.ShapeDtypeStruct((steps, model, width), BF16),
            jax.ShapeDtypeStruct((steps, model, width), BF16),
            jax.ShapeDtypeStruct((steps, 1, width), F32),
        ],
        compiler_params=pltpu.CompilerParams(vmem_limit_bytes=56 << 20),
        cost_estimate=pl.CostEstimate(
            flops=6 * row_count * model * hidden,
            bytes_accessed=40 << 20,
            transcendentals=row_count * hidden // 2,
        ),
    )(half, low, grad, full_weights, full_weights, bias.reshape(-1, 1, width))


def swap_bit(values, device_count, bit):
    return lax.ppermute(values, AXES, [(item, item ^ bit) for item in range(device_count)])


def total_of(terms):
    result = terms[0].astype(F32)
    for term in terms[1:]:
        result = result + term.astype(F32)
    return result


def pinned(*values):
    return lax.optimization_barrier(values)


def begin_sum(kept, got, device_count):
    bits = []
    bit = device_count // GROUPS // 2
    while bit > 1:
        bits.append(bit)
        bit //= 2
    rows = kept.shape[1] // 2
    parts = []
    for part in range(2):
        terms = [
            term[:, part * rows : (part + 1) * rows].reshape((2,) * len(bits) + (rows, -1))
            for term in (kept, got)
        ]
        parts.append((terms, list(bits)))
    return parts


def halve_sends(parts, device):
    sends = []
    for part, (terms, bits) in enumerate(parts):
        position = 0 if part == 0 else len(bits) - 1
        other = 1 - (device // bits[position]) % 2
        sends.append(
            total_of(
                [lax.dynamic_index_in_dim(term, other, position, keepdims=False) for term in terms]
            ).astype(BF16)
        )
    return sends


def halve_swaps(sends, parts, device_count):
    swapped = []
    for part, (_, bits) in enumerate(parts):
        swapped.append(swap_bit(sends[part], device_count, bits[0 if part == 0 else -1]))
    return swapped


def halve_keeps(parts, swapped, device):
    result = []
    for part, (terms, bits) in enumerate(parts):
        position = 0 if part == 0 else len(bits) - 1
        mine = (device // bits[position]) % 2
        kept = [lax.dynamic_index_in_dim(term, mine, position, keepdims=False) for term in terms]
        result.append((kept + [swapped[part]], bits[:position] + bits[position + 1 :]))
    return result


def fold_sends(parts):
    return [total_of(terms).astype(BF16) for terms, _ in parts]


def fold_near(sends, group, plane_size):
    pairs = []
    for plane in range(GROUPS):
        if (plane ^ group) & 1:
            for inner in range(plane_size):
                pairs.append((plane * plane_size + inner, (plane ^ 1) * plane_size + inner))
    return [lax.ppermute(sent, AXES, pairs) for sent in sends]


def fold_far(sends, group, plane_size):
    other = group ^ 2
    pairs = [
        (other * plane_size + inner, group * plane_size + inner) for inner in range(plane_size)
    ]
    return [lax.ppermute(sent, AXES, pairs) for sent in sends]


def fold_keeps(parts, got):
    return [(terms + [item], bits) for (terms, bits), item in zip(parts, got, strict=True)]


def end_sum(parts):
    return jnp.concatenate([total_of(terms) for terms, _ in parts], axis=0)


def column_half(values, half, width):
    rows, columns = values.shape
    if columns == 2 * width:
        return lax.dynamic_slice_in_dim(values, half * width, width, 1)
    pieces = values.reshape(rows, -1, 2, width)
    return lax.dynamic_index_in_dim(pieces, half, 2, keepdims=False).reshape(rows, -1)


def weight_half(pairs, width):
    terms = []
    for left, right in pairs:
        product = dot_rows(left, right).astype(BF16)
        if product.shape[1] == width:
            terms.append(product[None])
        else:
            terms.append(jnp.swapaxes(product.reshape(product.shape[0], -1, width), 0, 1))
    return jnp.concatenate(terms, axis=0)


def dot_high(left, right, dims):
    return lax.dot_general(
        left, right, (dims, ((), ())), precision=HIGHEST, preferred_element_type=F32
    )


def update_kernel(
    grad_ref,
    weight_ref,
    average_ref,
    moment1_ref,
    moment2_ref,
    stats_ref,
    bases_ref,
    first_ref,
    second_ref,
    new_ref,
    new_average_ref,
    copy_ref,
    new_stats_ref,
    new_bases_ref,
    square_ref,
):
    blocks = stats_ref.shape[0]

    @pl.when(pl.program_id(0) == 0)
    def _():
        square_ref[...] = jnp.zeros_like(square_ref)

    for block in range(blocks):
        columns = slice(block * BLK, (block + 1) * BLK)
        grad = grad_ref[:, columns]
        basis = bases_ref[block]
        turned = dot_high(grad, basis, ((1,), (0,)))
        first = BETA_ONE * moment1_ref[:, columns] + (1.0 - BETA_ONE) * turned
        second = BETA_TWO * moment2_ref[:, columns] + (1.0 - BETA_TWO) * turned * turned
        first_ref[:, columns] = first
        second_ref[:, columns] = second
        direction = (
            first
            / (1.0 - BETA_ONE**STEP)
            / (jnp.sqrt(second / (1.0 - BETA_TWO**STEP)) + ADAM_EPS)
        )
        returned = dot_high(direction, basis, ((1,), (1,)))
        weight = weight_ref[:, columns]
        updated = weight - RATE * (returned + DECAY * weight)
        new_ref[:, columns] = updated
        new_average_ref[:, columns] = AVERAGE * average_ref[:, columns] + (1.0 - AVERAGE) * updated
        copy_ref[:, columns] = updated.astype(BF16)
        square_ref[block] += dot_high(grad, grad, ((0,), (0,)))

    @pl.when(pl.program_id(0) == pl.num_programs(0) - 1)
    def _():
        state = []
        for block in range(blocks):
            renewed = BETA_TWO * stats_ref[block] + (1.0 - BETA_TWO) * square_ref[block]
            new_stats_ref[block] = renewed
            product = dot_high(renewed, bases_ref[block], ((1,), (0,)))
            gram = dot_high(product, product, ((0,), (0,)))
            state.append(jnp.concatenate([gram, product.T], axis=1))
        row_index = lax.broadcasted_iota(jnp.int32, (PANEL, 2 * BLK), 0)
        solved = [[] for _ in range(blocks)]
        for panel in range(BLK // PANEL):
            tops = [item[:PANEL] for item in state]
            for row in range(PANEL):
                lane = panel * PANEL + row
                for block in range(blocks):
                    top = tops[block]
                    pivot = top[row : row + 1, lane : lane + 1]
                    inverse = lax.rsqrt(pivot)
                    inverse = inverse * (1.5 - 0.5 * pivot * inverse * inverse)
                    scaled = top[row : row + 1] * inverse
                    reduced = top - (top[:, lane : lane + 1] * inverse) * scaled
                    tops[block] = jnp.where(
                        row_index == row, scaled, jnp.where(row_index > row, reduced, top)
                    )
            for block in range(blocks):
                solved[block].append(tops[block][:, BLK:])
                if panel + 1 < BLK // PANEL:
                    left = tops[block][:, (panel + 1) * PANEL : BLK]
                    state[block] = state[block][PANEL:] - dot_high(
                        left, tops[block], ((0,), (0,))
                    )
        for block in range(blocks):
            new_bases_ref[block] = jnp.concatenate(solved[block], axis=0).T


def rotated_update(grad, weights, average, moment1, moment2, stats, bases):
    rows, width = grad.shape
    big = pl.BlockSpec((QUERY_ROWS, width), lambda step: (step, 0))
    small = pl.BlockSpec(stats.shape, lambda step: (0, 0, 0))
    wide = jax.ShapeDtypeStruct(grad.shape, F32)
    return pl.pallas_call(
        update_kernel,
        grid=(rows // QUERY_ROWS,),
        in_specs=[big] * 5 + [small] * 2,
        out_specs=[big] * 5 + [small] * 2,
        out_shape=[wide] * 4
        + [jax.ShapeDtypeStruct(grad.shape, BF16)]
        + [jax.ShapeDtypeStruct(stats.shape, F32)] * 2,
        scratch_shapes=[pltpu.VMEM(stats.shape, F32)],
        compiler_params=pltpu.CompilerParams(vmem_limit_bytes=40 << 20),
        cost_estimate=pl.CostEstimate(
            flops=36 * rows * width * BLK, bytes_accessed=42 * rows * width, transcendentals=0
        ),
    )(grad, weights, average, moment1, moment2, stats, bases)


def adam_update(grad, values, moment1, moment2):
    first_moment = BETA_ONE * moment1 + (1.0 - BETA_ONE) * grad
    second_moment = BETA_TWO * moment2 + (1.0 - BETA_TWO) * grad * grad
    updated = values - VECTOR_RATE * (first_moment / (1.0 - BETA_ONE**STEP)) / (
        jnp.sqrt(second_moment / (1.0 - BETA_TWO**STEP)) + ADAM_EPS
    )
    return (first_moment, second_moment, updated)


def gather_parameters(weights, vectors, device_count):
    model, width = weights.shape
    vector_rows, vector_width = vectors.shape
    flat = vectors.astype(BF16).reshape(-1)
    flat = jnp.pad(flat, (0, VECTOR_PAD * width - flat.shape[0]))
    packed = jnp.concatenate([weights.astype(BF16), flat.reshape(VECTOR_PAD, width)], axis=0)
    full = lax.all_gather(packed, AXES, axis=1, tiled=True)
    tail = full[model:].reshape(VECTOR_PAD, device_count, width)
    tail = jnp.swapaxes(tail, 0, 1).reshape(device_count, -1)[:, : vector_rows * vector_width]
    tail = jnp.swapaxes(tail.reshape(device_count, vector_rows, vector_width), 0, 1)
    return full, tail.reshape(vector_rows, -1).astype(F32)


def local(
    tokens,
    memory,
    page_lengths,
    slot_masks,
    upstream,
    weights,
    weight_average,
    weight_moment1,
    weight_moment2,
    stats,
    bases,
    vectors,
    vector_average,
    vector_moment1,
    vector_moment2,
):
    row_count, model = tokens.shape
    width = weights.shape[1]
    group_size = lax.axis_size("mem")
    device_count = lax.axis_size("seq") * group_size
    device = lax.axis_index(AXES)
    member = lax.axis_index("mem")
    core = device % 2
    quarter = memory.shape[1]
    scale_q = HEAD ** (-0.5)
    plane_size = device_count // GROUPS

    memory_padded = jnp.pad(memory, ((0, 0), (0, SLOT_PAD - quarter), (0, 0)))
    memory_here = lax.all_to_all(memory_padded, "mem", split_axis=0, concat_axis=0, tiled=True)
    memory_here = memory_here.reshape(group_size * SLOT_PAD, model)
    full_weights, vector_rows = gather_parameters(weights, vectors, device_count)

    def block_columns(first, count):
        return full_weights[:model, first * model : (first + count) * model]

    inputs = tokens.astype(F32)
    live_rows = (jnp.arange(row_count) < page_lengths[0]).astype(F32)[:, None]
    slots_here = lax.dynamic_slice_in_dim(slot_masks, member, 1, 0).reshape(group_size, quarter)
    slots_here = jnp.pad(slots_here, ((0, 0), (0, SLOT_PAD - quarter))).reshape(-1, 1)
    slot_bias = jnp.broadcast_to(
        jnp.where(slots_here > 0, 0.0, MASKED).astype(F32), (group_size * SLOT_PAD, LANES)
    )

    normed_one, pull_one = jax.vjp(normalize, inputs, vector_rows[0], vector_rows[1])
    low_one = normed_one.astype(BF16)
    queries_self = ((dot(low_one, block_columns(0, 1)) + vector_rows[6]) * scale_q).astype(BF16)
    keys_self = dot(low_one, block_columns(1, 1)).astype(BF16)
    values_self = (dot(low_one, block_columns(2, 1)) + vector_rows[7]).astype(BF16)
    attended, self_log = attention_forward(queries_self, keys_self, values_self)
    after_self = inputs + dot(attended, block_columns(3, 1)) + vector_rows[8]
    normed_two, pull_two = jax.vjp(normalize, after_self, vector_rows[2], vector_rows[3])
    low_two = normed_two.astype(BF16)
    queries_cross = ((dot(low_two, block_columns(4, 1)) + vector_rows[9]) * scale_q).astype(BF16)
    keys_cross = dot(memory_here, block_columns(5, 1)).astype(BF16)
    values_cross = (dot(memory_here, block_columns(6, 1)) + vector_rows[10]).astype(BF16)
    merged, cross_log = attention_forward(queries_cross, keys_cross, values_cross, slot_bias)
    after_cross = after_self + dot(merged, block_columns(7, 1)) + vector_rows[11]
    normed_three, pull_three = jax.vjp(normalize, after_cross, vector_rows[4], vector_rows[5])
    low_three = normed_three.astype(BF16)
    bias_up = vector_rows[13:17].reshape(-1)

    grad_result = upstream.astype(F32) * live_rows
    grad_low_three = grad_result.astype(BF16)
    away = (1 - core).reshape(1).astype(jnp.int32)
    here = core.reshape(1).astype(jnp.int32)
    out_a, back_a, up_sent, down_sent, bias_sent = feed_half(
        away, low_three, grad_low_three, full_weights, bias_up, width
    )
    up_got = swap_bit(up_sent, device_count, 1)
    down_got = swap_bit(down_sent, device_count, 1)
    low_three, up_sent, down_sent = pinned(low_three, up_sent, down_sent)
    out_b, back_b, up_kept, down_kept, bias_kept = feed_half(
        here, low_three, grad_low_three, full_weights, bias_up, width
    )
    out_b, back_b, up_kept, down_kept, up_got, down_got = pinned(
        out_b, back_b, up_kept, down_kept, up_got, down_got
    )
    up_parts = begin_sum(up_kept, up_got, device_count)
    down_parts = begin_sum(down_kept, down_got, device_count)
    up_sends = halve_sends(up_parts, device)
    down_sends = halve_sends(down_parts, device)
    up_sends, down_sends, back_b = pinned(up_sends, down_sends, back_b)
    up_swaps = halve_swaps(up_sends, up_parts, device_count)
    down_swaps = halve_swaps(down_sends, down_parts, device_count)

    result = (after_cross + (out_a + out_b) + vector_rows[12]) * live_rows
    mixed = result.astype(BF16)
    bias_even = jnp.where(core == 0, bias_kept, bias_sent)
    bias_odd = jnp.where(core == 0, bias_sent, bias_kept)
    grad_bias_up = jnp.concatenate([bias_even, bias_odd], axis=1).reshape(4, model)
    back_three, gain_three, shift_three = pull_three(back_a + back_b)

    grad_two = grad_result + back_three
    grad_low_two = grad_two.astype(BF16)
    grad_merged = dot_last(grad_low_two, block_columns(7, 1)).astype(BF16)
    cross_operands = (
        queries_cross,
        keys_cross,
        values_cross,
        grad_merged,
        merged,
        cross_log,
        slot_bias,
    )
    cross_whole, (queries_part, keys_part, values_part) = attention_backward(
        away, width, *cross_operands, None
    )
    cross_whole, (queries_own, keys_own, values_own) = attention_backward(
        here, width, *cross_operands, cross_whole
    )
    grad_queries_cross, grad_keys_cross, grad_values_cross = cross_whole
    cross_sent = weight_half(
        (
            (low_two, queries_part),
            (memory_here, keys_part),
            (memory_here, values_part),
            (merged, column_half(grad_low_two, 1 - core, width)),
        ),
        width,
    )
    up_swaps, down_swaps, cross_sent = pinned(up_swaps, down_swaps, cross_sent)
    cross_got = swap_bit(cross_sent, device_count, 1)
    up_parts = halve_keeps(up_parts, up_swaps, device)
    down_parts = halve_keeps(down_parts, down_swaps, device)
    up_sends = halve_sends(up_parts, device)
    down_sends = halve_sends(down_parts, device)
    up_sends, down_sends, queries_own = pinned(up_sends, down_sends, queries_own)
    up_swaps = halve_swaps(up_sends, up_parts, device_count)
    down_swaps = halve_swaps(down_sends, down_parts, device_count)
    cross_kept = weight_half(
        (
            (low_two, queries_own),
            (memory_here, keys_own),
            (memory_here, values_own),
            (merged, column_half(grad_low_two, core, width)),
        ),
        width,
    )
    grad_normed_two = dot_last(grad_queries_cross, block_columns(4, 1))
    back_two, gain_two, shift_two = pull_two(grad_normed_two)

    grad_one = grad_two + back_two
    grad_low_one = grad_one.astype(BF16)
    grad_attended = dot_last(grad_low_one, block_columns(3, 1)).astype(BF16)
    up_swaps, down_swaps, cross_got, cross_kept, grad_attended = pinned(
        up_swaps, down_swaps, cross_got, cross_kept, grad_attended
    )
    up_parts = halve_keeps(up_parts, up_swaps, device)
    down_parts = halve_keeps(down_parts, down_swaps, device)
    while up_parts[0][1]:
        up_sends = halve_sends(up_parts, device)
        down_sends = halve_sends(down_parts, device)
        up_swaps = halve_swaps(up_sends, up_parts, device_count)
        down_swaps = halve_swaps(down_sends, down_parts, device_count)
        up_parts = halve_keeps(up_parts, up_swaps, device)
        down_parts = halve_keeps(down_parts, down_swaps, device)
    cross_parts = begin_sum(cross_kept, cross_got, device_count)
    up_sends = fold_sends(up_parts)
    down_sends = fold_sends(down_parts)
    cross_sends = halve_sends(cross_parts, device)
    up_sends, down_sends, cross_sends, grad_attended = pinned(
        up_sends, down_sends, cross_sends, grad_attended
    )
    up_swaps = fold_near(up_sends, 2, plane_size)
    down_swaps = fold_near(down_sends, 3, plane_size)
    cross_swaps = halve_swaps(cross_sends, cross_parts, device_count)
    self_operands = (
        queries_self,
        keys_self,
        values_self,
        grad_attended,
        attended,
        self_log,
        None,
    )
    self_whole, (queries_part, keys_part, values_part) = attention_backward(
        away, width, *self_operands, None
    )
    self_sent = weight_half(
        (
            (low_one, queries_part),
            (low_one, keys_part),
            (low_one, values_part),
            (attended, column_half(grad_low_one, 1 - core, width)),
        ),
        width,
    )
    up_swaps, down_swaps, cross_swaps, self_sent = pinned(
        up_swaps, down_swaps, cross_swaps, self_sent
    )
    up_parts = fold_keeps(up_parts, up_swaps)
    down_parts = fold_keeps(down_parts, down_swaps)
    cross_parts = halve_keeps(cross_parts, cross_swaps, device)
    while cross_parts[0][1]:
        cross_sends = halve_sends(cross_parts, device)
        cross_swaps = halve_swaps(cross_sends, cross_parts, device_count)
        cross_parts = halve_keeps(cross_parts, cross_swaps, device)
    up_sends = fold_sends(up_parts)
    down_sends = fold_sends(down_parts)
    up_sends, down_sends, self_sent, self_whole = pinned(
        up_sends, down_sends, self_sent, self_whole
    )
    self_got = swap_bit(self_sent, device_count, 1)
    up_swaps = fold_far(up_sends, 2, plane_size)
    down_swaps = fold_far(down_sends, 3, plane_size)
    self_whole, (queries_own, keys_own, values_own) = attention_backward(
        here, width, *self_operands, self_whole
    )
    grad_queries_self, grad_keys_self, grad_values_self = self_whole
    self_kept = weight_half(
        (
            (low_one, queries_own),
            (low_one, keys_own),
            (low_one, values_own),
            (attended, column_half(grad_low_one, core, width)),
        ),
        width,
    )
    up_swaps, down_swaps, self_got, self_kept = pinned(up_swaps, down_swaps, self_got, self_kept)
    group_two = end_sum(fold_keeps(up_parts, up_swaps))
    group_three = end_sum(fold_keeps(down_parts, down_swaps))
    self_parts = begin_sum(self_kept, self_got, device_count)
    self_sends = halve_sends(self_parts, device)
    cross_sends = fold_sends(cross_parts)
    self_sends, cross_sends, grad_queries_self = pinned(self_sends, cross_sends, grad_queries_self)
    self_swaps = halve_swaps(self_sends, self_parts, device_count)
    cross_swaps = fold_near(cross_sends, 1, plane_size)
    grad_normed_one = (
        dot_last(grad_queries_self, block_columns(0, 1))
        + dot_last(grad_keys_self, block_columns(1, 1))
        + dot_last(grad_values_self, block_columns(2, 1))
    )
    back_one, gain_one, shift_one = pull_one(grad_normed_one)
    input_grad = grad_one + back_one
    self_swaps, cross_swaps, back_one = pinned(self_swaps, cross_swaps, back_one)
    self_parts = halve_keeps(self_parts, self_swaps, device)
    cross_parts = fold_keeps(cross_parts, cross_swaps)
    cross_sends = fold_sends(cross_parts)
    cross_swaps = fold_far(cross_sends, 1, plane_size)
    while self_parts[0][1]:
        self_sends = halve_sends(self_parts, device)
        self_swaps = halve_swaps(self_sends, self_parts, device_count)
        self_parts = halve_keeps(self_parts, self_swaps, device)
    group_one = end_sum(fold_keeps(cross_parts, cross_swaps))
    self_swaps = fold_near(fold_sends(self_parts), 0, plane_size)
    self_parts = fold_keeps(self_parts, self_swaps)
    self_swaps = fold_far(fold_sends(self_parts), 0, plane_size)
    group_zero = end_sum(fold_keeps(self_parts, self_swaps))
    memory_back = dot_last(grad_keys_cross, block_columns(5, 1)) + dot_last(
        grad_values_cross, block_columns(6, 1)
    )
    memory_back = lax.all_to_all(
        memory_back.astype(BF16).reshape(group_size, SLOT_PAD, model),
        "mem",
        split_axis=0,
        concat_axis=0,
        tiled=True,
    )
    memory_back = memory_back[:, :quarter].astype(F32)

    vector_head = jnp.stack(
        [
            gain_one,
            shift_one,
            gain_two,
            shift_two,
            gain_three,
            shift_three,
            column_total(grad_queries_self),
            column_total(grad_values_self),
            column_total(grad_low_one),
            column_total(grad_queries_cross),
            column_total(grad_values_cross),
            column_total(grad_low_two),
            column_total(grad_low_three),
        ],
        axis=0,
    )
    vector_terms = jnp.concatenate([vector_head, grad_bias_up], axis=0)
    vector_grad = lax.psum_scatter(vector_terms, AXES, scatter_dimension=1, tiled=True)

    plane = device // plane_size
    weight_grad = jnp.where(
        plane < 2,
        jnp.where(plane == 0, group_zero, group_one),
        jnp.where(plane == 2, group_two, group_three),
    )
    (
        weight_first,
        weight_second,
        new_weights,
        new_average,
        weights_copy,
        new_stats,
        new_bases,
    ) = rotated_update(
        weight_grad, weights, weight_average, weight_moment1, weight_moment2, stats, bases
    )
    vector_first, vector_second, new_vectors = adam_update(
        vector_grad, vectors, vector_moment1, vector_moment2
    )
    new_vector_average = AVERAGE * vector_average + (1.0 - AVERAGE) * new_vectors
    return (
        mixed,
        input_grad,
        memory_back,
        weight_grad,
        weight_first,
        weight_second,
        new_weights,
        new_average,
        weights_copy,
        new_stats,
        new_bases,
        vector_grad,
        vector_first,
        vector_second,
        new_vectors,
        new_vector_average,
        new_vectors.astype(BF16),
        vector_grad[12],
    )


def solution(mesh):
    return jax.shard_map(
        local,
        mesh=mesh,
        in_specs=(
            P(("seq", "mem"), None),
            P("seq", "mem", None),
            P(("seq", "mem")),
            P("seq", None),
            P(("seq", "mem"), None),
            P(None, ("seq", "mem")),
            P(None, ("seq", "mem")),
            P(None, ("seq", "mem")),
            P(None, ("seq", "mem")),
            P(("seq", "mem"), None, None),
            P(("seq", "mem"), None, None),
            P(None, ("seq", "mem")),
            P(None, ("seq", "mem")),
            P(None, ("seq", "mem")),
            P(None, ("seq", "mem")),
        ),
        out_specs=(
            P(("seq", "mem"), None),
            P(("seq", "mem"), None),
            P("seq", "mem", None),
            P(None, ("seq", "mem")),
            P(None, ("seq", "mem")),
            P(None, ("seq", "mem")),
            P(None, ("seq", "mem")),
            P(None, ("seq", "mem")),
            P(None, ("seq", "mem")),
            P(("seq", "mem"), None, None),
            P(("seq", "mem"), None, None),
            P(None, ("seq", "mem")),
            P(None, ("seq", "mem")),
            P(None, ("seq", "mem")),
            P(None, ("seq", "mem")),
            P(None, ("seq", "mem")),
            P(None, ("seq", "mem")),
            P(("seq", "mem")),
        ),
        check_vma=False,
    )
```

```python
import functools

import jax
import jax.numpy as jnp
from jax import lax
from jax.experimental import pallas as pl
from jax.experimental.pallas import tpu as pltpu
from jax.sharding import PartitionSpec as P

HEADS = 16
HEAD = 64
BLK = 128
STEP = 10
LANES = 128
QUERY_ROWS = 256
FORWARD_ROWS = 512
SLOT_PAD = 160
PANEL = 8
GROUPS = 4
AXES = ("seq", "mem")
SMALL = pl.CostEstimate(flops=1 << 20, bytes_accessed=1 << 16, transcendentals=0)

F32 = jnp.float32
BF16 = jnp.bfloat16
HIGHEST = lax.Precision.HIGHEST
NORM_EPS = 1e-05
ADAM_EPS = 1e-08
BETA_ONE = 0.9
BETA_TWO = 0.95
RATE = 0.04
VECTOR_RATE = 0.4
DECAY = 0.01
AVERAGE = 0.999
MASKED = -1e30
CONTRACT_ROWS = (((0,), (0,)), ((), ()))
CONTRACT_LAST = (((1,), (1,)), ((), ()))


def dot(left, right):
    return jnp.dot(left, right, preferred_element_type=F32)


def dot_last(left, right):
    return lax.dot_general(left, right, CONTRACT_LAST, preferred_element_type=F32)


def dot_rows(left, right):
    return lax.dot_general(left, right, CONTRACT_ROWS, preferred_element_type=F32)


def normalize(values, scale_gain, offset):
    centre = jnp.mean(values, axis=-1, keepdims=True)
    centred = values - centre
    variance = jnp.mean(centred * centred, axis=-1, keepdims=True)
    return centred * lax.rsqrt(variance + NORM_EPS) * scale_gain + offset


def column_total(values):
    return jnp.sum(values.astype(F32), axis=0)


def causal_mask(scores, first_key, first_query):
    key_pos = lax.broadcasted_iota(jnp.int32, scores.shape, 0) + first_key
    query_pos = lax.broadcasted_iota(jnp.int32, scores.shape, 1) + first_query
    return jnp.where(key_pos <= query_pos, scores, MASKED)


def head_of_lane(shape):
    return lax.broadcasted_iota(jnp.int32, shape, 1) // HEAD


def one_head(values, lane_head, head):
    return jnp.where(lane_head == head, values, jnp.zeros_like(values))


def widen(bias, columns):
    return jnp.concatenate([bias] * (columns // LANES), axis=1)


def attention_forward_kernel(*refs, causal):
    if causal:
        q_ref, k_ref, v_ref, out_ref, log_ref = refs
    else:
        q_ref, k_ref, v_ref, bias_ref, out_ref, log_ref = refs
    keys = k_ref[...]
    key_count = keys.shape[0]
    values_turned = v_ref[...].T
    lane_head = head_of_lane(keys.shape)
    key_heads = [one_head(keys, lane_head, head) for head in range(2)]
    units = [
        (block, head) for block in range(q_ref.shape[0] // FORWARD_ROWS) for head in range(2)
    ]

    def scores_of(unit):
        block, head = unit
        seen = (block + 1) * FORWARD_ROWS if causal else key_count
        queries = q_ref[block * FORWARD_ROWS : (block + 1) * FORWARD_ROWS, :]
        scores = dot_last(key_heads[head][:seen], queries)
        if not causal:
            return scores + widen(bias_ref[...], FORWARD_ROWS)
        last = causal_mask(scores[seen - FORWARD_ROWS :], 0, 0)
        if seen == FORWARD_ROWS:
            return last
        return jnp.concatenate([scores[: seen - FORWARD_ROWS], last], axis=0)

    scores = scores_of(units[0])
    outs = []
    for item, (block, head) in enumerate(units):
        later = scores_of(units[item + 1]) if item + 1 < len(units) else None
        rows = slice(block * FORWARD_ROWS, (block + 1) * FORWARD_ROWS)
        largest = jnp.max(scores, axis=0, keepdims=True)
        raised = jnp.exp(scores - largest)
        summed = jnp.sum(raised, axis=0, keepdims=True)
        turned = values_turned[head * HEAD : (head + 1) * HEAD, : scores.shape[0]]
        outs.append(dot(turned, raised.astype(BF16)) / summed)
        log_ref[0, head : head + 1, rows] = largest + jnp.log(summed)
        if head == 1:
            out_ref[rows, :] = jnp.concatenate(outs, axis=0).T.astype(BF16)
            outs = []
        scores = later


def attention_backward_kernel(*refs, causal):
    _, q_ref, k_ref, v_ref, grad_ref, out_ref, log_ref = refs[:7]
    bias_ref = None if causal else refs[7]
    dq_ref, dk_ref, dv_ref, dq_half, dk_half, dv_half, chance_ref, score_ref = refs[-8:]
    keys = k_ref[...]
    values = v_ref[...]
    key_count = keys.shape[0]
    row_count = q_ref.shape[0]
    keys_turned = keys.T
    product = (grad_ref[...].astype(F32) * out_ref[...].astype(F32)).T
    inner = [
        jnp.sum(product[head * HEAD : (head + 1) * HEAD], axis=0, keepdims=True)
        for head in range(2)
    ]
    slots_of = chance_ref.shape[0]
    key_rows = chance_ref.shape[1]
    lane_head = head_of_lane((key_rows, LANES))
    blocks = row_count // QUERY_ROWS
    units = [
        (piece, head, block)
        for piece in range(key_count // key_rows)
        for head in range(2)
        for block in range(piece * key_rows // QUERY_ROWS if causal else 0, blocks)
    ]

    def products_of(unit):
        piece, head, block = unit
        slots = slice(piece * key_rows, (piece + 1) * key_rows)
        rows = slice(block * QUERY_ROWS, (block + 1) * QUERY_ROWS)
        return (
            dot_last(one_head(keys[slots], lane_head, head), q_ref[rows, :]),
            dot_last(one_head(values[slots], lane_head, head), grad_ref[rows, :]),
        )

    even_heads = {}

    def finish(piece, head):
        slots = slice(piece * key_rows, (piece + 1) * key_rows)
        first = piece * key_rows if causal else 0
        kept = chance_ref[(2 * piece + head) % slots_of, :, first:]
        grad_value = dot(kept, grad_ref[first:, :])
        grad_key = dot(score_ref[head, slots, first:], q_ref[first:, :])
        if head == 0:
            even_heads[piece] = (grad_key, grad_value)
            return
        even_key, even_value = even_heads.pop(piece)
        grad_key = jnp.where(lane_head == 0, even_key, grad_key).astype(BF16)
        grad_value = jnp.where(lane_head == 0, even_value, grad_value).astype(BF16)
        dk_ref[slots, :] = grad_key
        dk_half[slots, :] = grad_key
        dv_ref[slots, :] = grad_value
        dv_half[slots, :] = grad_value

    current = products_of(units[0])
    ended = None
    for item, (piece, head, block) in enumerate(units):
        later = products_of(units[item + 1]) if item + 1 < len(units) else None
        if ended is not None:
            finish(*ended)
            ended = None
        scores, grad_chance = current
        slots = slice(piece * key_rows, (piece + 1) * key_rows)
        rows = slice(block * QUERY_ROWS, (block + 1) * QUERY_ROWS)
        if not causal:
            scores = scores + widen(bias_ref[slots, :], QUERY_ROWS)
        elif (piece + 1) * key_rows > block * QUERY_ROWS:
            scores = causal_mask(scores, piece * key_rows, block * QUERY_ROWS)
        chance = jnp.exp(scores - log_ref[0, head : head + 1, rows])
        chance_ref[(2 * piece + head) % slots_of, :, rows] = chance.astype(BF16)
        score_ref[head, slots, rows] = (chance * (grad_chance - inner[head][:, rows])).astype(BF16)
        if block == blocks - 1:
            ended = (piece, head)
        current = later
    finish(*ended)
    for block in range(blocks):
        rows = slice(block * QUERY_ROWS, (block + 1) * QUERY_ROWS)
        seen = (block + 1) * QUERY_ROWS if causal else key_count
        parts = [
            dot(
                keys_turned[head * HEAD : (head + 1) * HEAD, :seen],
                score_ref[head, :seen, rows],
            )
            for head in range(2)
        ]
        grad_query = jnp.concatenate(parts, axis=0).T.astype(BF16)
        grad_query = (grad_query.astype(F32) * HEAD ** (-0.5)).astype(BF16)
        dq_ref[rows, :] = grad_query
        dq_half[rows, :] = grad_query


def head_pair(row_count, first):
    return pl.BlockSpec((row_count, LANES), lambda pair: (0, first + pair))


def attention_forward(queries, keys, values, firsts, bias=None):
    causal = bias is None
    row_count = queries.shape[0]
    key_count = keys.shape[0]
    pairs = HEADS // 2
    in_specs = [
        head_pair(row_count, firsts[0]),
        head_pair(key_count, firsts[1]),
        head_pair(key_count, firsts[2]),
    ]
    operands = [queries, keys, values]
    if not causal:
        in_specs.append(pl.BlockSpec((key_count, LANES), lambda pair: (0, 0)))
        operands.append(bias)
    return pl.pallas_call(
        functools.partial(attention_forward_kernel, causal=causal),
        grid=(pairs,),
        in_specs=in_specs,
        out_specs=[
            head_pair(row_count, 0),
            pl.BlockSpec((1, 8, row_count), lambda pair: (pair, 0, 0)),
        ],
        out_shape=[
            jax.ShapeDtypeStruct((row_count, pairs * LANES), BF16),
            jax.ShapeDtypeStruct((pairs, 8, row_count), F32),
        ],
        compiler_params=pltpu.CompilerParams(vmem_limit_bytes=40 << 20),
        cost_estimate=SMALL,
    )(*operands)


def attention_backward(
    half, width, queries, keys, values, firsts, grads, outs, log_total, bias, whole
):
    causal = bias is None
    row_count, model = grads.shape
    key_count = keys.shape[0]
    key_rows = QUERY_ROWS if causal else key_count // 2
    per_unit = width // LANES
    steps = HEADS // 4

    def chosen(step, side):
        return (2 * (step // per_unit) + side[0]) * per_unit + step % per_unit

    def in_whole(count, first=0):
        return pl.BlockSpec((count, LANES), lambda step, side: (0, first + chosen(step, side)))

    def alone(count):
        return pl.BlockSpec((count, LANES), lambda step, side: (0, step))

    in_specs = [
        in_whole(row_count, firsts[0]),
        in_whole(key_count, firsts[1]),
        in_whole(key_count, firsts[2]),
        in_whole(row_count),
        in_whole(row_count),
        pl.BlockSpec((1, 8, row_count), lambda step, side: (chosen(step, side), 0, 0)),
    ]
    operands = [queries, keys, values, grads, outs, log_total]
    if not causal:
        in_specs.append(pl.BlockSpec((key_count, LANES), lambda step, side: (0, 0)))
        operands.append(bias)
    aliases = {}
    if whole is not None:
        for item, array in enumerate(whole):
            aliases[1 + len(operands)] = item
            in_specs.append(pl.BlockSpec(memory_space=pl.ANY))
            operands.append(array)
    counts = (row_count, key_count, key_count)
    results = pl.pallas_call(
        functools.partial(attention_backward_kernel, causal=causal),
        grid_spec=pltpu.PrefetchScalarGridSpec(
            num_scalar_prefetch=1,
            grid=(steps,),
            in_specs=in_specs,
            out_specs=[in_whole(count) for count in counts] + [alone(count) for count in counts],
            scratch_shapes=[
                pltpu.VMEM((4, key_rows, row_count), BF16),
                pltpu.VMEM((2, key_count, row_count), BF16),
            ],
        ),
        out_shape=[jax.ShapeDtypeStruct((count, model), BF16) for count in counts]
        + [jax.ShapeDtypeStruct((count, model // 2), BF16) for count in counts],
        input_output_aliases=aliases,
        compiler_params=pltpu.CompilerParams(vmem_limit_bytes=40 << 20),
        cost_estimate=SMALL,
    )(half, *operands)
    return results[:3], results[3:]


def gelu_parts(values):
    slope = 0.7978845608028654
    square = values * values
    turned = jnp.tanh(slope * values * (1.0 + 0.044715 * square))
    weight = 0.5 * (1.0 + turned)
    derivative = weight + 0.5 * values * (1.0 - turned * turned) * (
        slope + (3.0 * 0.044715 * slope) * square
    )
    return values * weight, derivative


def feed_kernel(*refs, norm):
    refs = list(refs[1:])
    values_ref = refs.pop(0)
    if norm:
        gain_ref = refs.pop(0)
        shift_ref = refs.pop(0)
    grad_ref, up_ref, down_ref, bias_ref = refs[:4]
    out_ref, back_ref, grad_up_ref, grad_down_ref, grad_bias_ref = refs[4:9]
    low_ref = refs[9] if norm else values_ref
    low_turned, grad_turned, active_ref, hidden_ref = refs[-4:]

    @pl.when(pl.program_id(0) == 0)
    def _():
        if norm:
            for first in range(0, values_ref.shape[0], QUERY_ROWS):
                rows = slice(first, first + QUERY_ROWS)
                low_ref[rows, :] = normalize(
                    values_ref[rows, :], gain_ref[...], shift_ref[...]
                ).astype(BF16)
        low_turned[...] = low_ref[...].T
        grad_turned[...] = grad_ref[...].T
        out_ref[...] = jnp.zeros_like(out_ref)
        back_ref[...] = jnp.zeros_like(back_ref)

    up = up_ref[0]
    down = down_ref[0]
    total = jnp.zeros((1, up.shape[1]), F32)
    pieces = low_ref.shape[0] // QUERY_ROWS
    for piece in range(pieces):
        rows = slice(piece * QUERY_ROWS, (piece + 1) * QUERY_ROWS)
        active, derivative = gelu_parts(dot(low_ref[rows, :], up) + bias_ref[0])
        active_low = active.astype(BF16)
        hidden_low = (derivative * dot(grad_ref[rows, :], down)).astype(BF16)
        active_ref[rows, :] = active_low
        hidden_ref[rows, :] = hidden_low
        total = total + jnp.sum(hidden_low.astype(F32), axis=0, keepdims=True)
        out_ref[rows, :] += dot_last(active_low, down)
        back_ref[rows, :] += dot_last(hidden_low, up)
    grad_bias_ref[0] = total
    for piece in range(low_turned.shape[0] // QUERY_ROWS):
        rows = slice(piece * QUERY_ROWS, (piece + 1) * QUERY_ROWS)
        grad_down_ref[0, rows, :] = dot(grad_turned[rows, :], active_ref[...]).astype(BF16)
        grad_up_ref[0, rows, :] = dot(low_turned[rows, :], hidden_ref[...]).astype(BF16)


def feed_half(place, values, grad, ups, downs, bias, norm=None):
    row_count, model = values.shape
    steps, _, width = ups.shape

    def whole(shape):
        return pl.BlockSpec(shape, lambda step, place: (0, 0), pipeline_mode=pl.Buffered(1))

    total = pl.BlockSpec((row_count, model), lambda step, place: (0, 0))
    chunk = pl.BlockSpec((1, model, width), lambda step, place: (step, 0, 0))
    in_specs = [whole((row_count, model))]
    operands = [values]
    out_specs = [
        total,
        total,
        chunk,
        chunk,
        pl.BlockSpec((1, 1, width), lambda step, place: (step ^ place[1], 0, 0)),
    ]
    out_shape = [
        jax.ShapeDtypeStruct((row_count, model), F32),
        jax.ShapeDtypeStruct((row_count, model), F32),
        jax.ShapeDtypeStruct((steps, model, width), BF16),
        jax.ShapeDtypeStruct((steps, model, width), BF16),
        jax.ShapeDtypeStruct((steps, 1, width), F32),
    ]
    if norm is not None:
        in_specs += [whole((1, model))] * 2
        operands += [norm[0].reshape(1, model), norm[1].reshape(1, model)]
        out_specs.append(total)
        out_shape.append(jax.ShapeDtypeStruct((row_count, model), BF16))
    in_specs += [
        whole((row_count, model)),
        chunk,
        chunk,
        pl.BlockSpec((1, 1, width), lambda step, place: (2 * (step ^ place[1]) + place[0], 0, 0)),
    ]
    operands += [grad, ups, downs, bias.reshape(-1, 1, width)]
    return pl.pallas_call(
        functools.partial(feed_kernel, norm=norm is not None),
        grid_spec=pltpu.PrefetchScalarGridSpec(
            num_scalar_prefetch=1,
            grid=(steps,),
            in_specs=in_specs,
            out_specs=out_specs,
            scratch_shapes=[
                pltpu.VMEM((model, row_count), BF16),
                pltpu.VMEM((model, row_count), BF16),
                pltpu.VMEM((row_count, width), BF16),
                pltpu.VMEM((row_count, width), BF16),
            ],
        ),
        out_shape=out_shape,
        compiler_params=pltpu.CompilerParams(vmem_limit_bytes=58 << 20),
        cost_estimate=SMALL,
    )(place, *operands)


def norm_back_kernel(*refs, count):
    values_ref, gain_ref, stream_ref = refs[:3]
    grad_refs = refs[3 : 3 + count]
    out_ref, low_ref, sums_ref = refs[3 + count :]
    values = values_ref[...].astype(F32)
    grad = grad_refs[0][...]
    for grad_ref in grad_refs[1:]:
        grad = grad + grad_ref[...]
    centred = values - jnp.mean(values, axis=-1, keepdims=True)
    inverse = lax.rsqrt(jnp.mean(centred * centred, axis=-1, keepdims=True) + NORM_EPS)
    normal = centred * inverse
    scaled = grad * gain_ref[...]
    product = scaled * normal
    back = inverse * (
        scaled
        - jnp.mean(scaled, axis=-1, keepdims=True)
        - normal * jnp.mean(product, axis=-1, keepdims=True)
    )
    result = stream_ref[...].astype(F32) + back
    low = result.astype(BF16)
    out_ref[...] = result
    low_ref[...] = low

    @pl.when(pl.program_id(0) == 0)
    def _():
        sums_ref[...] = jnp.zeros_like(sums_ref)

    sums_ref[0:1, :] += jnp.sum(grad * normal, axis=0, keepdims=True)
    sums_ref[1:2, :] += jnp.sum(grad, axis=0, keepdims=True)
    sums_ref[2:3, :] += jnp.sum(low.astype(F32), axis=0, keepdims=True)
    sums_ref[3:4, :] += jnp.sum(stream_ref[...].astype(F32), axis=0, keepdims=True)


def norm_back(values, gain, stream, grads):
    row_count, model = values.shape
    panel = pl.BlockSpec((QUERY_ROWS, model), lambda step: (step, 0))
    return pl.pallas_call(
        functools.partial(norm_back_kernel, count=len(grads)),
        grid=(row_count // QUERY_ROWS,),
        in_specs=[panel, pl.BlockSpec((1, model), lambda step: (0, 0)), panel]
        + [panel] * len(grads),
        out_specs=[panel, panel, pl.BlockSpec((8, model), lambda step: (0, 0))],
        out_shape=[
            jax.ShapeDtypeStruct((row_count, model), F32),
            jax.ShapeDtypeStruct((row_count, model), BF16),
            jax.ShapeDtypeStruct((8, model), F32),
        ],
        compiler_params=pltpu.CompilerParams(vmem_limit_bytes=40 << 20),
        cost_estimate=SMALL,
    )(values, gain.reshape(1, model), stream, *grads)


def project_kernel(*refs, norm, residual):
    refs = list(refs[1:])
    values_ref = refs.pop(0)
    if norm:
        gain_ref = refs.pop(0)
        shift_ref = refs.pop(0)
    here_ref, away_ref, bias_ref, scale_ref = refs[:4]
    refs = refs[4:]
    if residual:
        residual_ref = refs.pop(0)
    out_ref = refs.pop(0)
    source = values_ref
    if norm:
        low_ref = refs.pop(0)
        source = low_ref

        @pl.when((pl.program_id(0) == 0) & (pl.program_id(1) == 0))
        def _():
            for first in range(0, values_ref.shape[0], QUERY_ROWS):
                rows = slice(first, first + QUERY_ROWS)
                low_ref[rows, :] = normalize(
                    values_ref[rows, :].astype(F32), gain_ref[...], shift_ref[...]
                ).astype(BF16)

    def product(columns_ref):
        columns = columns_ref[0]
        row_count = values_ref.shape[0]
        step = min(QUERY_ROWS, row_count // 2)
        for first in range(0, row_count, step):
            rows = slice(first, first + step)
            made = (dot(source[rows, :], columns) + bias_ref[0]) * scale_ref[0]
            if residual:
                made = residual_ref[rows, :].astype(F32) + made
            out_ref[rows, :] = made.astype(out_ref.dtype)

    @pl.when(pl.program_id(1) == 0)
    def _():
        product(here_ref)

    @pl.when(pl.program_id(1) == 1)
    def _():
        product(away_ref)


def project(
    place, values, here, away, block, bias, scale=None, norm=None, residual=None, out_type=BF16
):
    row_count, model = values.shape
    width = here.shape[2]
    parts = model // (2 * width)
    count = bias.shape[0]
    if scale is None:
        scale = jnp.ones_like(bias)

    def whole(shape):
        return pl.BlockSpec(shape, lambda *_: (0, 0), pipeline_mode=pl.Buffered(1))

    def column(step, side, place):
        return 2 * step + (side ^ place[0])

    chunk = pl.BlockSpec(
        (1, model, width),
        lambda step, side, place: ((block * parts + step) ^ place[1], 0, 0),
    )
    line = pl.BlockSpec(
        (1, 1, width), lambda step, side, place: (column(step, side, place), 0, 0)
    )
    panel = pl.BlockSpec(
        (row_count, width), lambda step, side, place: (0, column(step, side, place))
    )
    in_specs = [whole((row_count, model))]
    operands = [values]
    if norm is not None:
        in_specs += [whole((1, model))] * 2
        operands += [norm[0].reshape(1, model), norm[1].reshape(1, model)]
    in_specs += [chunk, chunk, line, line]
    operands += [here, away, bias.reshape(-1, 1, width), scale.reshape(-1, 1, width)]
    if residual is not None:
        in_specs.append(panel)
        operands.append(residual)
    out_specs = [panel]
    out_shape = [jax.ShapeDtypeStruct((row_count, count * model), out_type)]
    if norm is not None:
        out_specs.append(pl.BlockSpec((row_count, model), lambda *_: (0, 0)))
        out_shape.append(jax.ShapeDtypeStruct((row_count, model), BF16))
    results = pl.pallas_call(
        functools.partial(
            project_kernel, norm=norm is not None, residual=residual is not None
        ),
        grid_spec=pltpu.PrefetchScalarGridSpec(
            num_scalar_prefetch=1,
            grid=(count * parts, 2),
            in_specs=in_specs,
            out_specs=out_specs,
        ),
        out_shape=out_shape,
        compiler_params=pltpu.CompilerParams(vmem_limit_bytes=40 << 20),
        cost_estimate=SMALL,
    )(place, *operands)
    return results if norm is not None else results[0]


def project_back_kernel(*refs, parts):
    count = len(refs) - 5
    grad_refs = refs[1 : 1 + count]
    here_ref, away_ref, out_ref, total_ref = refs[1 + count :]
    step = pl.program_id(0)
    side = pl.program_id(1)

    @pl.when((step == 0) & (side == 0))
    def _():
        total_ref[...] = jnp.zeros_like(total_ref)

    for item, grad_ref in enumerate(grad_refs):
        for which, columns_ref in enumerate((here_ref, away_ref)):

            @pl.when((step // parts == item) & (side == which))
            def _(grad_ref=grad_ref, columns_ref=columns_ref):
                columns = columns_ref[0]
                row_count = grad_ref.shape[0]
                size = min(QUERY_ROWS, row_count // 2)
                for first in range(0, row_count, size):
                    rows = slice(first, first + size)
                    total_ref[rows, :] += dot_last(grad_ref[rows, :], columns)

    @pl.when((step == pl.num_programs(0) - 1) & (side == 1))
    def _():
        out_ref[...] = total_ref[...].astype(out_ref.dtype)


def project_back(place, grads, here, away, block, out_type):
    row_count, model = grads[0].shape
    width = here.shape[2]
    parts = model // (2 * width)

    def grad_panel(item):
        def index(step, side, place):
            inside = (step // parts) == item
            column = 2 * (step % parts) + (side ^ place[0])
            return 0, jnp.where(inside, column, 0)

        return pl.BlockSpec((row_count, width), index)

    chunk = pl.BlockSpec(
        (1, model, width),
        lambda step, side, place: ((block * parts + step) ^ place[1], 0, 0),
    )
    return pl.pallas_call(
        functools.partial(project_back_kernel, parts=parts),
        grid_spec=pltpu.PrefetchScalarGridSpec(
            num_scalar_prefetch=1,
            grid=(len(grads) * parts, 2),
            in_specs=[grad_panel(item) for item in range(len(grads))] + [chunk, chunk],
            out_specs=pl.BlockSpec((row_count, model), lambda *_: (0, 0)),
            scratch_shapes=[pltpu.VMEM((row_count, model), F32)],
        ),
        out_shape=jax.ShapeDtypeStruct((row_count, model), out_type),
        compiler_params=pltpu.CompilerParams(vmem_limit_bytes=40 << 20),
        cost_estimate=SMALL,
    )(place, *grads, here, away)


NEAR = ((0, 1), (1, 0), (2, 3), (3, 2))


def pinned(*values):
    return lax.optimization_barrier(values)


def swap_bit(values, device_count, bit):
    return lax.ppermute(values, AXES, [(item, item ^ bit) for item in range(device_count)])


def move_planes(values, moves, plane_size):
    pairs = [
        (source * plane_size + inner, target * plane_size + inner)
        for source, target in moves
        for inner in range(plane_size)
    ]
    return lax.ppermute(values, AXES, pairs)


def inner_bits(device_count):
    bits = []
    bit = device_count // GROUPS // 2
    while bit > 1:
        bits.append(bit)
        bit //= 2
    return bits


def spread_far(own, plane_size, outer):
    return move_planes(own, ((0, 2), (3, 1)) if outer else ((1, 3), (2, 0)), plane_size)


def spread_held(own, got, plane, outer):
    sources = (0, 3) if outer else (1, 2)
    return jnp.where((plane == sources[0]) | (plane == sources[1]), own, got)


def spread_sorted(held, near, plane, outer):
    even = plane % 2 == 0
    low_held = even if outer else ~even
    return jnp.where(low_held, held, near), jnp.where(low_held, near, held)


def spread_begin(own):
    rows = own.shape[-2] // 2
    return [own[..., :rows, :], own[..., rows:, :]]


def spread_swaps(parts, stage, device_count):
    bits = inner_bits(device_count)
    return [
        swap_bit(parts[0], device_count, bits[len(bits) - 1 - stage]),
        swap_bit(parts[1], device_count, bits[stage]),
    ]


def spread_joins(parts, got):
    return [jnp.stack([part, item]) for part, item in zip(parts, got, strict=True)]


def spread_end(parts, device_count):
    levels = len(inner_bits(device_count))
    turned = jnp.transpose(
        parts[1], tuple(reversed(range(levels))) + tuple(range(levels, parts[1].ndim))
    )
    joined = jnp.concatenate([parts[0], turned], axis=-2)
    return joined.reshape((-1,) + joined.shape[levels:])


def total_of(terms):
    result = terms[0].astype(F32)
    for term in terms[1:]:
        result = result + term.astype(F32)
    return result


class Part:
    def __init__(self, members, bits, from_end):
        self.members = members
        self.bits = bits
        self.from_end = from_end

    def position(self):
        return len(self.bits) - 1 if self.from_end else 0


def begin_sum(members, device_count):
    bits = inner_bits(device_count)
    rows = members[0][0].shape[1] // 2
    parts = []
    for part in range(2):
        cut = [
            [
                term[:, part * rows : (part + 1) * rows].reshape((2,) * len(bits) + (rows, -1))
                for term in terms
            ]
            for terms in members
        ]
        parts.append(Part(cut, list(bits), part == 1))
    return parts


def pick(terms, index, position):
    return [lax.dynamic_index_in_dim(term, index, position, keepdims=False) for term in terms]


def own_place(device, bit):
    return 0 if device is None else (device // bit) % 2


def halve_sends(parts, device):
    sends = []
    for part in parts:
        position = part.position()
        other = 1 - own_place(device, part.bits[position])
        sends.append(
            jnp.stack(
                [total_of(pick(terms, other, position)).astype(BF16) for terms in part.members]
            )
        )
    return sends


def halve_swaps(sends, parts, device_count):
    return [
        swap_bit(sent, device_count, part.bits[part.position()])
        for sent, part in zip(sends, parts, strict=True)
    ]


def halve_keeps(parts, got, device):
    result = []
    every, got = pinned([part.members for part in parts], got)
    for part, terms_of, items in zip(parts, every, got, strict=True):
        part = Part(terms_of, part.bits, part.from_end)
        position = part.position()
        mine = own_place(device, part.bits[position])
        members = [
            [total_of(pick(terms, mine, position) + [items[member]])]
            for member, terms in enumerate(part.members)
        ]
        bits = part.bits[:position] + part.bits[position + 1 :]
        result.append(Part(members, bits, part.from_end))
    return result


def finish_halving(parts, device, device_count):
    while parts[0].bits:
        swapped = halve_swaps(halve_sends(parts, device), parts, device_count)
        parts = halve_keeps(parts, swapped, device)
    return parts


def member_total(parts, member=0):
    return jnp.concatenate([total_of(part.members[member]) for part in parts], axis=0)


def column_half(values, half, width):
    rows, columns = values.shape
    if columns == 2 * width:
        return lax.dynamic_slice_in_dim(values, half * width, width, 1)
    pieces = values.reshape(rows, -1, 2, width)
    return lax.dynamic_index_in_dim(pieces, half, 2, keepdims=False).reshape(rows, -1)


def weight_half(pairs, width):
    terms = []
    for left, right in pairs:
        product = dot_rows(left, right).astype(BF16)
        if product.shape[1] == width:
            terms.append(product[None])
        else:
            terms.append(jnp.swapaxes(product.reshape(product.shape[0], -1, width), 0, 1))
    return jnp.concatenate(terms, axis=0)


def dot_high(left, right, dims):
    return lax.dot_general(
        left, right, (dims, ((), ())), precision=HIGHEST, preferred_element_type=F32
    )


def update_kernel(
    grad_ref,
    weight_ref,
    average_ref,
    moment1_ref,
    moment2_ref,
    stats_ref,
    bases_ref,
    first_ref,
    second_ref,
    new_ref,
    new_average_ref,
    copy_ref,
    new_stats_ref,
    new_bases_ref,
    square_ref,
):
    blocks = stats_ref.shape[0]

    @pl.when(pl.program_id(0) == 0)
    def _():
        square_ref[...] = jnp.zeros_like(square_ref)

    for block in range(blocks):
        columns = slice(block * BLK, (block + 1) * BLK)
        grad = grad_ref[:, columns]
        basis = bases_ref[block]
        turned = dot_high(grad, basis, ((1,), (0,)))
        first = BETA_ONE * moment1_ref[:, columns] + (1.0 - BETA_ONE) * turned
        second = BETA_TWO * moment2_ref[:, columns] + (1.0 - BETA_TWO) * turned * turned
        first_ref[:, columns] = first
        second_ref[:, columns] = second
        direction = (
            first
            / (1.0 - BETA_ONE**STEP)
            / (jnp.sqrt(second / (1.0 - BETA_TWO**STEP)) + ADAM_EPS)
        )
        returned = dot_high(direction, basis, ((1,), (1,)))
        weight = weight_ref[:, columns]
        updated = weight - RATE * (returned + DECAY * weight)
        new_ref[:, columns] = updated
        new_average_ref[:, columns] = AVERAGE * average_ref[:, columns] + (1.0 - AVERAGE) * updated
        copy_ref[:, columns] = updated.astype(BF16)
        square_ref[block] += dot_high(grad, grad, ((0,), (0,)))

    @pl.when(pl.program_id(0) == pl.num_programs(0) - 1)
    def _():
        state = []
        for block in range(blocks):
            renewed = BETA_TWO * stats_ref[block] + (1.0 - BETA_TWO) * square_ref[block]
            new_stats_ref[block] = renewed
            product = dot_high(renewed, bases_ref[block], ((1,), (0,)))
            gram = dot_high(product, product, ((0,), (0,)))
            state.append(jnp.concatenate([gram, product.T], axis=1))
        row_index = lax.broadcasted_iota(jnp.int32, (PANEL, 2 * BLK), 0)
        solved = [[] for _ in range(blocks)]
        for panel in range(BLK // PANEL):
            tops = [item[:PANEL] for item in state]
            for row in range(PANEL):
                lane = panel * PANEL + row
                for block in range(blocks):
                    top = tops[block]
                    pivot = top[row : row + 1, lane : lane + 1]
                    inverse = lax.rsqrt(pivot)
                    inverse = inverse * (1.5 - 0.5 * pivot * inverse * inverse)
                    scaled = top[row : row + 1] * inverse
                    reduced = top - (top[:, lane : lane + 1] * inverse) * scaled
                    tops[block] = jnp.where(
                        row_index == row, scaled, jnp.where(row_index > row, reduced, top)
                    )
            for block in range(blocks):
                solved[block].append(tops[block][:, BLK:])
                if panel + 1 < BLK // PANEL:
                    left = tops[block][:, (panel + 1) * PANEL : BLK]
                    state[block] = state[block][PANEL:] - dot_high(
                        left, tops[block], ((0,), (0,))
                    )
        for block in range(blocks):
            new_bases_ref[block] = jnp.concatenate(solved[block], axis=0).T


def rotated_update(grad, weights, average, moment1, moment2, stats, bases):
    rows, width = grad.shape
    big = pl.BlockSpec((QUERY_ROWS, width), lambda step: (step, 0))
    small = pl.BlockSpec(stats.shape, lambda step: (0, 0, 0))
    wide = jax.ShapeDtypeStruct(grad.shape, F32)
    return pl.pallas_call(
        update_kernel,
        grid=(rows // QUERY_ROWS,),
        in_specs=[big] * 5 + [small] * 2,
        out_specs=[big] * 5 + [small] * 2,
        out_shape=[wide] * 4
        + [jax.ShapeDtypeStruct(grad.shape, BF16)]
        + [jax.ShapeDtypeStruct(stats.shape, F32)] * 2,
        scratch_shapes=[pltpu.VMEM(stats.shape, F32)],
        compiler_params=pltpu.CompilerParams(vmem_limit_bytes=40 << 20),
        cost_estimate=SMALL,
    )(grad, weights, average, moment1, moment2, stats, bases)


def adam_update(grad, values, moment1, moment2):
    first_moment = BETA_ONE * moment1 + (1.0 - BETA_ONE) * grad
    second_moment = BETA_TWO * moment2 + (1.0 - BETA_TWO) * grad * grad
    updated = values - VECTOR_RATE * (first_moment / (1.0 - BETA_ONE**STEP)) / (
        jnp.sqrt(second_moment / (1.0 - BETA_TWO**STEP)) + ADAM_EPS
    )
    return (first_moment, second_moment, updated)


def exchange_vectors(pieces, rows, width):
    device_count = pieces.shape[0]
    sublanes = 8 if pieces.dtype == F32 else 16
    room = sublanes * LANES
    size = rows * width
    tiles = -(-size // room)
    padded = jnp.pad(pieces, ((0, 0), (0, tiles * room - size)))
    padded = padded.reshape(device_count, tiles * sublanes, LANES)
    got = lax.all_to_all(padded, AXES, split_axis=0, concat_axis=0, tiled=True)
    return got.reshape(device_count, -1)[:, :size].reshape(device_count, rows, width)


def local(
    tokens,
    memory,
    page_lengths,
    slot_masks,
    upstream,
    weights,
    weight_average,
    weight_moment1,
    weight_moment2,
    stats,
    bases,
    vectors,
    vector_average,
    vector_moment1,
    vector_moment2,
):
    row_count, model = tokens.shape
    width = weights.shape[1]
    group_size = lax.axis_size("mem")
    device_count = lax.axis_size("seq") * group_size
    device = lax.axis_index(AXES)
    member = lax.axis_index("mem")
    core = device % 2
    quarter = memory.shape[1]
    scale_q = HEAD ** (-0.5)
    plane_size = device_count // GROUPS
    plane = device // plane_size
    inner = (device % plane_size) // 2
    levels = len(inner_bits(device_count))
    here = jnp.stack([core, inner]).astype(jnp.int32)
    away = jnp.stack([1 - core, inner]).astype(jnp.int32)

    vector_shape = vectors.shape
    own = weights.astype(BF16)
    outer_far = spread_far(own, plane_size, True)
    pieces = jnp.broadcast_to(
        vectors.astype(BF16).reshape(1, -1), (device_count, vectors.size)
    )
    vector_pieces = exchange_vectors(pieces, *vector_shape)
    memory_padded = jnp.pad(memory, ((0, 0), (0, SLOT_PAD - quarter), (0, 0)))
    memory_here = lax.all_to_all(memory_padded, "mem", split_axis=0, concat_axis=0, tiled=True)
    outer_held = spread_held(own, outer_far, plane, True)
    outer_near = move_planes(outer_held, NEAR, plane_size)
    outer_near, vector_pieces, own = pinned(outer_near, vector_pieces, own)
    self_own, down_own = spread_sorted(outer_held, outer_near, plane, True)
    self_stack = spread_begin(self_own)
    self_swaps = spread_swaps(self_stack, 0, device_count)
    inner_far = spread_far(own, plane_size, False)
    self_swaps, memory_here = pinned(self_swaps, memory_here)
    self_stack = spread_joins(self_stack, self_swaps)
    for stage in range(1, levels):
        self_swaps = spread_swaps(self_stack, stage, device_count)
        if stage < levels - 1:
            self_stack = spread_joins(self_stack, self_swaps)
    inner_held = spread_held(own, inner_far, plane, False)
    inner_held, self_swaps, down_own = pinned(inner_held, self_swaps, down_own)
    inner_near = move_planes(inner_held, NEAR, plane_size)
    down_stack = spread_begin(down_own)
    down_swaps = spread_swaps(down_stack, 0, device_count)
    self_here = spread_end(spread_joins(self_stack, self_swaps), device_count)
    self_away = swap_bit(self_here, device_count, 1)
    inner_near, self_away, down_swaps = pinned(inner_near, self_away, down_swaps)
    down_stack = spread_joins(down_stack, down_swaps)
    cross_own, up_own = spread_sorted(inner_held, inner_near, plane, False)
    cross_stack = spread_begin(cross_own)
    cross_stack, self_away = pinned(cross_stack, self_away)
    cross_swaps = spread_swaps(cross_stack, 0, device_count)
    memory_here = memory_here.reshape(group_size * SLOT_PAD, model)
    vector_rows = jnp.swapaxes(vector_pieces, 0, 1).reshape(vector_shape[0], model).astype(F32)

    live_rows = (jnp.arange(row_count) < page_lengths[0]).astype(F32)[:, None]
    slots_here = lax.dynamic_slice_in_dim(slot_masks, member, 1, 0).reshape(group_size, quarter)
    slots_here = jnp.pad(slots_here, ((0, 0), (0, SLOT_PAD - quarter))).reshape(-1, 1)
    slot_bias = jnp.broadcast_to(
        jnp.where(slots_here > 0, 0.0, MASKED).astype(F32), (group_size * SLOT_PAD, LANES)
    )
    nothing = jnp.zeros((model,), F32)
    ones = jnp.ones((model,), F32)
    scales = jnp.stack([scale_q * ones, ones, ones])
    pairs = HEADS // 2
    self_firsts = (0, pairs, 2 * pairs)
    cross_firsts = (0, 0, pairs)

    self_low, low_one = project(
        here,
        tokens,
        self_here,
        self_away,
        0,
        jnp.stack([vector_rows[6], nothing, vector_rows[7]]),
        scales,
        norm=(vector_rows[0], vector_rows[1]),
    )
    cross_swaps, self_low = pinned(cross_swaps, self_low)
    cross_stack = spread_joins(cross_stack, cross_swaps)
    for stage in range(1, levels):
        cross_swaps = spread_swaps(cross_stack, stage, device_count)
        if stage < levels - 1:
            cross_stack = spread_joins(cross_stack, cross_swaps)
    attended, self_log = attention_forward(self_low, self_low, self_low, self_firsts)
    cross_swaps, attended, up_own = pinned(cross_swaps, attended, up_own)
    cross_here = spread_end(spread_joins(cross_stack, cross_swaps), device_count)
    cross_away = swap_bit(cross_here, device_count, 1)
    for stage in range(1, levels):
        down_swaps = spread_swaps(down_stack, stage, device_count)
        if stage < levels - 1:
            down_stack = spread_joins(down_stack, down_swaps)
    after_self = project(
        here,
        attended,
        self_here,
        self_away,
        3,
        vector_rows[8:9],
        residual=tokens,
        out_type=F32,
    )
    cross_away, after_self = pinned(cross_away, after_self)
    queries_cross, low_two = project(
        here,
        after_self,
        cross_here,
        cross_away,
        0,
        vector_rows[9:10],
        scales[:1],
        norm=(vector_rows[2], vector_rows[3]),
    )
    cross_low = project(
        here,
        memory_here,
        cross_here,
        cross_away,
        1,
        jnp.stack([nothing, vector_rows[10]]),
    )
    down_swaps, queries_cross, cross_low, up_own = pinned(
        down_swaps, queries_cross, cross_low, up_own
    )
    up_stack = spread_begin(up_own)
    up_swaps = spread_swaps(up_stack, 0, device_count)
    down_here = spread_end(spread_joins(down_stack, down_swaps), device_count)
    down_away = swap_bit(down_here, device_count, 1)
    merged, cross_log = attention_forward(
        queries_cross, cross_low, cross_low, cross_firsts, slot_bias
    )
    up_swaps, down_away, merged = pinned(up_swaps, down_away, merged)
    up_stack = spread_joins(up_stack, up_swaps)
    for stage in range(1, levels):
        up_swaps = spread_swaps(up_stack, stage, device_count)
        if stage < levels - 1:
            up_stack = spread_joins(up_stack, up_swaps)
    after_cross = project(
        here,
        merged,
        cross_here,
        cross_away,
        3,
        vector_rows[11:12],
        residual=after_self,
        out_type=F32,
    )
    grad_low_three = (upstream.astype(F32) * live_rows).astype(BF16)
    up_swaps, after_cross, grad_low_three = pinned(up_swaps, after_cross, grad_low_three)
    up_here = spread_end(spread_joins(up_stack, up_swaps), device_count)
    up_away = swap_bit(up_here, device_count, 1)
    bias_up = vector_rows[13:17].reshape(-1)

    out_a, back_a, up_sent, down_sent, bias_sent, low_three = feed_half(
        away,
        after_cross,
        grad_low_three,
        up_away,
        down_away,
        bias_up,
        (vector_rows[4], vector_rows[5]),
    )
    up_got = swap_bit(up_sent, device_count, 1)
    down_got = swap_bit(down_sent, device_count, 1)
    low_three, up_sent, down_sent = pinned(low_three, up_sent, down_sent)
    out_b, back_b, up_kept, down_kept, bias_kept = feed_half(
        here, low_three, grad_low_three, up_here, down_here, bias_up
    )
    up_got, down_got, out_b, back_b, up_kept, down_kept = pinned(
        up_got, down_got, out_b, back_b, up_kept, down_kept
    )
    feed_parts = begin_sum(((up_kept, up_got), (down_kept, down_got)), device_count)
    feed_sends = halve_sends(feed_parts, None)
    feed_sends, back_b = pinned(feed_sends, back_b)
    feed_swaps = halve_swaps(feed_sends, feed_parts, device_count)

    result = (after_cross + (out_a + out_b) + vector_rows[12]) * live_rows
    mixed = result.astype(BF16)
    bias_even = jnp.where(core == 0, bias_kept, bias_sent)
    bias_odd = jnp.where(core == 0, bias_sent, bias_kept)
    grad_bias_up = jnp.concatenate([bias_even, bias_odd], axis=1).reshape(4, model)

    grad_two, grad_low_two, sums_three = norm_back(
        after_cross, vector_rows[4], grad_low_three, (back_a, back_b)
    )
    grad_merged = project_back(here, (grad_low_two,), cross_here, cross_away, 3, BF16)
    cross_operands = (
        queries_cross,
        cross_low,
        cross_low,
        cross_firsts,
        grad_merged,
        merged,
        cross_log,
        slot_bias,
    )
    cross_whole, (queries_part, keys_part, values_part) = attention_backward(
        away, width, *cross_operands, None
    )
    cross_whole, (queries_own, keys_own, values_own) = attention_backward(
        here, width, *cross_operands, cross_whole
    )
    grad_queries_cross, grad_keys_cross, grad_values_cross = cross_whole
    feed_swaps, queries_part, queries_own, grad_queries_cross = pinned(
        feed_swaps, queries_part, queries_own, grad_queries_cross
    )
    feed_parts = halve_keeps(feed_parts, feed_swaps, None)
    feed_sends = halve_sends(feed_parts, None)
    feed_sends, queries_part, queries_own, grad_queries_cross = pinned(
        feed_sends, queries_part, queries_own, grad_queries_cross
    )
    feed_swaps = halve_swaps(feed_sends, feed_parts, device_count)
    cross_sent = weight_half(
        (
            (low_two, queries_part),
            (memory_here, keys_part),
            (memory_here, values_part),
            (merged, column_half(grad_low_two, 1 - core, width)),
        ),
        width,
    )
    cross_sent, queries_own, grad_queries_cross = pinned(
        cross_sent, queries_own, grad_queries_cross
    )
    cross_got = swap_bit(cross_sent, device_count, 1)
    cross_kept = weight_half(
        (
            (low_two, queries_own),
            (memory_here, keys_own),
            (memory_here, values_own),
            (merged, column_half(grad_low_two, core, width)),
        ),
        width,
    )
    grad_normed_two = project_back(here, (grad_queries_cross,), cross_here, cross_away, 0, F32)

    grad_one, grad_low_one, sums_two = norm_back(
        after_self, vector_rows[2], grad_two, (grad_normed_two,)
    )
    grad_attended = project_back(here, (grad_low_one,), self_here, self_away, 3, BF16)
    feed_swaps, cross_got, cross_kept, grad_attended = pinned(
        feed_swaps, cross_got, cross_kept, grad_attended
    )
    feed_parts = finish_halving(
        halve_keeps(feed_parts, feed_swaps, None), None, device_count
    )
    even = plane % 2 == 0
    up_total = member_total(feed_parts, 0)
    down_total = member_total(feed_parts, 1)
    feed_sent = jnp.where(even, down_total, up_total).astype(BF16)
    feed_kept = jnp.where(even, up_total, down_total)
    cross_parts = begin_sum(((cross_kept, cross_got),), device_count)
    cross_sends = halve_sends(cross_parts, device)
    feed_sent, cross_sends, grad_attended = pinned(feed_sent, cross_sends, grad_attended)
    feed_got = move_planes(feed_sent, NEAR, plane_size)
    cross_swaps = halve_swaps(cross_sends, cross_parts, device_count)
    self_operands = (
        self_low,
        self_low,
        self_low,
        self_firsts,
        grad_attended,
        attended,
        self_log,
        None,
    )
    self_whole, (queries_part, keys_part, values_part) = attention_backward(
        away, width, *self_operands, None
    )
    self_sent = weight_half(
        (
            (low_one, queries_part),
            (low_one, keys_part),
            (low_one, values_part),
            (attended, column_half(grad_low_one, 1 - core, width)),
        ),
        width,
    )
    feed_got, cross_swaps, self_sent, self_whole = pinned(
        feed_got, cross_swaps, self_sent, self_whole
    )
    feed_kept = feed_kept + feed_got.astype(F32)
    cross_parts = halve_keeps(cross_parts, cross_swaps, device)
    cross_sends = halve_sends(cross_parts, device)
    feed_sent, cross_sends, self_sent, self_whole = pinned(
        feed_kept.astype(BF16), cross_sends, self_sent, self_whole
    )
    self_got = swap_bit(self_sent, device_count, 1)
    cross_swaps = halve_swaps(cross_sends, cross_parts, device_count)
    feed_got = move_planes(feed_sent, ((0, 2), (1, 3)), plane_size)
    self_whole, (queries_own, keys_own, values_own) = attention_backward(
        here, width, *self_operands, self_whole
    )
    grad_queries_self, grad_keys_self, grad_values_self = self_whole
    self_kept = weight_half(
        (
            (low_one, queries_own),
            (low_one, keys_own),
            (low_one, values_own),
            (attended, column_half(grad_low_one, core, width)),
        ),
        width,
    )
    self_got, cross_swaps, self_kept = pinned(self_got, cross_swaps, self_kept)
    self_parts = begin_sum(((self_kept, self_got),), device_count)
    self_sends = halve_sends(self_parts, device)
    cross_parts = finish_halving(
        halve_keeps(cross_parts, cross_swaps, device), device, device_count
    )
    cross_total = member_total(cross_parts)
    cross_sent = cross_total.astype(BF16)
    self_sends, cross_sent, grad_queries_self = pinned(self_sends, cross_sent, grad_queries_self)
    self_swaps = halve_swaps(self_sends, self_parts, device_count)
    cross_got = move_planes(cross_sent, ((0, 1), (2, 3)), plane_size)
    grad_normed_one = project_back(
        here,
        (grad_queries_self, grad_keys_self, grad_values_self),
        self_here,
        self_away,
        0,
        F32,
    )
    feed_got, self_swaps, cross_got, grad_normed_one = pinned(
        feed_got, self_swaps, cross_got, grad_normed_one
    )
    self_parts = halve_keeps(self_parts, self_swaps, device)
    self_sends = halve_sends(self_parts, device)
    cross_total = cross_total + cross_got.astype(F32)
    cross_sent = cross_total.astype(BF16)
    self_sends, cross_sent, grad_normed_one = pinned(self_sends, cross_sent, grad_normed_one)
    self_swaps = halve_swaps(self_sends, self_parts, device_count)
    cross_got = move_planes(cross_sent, ((3, 1),), plane_size)
    input_grad, _, sums_one = norm_back(tokens, vector_rows[0], grad_one, (grad_normed_one,))
    self_swaps, sums_one = pinned(self_swaps, sums_one)
    self_parts = finish_halving(
        halve_keeps(self_parts, self_swaps, device), device, device_count
    )
    self_total = member_total(self_parts)
    self_sent, grad_keys_cross = pinned(self_total.astype(BF16), grad_keys_cross)
    self_got = move_planes(self_sent, ((1, 0), (3, 2)), plane_size)
    vector_head = jnp.stack(
        [
            sums_one[0],
            sums_one[1],
            sums_two[0],
            sums_two[1],
            sums_three[0],
            sums_three[1],
            column_total(grad_queries_self),
            column_total(grad_values_self),
            sums_two[2],
            column_total(grad_queries_cross),
            column_total(grad_values_cross),
            sums_three[2],
            sums_three[3],
        ],
        axis=0,
    )
    vector_terms = jnp.concatenate([vector_head, grad_bias_up], axis=0)
    vector_terms = jnp.swapaxes(
        vector_terms.reshape(vector_shape[0], device_count, vector_shape[1]), 0, 1
    )
    vector_parts = exchange_vectors(vector_terms.reshape(device_count, -1), *vector_shape)
    vector_grad = jnp.sum(vector_parts, axis=0)

    memory_back = project_back(
        here, (grad_keys_cross, grad_values_cross), cross_here, cross_away, 1, BF16
    )
    memory_back = lax.all_to_all(
        memory_back.reshape(group_size, SLOT_PAD, model),
        "mem",
        split_axis=0,
        concat_axis=0,
        tiled=True,
    )
    memory_back = memory_back[:, :quarter].astype(F32)
    self_got, cross_got, memory_back = pinned(self_got, cross_got, memory_back)
    self_total = self_total + self_got.astype(F32)
    self_got = move_planes(self_total.astype(BF16), ((2, 0),), plane_size)
    group_zero = self_total + self_got.astype(F32)
    group_one = cross_total + cross_got.astype(F32)
    group_feed = feed_kept + feed_got.astype(F32)

    weight_grad = jnp.where(plane < 2, jnp.where(plane == 0, group_zero, group_one), group_feed)
    (
        weight_first,
        weight_second,
        new_weights,
        new_average,
        weights_copy,
        new_stats,
        new_bases,
    ) = rotated_update(
        weight_grad, weights, weight_average, weight_moment1, weight_moment2, stats, bases
    )
    vector_first, vector_second, new_vectors = adam_update(
        vector_grad, vectors, vector_moment1, vector_moment2
    )
    new_vector_average = AVERAGE * vector_average + (1.0 - AVERAGE) * new_vectors
    return (
        mixed,
        input_grad,
        memory_back,
        weight_grad,
        weight_first,
        weight_second,
        new_weights,
        new_average,
        weights_copy,
        new_stats,
        new_bases,
        vector_grad,
        vector_first,
        vector_second,
        new_vectors,
        new_vector_average,
        new_vectors.astype(BF16),
        vector_grad[12],
    )


def solution(mesh):
    return jax.shard_map(
        local,
        mesh=mesh,
        in_specs=(
            P(("seq", "mem"), None),
            P("seq", "mem", None),
            P(("seq", "mem")),
            P("seq", None),
            P(("seq", "mem"), None),
            P(None, ("seq", "mem")),
            P(None, ("seq", "mem")),
            P(None, ("seq", "mem")),
            P(None, ("seq", "mem")),
            P(("seq", "mem"), None, None),
            P(("seq", "mem"), None, None),
            P(None, ("seq", "mem")),
            P(None, ("seq", "mem")),
            P(None, ("seq", "mem")),
            P(None, ("seq", "mem")),
        ),
        out_specs=(
            P(("seq", "mem"), None),
            P(("seq", "mem"), None),
            P("seq", "mem", None),
            P(None, ("seq", "mem")),
            P(None, ("seq", "mem")),
            P(None, ("seq", "mem")),
            P(None, ("seq", "mem")),
            P(None, ("seq", "mem")),
            P(None, ("seq", "mem")),
            P(("seq", "mem"), None, None),
            P(("seq", "mem"), None, None),
            P(None, ("seq", "mem")),
            P(None, ("seq", "mem")),
            P(None, ("seq", "mem")),
            P(None, ("seq", "mem")),
            P(None, ("seq", "mem")),
            P(None, ("seq", "mem")),
            P(("seq", "mem")),
        ),
        check_vma=False,
    )
```

```python
import functools

import jax
import jax.numpy as jnp
from jax import lax
from jax.experimental import pallas as pl
from jax.experimental.pallas import tpu as pltpu
from jax.sharding import PartitionSpec as P

HEADS = 16
HEAD = 64
BLK = 128
STEP = 10
LANES = 128
QUERY_ROWS = 256
FORWARD_ROWS = 512
SLOT_PAD = 160
PANEL = 8
GROUPS = 4
AXES = ("seq", "mem")
SMALL = pl.CostEstimate(flops=1 << 20, bytes_accessed=1 << 16, transcendentals=0)

F32 = jnp.float32
BF16 = jnp.bfloat16
HIGHEST = lax.Precision.HIGHEST
NORM_EPS = 1e-05
ADAM_EPS = 1e-08
BETA_ONE = 0.9
BETA_TWO = 0.95
RATE = 0.04
VECTOR_RATE = 0.4
DECAY = 0.01
AVERAGE = 0.999
MASKED = -1e30
CONTRACT_ROWS = (((0,), (0,)), ((), ()))
CONTRACT_LAST = (((1,), (1,)), ((), ()))


def dot(left, right):
    return jnp.dot(left, right, preferred_element_type=F32)


def dot_last(left, right):
    return lax.dot_general(left, right, CONTRACT_LAST, preferred_element_type=F32)


def dot_rows(left, right):
    return lax.dot_general(left, right, CONTRACT_ROWS, preferred_element_type=F32)


def normalize(values, scale_gain, offset):
    centre = jnp.mean(values, axis=-1, keepdims=True)
    centred = values - centre
    variance = jnp.mean(centred * centred, axis=-1, keepdims=True)
    return centred * lax.rsqrt(variance + NORM_EPS) * scale_gain + offset


def column_total(values):
    return jnp.sum(values.astype(F32), axis=0)


def causal_mask(scores, first_key, first_query):
    key_pos = lax.broadcasted_iota(jnp.int32, scores.shape, 0) + first_key
    query_pos = lax.broadcasted_iota(jnp.int32, scores.shape, 1) + first_query
    return jnp.where(key_pos <= query_pos, scores, MASKED)


def head_of_lane(shape):
    return lax.broadcasted_iota(jnp.int32, shape, 1) // HEAD


def one_head(values, lane_head, head):
    return jnp.where(lane_head == head, values, jnp.zeros_like(values))


def widen(bias, columns):
    return jnp.concatenate([bias] * (columns // LANES), axis=1)


def attention_forward_kernel(*refs, causal):
    if causal:
        q_ref, k_ref, v_ref, out_ref, log_ref = refs
    else:
        q_ref, k_ref, v_ref, bias_ref, out_ref, log_ref = refs
    keys = k_ref[...]
    key_count = keys.shape[0]
    values_turned = v_ref[...].T
    lane_head = head_of_lane(keys.shape)
    key_heads = [one_head(keys, lane_head, head) for head in range(2)]
    units = [
        (block, head) for block in range(q_ref.shape[0] // FORWARD_ROWS) for head in range(2)
    ]

    def scores_of(unit):
        block, head = unit
        seen = (block + 1) * FORWARD_ROWS if causal else key_count
        queries = q_ref[block * FORWARD_ROWS : (block + 1) * FORWARD_ROWS, :]
        scores = dot_last(key_heads[head][:seen], queries)
        if not causal:
            return scores + widen(bias_ref[...], FORWARD_ROWS)
        last = causal_mask(scores[seen - FORWARD_ROWS :], 0, 0)
        if seen == FORWARD_ROWS:
            return last
        return jnp.concatenate([scores[: seen - FORWARD_ROWS], last], axis=0)

    scores = scores_of(units[0])
    outs = []
    for item, (block, head) in enumerate(units):
        later = scores_of(units[item + 1]) if item + 1 < len(units) else None
        rows = slice(block * FORWARD_ROWS, (block + 1) * FORWARD_ROWS)
        largest = jnp.max(scores, axis=0, keepdims=True)
        raised = jnp.exp(scores - largest)
        summed = jnp.sum(raised, axis=0, keepdims=True)
        turned = values_turned[head * HEAD : (head + 1) * HEAD, : scores.shape[0]]
        outs.append(dot(turned, raised.astype(BF16)) / summed)
        log_ref[0, head : head + 1, rows] = largest + jnp.log(summed)
        if head == 1:
            out_ref[rows, :] = jnp.concatenate(outs, axis=0).T.astype(BF16)
            outs = []
        scores = later


def attention_backward_kernel(*refs, causal):
    _, q_ref, k_ref, v_ref, grad_ref, out_ref, log_ref = refs[:7]
    bias_ref = None if causal else refs[7]
    dq_ref, dk_ref, dv_ref, dq_half, dk_half, dv_half, chance_ref, score_ref = refs[-8:]
    keys = k_ref[...]
    values = v_ref[...]
    key_count = keys.shape[0]
    row_count = q_ref.shape[0]
    keys_turned = keys.T
    product = (grad_ref[...].astype(F32) * out_ref[...].astype(F32)).T
    inner = [
        jnp.sum(product[head * HEAD : (head + 1) * HEAD], axis=0, keepdims=True)
        for head in range(2)
    ]
    slots_of = chance_ref.shape[0]
    key_rows = chance_ref.shape[1]
    lane_head = head_of_lane((key_rows, LANES))
    blocks = row_count // QUERY_ROWS
    units = [
        (piece, head, block)
        for piece in range(key_count // key_rows)
        for head in range(2)
        for block in range(piece * key_rows // QUERY_ROWS if causal else 0, blocks)
    ]

    def products_of(unit):
        piece, head, block = unit
        slots = slice(piece * key_rows, (piece + 1) * key_rows)
        rows = slice(block * QUERY_ROWS, (block + 1) * QUERY_ROWS)
        return (
            dot_last(one_head(keys[slots], lane_head, head), q_ref[rows, :]),
            dot_last(one_head(values[slots], lane_head, head), grad_ref[rows, :]),
        )

    even_heads = {}

    def finish(piece, head):
        slots = slice(piece * key_rows, (piece + 1) * key_rows)
        first = piece * key_rows if causal else 0
        kept = chance_ref[(2 * piece + head) % slots_of, :, first:]
        grad_value = dot(kept, grad_ref[first:, :])
        grad_key = dot(score_ref[head, slots, first:], q_ref[first:, :])
        if head == 0:
            even_heads[piece] = (grad_key, grad_value)
            return
        even_key, even_value = even_heads.pop(piece)
        grad_key = jnp.where(lane_head == 0, even_key, grad_key).astype(BF16)
        grad_value = jnp.where(lane_head == 0, even_value, grad_value).astype(BF16)
        dk_ref[slots, :] = grad_key
        dk_half[slots, :] = grad_key
        dv_ref[slots, :] = grad_value
        dv_half[slots, :] = grad_value

    current = products_of(units[0])
    ended = None
    for item, (piece, head, block) in enumerate(units):
        later = products_of(units[item + 1]) if item + 1 < len(units) else None
        if ended is not None:
            finish(*ended)
            ended = None
        scores, grad_chance = current
        slots = slice(piece * key_rows, (piece + 1) * key_rows)
        rows = slice(block * QUERY_ROWS, (block + 1) * QUERY_ROWS)
        if not causal:
            scores = scores + widen(bias_ref[slots, :], QUERY_ROWS)
        elif (piece + 1) * key_rows > block * QUERY_ROWS:
            scores = causal_mask(scores, piece * key_rows, block * QUERY_ROWS)
        chance = jnp.exp(scores - log_ref[0, head : head + 1, rows])
        chance_ref[(2 * piece + head) % slots_of, :, rows] = chance.astype(BF16)
        score_ref[head, slots, rows] = (chance * (grad_chance - inner[head][:, rows])).astype(BF16)
        if block == blocks - 1:
            ended = (piece, head)
        current = later
    finish(*ended)
    for block in range(blocks):
        rows = slice(block * QUERY_ROWS, (block + 1) * QUERY_ROWS)
        seen = (block + 1) * QUERY_ROWS if causal else key_count
        parts = [
            dot(
                keys_turned[head * HEAD : (head + 1) * HEAD, :seen],
                score_ref[head, :seen, rows],
            )
            for head in range(2)
        ]
        grad_query = jnp.concatenate(parts, axis=0).T.astype(BF16)
        grad_query = (grad_query.astype(F32) * HEAD ** (-0.5)).astype(BF16)
        dq_ref[rows, :] = grad_query
        dq_half[rows, :] = grad_query


def head_pair(row_count, first):
    return pl.BlockSpec((row_count, LANES), lambda pair: (0, first + pair))


def attention_forward(queries, keys, values, firsts, bias=None):
    causal = bias is None
    row_count = queries.shape[0]
    key_count = keys.shape[0]
    pairs = HEADS // 2
    in_specs = [
        head_pair(row_count, firsts[0]),
        head_pair(key_count, firsts[1]),
        head_pair(key_count, firsts[2]),
    ]
    operands = [queries, keys, values]
    if not causal:
        in_specs.append(pl.BlockSpec((key_count, LANES), lambda pair: (0, 0)))
        operands.append(bias)
    return pl.pallas_call(
        functools.partial(attention_forward_kernel, causal=causal),
        grid=(pairs,),
        in_specs=in_specs,
        out_specs=[
            head_pair(row_count, 0),
            pl.BlockSpec((1, 8, row_count), lambda pair: (pair, 0, 0)),
        ],
        out_shape=[
            jax.ShapeDtypeStruct((row_count, pairs * LANES), BF16),
            jax.ShapeDtypeStruct((pairs, 8, row_count), F32),
        ],
        compiler_params=pltpu.CompilerParams(vmem_limit_bytes=40 << 20),
        cost_estimate=SMALL,
    )(*operands)


def attention_backward(
    half, width, queries, keys, values, firsts, grads, outs, log_total, bias, whole
):
    causal = bias is None
    row_count, model = grads.shape
    key_count = keys.shape[0]
    key_rows = QUERY_ROWS if causal else key_count // 2
    per_unit = width // LANES
    steps = HEADS // 4

    def chosen(step, side):
        return (2 * (step // per_unit) + side[0]) * per_unit + step % per_unit

    def in_whole(count, first=0):
        return pl.BlockSpec((count, LANES), lambda step, side: (0, first + chosen(step, side)))

    def alone(count):
        return pl.BlockSpec((count, LANES), lambda step, side: (0, step))

    in_specs = [
        in_whole(row_count, firsts[0]),
        in_whole(key_count, firsts[1]),
        in_whole(key_count, firsts[2]),
        in_whole(row_count),
        in_whole(row_count),
        pl.BlockSpec((1, 8, row_count), lambda step, side: (chosen(step, side), 0, 0)),
    ]
    operands = [queries, keys, values, grads, outs, log_total]
    if not causal:
        in_specs.append(pl.BlockSpec((key_count, LANES), lambda step, side: (0, 0)))
        operands.append(bias)
    aliases = {}
    if whole is not None:
        for item, array in enumerate(whole):
            aliases[1 + len(operands)] = item
            in_specs.append(pl.BlockSpec(memory_space=pl.ANY))
            operands.append(array)
    counts = (row_count, key_count, key_count)
    results = pl.pallas_call(
        functools.partial(attention_backward_kernel, causal=causal),
        grid_spec=pltpu.PrefetchScalarGridSpec(
            num_scalar_prefetch=1,
            grid=(steps,),
            in_specs=in_specs,
            out_specs=[in_whole(count) for count in counts] + [alone(count) for count in counts],
            scratch_shapes=[
                pltpu.VMEM((4, key_rows, row_count), BF16),
                pltpu.VMEM((2, key_count, row_count), BF16),
            ],
        ),
        out_shape=[jax.ShapeDtypeStruct((count, model), BF16) for count in counts]
        + [jax.ShapeDtypeStruct((count, model // 2), BF16) for count in counts],
        input_output_aliases=aliases,
        compiler_params=pltpu.CompilerParams(vmem_limit_bytes=40 << 20),
        cost_estimate=SMALL,
    )(half, *operands)
    return results[:3], results[3:]


def gelu_parts(values):
    slope = 0.7978845608028654
    square = values * values
    turned = jnp.tanh(slope * values * (1.0 + 0.044715 * square))
    weight = 0.5 * (1.0 + turned)
    derivative = weight + 0.5 * values * (1.0 - turned * turned) * (
        slope + (3.0 * 0.044715 * slope) * square
    )
    return values * weight, derivative


def feed_kernel(*refs, norm):
    refs = list(refs[1:])
    values_ref = refs.pop(0)
    if norm:
        gain_ref = refs.pop(0)
        shift_ref = refs.pop(0)
    grad_ref, up_ref, down_ref, bias_ref = refs[:4]
    out_ref, back_ref, grad_up_ref, grad_down_ref, grad_bias_ref = refs[4:9]
    low_ref = refs[9] if norm else values_ref
    low_turned, grad_turned, active_ref, hidden_ref = refs[-4:]

    @pl.when(pl.program_id(0) == 0)
    def _():
        if norm:
            for first in range(0, values_ref.shape[0], QUERY_ROWS):
                rows = slice(first, first + QUERY_ROWS)
                low_ref[rows, :] = normalize(
                    values_ref[rows, :], gain_ref[...], shift_ref[...]
                ).astype(BF16)
        low_turned[...] = low_ref[...].T
        grad_turned[...] = grad_ref[...].T
        out_ref[...] = jnp.zeros_like(out_ref)
        back_ref[...] = jnp.zeros_like(back_ref)

    up = up_ref[0]
    down = down_ref[0]
    total = jnp.zeros((1, up.shape[1]), F32)
    pieces = low_ref.shape[0] // QUERY_ROWS
    for piece in range(pieces):
        rows = slice(piece * QUERY_ROWS, (piece + 1) * QUERY_ROWS)
        active, derivative = gelu_parts(dot(low_ref[rows, :], up) + bias_ref[0])
        active_low = active.astype(BF16)
        hidden_low = (derivative * dot(grad_ref[rows, :], down)).astype(BF16)
        active_ref[rows, :] = active_low
        hidden_ref[rows, :] = hidden_low
        total = total + jnp.sum(hidden_low.astype(F32), axis=0, keepdims=True)
        out_ref[rows, :] += dot_last(active_low, down)
        back_ref[rows, :] += dot_last(hidden_low, up)
    grad_bias_ref[0] = total
    for piece in range(low_turned.shape[0] // QUERY_ROWS):
        rows = slice(piece * QUERY_ROWS, (piece + 1) * QUERY_ROWS)
        grad_down_ref[0, rows, :] = dot(grad_turned[rows, :], active_ref[...]).astype(BF16)
        grad_up_ref[0, rows, :] = dot(low_turned[rows, :], hidden_ref[...]).astype(BF16)


def feed_half(place, values, grad, ups, downs, bias, norm=None):
    row_count, model = values.shape
    steps, _, width = ups.shape

    def whole(shape):
        return pl.BlockSpec(shape, lambda step, place: (0, 0), pipeline_mode=pl.Buffered(1))

    total = pl.BlockSpec((row_count, model), lambda step, place: (0, 0))
    chunk = pl.BlockSpec((1, model, width), lambda step, place: (step, 0, 0))
    in_specs = [whole((row_count, model))]
    operands = [values]
    out_specs = [
        total,
        total,
        chunk,
        chunk,
        pl.BlockSpec((1, 1, width), lambda step, place: (step ^ place[1], 0, 0)),
    ]
    out_shape = [
        jax.ShapeDtypeStruct((row_count, model), F32),
        jax.ShapeDtypeStruct((row_count, model), F32),
        jax.ShapeDtypeStruct((steps, model, width), BF16),
        jax.ShapeDtypeStruct((steps, model, width), BF16),
        jax.ShapeDtypeStruct((steps, 1, width), F32),
    ]
    if norm is not None:
        in_specs += [whole((1, model))] * 2
        operands += [norm[0].reshape(1, model), norm[1].reshape(1, model)]
        out_specs.append(total)
        out_shape.append(jax.ShapeDtypeStruct((row_count, model), BF16))
    in_specs += [
        whole((row_count, model)),
        chunk,
        chunk,
        pl.BlockSpec((1, 1, width), lambda step, place: (2 * (step ^ place[1]) + place[0], 0, 0)),
    ]
    operands += [grad, ups, downs, bias.reshape(-1, 1, width)]
    return pl.pallas_call(
        functools.partial(feed_kernel, norm=norm is not None),
        grid_spec=pltpu.PrefetchScalarGridSpec(
            num_scalar_prefetch=1,
            grid=(steps,),
            in_specs=in_specs,
            out_specs=out_specs,
            scratch_shapes=[
                pltpu.VMEM((model, row_count), BF16),
                pltpu.VMEM((model, row_count), BF16),
                pltpu.VMEM((row_count, width), BF16),
                pltpu.VMEM((row_count, width), BF16),
            ],
        ),
        out_shape=out_shape,
        compiler_params=pltpu.CompilerParams(vmem_limit_bytes=58 << 20),
        cost_estimate=SMALL,
    )(place, *operands)


def norm_back_kernel(*refs, count):
    values_ref, gain_ref, stream_ref = refs[:3]
    grad_refs = refs[3 : 3 + count]
    out_ref, low_ref, sums_ref = refs[3 + count :]
    values = values_ref[...].astype(F32)
    grad = grad_refs[0][...]
    for grad_ref in grad_refs[1:]:
        grad = grad + grad_ref[...]
    centred = values - jnp.mean(values, axis=-1, keepdims=True)
    inverse = lax.rsqrt(jnp.mean(centred * centred, axis=-1, keepdims=True) + NORM_EPS)
    normal = centred * inverse
    scaled = grad * gain_ref[...]
    product = scaled * normal
    back = inverse * (
        scaled
        - jnp.mean(scaled, axis=-1, keepdims=True)
        - normal * jnp.mean(product, axis=-1, keepdims=True)
    )
    result = stream_ref[...].astype(F32) + back
    low = result.astype(BF16)
    out_ref[...] = result
    low_ref[...] = low

    @pl.when(pl.program_id(0) == 0)
    def _():
        sums_ref[...] = jnp.zeros_like(sums_ref)

    sums_ref[0:1, :] += jnp.sum(grad * normal, axis=0, keepdims=True)
    sums_ref[1:2, :] += jnp.sum(grad, axis=0, keepdims=True)
    sums_ref[2:3, :] += jnp.sum(low.astype(F32), axis=0, keepdims=True)
    sums_ref[3:4, :] += jnp.sum(stream_ref[...].astype(F32), axis=0, keepdims=True)


def norm_back(values, gain, stream, grads):
    row_count, model = values.shape
    panel = pl.BlockSpec((QUERY_ROWS, model), lambda step: (step, 0))
    return pl.pallas_call(
        functools.partial(norm_back_kernel, count=len(grads)),
        grid=(row_count // QUERY_ROWS,),
        in_specs=[panel, pl.BlockSpec((1, model), lambda step: (0, 0)), panel]
        + [panel] * len(grads),
        out_specs=[panel, panel, pl.BlockSpec((8, model), lambda step: (0, 0))],
        out_shape=[
            jax.ShapeDtypeStruct((row_count, model), F32),
            jax.ShapeDtypeStruct((row_count, model), BF16),
            jax.ShapeDtypeStruct((8, model), F32),
        ],
        compiler_params=pltpu.CompilerParams(vmem_limit_bytes=40 << 20),
        cost_estimate=SMALL,
    )(values, gain.reshape(1, model), stream, *grads)


def project_kernel(*refs, norm, residual):
    refs = list(refs[1:])
    values_ref = refs.pop(0)
    if norm:
        gain_ref = refs.pop(0)
        shift_ref = refs.pop(0)
    here_ref, away_ref, bias_ref, scale_ref = refs[:4]
    refs = refs[4:]
    if residual:
        residual_ref = refs.pop(0)
    out_ref = refs.pop(0)
    source = values_ref
    if norm:
        low_ref = refs.pop(0)
        source = low_ref

        @pl.when((pl.program_id(0) == 0) & (pl.program_id(1) == 0))
        def _():
            for first in range(0, values_ref.shape[0], QUERY_ROWS):
                rows = slice(first, first + QUERY_ROWS)
                low_ref[rows, :] = normalize(
                    values_ref[rows, :].astype(F32), gain_ref[...], shift_ref[...]
                ).astype(BF16)

    def product(columns_ref):
        columns = columns_ref[0]
        row_count = values_ref.shape[0]
        step = min(QUERY_ROWS, row_count // 2)
        for first in range(0, row_count, step):
            rows = slice(first, first + step)
            made = (dot(source[rows, :], columns) + bias_ref[0]) * scale_ref[0]
            if residual:
                made = residual_ref[rows, :].astype(F32) + made
            out_ref[rows, :] = made.astype(out_ref.dtype)

    @pl.when(pl.program_id(1) == 0)
    def _():
        product(here_ref)

    @pl.when(pl.program_id(1) == 1)
    def _():
        product(away_ref)


def project(
    place, values, here, away, block, bias, scale=None, norm=None, residual=None, out_type=BF16
):
    row_count, model = values.shape
    width = here.shape[2]
    parts = model // (2 * width)
    count = bias.shape[0]
    if scale is None:
        scale = jnp.ones_like(bias)

    def whole(shape):
        return pl.BlockSpec(shape, lambda *_: (0, 0), pipeline_mode=pl.Buffered(1))

    def column(step, side, place):
        return 2 * step + (side ^ place[0])

    chunk = pl.BlockSpec(
        (1, model, width),
        lambda step, side, place: ((block * parts + step) ^ place[1], 0, 0),
    )
    line = pl.BlockSpec(
        (1, 1, width), lambda step, side, place: (column(step, side, place), 0, 0)
    )
    panel = pl.BlockSpec(
        (row_count, width), lambda step, side, place: (0, column(step, side, place))
    )
    in_specs = [whole((row_count, model))]
    operands = [values]
    if norm is not None:
        in_specs += [whole((1, model))] * 2
        operands += [norm[0].reshape(1, model), norm[1].reshape(1, model)]
    in_specs += [chunk, chunk, line, line]
    operands += [here, away, bias.reshape(-1, 1, width), scale.reshape(-1, 1, width)]
    if residual is not None:
        in_specs.append(panel)
        operands.append(residual)
    out_specs = [panel]
    out_shape = [jax.ShapeDtypeStruct((row_count, count * model), out_type)]
    if norm is not None:
        out_specs.append(pl.BlockSpec((row_count, model), lambda *_: (0, 0)))
        out_shape.append(jax.ShapeDtypeStruct((row_count, model), BF16))
    results = pl.pallas_call(
        functools.partial(
            project_kernel, norm=norm is not None, residual=residual is not None
        ),
        grid_spec=pltpu.PrefetchScalarGridSpec(
            num_scalar_prefetch=1,
            grid=(count * parts, 2),
            in_specs=in_specs,
            out_specs=out_specs,
        ),
        out_shape=out_shape,
        compiler_params=pltpu.CompilerParams(vmem_limit_bytes=40 << 20),
        cost_estimate=SMALL,
    )(place, *operands)
    return results if norm is not None else results[0]


def project_back_kernel(*refs, parts):
    count = len(refs) - 5
    grad_refs = refs[1 : 1 + count]
    here_ref, away_ref, out_ref, total_ref = refs[1 + count :]
    step = pl.program_id(0)
    side = pl.program_id(1)

    @pl.when((step == 0) & (side == 0))
    def _():
        total_ref[...] = jnp.zeros_like(total_ref)

    for item, grad_ref in enumerate(grad_refs):
        for which, columns_ref in enumerate((here_ref, away_ref)):

            @pl.when((step // parts == item) & (side == which))
            def _(grad_ref=grad_ref, columns_ref=columns_ref):
                columns = columns_ref[0]
                row_count = grad_ref.shape[0]
                size = min(QUERY_ROWS, row_count // 2)
                for first in range(0, row_count, size):
                    rows = slice(first, first + size)
                    total_ref[rows, :] += dot_last(grad_ref[rows, :], columns)

    @pl.when((step == pl.num_programs(0) - 1) & (side == 1))
    def _():
        out_ref[...] = total_ref[...].astype(out_ref.dtype)


def project_back(place, grads, here, away, block, out_type):
    row_count, model = grads[0].shape
    width = here.shape[2]
    parts = model // (2 * width)

    def grad_panel(item):
        def index(step, side, place):
            inside = (step // parts) == item
            column = 2 * (step % parts) + (side ^ place[0])
            return 0, jnp.where(inside, column, 0)

        return pl.BlockSpec((row_count, width), index)

    chunk = pl.BlockSpec(
        (1, model, width),
        lambda step, side, place: ((block * parts + step) ^ place[1], 0, 0),
    )
    return pl.pallas_call(
        functools.partial(project_back_kernel, parts=parts),
        grid_spec=pltpu.PrefetchScalarGridSpec(
            num_scalar_prefetch=1,
            grid=(len(grads) * parts, 2),
            in_specs=[grad_panel(item) for item in range(len(grads))] + [chunk, chunk],
            out_specs=pl.BlockSpec((row_count, model), lambda *_: (0, 0)),
            scratch_shapes=[pltpu.VMEM((row_count, model), F32)],
        ),
        out_shape=jax.ShapeDtypeStruct((row_count, model), out_type),
        compiler_params=pltpu.CompilerParams(vmem_limit_bytes=40 << 20),
        cost_estimate=SMALL,
    )(place, *grads, here, away)


NEAR = ((0, 1), (1, 0), (2, 3), (3, 2))


def pinned(*values):
    return lax.optimization_barrier(values)


def swap_bit(values, device_count, bit):
    return lax.ppermute(values, AXES, [(item, item ^ bit) for item in range(device_count)])


def move_planes(values, moves, plane_size):
    pairs = [
        (source * plane_size + inner, target * plane_size + inner)
        for source, target in moves
        for inner in range(plane_size)
    ]
    return lax.ppermute(values, AXES, pairs)


def inner_bits(device_count):
    bits = []
    bit = device_count // GROUPS // 2
    while bit > 1:
        bits.append(bit)
        bit //= 2
    return bits


def spread_first(own, plane_size):
    return move_planes(own, ((0, 2), (1, 0), (2, 3), (3, 1)), plane_size)


def spread_second(own, first, plane, plane_size):
    held = jnp.where((plane == 0) | (plane == 3), own, first)
    near = move_planes(held, NEAR, plane_size)
    middle = move_planes(own, ((1, 2), (2, 1)), plane_size)
    return held, near, middle


def spread_outer(held, near, plane):
    even = plane % 2 == 0
    return jnp.where(even, held, near), jnp.where(even, near, held)


def spread_inner(own, first, middle, last, plane):
    chunk_one = jnp.where(
        plane < 2, jnp.where(plane == 0, first, own), jnp.where(plane == 2, middle, last)
    )
    chunk_two = jnp.where(
        plane < 2, jnp.where(plane == 0, last, middle), jnp.where(plane == 2, own, first)
    )
    return chunk_one, chunk_two


def spread_begin(own):
    rows = own.shape[-2] // 2
    return [own[..., :rows, :], own[..., rows:, :]]


def spread_swaps(parts, stage, device_count):
    bits = inner_bits(device_count)
    return [
        swap_bit(parts[0], device_count, bits[len(bits) - 1 - stage]),
        swap_bit(parts[1], device_count, bits[stage]),
    ]


def spread_joins(parts, got):
    return [jnp.stack([part, item]) for part, item in zip(parts, got, strict=True)]


def assemble_kernel(upper_ref, upper_got, lower_ref, lower_got, out_ref, *, top):
    chunk = pl.program_id(0)
    part = pl.program_id(1)
    sources = (
        ((part == 0) & (chunk < top), upper_ref),
        ((part == 0) & (chunk >= top), upper_got),
        ((part == 1) & (chunk % 2 == 0), lower_ref),
        ((part == 1) & (chunk % 2 == 1), lower_got),
    )
    for chosen, source in sources:

        @pl.when(chosen)
        def _(source=source):
            out_ref[0] = source[0]


def assemble(parts, got):
    half, width = parts[0].shape[-2:]
    flat = [item.reshape(-1, half, width) for item in (parts[0], got[0], parts[1], got[1])]
    top = flat[0].shape[0]

    def upper(chunk, part):
        return chunk % top, 0, 0

    def lower(chunk, part):
        place = 0
        rest = chunk // 2
        size = top
        while size > 1:
            place = place * 2 + rest % 2
            rest = rest // 2
            size //= 2
        return place, 0, 0

    def block(index):
        return pl.BlockSpec((1, half, width), index)

    return pl.pallas_call(
        functools.partial(assemble_kernel, top=top),
        grid=(2 * top, 2),
        in_specs=[block(upper), block(upper), block(lower), block(lower)],
        out_specs=pl.BlockSpec((1, half, width), lambda chunk, part: (chunk, part, 0)),
        out_shape=jax.ShapeDtypeStruct((2 * top, 2 * half, width), BF16),
        compiler_params=pltpu.CompilerParams(vmem_limit_bytes=32 << 20),
        cost_estimate=SMALL,
    )(*flat)


class Sum:
    def __init__(self, kept, got, absolute, swaps=()):
        self.kept = kept
        self.got = got
        self.absolute = absolute
        self.swaps = list(swaps)

    def joined(self, got):
        return Sum(self.kept, self.got, self.absolute, self.swaps + [got])


def stage_kernel(*refs, members, terms, parts):
    ins = refs[1:-parts]
    outs = refs[-parts:]
    per_part = 2 * members + terms
    for part, out_ref in enumerate(outs):
        mine = ins[part * per_part : (part + 1) * per_part]
        for member in range(members):
            total = mine[2 * member][0].astype(F32) + mine[2 * member + 1][0].astype(F32)
            for swap_ref in mine[2 * members :]:
                total = total + swap_ref[member, 0].astype(F32)
            out_ref[member, 0] = total.astype(BF16)


def stage_sends(place, pending, device_count):
    levels = len(inner_bits(device_count))
    stage = len(pending.swaps)
    chunks, rows, width = pending.kept[0].shape
    half = rows // 2
    count = chunks >> (stage + 1)
    members = len(pending.kept)

    def relative(part, step):
        if part == 0:
            return count + step
        return (step << (stage + 1)) + (1 << stage)

    def stored(part):
        def index(step, place):
            chunk = relative(part, step)
            return (chunk ^ place[1] if pending.absolute else chunk), part, 0

        return pl.BlockSpec((1, half, width), index)

    def swapped(part, earlier):
        def index(step, place):
            chunk = relative(part, step)
            return 0, (chunk if part == 0 else chunk >> (earlier + 1)), 0, 0

        return pl.BlockSpec((members, 1, half, width), index)

    in_specs = []
    operands = []
    for part in range(2):
        for kept, got in zip(pending.kept, pending.got, strict=True):
            in_specs += [stored(part)] * 2
            operands += [kept, got]
        for earlier, items in enumerate(pending.swaps):
            in_specs.append(swapped(part, earlier))
            operands.append(items[part])
    assert stage < levels
    return pl.pallas_call(
        functools.partial(stage_kernel, members=members, terms=stage, parts=2),
        grid_spec=pltpu.PrefetchScalarGridSpec(
            num_scalar_prefetch=1,
            grid=(count,),
            in_specs=in_specs,
            out_specs=[pl.BlockSpec((members, 1, half, width), lambda step, place: (0, step, 0, 0))]
            * 2,
        ),
        out_shape=[jax.ShapeDtypeStruct((members, count, half, width), BF16)] * 2,
        compiler_params=pltpu.CompilerParams(vmem_limit_bytes=32 << 20),
        cost_estimate=SMALL,
    )(place, *operands)


def stage_swaps(sends, pending, device_count):
    bits = inner_bits(device_count)
    stage = len(pending.swaps)
    return [
        swap_bit(sends[0], device_count, bits[stage]),
        swap_bit(sends[1], device_count, bits[len(bits) - 1 - stage]),
    ]


def finish_stages(place, pending, device_count):
    while len(pending.swaps) < len(inner_bits(device_count)):
        sends = stage_sends(place, pending, device_count)
        pending = pending.joined(stage_swaps(sends, pending, device_count))
    return pending


def total_kernel(*refs, members, stages):
    place_ref = refs[0]
    stored = refs[1 : 1 + 2 * members]
    swaps = refs[1 + 2 * members : 1 + 2 * members + 2 * stages]
    kept_ref, sent_ref = refs[1 + 2 * members + 2 * stages :]

    def total(part, member):
        result = stored[2 * member][0].astype(F32) + stored[2 * member + 1][0].astype(F32)
        for stage in range(stages):
            result = result + swaps[2 * stage + part][member, 0].astype(F32)
        return result

    for part in range(2):

        @pl.when(pl.program_id(0) // 2 == part)
        def _(part=part):
            if members == 1:
                made = total(part, 0)
                kept_ref[...] = made
                sent_ref[...] = made.astype(BF16)
            else:
                low = total(part, 0)
                high = total(part, 1)
                even = place_ref[2] == 0
                kept_ref[...] = jnp.where(even, low, high)
                sent_ref[...] = jnp.where(even, high, low).astype(BF16)


def plane_totals(place, pending):
    chunks, rows, width = pending.kept[0].shape
    quarter = rows // 4
    members = len(pending.kept)

    def stored(step, place):
        return (place[1] if pending.absolute else 0), step, 0

    in_specs = []
    operands = []
    for kept, got in zip(pending.kept, pending.got, strict=True):
        in_specs += [pl.BlockSpec((1, quarter, width), stored)] * 2
        operands += [kept, got]
    for items in pending.swaps:
        for part in range(2):
            in_specs.append(
                pl.BlockSpec(
                    (members, 1, quarter, width),
                    (lambda step, place: (0, 0, jnp.minimum(step, 1), 0))
                    if part == 0
                    else (lambda step, place: (0, 0, jnp.maximum(step - 2, 0), 0)),
                )
            )
            operands.append(items[part])
    panel = pl.BlockSpec((quarter, width), lambda step, place: (step, 0))
    return pl.pallas_call(
        functools.partial(total_kernel, members=members, stages=len(pending.swaps)),
        grid_spec=pltpu.PrefetchScalarGridSpec(
            num_scalar_prefetch=1,
            grid=(4,),
            in_specs=in_specs,
            out_specs=[panel, panel],
        ),
        out_shape=[
            jax.ShapeDtypeStruct((rows, width), F32),
            jax.ShapeDtypeStruct((rows, width), BF16),
        ],
        compiler_params=pltpu.CompilerParams(vmem_limit_bytes=32 << 20),
        cost_estimate=SMALL,
    )(place, *operands)


def column_half(values, half, width):
    rows, columns = values.shape
    if columns == 2 * width:
        return lax.dynamic_slice_in_dim(values, half * width, width, 1)
    pieces = values.reshape(rows, -1, 2, width)
    return lax.dynamic_index_in_dim(pieces, half, 2, keepdims=False).reshape(rows, -1)


def weight_half(pairs, width):
    terms = []
    for left, right in pairs:
        product = dot_rows(left, right).astype(BF16)
        if product.shape[1] == width:
            terms.append(product[None])
        else:
            terms.append(jnp.swapaxes(product.reshape(product.shape[0], -1, width), 0, 1))
    return jnp.concatenate(terms, axis=0)


def dot_high(left, right, dims):
    return lax.dot_general(
        left, right, (dims, ((), ())), precision=HIGHEST, preferred_element_type=F32
    )


def update_kernel(
    grad_ref,
    weight_ref,
    average_ref,
    moment1_ref,
    moment2_ref,
    stats_ref,
    bases_ref,
    first_ref,
    second_ref,
    new_ref,
    new_average_ref,
    copy_ref,
    new_stats_ref,
    new_bases_ref,
    square_ref,
):
    blocks = stats_ref.shape[0]

    @pl.when(pl.program_id(0) == 0)
    def _():
        square_ref[...] = jnp.zeros_like(square_ref)

    for block in range(blocks):
        columns = slice(block * BLK, (block + 1) * BLK)
        grad = grad_ref[:, columns]
        basis = bases_ref[block]
        turned = dot_high(grad, basis, ((1,), (0,)))
        first = BETA_ONE * moment1_ref[:, columns] + (1.0 - BETA_ONE) * turned
        second = BETA_TWO * moment2_ref[:, columns] + (1.0 - BETA_TWO) * turned * turned
        first_ref[:, columns] = first
        second_ref[:, columns] = second
        direction = (
            first
            / (1.0 - BETA_ONE**STEP)
            / (jnp.sqrt(second / (1.0 - BETA_TWO**STEP)) + ADAM_EPS)
        )
        returned = dot_high(direction, basis, ((1,), (1,)))
        weight = weight_ref[:, columns]
        updated = weight - RATE * (returned + DECAY * weight)
        new_ref[:, columns] = updated
        new_average_ref[:, columns] = AVERAGE * average_ref[:, columns] + (1.0 - AVERAGE) * updated
        copy_ref[:, columns] = updated.astype(BF16)
        square_ref[block] += dot_high(grad, grad, ((0,), (0,)))

    @pl.when(pl.program_id(0) == pl.num_programs(0) - 1)
    def _():
        state = []
        for block in range(blocks):
            renewed = BETA_TWO * stats_ref[block] + (1.0 - BETA_TWO) * square_ref[block]
            new_stats_ref[block] = renewed
            product = dot_high(renewed, bases_ref[block], ((1,), (0,)))
            gram = dot_high(product, product, ((0,), (0,)))
            state.append(jnp.concatenate([gram, product.T], axis=1))
        row_index = lax.broadcasted_iota(jnp.int32, (PANEL, 2 * BLK), 0)
        solved = [[] for _ in range(blocks)]
        for panel in range(BLK // PANEL):
            tops = [item[:PANEL] for item in state]
            for row in range(PANEL):
                lane = panel * PANEL + row
                for block in range(blocks):
                    top = tops[block]
                    pivot = top[row : row + 1, lane : lane + 1]
                    inverse = lax.rsqrt(pivot)
                    inverse = inverse * (1.5 - 0.5 * pivot * inverse * inverse)
                    scaled = top[row : row + 1] * inverse
                    reduced = top - (top[:, lane : lane + 1] * inverse) * scaled
                    tops[block] = jnp.where(
                        row_index == row, scaled, jnp.where(row_index > row, reduced, top)
                    )
            for block in range(blocks):
                solved[block].append(tops[block][:, BLK:])
                if panel + 1 < BLK // PANEL:
                    left = tops[block][:, (panel + 1) * PANEL : BLK]
                    state[block] = state[block][PANEL:] - dot_high(
                        left, tops[block], ((0,), (0,))
                    )
        for block in range(blocks):
            new_bases_ref[block] = jnp.concatenate(solved[block], axis=0).T


def rotated_update(grad, weights, average, moment1, moment2, stats, bases):
    rows, width = grad.shape
    big = pl.BlockSpec((QUERY_ROWS, width), lambda step: (step, 0))
    small = pl.BlockSpec(stats.shape, lambda step: (0, 0, 0))
    wide = jax.ShapeDtypeStruct(grad.shape, F32)
    return pl.pallas_call(
        update_kernel,
        grid=(rows // QUERY_ROWS,),
        in_specs=[big] * 5 + [small] * 2,
        out_specs=[big] * 5 + [small] * 2,
        out_shape=[wide] * 4
        + [jax.ShapeDtypeStruct(grad.shape, BF16)]
        + [jax.ShapeDtypeStruct(stats.shape, F32)] * 2,
        scratch_shapes=[pltpu.VMEM(stats.shape, F32)],
        compiler_params=pltpu.CompilerParams(vmem_limit_bytes=40 << 20),
        cost_estimate=SMALL,
    )(grad, weights, average, moment1, moment2, stats, bases)


def adam_update(grad, values, moment1, moment2):
    first_moment = BETA_ONE * moment1 + (1.0 - BETA_ONE) * grad
    second_moment = BETA_TWO * moment2 + (1.0 - BETA_TWO) * grad * grad
    updated = values - VECTOR_RATE * (first_moment / (1.0 - BETA_ONE**STEP)) / (
        jnp.sqrt(second_moment / (1.0 - BETA_TWO**STEP)) + ADAM_EPS
    )
    return (first_moment, second_moment, updated)


def exchange_vectors(pieces, rows, width):
    device_count = pieces.shape[0]
    sublanes = 8 if pieces.dtype == F32 else 16
    room = sublanes * LANES
    size = rows * width
    tiles = -(-size // room)
    padded = jnp.pad(pieces, ((0, 0), (0, tiles * room - size)))
    padded = padded.reshape(device_count, tiles * sublanes, LANES)
    got = lax.all_to_all(padded, AXES, split_axis=0, concat_axis=0, tiled=True)
    return got.reshape(device_count, -1)[:, :size].reshape(device_count, rows, width)


def local(
    tokens,
    memory,
    page_lengths,
    slot_masks,
    upstream,
    weights,
    weight_average,
    weight_moment1,
    weight_moment2,
    stats,
    bases,
    vectors,
    vector_average,
    vector_moment1,
    vector_moment2,
):
    row_count, model = tokens.shape
    width = weights.shape[1]
    group_size = lax.axis_size("mem")
    device_count = lax.axis_size("seq") * group_size
    device = lax.axis_index(AXES)
    member = lax.axis_index("mem")
    core = device % 2
    quarter = memory.shape[1]
    scale_q = HEAD ** (-0.5)
    plane_size = device_count // GROUPS
    plane = device // plane_size
    inner = (device % plane_size) // 2
    levels = len(inner_bits(device_count))
    here = jnp.stack([core, inner, plane % 2]).astype(jnp.int32)
    away = jnp.stack([1 - core, inner, plane % 2]).astype(jnp.int32)

    vector_shape = vectors.shape
    own = weights.astype(BF16)
    first = spread_first(own, plane_size)
    pieces = jnp.broadcast_to(
        vectors.astype(BF16).reshape(1, -1), (device_count, vectors.size)
    )
    vector_pieces = exchange_vectors(pieces, *vector_shape)
    first, vector_pieces, own = pinned(first, vector_pieces, own)
    held, near, middle = spread_second(own, first, plane, plane_size)
    memory_padded = jnp.pad(memory, ((0, 0), (0, SLOT_PAD - quarter), (0, 0)))
    memory_here = lax.all_to_all(memory_padded, "mem", split_axis=0, concat_axis=0, tiled=True)
    near, middle, memory_here = pinned(near, middle, memory_here)
    memory_here = memory_here.reshape(group_size * SLOT_PAD, model)
    self_own, down_own = spread_outer(held, near, plane)
    self_stack = spread_begin(self_own)
    self_swaps = spread_swaps(self_stack, 0, device_count)
    last = move_planes(middle, ((1, 0), (2, 3)), plane_size)
    self_stack = spread_joins(self_stack, self_swaps)
    for stage in range(1, levels):
        self_swaps = spread_swaps(self_stack, stage, device_count)
        if stage < levels - 1:
            self_stack = spread_joins(self_stack, self_swaps)
    self_swaps, last, down_own = pinned(self_swaps, last, down_own)
    cross_own, up_own = spread_inner(own, first, middle, last, plane)
    cross_stack = spread_begin(cross_own)
    cross_stack, self_swaps = pinned(cross_stack, self_swaps)
    cross_swaps = spread_swaps(cross_stack, 0, device_count)
    self_here = assemble(self_stack, self_swaps)
    self_away = swap_bit(self_here, device_count, 1)
    cross_stack = spread_joins(cross_stack, cross_swaps)
    cross_stack, self_away, down_own, up_own = pinned(cross_stack, self_away, down_own, up_own)
    for stage in range(1, levels):
        cross_swaps = spread_swaps(cross_stack, stage, device_count)
        if stage < levels - 1:
            cross_stack = spread_joins(cross_stack, cross_swaps)
    down_stack = spread_begin(down_own)
    down_swaps = spread_swaps(down_stack, 0, device_count)
    up_stack = spread_begin(up_own)
    up_swaps = spread_swaps(up_stack, 0, device_count)
    vector_rows = jnp.swapaxes(vector_pieces, 0, 1).reshape(vector_shape[0], model).astype(F32)

    live_rows = (jnp.arange(row_count) < page_lengths[0]).astype(F32)[:, None]
    slots_here = lax.dynamic_slice_in_dim(slot_masks, member, 1, 0).reshape(group_size, quarter)
    slots_here = jnp.pad(slots_here, ((0, 0), (0, SLOT_PAD - quarter))).reshape(-1, 1)
    slot_bias = jnp.broadcast_to(
        jnp.where(slots_here > 0, 0.0, MASKED).astype(F32), (group_size * SLOT_PAD, LANES)
    )
    nothing = jnp.zeros((model,), F32)
    ones = jnp.ones((model,), F32)
    scales = jnp.stack([scale_q * ones, ones, ones])
    pairs = HEADS // 2
    self_firsts = (0, pairs, 2 * pairs)
    cross_firsts = (0, 0, pairs)

    self_low, low_one = project(
        here,
        tokens,
        self_here,
        self_away,
        0,
        jnp.stack([vector_rows[6], nothing, vector_rows[7]]),
        scales,
        norm=(vector_rows[0], vector_rows[1]),
    )
    attended, self_log = attention_forward(self_low, self_low, self_low, self_firsts)
    cross_swaps, down_swaps, up_swaps, attended = pinned(
        cross_swaps, down_swaps, up_swaps, attended
    )
    down_stack = spread_joins(down_stack, down_swaps)
    up_stack = spread_joins(up_stack, up_swaps)
    for stage in range(1, levels):
        down_swaps = spread_swaps(down_stack, stage, device_count)
        if stage < levels - 1:
            down_stack = spread_joins(down_stack, down_swaps)
    cross_here = assemble(cross_stack, cross_swaps)
    cross_away = swap_bit(cross_here, device_count, 1)
    after_self = project(
        here,
        attended,
        self_here,
        self_away,
        3,
        vector_rows[8:9],
        residual=tokens,
        out_type=F32,
    )
    cross_away, after_self, up_stack = pinned(cross_away, after_self, up_stack)
    for stage in range(1, levels):
        up_swaps = spread_swaps(up_stack, stage, device_count)
        if stage < levels - 1:
            up_stack = spread_joins(up_stack, up_swaps)
    queries_cross, low_two = project(
        here,
        after_self,
        cross_here,
        cross_away,
        0,
        vector_rows[9:10],
        scales[:1],
        norm=(vector_rows[2], vector_rows[3]),
    )
    cross_low = project(
        here,
        memory_here,
        cross_here,
        cross_away,
        1,
        jnp.stack([nothing, vector_rows[10]]),
    )
    down_swaps, queries_cross, cross_low = pinned(down_swaps, queries_cross, cross_low)
    down_here = assemble(down_stack, down_swaps)
    down_away = swap_bit(down_here, device_count, 1)
    merged, cross_log = attention_forward(
        queries_cross, cross_low, cross_low, cross_firsts, slot_bias
    )
    up_swaps, down_away, merged = pinned(up_swaps, down_away, merged)
    up_here = assemble(up_stack, up_swaps)
    up_away = swap_bit(up_here, device_count, 1)
    after_cross = project(
        here,
        merged,
        cross_here,
        cross_away,
        3,
        vector_rows[11:12],
        residual=after_self,
        out_type=F32,
    )
    grad_low_three = (upstream.astype(F32) * live_rows).astype(BF16)
    up_away, after_cross, grad_low_three = pinned(up_away, after_cross, grad_low_three)
    bias_up = vector_rows[13:17].reshape(-1)

    out_a, back_a, up_sent, down_sent, bias_sent, low_three = feed_half(
        away,
        after_cross,
        grad_low_three,
        up_away,
        down_away,
        bias_up,
        (vector_rows[4], vector_rows[5]),
    )
    up_got = swap_bit(up_sent, device_count, 1)
    down_got = swap_bit(down_sent, device_count, 1)
    low_three, up_sent, down_sent = pinned(low_three, up_sent, down_sent)
    out_b, back_b, up_kept, down_kept, bias_kept = feed_half(
        here, low_three, grad_low_three, up_here, down_here, bias_up
    )
    up_got, down_got, out_b, back_b, up_kept, down_kept = pinned(
        up_got, down_got, out_b, back_b, up_kept, down_kept
    )
    feed_sum = Sum((up_kept, down_kept), (up_got, down_got), False)
    feed_sends = stage_sends(here, feed_sum, device_count)
    feed_sends, back_b = pinned(feed_sends, back_b)
    feed_swaps = stage_swaps(feed_sends, feed_sum, device_count)

    result = (after_cross + (out_a + out_b) + vector_rows[12]) * live_rows
    mixed = result.astype(BF16)
    bias_even = jnp.where(core == 0, bias_kept, bias_sent)
    bias_odd = jnp.where(core == 0, bias_sent, bias_kept)
    grad_bias_up = jnp.concatenate([bias_even, bias_odd], axis=1).reshape(4, model)

    grad_two, grad_low_two, sums_three = norm_back(
        after_cross, vector_rows[4], grad_low_three, (back_a, back_b)
    )
    grad_merged = project_back(here, (grad_low_two,), cross_here, cross_away, 3, BF16)
    cross_operands = (
        queries_cross,
        cross_low,
        cross_low,
        cross_firsts,
        grad_merged,
        merged,
        cross_log,
        slot_bias,
    )
    cross_whole, (queries_part, keys_part, values_part) = attention_backward(
        away, width, *cross_operands, None
    )
    cross_whole, (queries_own, keys_own, values_own) = attention_backward(
        here, width, *cross_operands, cross_whole
    )
    grad_queries_cross, grad_keys_cross, grad_values_cross = cross_whole
    feed_swaps, queries_part, queries_own, grad_queries_cross = pinned(
        feed_swaps, queries_part, queries_own, grad_queries_cross
    )
    feed_sum = feed_sum.joined(feed_swaps)
    feed_sends = stage_sends(here, feed_sum, device_count)
    feed_sends, queries_part, queries_own, grad_queries_cross = pinned(
        feed_sends, queries_part, queries_own, grad_queries_cross
    )
    feed_swaps = stage_swaps(feed_sends, feed_sum, device_count)
    cross_sent = weight_half(
        (
            (low_two, queries_part),
            (memory_here, keys_part),
            (memory_here, values_part),
            (merged, column_half(grad_low_two, 1 - core, width)),
        ),
        width,
    )
    cross_sent, queries_own, grad_queries_cross = pinned(
        cross_sent, queries_own, grad_queries_cross
    )
    cross_got = swap_bit(cross_sent, device_count, 1)
    cross_kept = weight_half(
        (
            (low_two, queries_own),
            (memory_here, keys_own),
            (memory_here, values_own),
            (merged, column_half(grad_low_two, core, width)),
        ),
        width,
    )
    grad_normed_two = project_back(here, (grad_queries_cross,), cross_here, cross_away, 0, F32)

    grad_one, grad_low_one, sums_two = norm_back(
        after_self, vector_rows[2], grad_two, (grad_normed_two,)
    )
    grad_attended = project_back(here, (grad_low_one,), self_here, self_away, 3, BF16)
    feed_swaps, cross_got, cross_kept, grad_attended = pinned(
        feed_swaps, cross_got, cross_kept, grad_attended
    )
    feed_sum = finish_stages(here, feed_sum.joined(feed_swaps), device_count)
    feed_kept, feed_sent = plane_totals(here, feed_sum)
    cross_sum = Sum((cross_kept,), (cross_got,), True)
    cross_sends = stage_sends(here, cross_sum, device_count)
    feed_sent, cross_sends, grad_attended = pinned(feed_sent, cross_sends, grad_attended)
    feed_got = move_planes(feed_sent, NEAR, plane_size)
    cross_swaps = stage_swaps(cross_sends, cross_sum, device_count)
    self_operands = (
        self_low,
        self_low,
        self_low,
        self_firsts,
        grad_attended,
        attended,
        self_log,
        None,
    )
    self_whole, (queries_part, keys_part, values_part) = attention_backward(
        away, width, *self_operands, None
    )
    self_sent = weight_half(
        (
            (low_one, queries_part),
            (low_one, keys_part),
            (low_one, values_part),
            (attended, column_half(grad_low_one, 1 - core, width)),
        ),
        width,
    )
    feed_got, cross_swaps, self_sent, self_whole = pinned(
        feed_got, cross_swaps, self_sent, self_whole
    )
    self_got = swap_bit(self_sent, device_count, 1)
    feed_kept = feed_kept + feed_got.astype(F32)
    cross_sum = cross_sum.joined(cross_swaps)
    cross_sends = stage_sends(here, cross_sum, device_count)
    feed_sent, cross_sends, self_whole = pinned(
        feed_kept.astype(BF16), cross_sends, self_whole
    )
    feed_got = move_planes(feed_sent, ((0, 2), (1, 3)), plane_size)
    cross_swaps = stage_swaps(cross_sends, cross_sum, device_count)
    self_whole, (queries_own, keys_own, values_own) = attention_backward(
        here, width, *self_operands, self_whole
    )
    grad_queries_self, grad_keys_self, grad_values_self = self_whole
    self_kept = weight_half(
        (
            (low_one, queries_own),
            (low_one, keys_own),
            (low_one, values_own),
            (attended, column_half(grad_low_one, core, width)),
        ),
        width,
    )
    self_got, cross_swaps, self_kept = pinned(self_got, cross_swaps, self_kept)
    self_sum = Sum((self_kept,), (self_got,), True)
    self_sends = stage_sends(here, self_sum, device_count)
    self_sends, grad_queries_self, cross_swaps, grad_keys_cross = pinned(
        self_sends, grad_queries_self, cross_swaps, grad_keys_cross
    )
    self_swaps = stage_swaps(self_sends, self_sum, device_count)
    cross_sum = finish_stages(here, cross_sum.joined(cross_swaps), device_count)
    cross_total, cross_sent = plane_totals(here, cross_sum)
    cross_got = move_planes(cross_sent, ((0, 1), (3, 2)), plane_size)
    grad_normed_one = project_back(
        here,
        (grad_queries_self, grad_keys_self, grad_values_self),
        self_here,
        self_away,
        0,
        F32,
    )
    memory_back = project_back(
        here, (grad_keys_cross, grad_values_cross), cross_here, cross_away, 1, BF16
    )
    self_swaps, grad_normed_one, memory_back = pinned(self_swaps, grad_normed_one, memory_back)
    self_sum = self_sum.joined(self_swaps)
    self_sends = stage_sends(here, self_sum, device_count)
    self_sends, grad_normed_one, memory_back = pinned(self_sends, grad_normed_one, memory_back)
    self_swaps = stage_swaps(self_sends, self_sum, device_count)
    input_grad, _, sums_one = norm_back(tokens, vector_rows[0], grad_one, (grad_normed_one,))
    self_swaps, sums_one = pinned(self_swaps, sums_one)
    self_sum = finish_stages(here, self_sum.joined(self_swaps), device_count)
    self_total, self_sent = plane_totals(here, self_sum)
    self_sent, memory_back, sums_one = pinned(self_sent, memory_back, sums_one)
    self_got = move_planes(self_sent, ((1, 0), (3, 2)), plane_size)
    cross_total = cross_total + cross_got.astype(F32)
    cross_got = move_planes(cross_total.astype(BF16), ((2, 1),), plane_size)
    vector_head = jnp.stack(
        [
            sums_one[0],
            sums_one[1],
            sums_two[0],
            sums_two[1],
            sums_three[0],
            sums_three[1],
            column_total(grad_queries_self),
            column_total(grad_values_self),
            sums_two[2],
            column_total(grad_queries_cross),
            column_total(grad_values_cross),
            sums_three[2],
            sums_three[3],
        ],
        axis=0,
    )
    vector_terms = jnp.concatenate([vector_head, grad_bias_up], axis=0)
    vector_terms = jnp.swapaxes(
        vector_terms.reshape(vector_shape[0], device_count, vector_shape[1]), 0, 1
    )
    vector_parts = exchange_vectors(vector_terms.reshape(device_count, -1), *vector_shape)
    vector_grad = jnp.sum(vector_parts, axis=0)

    self_got, vector_grad = pinned(self_got, vector_grad)
    self_total = self_total + self_got.astype(F32)
    self_sent, memory_back = pinned(self_total.astype(BF16), memory_back)
    self_got = move_planes(self_sent, ((2, 0),), plane_size)
    memory_back = lax.all_to_all(
        memory_back.reshape(group_size, SLOT_PAD, model),
        "mem",
        split_axis=0,
        concat_axis=0,
        tiled=True,
    )
    memory_back = memory_back[:, :quarter].astype(F32)
    group_other = jnp.where(
        plane < 2,
        cross_total + cross_got.astype(F32),
        feed_kept + feed_got.astype(F32),
    )
    group_other, self_got, memory_back = pinned(group_other, self_got, memory_back)
    weight_grad = jnp.where(plane == 0, self_total + self_got.astype(F32), group_other)
    (
        weight_first,
        weight_second,
        new_weights,
        new_average,
        weights_copy,
        new_stats,
        new_bases,
    ) = rotated_update(
        weight_grad, weights, weight_average, weight_moment1, weight_moment2, stats, bases
    )
    vector_first, vector_second, new_vectors = adam_update(
        vector_grad, vectors, vector_moment1, vector_moment2
    )
    new_vector_average = AVERAGE * vector_average + (1.0 - AVERAGE) * new_vectors
    return (
        mixed,
        input_grad,
        memory_back,
        weight_grad,
        weight_first,
        weight_second,
        new_weights,
        new_average,
        weights_copy,
        new_stats,
        new_bases,
        vector_grad,
        vector_first,
        vector_second,
        new_vectors,
        new_vector_average,
        new_vectors.astype(BF16),
        vector_grad[12],
    )


def solution(mesh):
    return jax.shard_map(
        local,
        mesh=mesh,
        in_specs=(
            P(("seq", "mem"), None),
            P("seq", "mem", None),
            P(("seq", "mem")),
            P("seq", None),
            P(("seq", "mem"), None),
            P(None, ("seq", "mem")),
            P(None, ("seq", "mem")),
            P(None, ("seq", "mem")),
            P(None, ("seq", "mem")),
            P(("seq", "mem"), None, None),
            P(("seq", "mem"), None, None),
            P(None, ("seq", "mem")),
            P(None, ("seq", "mem")),
            P(None, ("seq", "mem")),
            P(None, ("seq", "mem")),
        ),
        out_specs=(
            P(("seq", "mem"), None),
            P(("seq", "mem"), None),
            P("seq", "mem", None),
            P(None, ("seq", "mem")),
            P(None, ("seq", "mem")),
            P(None, ("seq", "mem")),
            P(None, ("seq", "mem")),
            P(None, ("seq", "mem")),
            P(None, ("seq", "mem")),
            P(("seq", "mem"), None, None),
            P(("seq", "mem"), None, None),
            P(None, ("seq", "mem")),
            P(None, ("seq", "mem")),
            P(None, ("seq", "mem")),
            P(None, ("seq", "mem")),
            P(None, ("seq", "mem")),
            P(None, ("seq", "mem")),
            P(("seq", "mem")),
        ),
        check_vma=False,
    )
```

```python
import functools

import jax
import jax.numpy as jnp
from jax import lax
from jax.experimental import pallas as pl
from jax.experimental.pallas import tpu as pltpu
from jax.sharding import PartitionSpec as P

HEADS = 16
HEAD = 64
BLK = 128
STEP = 10
LANES = 128
QUERY_ROWS = 256
FORWARD_ROWS = 512
FEED_ROWS = 1024
SLOT_PAD = 160
PANEL = 8
GROUPS = 4
AXES = ("seq", "mem")
SMALL = pl.CostEstimate(flops=1 << 20, bytes_accessed=1 << 16, transcendentals=0)

F32 = jnp.float32
BF16 = jnp.bfloat16
HIGHEST = lax.Precision.HIGHEST
NORM_EPS = 1e-05
ADAM_EPS = 1e-08
BETA_ONE = 0.9
BETA_TWO = 0.95
RATE = 0.04
VECTOR_RATE = 0.4
DECAY = 0.01
AVERAGE = 0.999
MASKED = -1e30
CONTRACT_ROWS = (((0,), (0,)), ((), ()))
CONTRACT_LAST = (((1,), (1,)), ((), ()))


def dot(left, right):
    return jnp.dot(left, right, preferred_element_type=F32)


def dot_last(left, right):
    return lax.dot_general(left, right, CONTRACT_LAST, preferred_element_type=F32)


def dot_rows(left, right):
    return lax.dot_general(left, right, CONTRACT_ROWS, preferred_element_type=F32)


def normalize(values, scale_gain, offset):
    centre = jnp.mean(values, axis=-1, keepdims=True)
    centred = values - centre
    variance = jnp.mean(centred * centred, axis=-1, keepdims=True)
    return centred * lax.rsqrt(variance + NORM_EPS) * scale_gain + offset


def column_total(values):
    return jnp.sum(values.astype(F32), axis=0)


def causal_mask(scores, first_key, first_query):
    key_pos = lax.broadcasted_iota(jnp.int32, scores.shape, 0) + first_key
    query_pos = lax.broadcasted_iota(jnp.int32, scores.shape, 1) + first_query
    return jnp.where(key_pos <= query_pos, scores, MASKED)


def head_of_lane(shape):
    return lax.broadcasted_iota(jnp.int32, shape, 1) // HEAD


def one_head(values, lane_head, head):
    return jnp.where(lane_head == head, values, jnp.zeros_like(values))


def widen(bias, columns):
    return jnp.concatenate([bias] * (columns // LANES), axis=1)


def attention_forward_kernel(*refs, causal):
    if causal:
        q_ref, k_ref, v_ref, out_ref, log_ref = refs
    else:
        q_ref, k_ref, v_ref, bias_ref, out_ref, log_ref = refs
    keys = k_ref[...]
    key_count = keys.shape[0]
    values_turned = v_ref[...].T
    lane_head = head_of_lane(keys.shape)
    key_heads = [one_head(keys, lane_head, head) for head in range(2)]
    units = [
        (block, head) for block in range(q_ref.shape[0] // FORWARD_ROWS) for head in range(2)
    ]

    def scores_of(unit):
        block, head = unit
        seen = (block + 1) * FORWARD_ROWS if causal else key_count
        queries = q_ref[block * FORWARD_ROWS : (block + 1) * FORWARD_ROWS, :]
        scores = dot_last(key_heads[head][:seen], queries)
        if not causal:
            return scores + widen(bias_ref[...], FORWARD_ROWS)
        last = causal_mask(scores[seen - FORWARD_ROWS :], 0, 0)
        if seen == FORWARD_ROWS:
            return last
        return jnp.concatenate([scores[: seen - FORWARD_ROWS], last], axis=0)

    scores = scores_of(units[0])
    outs = []
    for item, (block, head) in enumerate(units):
        later = scores_of(units[item + 1]) if item + 1 < len(units) else None
        rows = slice(block * FORWARD_ROWS, (block + 1) * FORWARD_ROWS)
        largest = jnp.max(scores, axis=0, keepdims=True)
        raised = jnp.exp(scores - largest)
        summed = jnp.sum(raised, axis=0, keepdims=True)
        turned = values_turned[head * HEAD : (head + 1) * HEAD, : scores.shape[0]]
        outs.append(dot(turned, raised.astype(BF16)) / summed)
        log_ref[0, head : head + 1, rows] = largest + jnp.log(summed)
        if head == 1:
            out_ref[rows, :] = jnp.concatenate(outs, axis=0).T.astype(BF16)
            outs = []
        scores = later


def attention_backward_kernel(*refs, causal):
    _, q_ref, k_ref, v_ref, grad_ref, out_ref, log_ref = refs[:7]
    bias_ref = None if causal else refs[7]
    dq_ref, dk_ref, dv_ref, dq_half, dk_half, dv_half, chance_ref, score_ref = refs[-8:]
    keys = k_ref[...]
    values = v_ref[...]
    key_count = keys.shape[0]
    row_count = q_ref.shape[0]
    keys_turned = keys.T
    product = (grad_ref[...].astype(F32) * out_ref[...].astype(F32)).T
    inner = [
        jnp.sum(product[head * HEAD : (head + 1) * HEAD], axis=0, keepdims=True)
        for head in range(2)
    ]
    slots_of = chance_ref.shape[0]
    key_rows = chance_ref.shape[1]
    lane_head = head_of_lane((key_rows, LANES))
    blocks = row_count // QUERY_ROWS
    units = [
        (piece, head, block)
        for piece in range(key_count // key_rows)
        for head in range(2)
        for block in range(piece * key_rows // QUERY_ROWS if causal else 0, blocks)
    ]

    def products_of(unit):
        piece, head, block = unit
        slots = slice(piece * key_rows, (piece + 1) * key_rows)
        rows = slice(block * QUERY_ROWS, (block + 1) * QUERY_ROWS)
        return (
            dot_last(one_head(keys[slots], lane_head, head), q_ref[rows, :]),
            dot_last(one_head(values[slots], lane_head, head), grad_ref[rows, :]),
        )

    even_heads = {}

    def finish(piece, head):
        slots = slice(piece * key_rows, (piece + 1) * key_rows)
        first = piece * key_rows if causal else 0
        kept = chance_ref[(2 * piece + head) % slots_of, :, first:]
        grad_value = dot(kept, grad_ref[first:, :])
        grad_key = dot(score_ref[head, slots, first:], q_ref[first:, :])
        if head == 0:
            even_heads[piece] = (grad_key, grad_value)
            return
        even_key, even_value = even_heads.pop(piece)
        grad_key = jnp.where(lane_head == 0, even_key, grad_key).astype(BF16)
        grad_value = jnp.where(lane_head == 0, even_value, grad_value).astype(BF16)
        dk_ref[slots, :] = grad_key
        dk_half[slots, :] = grad_key
        dv_ref[slots, :] = grad_value
        dv_half[slots, :] = grad_value

    current = products_of(units[0])
    ended = None
    for item, (piece, head, block) in enumerate(units):
        later = products_of(units[item + 1]) if item + 1 < len(units) else None
        if ended is not None:
            finish(*ended)
            ended = None
        scores, grad_chance = current
        slots = slice(piece * key_rows, (piece + 1) * key_rows)
        rows = slice(block * QUERY_ROWS, (block + 1) * QUERY_ROWS)
        if not causal:
            scores = scores + widen(bias_ref[slots, :], QUERY_ROWS)
        elif (piece + 1) * key_rows > block * QUERY_ROWS:
            scores = causal_mask(scores, piece * key_rows, block * QUERY_ROWS)
        chance = jnp.exp(scores - log_ref[0, head : head + 1, rows])
        chance_ref[(2 * piece + head) % slots_of, :, rows] = chance.astype(BF16)
        score_ref[head, slots, rows] = (chance * (grad_chance - inner[head][:, rows])).astype(BF16)
        if block == blocks - 1:
            ended = (piece, head)
        current = later
    finish(*ended)
    for block in range(blocks):
        rows = slice(block * QUERY_ROWS, (block + 1) * QUERY_ROWS)
        seen = (block + 1) * QUERY_ROWS if causal else key_count
        parts = [
            dot(
                keys_turned[head * HEAD : (head + 1) * HEAD, :seen],
                score_ref[head, :seen, rows],
            )
            for head in range(2)
        ]
        grad_query = jnp.concatenate(parts, axis=0).T.astype(BF16)
        grad_query = (grad_query.astype(F32) * HEAD ** (-0.5)).astype(BF16)
        dq_ref[rows, :] = grad_query
        dq_half[rows, :] = grad_query


def head_pair(row_count, first):
    return pl.BlockSpec((row_count, LANES), lambda pair: (0, first + pair))


def attention_forward(queries, keys, values, firsts, bias=None):
    causal = bias is None
    row_count = queries.shape[0]
    key_count = keys.shape[0]
    pairs = HEADS // 2
    in_specs = [
        head_pair(row_count, firsts[0]),
        head_pair(key_count, firsts[1]),
        head_pair(key_count, firsts[2]),
    ]
    operands = [queries, keys, values]
    if not causal:
        in_specs.append(pl.BlockSpec((key_count, LANES), lambda pair: (0, 0)))
        operands.append(bias)
    return pl.pallas_call(
        functools.partial(attention_forward_kernel, causal=causal),
        grid=(pairs,),
        in_specs=in_specs,
        out_specs=[
            head_pair(row_count, 0),
            pl.BlockSpec((1, 8, row_count), lambda pair: (pair, 0, 0)),
        ],
        out_shape=[
            jax.ShapeDtypeStruct((row_count, pairs * LANES), BF16),
            jax.ShapeDtypeStruct((pairs, 8, row_count), F32),
        ],
        compiler_params=pltpu.CompilerParams(vmem_limit_bytes=60 << 20),
        cost_estimate=SMALL,
    )(*operands)


def attention_backward(
    half, width, queries, keys, values, firsts, grads, outs, log_total, bias, whole
):
    causal = bias is None
    row_count, model = grads.shape
    key_count = keys.shape[0]
    key_rows = QUERY_ROWS if causal else key_count // 2
    per_unit = width // LANES
    steps = HEADS // 4

    def chosen(step, side):
        return (2 * (step // per_unit) + side[0]) * per_unit + step % per_unit

    def in_whole(count, first=0):
        return pl.BlockSpec((count, LANES), lambda step, side: (0, first + chosen(step, side)))

    def alone(count):
        return pl.BlockSpec((count, LANES), lambda step, side: (0, step))

    in_specs = [
        in_whole(row_count, firsts[0]),
        in_whole(key_count, firsts[1]),
        in_whole(key_count, firsts[2]),
        in_whole(row_count),
        in_whole(row_count),
        pl.BlockSpec((1, 8, row_count), lambda step, side: (chosen(step, side), 0, 0)),
    ]
    operands = [queries, keys, values, grads, outs, log_total]
    if not causal:
        in_specs.append(pl.BlockSpec((key_count, LANES), lambda step, side: (0, 0)))
        operands.append(bias)
    aliases = {}
    if whole is not None:
        for item, array in enumerate(whole):
            aliases[1 + len(operands)] = item
            in_specs.append(pl.BlockSpec(memory_space=pl.ANY))
            operands.append(array)
    counts = (row_count, key_count, key_count)
    results = pl.pallas_call(
        functools.partial(attention_backward_kernel, causal=causal),
        grid_spec=pltpu.PrefetchScalarGridSpec(
            num_scalar_prefetch=1,
            grid=(steps,),
            in_specs=in_specs,
            out_specs=[in_whole(count) for count in counts] + [alone(count) for count in counts],
            scratch_shapes=[
                pltpu.VMEM((4, key_rows, row_count), BF16),
                pltpu.VMEM((2, key_count, row_count), BF16),
            ],
        ),
        out_shape=[jax.ShapeDtypeStruct((count, model), BF16) for count in counts]
        + [jax.ShapeDtypeStruct((count, model // 2), BF16) for count in counts],
        input_output_aliases=aliases,
        compiler_params=pltpu.CompilerParams(vmem_limit_bytes=60 << 20),
        cost_estimate=SMALL,
    )(half, *operands)
    return results[:3], results[3:]


PLACE_PLANE = 3
VECTOR_ROWS = 24


def holders(group, plane):
    if group == 0:
        return ((1, plane != 0), (0, plane == 0))
    if group == 1:
        return ((2, plane > 1), (0, plane == 1), (1, plane == 0))
    if group == 2:
        return ((2, plane < 2), (0, plane == 2), (3, plane == 3))
    return ((3, plane != 3), (0, plane == 3))


class Source:
    def __init__(self, slots, group, sides):
        self.group = group
        self.sides = sides
        self.which = [slot for slot, _ in holders(group, 0)]
        self.operands = [
            array for slot in self.which for side in sides for array in slots[slot][side]
        ]
        self.shape = self.operands[0].shape
        self.dtype = self.operands[0].dtype

    def chunks(self):
        return 2 * self.shape[0]

    def specs(self):
        return [pl.BlockSpec(memory_space=pl.ANY)] * len(self.operands)

    def scratch(self):
        return [
            pltpu.VMEM((2, 2 * self.shape[1], self.shape[2]), self.dtype),
            pltpu.SemaphoreType.DMA((2, 2)),
        ]


def start_fetch(source, refs, buffer, semaphores, plane, side, chunk, turn):
    top, half = source.shape[:2]
    lower_place = 0
    rest = chunk // 2
    size = top
    while size > 1:
        lower_place = lower_place * 2 + rest % 2
        rest = rest // 2
        size //= 2
    item = 0
    for _, chosen in holders(source.group, plane):
        for number in range(len(source.sides)):
            wanted = chosen & (side == number)
            lows, highs, evens, odds = refs[item : item + 4]
            item += 4
            copies = (
                (chunk < top, lows, chunk, 0),
                (chunk >= top, highs, chunk - top, 0),
                (chunk % 2 == 0, evens, lower_place, 1),
                (chunk % 2 == 1, odds, lower_place, 1),
            )
            for condition, array, index, part in copies:

                @pl.when(wanted & condition)
                def _(array=array, index=index, part=part):
                    pltpu.make_async_copy(
                        array.at[index],
                        buffer.at[turn, pl.ds(part * half, half), :],
                        semaphores.at[turn, part],
                    ).start()


def wait_fetch(source, refs, buffer, semaphores, turn):
    half = source.shape[1]
    for part in range(2):
        pltpu.make_async_copy(
            refs[0].at[0],
            buffer.at[turn, pl.ds(part * half, half), :],
            semaphores.at[turn, part],
        ).wait()


def fetched(source, refs, buffer, semaphores, plane, order, item, count):
    turn = item % 2

    @pl.when(item == 0)
    def _():
        side, chunk = order(0)
        start_fetch(source, refs, buffer, semaphores, plane, side, chunk, 0)

    @pl.when(item + 1 < count)
    def _():
        side, chunk = order(item + 1)
        start_fetch(source, refs, buffer, semaphores, plane, side, chunk, (item + 1) % 2)

    wait_fetch(source, refs, buffer, semaphores, turn)
    return buffer.at[turn]


def vector_part(vectors_ref, row, first, width):
    return vectors_ref[row : row + 1, pl.ds(pl.multiple_of(first, width), width)]


def gelu_parts(values):
    slope = 0.7978845608028654
    square = values * values
    turned = jnp.tanh(slope * values * (1.0 + 0.044715 * square))
    weight = 0.5 * (1.0 + turned)
    derivative = weight + 0.5 * values * (1.0 - turned * turned) * (
        slope + (3.0 * 0.044715 * slope) * square
    )
    return values * weight, derivative


def feed_kernel(*refs, norm, up_source, down_source):
    refs = list(refs)
    place_ref = refs.pop(0)
    values_ref = refs.pop(0)
    grad_ref = refs.pop(0)
    vectors_ref = refs.pop(0)
    bias_ref = refs.pop(0)
    up_refs = refs[: len(up_source.operands)]
    refs = refs[len(up_refs) :]
    down_refs = refs[: len(down_source.operands)]
    refs = refs[len(down_refs) :]
    out_ref, back_ref, grad_up_ref, grad_down_ref, grad_bias_ref = refs[:5]
    low_ref = refs[5] if norm else values_ref
    low_turned, grad_turned, active_ref, hidden_ref = refs[-8:-4]
    up_buffer, up_semaphores, down_buffer, down_semaphores = refs[-4:]
    plane = place_ref[PLACE_PLANE]
    step = pl.program_id(0)
    count = up_source.chunks()

    def order(item):
        return 0, item

    up_chunk = fetched(up_source, up_refs, up_buffer, up_semaphores, plane, order, step, count)
    down_chunk = fetched(
        down_source, down_refs, down_buffer, down_semaphores, plane, order, step, count
    )

    @pl.when(step == 0)
    def _():
        if norm:
            for first in range(0, values_ref.shape[0], QUERY_ROWS):
                rows = slice(first, first + QUERY_ROWS)
                low_ref[rows, :] = normalize(
                    values_ref[rows, :], vectors_ref[4:5, :], vectors_ref[5:6, :]
                ).astype(BF16)
        low_turned[...] = low_ref[...].T
        grad_turned[...] = grad_ref[...].T
        out_ref[...] = jnp.zeros_like(out_ref)
        back_ref[...] = jnp.zeros_like(back_ref)

    up = up_chunk[...]
    down = down_chunk[...]
    total = jnp.zeros((1, up.shape[1]), F32)
    pieces = low_ref.shape[0] // FEED_ROWS
    for piece in range(pieces):
        rows = slice(piece * FEED_ROWS, (piece + 1) * FEED_ROWS)
        active, derivative = gelu_parts(dot(low_ref[rows, :], up) + bias_ref[0])
        active_low = active.astype(BF16)
        hidden_low = (derivative * dot(grad_ref[rows, :], down)).astype(BF16)
        active_ref[rows, :] = active_low
        hidden_ref[rows, :] = hidden_low
        total = total + jnp.sum(hidden_low.astype(F32), axis=0, keepdims=True)
        out_ref[rows, :] += dot_last(active_low, down)
        back_ref[rows, :] += dot_last(hidden_low, up)
    grad_bias_ref[0] = total
    for piece in range(low_turned.shape[0] // FEED_ROWS):
        rows = slice(piece * FEED_ROWS, (piece + 1) * FEED_ROWS)
        grad_down_ref[0, rows, :] = dot(grad_turned[rows, :], active_ref[...]).astype(BF16)
        grad_up_ref[0, rows, :] = dot(low_turned[rows, :], hidden_ref[...]).astype(BF16)


def feed_half(place, values, grad, vectors, bias, slots, side, norm):
    row_count, model = values.shape
    up_source = Source(slots, 2, (side,))
    down_source = Source(slots, 3, (side,))
    steps = up_source.chunks()
    width = up_source.shape[2]

    def whole(shape):
        return pl.BlockSpec(shape, lambda step, place: (0, 0), pipeline_mode=pl.Buffered(1))

    total = pl.BlockSpec((row_count, model), lambda step, place: (0, 0))
    chunk = pl.BlockSpec((1, model, width), lambda step, place: (step, 0, 0))
    out_specs = [
        total,
        total,
        chunk,
        chunk,
        pl.BlockSpec((1, 1, width), lambda step, place: (step ^ place[1], 0, 0)),
    ]
    out_shape = [
        jax.ShapeDtypeStruct((row_count, model), F32),
        jax.ShapeDtypeStruct((row_count, model), F32),
        jax.ShapeDtypeStruct((steps, model, width), BF16),
        jax.ShapeDtypeStruct((steps, model, width), BF16),
        jax.ShapeDtypeStruct((steps, 1, width), F32),
    ]
    if norm:
        out_specs.append(total)
        out_shape.append(jax.ShapeDtypeStruct((row_count, model), BF16))
    return pl.pallas_call(
        functools.partial(
            feed_kernel, norm=norm, up_source=up_source, down_source=down_source
        ),
        grid_spec=pltpu.PrefetchScalarGridSpec(
            num_scalar_prefetch=1,
            grid=(steps,),
            in_specs=[
                whole((row_count, model)),
                whole((row_count, model)),
                whole((VECTOR_ROWS, model)),
                pl.BlockSpec(
                    (1, 1, width), lambda step, place: (2 * (step ^ place[1]) + place[0], 0, 0)
                ),
            ]
            + up_source.specs()
            + down_source.specs(),
            out_specs=out_specs,
            scratch_shapes=[
                pltpu.VMEM((model, row_count), BF16),
                pltpu.VMEM((model, row_count), BF16),
                pltpu.VMEM((row_count, width), BF16),
                pltpu.VMEM((row_count, width), BF16),
            ]
            + up_source.scratch()
            + down_source.scratch(),
        ),
        out_shape=out_shape,
        compiler_params=pltpu.CompilerParams(vmem_limit_bytes=60 << 20),
        cost_estimate=SMALL,
    )(place, values, grad, vectors, bias, *up_source.operands, *down_source.operands)


def norm_back_kernel(*refs, count, row):
    values_ref, vectors_ref, stream_ref = refs[:3]
    grad_refs = refs[3 : 3 + count]
    out_ref, low_ref, sums_ref = refs[3 + count :]
    values = values_ref[...].astype(F32)
    grad = grad_refs[0][...]
    for grad_ref in grad_refs[1:]:
        grad = grad + grad_ref[...]
    centred = values - jnp.mean(values, axis=-1, keepdims=True)
    inverse = lax.rsqrt(jnp.mean(centred * centred, axis=-1, keepdims=True) + NORM_EPS)
    normal = centred * inverse
    scaled = grad * vectors_ref[row : row + 1, :]
    product = scaled * normal
    back = inverse * (
        scaled
        - jnp.mean(scaled, axis=-1, keepdims=True)
        - normal * jnp.mean(product, axis=-1, keepdims=True)
    )
    result = stream_ref[...].astype(F32) + back
    low = result.astype(BF16)
    out_ref[...] = result
    low_ref[...] = low

    @pl.when(pl.program_id(0) == 0)
    def _():
        sums_ref[...] = jnp.zeros_like(sums_ref)

    sums_ref[0:1, :] += jnp.sum(grad * normal, axis=0, keepdims=True)
    sums_ref[1:2, :] += jnp.sum(grad, axis=0, keepdims=True)
    sums_ref[2:3, :] += jnp.sum(low.astype(F32), axis=0, keepdims=True)
    sums_ref[3:4, :] += jnp.sum(stream_ref[...].astype(F32), axis=0, keepdims=True)


def norm_back(values, vectors, row, stream, grads):
    row_count, model = values.shape
    panel = pl.BlockSpec((QUERY_ROWS, model), lambda step: (step, 0))
    return pl.pallas_call(
        functools.partial(norm_back_kernel, count=len(grads), row=row),
        grid=(row_count // QUERY_ROWS,),
        in_specs=[panel, pl.BlockSpec((VECTOR_ROWS, model), lambda step: (0, 0)), panel]
        + [panel] * len(grads),
        out_specs=[panel, panel, pl.BlockSpec((8, model), lambda step: (0, 0))],
        out_shape=[
            jax.ShapeDtypeStruct((row_count, model), F32),
            jax.ShapeDtypeStruct((row_count, model), BF16),
            jax.ShapeDtypeStruct((8, model), F32),
        ],
        compiler_params=pltpu.CompilerParams(vmem_limit_bytes=60 << 20),
        cost_estimate=SMALL,
    )(values, vectors, stream, *grads)


def project_kernel(*refs, source, block, lines, norm, residual):
    refs = list(refs)
    place_ref = refs.pop(0)
    values_ref = refs.pop(0)
    vectors_ref = refs.pop(0)
    residual_ref = refs.pop(0) if residual else None
    source_refs = refs[: len(source.operands)]
    refs = refs[len(source_refs) :]
    out_ref = refs.pop(0)
    low_ref = refs.pop(0) if norm is not None else values_ref
    buffer, semaphores = refs
    model = values_ref.shape[1]
    width = out_ref.shape[1]
    parts = model // (2 * width)
    item = pl.program_id(0)
    count = 2 * parts * len(lines)

    def order(item):
        return item % 2, (block * parts + item // 2) ^ place_ref[1]

    columns_ref = fetched(
        source, source_refs, buffer, semaphores, place_ref[PLACE_PLANE], order, item, count
    )
    if norm is not None:

        @pl.when(item == 0)
        def _():
            for first in range(0, values_ref.shape[0], QUERY_ROWS):
                rows = slice(first, first + QUERY_ROWS)
                low_ref[rows, :] = normalize(
                    values_ref[rows, :].astype(F32),
                    vectors_ref[norm : norm + 1, :],
                    vectors_ref[norm + 1 : norm + 2, :],
                ).astype(BF16)

    inside = item // 2 % parts
    column = (2 * inside + (item % 2 ^ place_ref[0])) * width
    row_count = values_ref.shape[0]
    step = row_count // 2
    for number, (line, scale) in enumerate(lines):

        @pl.when(item // (2 * parts) == number)
        def _(line=line, scale=scale):
            columns = columns_ref[...]
            for first in range(0, row_count, step):
                rows = slice(first, first + step)
                made = dot(low_ref[rows, :], columns)
                if line is not None:
                    made = made + vector_part(vectors_ref, line, column, width)
                if scale != 1.0:
                    made = made * scale
                if residual:
                    made = residual_ref[rows, :].astype(F32) + made
                out_ref[rows, :] = made.astype(out_ref.dtype)


def project(
    place, values, vectors, slots, group, block, lines, norm=None, residual=None, out_type=BF16
):
    row_count, model = values.shape
    source = Source(slots, group, (0, 1))
    width = source.shape[2]
    parts = model // (2 * width)

    def whole(shape):
        return pl.BlockSpec(shape, lambda *_: (0, 0), pipeline_mode=pl.Buffered(1))

    panel = pl.BlockSpec(
        (row_count, width),
        lambda item, place: (0, 2 * (item // 2) + (item % 2 ^ place[0])),
    )
    in_specs = [whole((row_count, model)), whole((VECTOR_ROWS, model))]
    operands = [values, vectors]
    if residual is not None:
        in_specs.append(panel)
        operands.append(residual)
    out_specs = [panel]
    out_shape = [jax.ShapeDtypeStruct((row_count, len(lines) * model), out_type)]
    if norm is not None:
        out_specs.append(pl.BlockSpec((row_count, model), lambda *_: (0, 0)))
        out_shape.append(jax.ShapeDtypeStruct((row_count, model), BF16))
    results = pl.pallas_call(
        functools.partial(
            project_kernel,
            source=source,
            block=block,
            lines=lines,
            norm=norm,
            residual=residual is not None,
        ),
        grid_spec=pltpu.PrefetchScalarGridSpec(
            num_scalar_prefetch=1,
            grid=(2 * parts * len(lines),),
            in_specs=in_specs + source.specs(),
            out_specs=out_specs,
            scratch_shapes=source.scratch(),
        ),
        out_shape=out_shape,
        compiler_params=pltpu.CompilerParams(vmem_limit_bytes=60 << 20),
        cost_estimate=SMALL,
    )(place, *operands, *source.operands)
    return results if norm is not None else results[0]


def project_back_kernel(*refs, source, block, count):
    refs = list(refs)
    place_ref = refs.pop(0)
    grad_refs = refs[:count]
    source_refs = refs[count : count + len(source.operands)]
    out_ref, total_ref, buffer, semaphores = refs[count + len(source.operands) :]
    model = out_ref.shape[1]
    width = grad_refs[0].shape[1]
    parts = model // (2 * width)
    item = pl.program_id(0)
    steps = 2 * parts * count

    def order(item):
        return item % 2, (block * parts + item // 2) ^ place_ref[1]

    columns_ref = fetched(
        source, source_refs, buffer, semaphores, place_ref[PLACE_PLANE], order, item, steps
    )

    @pl.when(item == 0)
    def _():
        total_ref[...] = jnp.zeros_like(total_ref)

    for number, grad_ref in enumerate(grad_refs):

        @pl.when(item // (2 * parts) == number)
        def _(grad_ref=grad_ref):
            columns = columns_ref[...]
            row_count = grad_ref.shape[0]
            size = row_count // 2
            for first in range(0, row_count, size):
                rows = slice(first, first + size)
                total_ref[rows, :] += dot_last(grad_ref[rows, :], columns)

    @pl.when(item == steps - 1)
    def _():
        out_ref[...] = total_ref[...].astype(out_ref.dtype)


def project_back(place, grads, slots, group, block, out_type):
    row_count, model = grads[0].shape
    source = Source(slots, group, (0, 1))
    width = source.shape[2]
    parts = model // (2 * width)

    def grad_panel(number):
        def index(item, place):
            column = 2 * (item // 2 % parts) + (item % 2 ^ place[0])
            last = 2 * (parts - 1) + (1 ^ place[0])
            done = item // (2 * parts) > number
            return 0, jnp.where(item // (2 * parts) == number, column, jnp.where(done, last, place[0]))

        return pl.BlockSpec((row_count, width), index)

    return pl.pallas_call(
        functools.partial(project_back_kernel, source=source, block=block, count=len(grads)),
        grid_spec=pltpu.PrefetchScalarGridSpec(
            num_scalar_prefetch=1,
            grid=(2 * parts * len(grads),),
            in_specs=[grad_panel(number) for number in range(len(grads))] + source.specs(),
            out_specs=pl.BlockSpec((row_count, model), lambda *_: (0, 0)),
            scratch_shapes=[pltpu.VMEM((row_count, model), F32)] + source.scratch(),
        ),
        out_shape=jax.ShapeDtypeStruct((row_count, model), out_type),
        compiler_params=pltpu.CompilerParams(vmem_limit_bytes=60 << 20),
        cost_estimate=SMALL,
    )(place, *grads, *source.operands)


NEAR = ((0, 1), (1, 0), (2, 3), (3, 2))


def pinned(*values):
    return lax.optimization_barrier(values)


def swap_bit(values, device_count, bit):
    return lax.ppermute(values, AXES, [(item, item ^ bit) for item in range(device_count)])


def move_planes(values, moves, plane_size):
    pairs = [
        (source * plane_size + inner, target * plane_size + inner)
        for source, target in moves
        for inner in range(plane_size)
    ]
    return lax.ppermute(values, AXES, pairs)


def inner_bits(device_count):
    bits = []
    bit = device_count // GROUPS // 2
    while bit > 1:
        bits.append(bit)
        bit //= 2
    return bits


def spread_begin(own):
    rows = own.shape[-2] // 2
    return [own[..., :rows, :], own[..., rows:, :]]


def spread_swaps(parts, stage, device_count):
    bits = inner_bits(device_count)
    return [
        swap_bit(parts[0], device_count, bits[len(bits) - 1 - stage]),
        swap_bit(parts[1], device_count, bits[stage]),
    ]


def spread_on(parts, got, device_count):
    for stage in range(1, len(inner_bits(device_count))):
        parts = [jnp.stack([part, item]) for part, item in zip(parts, got, strict=True)]
        got = spread_swaps(parts, stage, device_count)
    return parts, got


def swap_cores(items, device_count):
    return [swap_bit(item, device_count, 1) for item in items]


def flat_slot(parts, got):
    shape = (-1,) + parts[0].shape[-2:]
    return tuple(item.reshape(shape) for item in (parts[0], got[0], parts[1], got[1]))


class Sum:
    def __init__(self, kept, got, absolute, swaps=()):
        self.kept = kept
        self.got = got
        self.absolute = absolute
        self.swaps = list(swaps)

    def joined(self, got):
        return Sum(self.kept, self.got, self.absolute, self.swaps + [got])


def stage_kernel(*refs, members, terms, parts):
    ins = refs[1:-parts]
    outs = refs[-parts:]
    per_part = 2 * members + terms
    for part, out_ref in enumerate(outs):
        mine = ins[part * per_part : (part + 1) * per_part]
        for member in range(members):
            total = mine[2 * member][0].astype(F32) + mine[2 * member + 1][0].astype(F32)
            for swap_ref in mine[2 * members :]:
                total = total + swap_ref[member, 0].astype(F32)
            out_ref[member, 0] = total.astype(BF16)


def stage_sends(place, pending, device_count):
    levels = len(inner_bits(device_count))
    stage = len(pending.swaps)
    chunks, rows, width = pending.kept[0].shape
    half = rows // 2
    count = chunks >> (stage + 1)
    members = len(pending.kept)

    def relative(part, step):
        if part == 0:
            return count + step
        return (step << (stage + 1)) + (1 << stage)

    def stored(part):
        def index(step, place):
            chunk = relative(part, step)
            return (chunk ^ place[1] if pending.absolute else chunk), part, 0

        return pl.BlockSpec((1, half, width), index)

    def swapped(part, earlier):
        def index(step, place):
            chunk = relative(part, step)
            return 0, (chunk if part == 0 else chunk >> (earlier + 1)), 0, 0

        return pl.BlockSpec((members, 1, half, width), index)

    in_specs = []
    operands = []
    for part in range(2):
        for kept, got in zip(pending.kept, pending.got, strict=True):
            in_specs += [stored(part)] * 2
            operands += [kept, got]
        for earlier, items in enumerate(pending.swaps):
            in_specs.append(swapped(part, earlier))
            operands.append(items[part])
    assert stage < levels
    return pl.pallas_call(
        functools.partial(stage_kernel, members=members, terms=stage, parts=2),
        grid_spec=pltpu.PrefetchScalarGridSpec(
            num_scalar_prefetch=1,
            grid=(count,),
            in_specs=in_specs,
            out_specs=[pl.BlockSpec((members, 1, half, width), lambda step, place: (0, step, 0, 0))]
            * 2,
        ),
        out_shape=[jax.ShapeDtypeStruct((members, count, half, width), BF16)] * 2,
        compiler_params=pltpu.CompilerParams(vmem_limit_bytes=60 << 20),
        cost_estimate=SMALL,
    )(place, *operands)


def stage_swaps(sends, pending, device_count):
    bits = inner_bits(device_count)
    stage = len(pending.swaps)
    return [
        swap_bit(sends[0], device_count, bits[stage]),
        swap_bit(sends[1], device_count, bits[len(bits) - 1 - stage]),
    ]


def finish_stages(place, pending, device_count):
    while len(pending.swaps) < len(inner_bits(device_count)):
        sends = stage_sends(place, pending, device_count)
        pending = pending.joined(stage_swaps(sends, pending, device_count))
    return pending


def total_kernel(*refs, members, stages):
    place_ref = refs[0]
    stored = refs[1 : 1 + 2 * members]
    swaps = refs[1 + 2 * members : 1 + 2 * members + 2 * stages]
    kept_ref, sent_ref = refs[1 + 2 * members + 2 * stages :]

    def total(part, member):
        result = stored[2 * member][0].astype(F32) + stored[2 * member + 1][0].astype(F32)
        for stage in range(stages):
            result = result + swaps[2 * stage + part][member, 0].astype(F32)
        return result

    for part in range(2):

        @pl.when(pl.program_id(0) // 2 == part)
        def _(part=part):
            if members == 1:
                made = total(part, 0)
                kept_ref[...] = made
                sent_ref[...] = made.astype(BF16)
            else:
                low = total(part, 0)
                high = total(part, 1)
                even = place_ref[2] == 0
                kept_ref[...] = jnp.where(even, low, high)
                sent_ref[...] = jnp.where(even, high, low).astype(BF16)


def plane_totals(place, pending):
    chunks, rows, width = pending.kept[0].shape
    quarter = rows // 4
    members = len(pending.kept)

    def stored(step, place):
        return (place[1] if pending.absolute else 0), step, 0

    in_specs = []
    operands = []
    for kept, got in zip(pending.kept, pending.got, strict=True):
        in_specs += [pl.BlockSpec((1, quarter, width), stored)] * 2
        operands += [kept, got]
    for items in pending.swaps:
        for part in range(2):
            in_specs.append(
                pl.BlockSpec(
                    (members, 1, quarter, width),
                    (lambda step, place: (0, 0, jnp.minimum(step, 1), 0))
                    if part == 0
                    else (lambda step, place: (0, 0, jnp.maximum(step - 2, 0), 0)),
                )
            )
            operands.append(items[part])
    panel = pl.BlockSpec((quarter, width), lambda step, place: (step, 0))
    return pl.pallas_call(
        functools.partial(total_kernel, members=members, stages=len(pending.swaps)),
        grid_spec=pltpu.PrefetchScalarGridSpec(
            num_scalar_prefetch=1,
            grid=(4,),
            in_specs=in_specs,
            out_specs=[panel, panel],
        ),
        out_shape=[
            jax.ShapeDtypeStruct((rows, width), F32),
            jax.ShapeDtypeStruct((rows, width), BF16),
        ],
        compiler_params=pltpu.CompilerParams(vmem_limit_bytes=60 << 20),
        cost_estimate=SMALL,
    )(place, *operands)


def column_half(values, half, width):
    rows, columns = values.shape
    if columns == 2 * width:
        return lax.dynamic_slice_in_dim(values, half * width, width, 1)
    pieces = values.reshape(rows, -1, 2, width)
    return lax.dynamic_index_in_dim(pieces, half, 2, keepdims=False).reshape(rows, -1)


def weight_half(pairs, width):
    terms = []
    for left, right in pairs:
        product = dot_rows(left, right).astype(BF16)
        if product.shape[1] == width:
            terms.append(product[None])
        else:
            terms.append(jnp.swapaxes(product.reshape(product.shape[0], -1, width), 0, 1))
    return jnp.concatenate(terms, axis=0)


def dot_high(left, right, dims):
    return lax.dot_general(
        left, right, (dims, ((), ())), precision=HIGHEST, preferred_element_type=F32
    )


def update_kernel(
    place_ref,
    total_ref,
    near_ref,
    far_ref,
    other_ref,
    weight_ref,
    average_ref,
    moment1_ref,
    moment2_ref,
    stats_ref,
    bases_ref,
    grad_ref,
    first_ref,
    second_ref,
    new_ref,
    new_average_ref,
    copy_ref,
    new_stats_ref,
    new_bases_ref,
    state_ref,
    solved_ref,
    *,
    chunks,
):
    blocks = stats_ref.shape[0]
    step = pl.program_id(0)
    rows = weight_ref.shape[0]

    @pl.when(step == 0)
    def _():
        @pl.when(place_ref[PLACE_PLANE] == 0)
        def _():
            grad_ref[...] = total_ref[...] + near_ref[...].astype(F32) + far_ref[...].astype(F32)

        @pl.when(place_ref[PLACE_PLANE] != 0)
        def _():
            grad_ref[...] = other_ref[...]

        for block in range(blocks):
            grad = grad_ref[:, block * BLK : (block + 1) * BLK]
            square = dot_high(grad, grad, ((0,), (0,)))
            renewed = BETA_TWO * stats_ref[block] + (1.0 - BETA_TWO) * square
            new_stats_ref[block] = renewed
            product = dot_high(renewed, bases_ref[block], ((1,), (0,)))
            gram = dot_high(product, product, ((0,), (0,)))
            state_ref[block] = jnp.concatenate([gram, product.T], axis=1)

    def rotate(chunk):
        for block in range(blocks):
            columns = slice(block * BLK, (block + 1) * BLK)
            basis = bases_ref[block]
            turned = dot_high(
                grad_ref[chunk * rows : (chunk + 1) * rows, columns], basis, ((1,), (0,))
            )
            first = BETA_ONE * moment1_ref[:, columns] + (1.0 - BETA_ONE) * turned
            second = BETA_TWO * moment2_ref[:, columns] + (1.0 - BETA_TWO) * turned * turned
            first_ref[:, columns] = first
            second_ref[:, columns] = second
            direction = (
                first
                / (1.0 - BETA_ONE**STEP)
                / (jnp.sqrt(second / (1.0 - BETA_TWO**STEP)) + ADAM_EPS)
            )
            returned = dot_high(direction, basis, ((1,), (1,)))
            weight = weight_ref[:, columns]
            updated = weight - RATE * (returned + DECAY * weight)
            new_ref[:, columns] = updated
            new_average_ref[:, columns] = (
                AVERAGE * average_ref[:, columns] + (1.0 - AVERAGE) * updated
            )
            copy_ref[:, columns] = updated.astype(BF16)

    row_index = lax.broadcasted_iota(jnp.int32, (PANEL, 2 * BLK), 0)
    panels = BLK // PANEL

    def eliminate(panel):
        top_rows = slice(panel * PANEL, (panel + 1) * PANEL)
        tops = [state_ref[block, top_rows, :] for block in range(blocks)]
        for row in range(PANEL):
            lane = panel * PANEL + row
            for block in range(blocks):
                top = tops[block]
                pivot = top[row : row + 1, lane : lane + 1]
                inverse = lax.rsqrt(pivot)
                inverse = inverse * (1.5 - 0.5 * pivot * inverse * inverse)
                scaled = top[row : row + 1] * inverse
                reduced = top - (top[:, lane : lane + 1] * inverse) * scaled
                tops[block] = jnp.where(
                    row_index == row, scaled, jnp.where(row_index > row, reduced, top)
                )
        for block in range(blocks):
            solved_ref[block, top_rows, :] = tops[block][:, BLK:]
            if panel + 1 < panels:
                rest = slice((panel + 1) * PANEL, BLK)
                state_ref[block, rest, :] -= dot_high(
                    tops[block][:, rest], tops[block], ((0,), (0,))
                )

    for chunk in range(chunks):

        @pl.when(step == chunk)
        def _(chunk=chunk):
            rotate(chunk)
            for panel in range(panels * chunk // chunks, panels * (chunk + 1) // chunks):
                eliminate(panel)
            if chunk == chunks - 1:
                for block in range(blocks):
                    new_bases_ref[block] = solved_ref[block].T


def rotated_update(
    place, total, near, far, other, weights, average, moment1, moment2, stats, bases
):
    rows, width = weights.shape
    chunks = rows // QUERY_ROWS
    whole = pl.BlockSpec(
        (rows, width), lambda step, place: (0, 0), pipeline_mode=pl.Buffered(1)
    )
    big = pl.BlockSpec((QUERY_ROWS, width), lambda step, place: (step, 0))
    small = pl.BlockSpec(stats.shape, lambda step, place: (0, 0, 0))
    wide = jax.ShapeDtypeStruct(weights.shape, F32)
    return pl.pallas_call(
        functools.partial(update_kernel, chunks=chunks),
        grid_spec=pltpu.PrefetchScalarGridSpec(
            num_scalar_prefetch=1,
            grid=(chunks,),
            in_specs=[whole] * 4 + [big] * 4 + [small] * 2,
            out_specs=[pl.BlockSpec((rows, width), lambda step, place: (0, 0))]
            + [big] * 5
            + [small] * 2,
            scratch_shapes=[
                pltpu.VMEM(stats.shape[:2] + (2 * BLK,), F32),
                pltpu.VMEM(stats.shape, F32),
            ],
        ),
        out_shape=[wide] * 5
        + [jax.ShapeDtypeStruct(weights.shape, BF16)]
        + [jax.ShapeDtypeStruct(stats.shape, F32)] * 2,
        compiler_params=pltpu.CompilerParams(vmem_limit_bytes=60 << 20),
        cost_estimate=SMALL,
    )(place, total, near, far, other, weights, average, moment1, moment2, stats, bases)


def adam_update(grad, values, moment1, moment2):
    first_moment = BETA_ONE * moment1 + (1.0 - BETA_ONE) * grad
    second_moment = BETA_TWO * moment2 + (1.0 - BETA_TWO) * grad * grad
    updated = values - VECTOR_RATE * (first_moment / (1.0 - BETA_ONE**STEP)) / (
        jnp.sqrt(second_moment / (1.0 - BETA_TWO**STEP)) + ADAM_EPS
    )
    return (first_moment, second_moment, updated)


def exchange_vectors(pieces, rows, width):
    device_count = pieces.shape[0]
    sublanes = 8 if pieces.dtype == F32 else 16
    room = sublanes * LANES
    size = rows * width
    tiles = -(-size // room)
    padded = jnp.pad(pieces, ((0, 0), (0, tiles * room - size)))
    padded = padded.reshape(device_count, tiles * sublanes, LANES)
    got = lax.all_to_all(padded, AXES, split_axis=0, concat_axis=0, tiled=True)
    return got.reshape(device_count, -1)[:, :size].reshape(device_count, rows, width)


def local(
    tokens,
    memory,
    page_lengths,
    slot_masks,
    upstream,
    weights,
    weight_average,
    weight_moment1,
    weight_moment2,
    stats,
    bases,
    vectors,
    vector_average,
    vector_moment1,
    vector_moment2,
):
    row_count, model = tokens.shape
    width = weights.shape[1]
    group_size = lax.axis_size("mem")
    device_count = lax.axis_size("seq") * group_size
    device = lax.axis_index(AXES)
    member = lax.axis_index("mem")
    core = device % 2
    quarter = memory.shape[1]
    scale_q = HEAD ** (-0.5)
    plane_size = device_count // GROUPS
    plane = device // plane_size
    inner = (device % plane_size) // 2
    here = jnp.stack([core, inner, plane % 2, plane]).astype(jnp.int32)
    away = jnp.stack([1 - core, inner, plane % 2, plane]).astype(jnp.int32)

    vector_shape = vectors.shape
    own = weights.astype(BF16)
    first = move_planes(own, ((0, 2), (1, 0), (2, 3), (3, 1)), plane_size)
    memory_padded = jnp.pad(memory, ((0, 0), (0, SLOT_PAD - quarter), (0, 0)))
    memory_here = lax.all_to_all(memory_padded, "mem", split_axis=0, concat_axis=0, tiled=True)
    memory_here = memory_here.reshape(group_size * SLOT_PAD, model)
    parts = spread_begin(own)
    got = spread_swaps(parts, 0, device_count)
    first, got, memory_here, own = pinned(first, got, memory_here, own)
    held = jnp.where((plane == 0) | (plane == 3), own, first)
    near = move_planes(held, NEAR, plane_size)
    middle = move_planes(own, ((1, 2), (2, 1)), plane_size)
    parts, got = spread_on(parts, got, device_count)
    pieces = jnp.broadcast_to(
        vectors.astype(BF16).reshape(1, -1), (device_count, vectors.size)
    )
    vector_pieces = exchange_vectors(pieces, *vector_shape)
    near, middle, first, got, vector_pieces = pinned(near, middle, first, got, vector_pieces)
    slot_zero = flat_slot(parts, got)
    even = plane % 2 == 0
    parts_one = spread_begin(jnp.where(even, first, near))
    got_one = spread_swaps(parts_one, 0, device_count)
    last = move_planes(middle, ((1, 0), (2, 3)), plane_size)
    zero_away = swap_cores(slot_zero, device_count)
    vector_rows = jnp.swapaxes(vector_pieces, 0, 1).reshape(vector_shape[0], model).astype(F32)
    table = jnp.pad(vector_rows, ((0, VECTOR_ROWS - vector_shape[0]), (0, 0)))
    got_one, zero_away, vector_rows, table = pinned(got_one, zero_away, vector_rows, table)
    parts_one, got_one = spread_on(parts_one, got_one, device_count)
    one_away = swap_cores(parts_one, device_count)
    got_one, one_away, last = pinned(got_one, one_away, last)
    got_one_away = swap_cores(got_one, device_count)
    parts_two = spread_begin(jnp.where((plane == 1) | (plane == 2), middle, last))
    got_two = spread_swaps(parts_two, 0, device_count)
    slots = [
        (slot_zero, tuple(zero_away)),
        (flat_slot(parts_one, got_one), flat_slot(one_away, got_one_away)),
    ]

    live_rows = (jnp.arange(row_count) < page_lengths[0]).astype(F32)[:, None]
    slots_here = lax.dynamic_slice_in_dim(slot_masks, member, 1, 0).reshape(group_size, quarter)
    slots_here = jnp.pad(slots_here, ((0, 0), (0, SLOT_PAD - quarter))).reshape(-1, 1)
    slot_bias = jnp.broadcast_to(
        jnp.where(slots_here > 0, 0.0, MASKED).astype(F32), (group_size * SLOT_PAD, LANES)
    )
    pairs = HEADS // 2
    self_firsts = (0, pairs, 2 * pairs)
    cross_firsts = (0, 0, pairs)

    self_low, low_one = project(
        here, tokens, table, slots, 0, 0, ((6, scale_q), (None, 1.0), (7, 1.0)), norm=0
    )
    got_two, self_low = pinned(got_two, self_low)
    parts_two, got_two = spread_on(parts_two, got_two, device_count)
    two_away = swap_cores(parts_two, device_count)
    attended, self_log = attention_forward(self_low, self_low, self_low, self_firsts)
    got_two, two_away, attended = pinned(got_two, two_away, attended)
    got_two_away = swap_cores(got_two, device_count)
    parts_three = spread_begin(jnp.where(even, near, first))
    got_three = spread_swaps(parts_three, 0, device_count)
    after_self = project(
        here, attended, table, slots, 0, 3, ((8, 1.0),), residual=tokens, out_type=F32
    )
    got_two_away, after_self = pinned(got_two_away, after_self)
    slots.append((flat_slot(parts_two, got_two), flat_slot(two_away, got_two_away)))
    queries_cross, low_two = project(
        here, after_self, table, slots, 1, 0, ((9, scale_q),), norm=2
    )
    got_three, queries_cross, memory_here = pinned(got_three, queries_cross, memory_here)
    parts_three, got_three = spread_on(parts_three, got_three, device_count)
    three_away = swap_cores(parts_three, device_count)
    cross_low = project(here, memory_here, table, slots, 1, 1, ((None, 1.0), (10, 1.0)))
    merged, cross_log = attention_forward(
        queries_cross, cross_low, cross_low, cross_firsts, slot_bias
    )
    got_three, three_away, merged = pinned(got_three, three_away, merged)
    got_three_away = swap_cores(got_three, device_count)
    after_cross = project(
        here, merged, table, slots, 1, 3, ((11, 1.0),), residual=after_self, out_type=F32
    )
    grad_low_three = (upstream.astype(F32) * live_rows).astype(BF16)
    got_three_away, after_cross, grad_low_three = pinned(
        got_three_away, after_cross, grad_low_three
    )
    slots.append((flat_slot(parts_three, got_three), flat_slot(three_away, got_three_away)))

    bias_up = vector_rows[13:17].reshape(-1, 1, width)
    out_a, back_a, up_sent, down_sent, bias_sent, low_three = feed_half(
        away, after_cross, grad_low_three, table, bias_up, slots, 1, True
    )
    up_got = swap_bit(up_sent, device_count, 1)
    down_got = swap_bit(down_sent, device_count, 1)
    low_three, up_sent, down_sent = pinned(low_three, up_sent, down_sent)
    out_b, back_b, up_kept, down_kept, bias_kept = feed_half(
        here, low_three, grad_low_three, table, bias_up, slots, 0, False
    )
    up_got, down_got, out_b, back_b, up_kept, down_kept = pinned(
        up_got, down_got, out_b, back_b, up_kept, down_kept
    )
    feed_sum = Sum((up_kept, down_kept), (up_got, down_got), False)
    feed_sends = stage_sends(here, feed_sum, device_count)
    feed_sends, back_b = pinned(feed_sends, back_b)
    feed_swaps = stage_swaps(feed_sends, feed_sum, device_count)

    result = (after_cross + (out_a + out_b) + vector_rows[12]) * live_rows
    mixed = result.astype(BF16)
    bias_even = jnp.where(core == 0, bias_kept, bias_sent)
    bias_odd = jnp.where(core == 0, bias_sent, bias_kept)
    grad_bias_up = jnp.concatenate([bias_even, bias_odd], axis=1).reshape(4, model)

    grad_two, grad_low_two, sums_three = norm_back(
        after_cross, table, 4, grad_low_three, (back_a, back_b)
    )
    grad_merged = project_back(here, (grad_low_two,), slots, 1, 3, BF16)
    cross_operands = (
        queries_cross,
        cross_low,
        cross_low,
        cross_firsts,
        grad_merged,
        merged,
        cross_log,
        slot_bias,
    )
    cross_whole, (queries_part, keys_part, values_part) = attention_backward(
        away, width, *cross_operands, None
    )
    cross_whole, (queries_own, keys_own, values_own) = attention_backward(
        here, width, *cross_operands, cross_whole
    )
    grad_queries_cross, grad_keys_cross, grad_values_cross = cross_whole
    feed_swaps, queries_part, queries_own, grad_queries_cross = pinned(
        feed_swaps, queries_part, queries_own, grad_queries_cross
    )
    feed_sum = feed_sum.joined(feed_swaps)
    feed_sends = stage_sends(here, feed_sum, device_count)
    feed_sends, queries_part, queries_own, grad_queries_cross = pinned(
        feed_sends, queries_part, queries_own, grad_queries_cross
    )
    feed_swaps = stage_swaps(feed_sends, feed_sum, device_count)
    cross_sent = weight_half(
        (
            (low_two, queries_part),
            (memory_here, keys_part),
            (memory_here, values_part),
            (merged, column_half(grad_low_two, 1 - core, width)),
        ),
        width,
    )
    cross_sent, queries_own, grad_queries_cross = pinned(
        cross_sent, queries_own, grad_queries_cross
    )
    cross_got = swap_bit(cross_sent, device_count, 1)
    cross_kept = weight_half(
        (
            (low_two, queries_own),
            (memory_here, keys_own),
            (memory_here, values_own),
            (merged, column_half(grad_low_two, core, width)),
        ),
        width,
    )
    grad_normed_two = project_back(here, (grad_queries_cross,), slots, 1, 0, F32)

    grad_one, grad_low_one, sums_two = norm_back(
        after_self, table, 2, grad_two, (grad_normed_two,)
    )
    grad_attended = project_back(here, (grad_low_one,), slots, 0, 3, BF16)
    feed_swaps, cross_got, cross_kept, grad_attended = pinned(
        feed_swaps, cross_got, cross_kept, grad_attended
    )
    feed_sum = finish_stages(here, feed_sum.joined(feed_swaps), device_count)
    feed_kept, feed_sent = plane_totals(here, feed_sum)
    cross_sum = Sum((cross_kept,), (cross_got,), True)
    cross_sends = stage_sends(here, cross_sum, device_count)
    feed_sent, cross_sends, grad_attended = pinned(feed_sent, cross_sends, grad_attended)
    feed_got = move_planes(feed_sent, NEAR, plane_size)
    cross_swaps = stage_swaps(cross_sends, cross_sum, device_count)
    self_operands = (
        self_low,
        self_low,
        self_low,
        self_firsts,
        grad_attended,
        attended,
        self_log,
        None,
    )
    self_whole, (queries_part, keys_part, values_part) = attention_backward(
        away, width, *self_operands, None
    )
    self_sent = weight_half(
        (
            (low_one, queries_part),
            (low_one, keys_part),
            (low_one, values_part),
            (attended, column_half(grad_low_one, 1 - core, width)),
        ),
        width,
    )
    feed_got, cross_swaps, self_sent, self_whole = pinned(
        feed_got, cross_swaps, self_sent, self_whole
    )
    self_got = swap_bit(self_sent, device_count, 1)
    feed_kept = feed_kept + feed_got.astype(F32)
    cross_sum = cross_sum.joined(cross_swaps)
    cross_sends = stage_sends(here, cross_sum, device_count)
    feed_sent, cross_sends, self_whole = pinned(
        feed_kept.astype(BF16), cross_sends, self_whole
    )
    feed_got = move_planes(feed_sent, ((0, 2), (1, 3)), plane_size)
    cross_swaps = stage_swaps(cross_sends, cross_sum, device_count)
    self_whole, (queries_own, keys_own, values_own) = attention_backward(
        here, width, *self_operands, self_whole
    )
    grad_queries_self, grad_keys_self, grad_values_self = self_whole
    self_kept = weight_half(
        (
            (low_one, queries_own),
            (low_one, keys_own),
            (low_one, values_own),
            (attended, column_half(grad_low_one, core, width)),
        ),
        width,
    )
    self_got, cross_swaps, self_kept = pinned(self_got, cross_swaps, self_kept)
    self_sum = Sum((self_kept,), (self_got,), True)
    self_sends = stage_sends(here, self_sum, device_count)
    self_sends, grad_queries_self, cross_swaps = pinned(
        self_sends, grad_queries_self, cross_swaps
    )
    self_swaps = stage_swaps(self_sends, self_sum, device_count)
    cross_sum = finish_stages(here, cross_sum.joined(cross_swaps), device_count)
    grad_normed_one = project_back(
        here,
        (grad_queries_self, grad_keys_self, grad_values_self),
        slots,
        0,
        0,
        F32,
    )
    grad_normed_one, cross_swaps = pinned(grad_normed_one, cross_sum.swaps)
    cross_sum.swaps = list(cross_swaps)
    cross_total, cross_sent = plane_totals(here, cross_sum)
    self_swaps, cross_sent, grad_normed_one = pinned(self_swaps, cross_sent, grad_normed_one)
    cross_got = move_planes(cross_sent, ((0, 1), (3, 2)), plane_size)
    self_sum = self_sum.joined(self_swaps)
    self_sends = stage_sends(here, self_sum, device_count)
    self_sends, grad_normed_one = pinned(self_sends, grad_normed_one)
    self_swaps = stage_swaps(self_sends, self_sum, device_count)
    input_grad, _, sums_one = norm_back(tokens, table, 0, grad_one, (grad_normed_one,))
    self_swaps, cross_got, sums_one, grad_keys_cross = pinned(
        self_swaps, cross_got, sums_one, grad_keys_cross
    )
    self_sum = finish_stages(here, self_sum.joined(self_swaps), device_count)
    self_total, self_sent = plane_totals(here, self_sum)
    self_sent, sums_one, grad_keys_cross = pinned(self_sent, sums_one, grad_keys_cross)
    self_got = move_planes(self_sent, ((1, 0), (3, 2)), plane_size)
    cross_total = cross_total + cross_got.astype(F32)
    cross_sent, grad_keys_cross = pinned(cross_total.astype(BF16), grad_keys_cross)
    cross_got = move_planes(cross_sent, ((2, 1),), plane_size)
    memory_back = project_back(
        here, (grad_keys_cross, grad_values_cross), slots, 1, 1, BF16
    )
    memory_back = lax.all_to_all(
        memory_back.reshape(group_size, SLOT_PAD, model),
        "mem",
        split_axis=0,
        concat_axis=0,
        tiled=True,
    )
    memory_back = memory_back[:, :quarter].astype(F32)
    vector_head = jnp.stack(
        [
            sums_one[0],
            sums_one[1],
            sums_two[0],
            sums_two[1],
            sums_three[0],
            sums_three[1],
            column_total(grad_queries_self),
            column_total(grad_values_self),
            sums_two[2],
            column_total(grad_queries_cross),
            column_total(grad_values_cross),
            sums_three[2],
            sums_three[3],
        ],
        axis=0,
    )
    vector_terms = jnp.concatenate([vector_head, grad_bias_up], axis=0)
    vector_terms = jnp.swapaxes(
        vector_terms.reshape(vector_shape[0], device_count, vector_shape[1]), 0, 1
    )
    vector_parts = exchange_vectors(vector_terms.reshape(device_count, -1), *vector_shape)
    vector_grad = jnp.sum(vector_parts, axis=0)

    self_got, cross_got, feed_got = pinned(self_got, cross_got, feed_got)
    self_sent = (self_total + self_got.astype(F32)).astype(BF16)
    self_sent, cross_got, feed_got = pinned(self_sent, cross_got, feed_got)
    self_far = move_planes(self_sent, ((2, 0),), plane_size)
    group_other = jnp.where(
        plane < 2,
        cross_total + cross_got.astype(F32),
        feed_kept + feed_got.astype(F32),
    )
    group_other, self_far, memory_back, vector_grad, mixed = pinned(
        group_other, self_far, memory_back, vector_grad, mixed
    )
    (
        weight_grad,
        weight_first,
        weight_second,
        new_weights,
        new_average,
        weights_copy,
        new_stats,
        new_bases,
    ) = rotated_update(
        here,
        self_total,
        self_got,
        self_far,
        group_other,
        weights,
        weight_average,
        weight_moment1,
        weight_moment2,
        stats,
        bases,
    )
    vector_first, vector_second, new_vectors = adam_update(
        vector_grad, vectors, vector_moment1, vector_moment2
    )
    new_vector_average = AVERAGE * vector_average + (1.0 - AVERAGE) * new_vectors
    return (
        mixed,
        input_grad,
        memory_back,
        weight_grad,
        weight_first,
        weight_second,
        new_weights,
        new_average,
        weights_copy,
        new_stats,
        new_bases,
        vector_grad,
        vector_first,
        vector_second,
        new_vectors,
        new_vector_average,
        new_vectors.astype(BF16),
        vector_grad[12],
    )


def solution(mesh):
    return jax.shard_map(
        local,
        mesh=mesh,
        in_specs=(
            P(("seq", "mem"), None),
            P("seq", "mem", None),
            P(("seq", "mem")),
            P("seq", None),
            P(("seq", "mem"), None),
            P(None, ("seq", "mem")),
            P(None, ("seq", "mem")),
            P(None, ("seq", "mem")),
            P(None, ("seq", "mem")),
            P(("seq", "mem"), None, None),
            P(("seq", "mem"), None, None),
            P(None, ("seq", "mem")),
            P(None, ("seq", "mem")),
            P(None, ("seq", "mem")),
            P(None, ("seq", "mem")),
        ),
        out_specs=(
            P(("seq", "mem"), None),
            P(("seq", "mem"), None),
            P("seq", "mem", None),
            P(None, ("seq", "mem")),
            P(None, ("seq", "mem")),
            P(None, ("seq", "mem")),
            P(None, ("seq", "mem")),
            P(None, ("seq", "mem")),
            P(None, ("seq", "mem")),
            P(("seq", "mem"), None, None),
            P(("seq", "mem"), None, None),
            P(None, ("seq", "mem")),
            P(None, ("seq", "mem")),
            P(None, ("seq", "mem")),
            P(None, ("seq", "mem")),
            P(None, ("seq", "mem")),
            P(None, ("seq", "mem")),
            P(("seq", "mem")),
        ),
        check_vma=False,
    )
```

```python
import functools

import jax
import jax.numpy as jnp
from jax import lax
from jax.experimental import pallas as pl
from jax.experimental.pallas import tpu as pltpu
from jax.sharding import PartitionSpec as P

HEADS = 16
HEAD = 64
BLK = 128
STEP = 10
LANES = 128
QUERY_ROWS = 256
FORWARD_ROWS = 512
FEED_ROWS = 1024
SLOT_PAD = 160
PANEL = 32
GROUPS = 4
AXES = ("seq", "mem")
SMALL = pl.CostEstimate(flops=1 << 20, bytes_accessed=1 << 16, transcendentals=0)

F32 = jnp.float32
BF16 = jnp.bfloat16
HIGHEST = lax.Precision.HIGHEST
NORM_EPS = 1e-05
ADAM_EPS = 1e-08
BETA_ONE = 0.9
BETA_TWO = 0.95
RATE = 0.04
VECTOR_RATE = 0.4
DECAY = 0.01
AVERAGE = 0.999
MASKED = -1e30
CONTRACT_ROWS = (((0,), (0,)), ((), ()))
CONTRACT_LAST = (((1,), (1,)), ((), ()))


def dot(left, right):
    return jnp.dot(left, right, preferred_element_type=F32)


def dot_last(left, right):
    return lax.dot_general(left, right, CONTRACT_LAST, preferred_element_type=F32)


def dot_rows(left, right):
    return lax.dot_general(left, right, CONTRACT_ROWS, preferred_element_type=F32)


def normalize(values, scale_gain, offset):
    centre = jnp.mean(values, axis=-1, keepdims=True)
    centred = values - centre
    variance = jnp.mean(centred * centred, axis=-1, keepdims=True)
    return centred * lax.rsqrt(variance + NORM_EPS) * scale_gain + offset


def causal_mask(scores, first_key, first_query):
    key_pos = lax.broadcasted_iota(jnp.int32, scores.shape, 0) + first_key
    query_pos = lax.broadcasted_iota(jnp.int32, scores.shape, 1) + first_query
    return jnp.where(key_pos <= query_pos, scores, MASKED)


def head_of_lane(shape):
    return lax.broadcasted_iota(jnp.int32, shape, 1) // HEAD


def one_head(values, lane_head, head):
    return jnp.where(lane_head == head, values, jnp.zeros_like(values))


def widen(bias, columns):
    return jnp.concatenate([bias] * (columns // LANES), axis=1)


def attention_forward_kernel(*refs, causal):
    if causal:
        q_ref, k_ref, v_ref, out_ref, log_ref = refs
    else:
        q_ref, k_ref, v_ref, bias_ref, out_ref, log_ref = refs
    keys = k_ref[...]
    key_count = keys.shape[0]
    values_turned = v_ref[...].T
    lane_head = head_of_lane(keys.shape)
    key_heads = [one_head(keys, lane_head, head) for head in range(2)]
    units = [
        (block, head) for block in range(q_ref.shape[0] // FORWARD_ROWS) for head in range(2)
    ]

    def scores_of(unit):
        block, head = unit
        seen = (block + 1) * FORWARD_ROWS if causal else key_count
        queries = q_ref[block * FORWARD_ROWS : (block + 1) * FORWARD_ROWS, :]
        scores = dot_last(key_heads[head][:seen], queries)
        if not causal:
            return scores + widen(bias_ref[...], FORWARD_ROWS)
        last = causal_mask(scores[seen - FORWARD_ROWS :], 0, 0)
        if seen == FORWARD_ROWS:
            return last
        return jnp.concatenate([scores[: seen - FORWARD_ROWS], last], axis=0)

    scores = scores_of(units[0])
    outs = []
    for item, (block, head) in enumerate(units):
        later = scores_of(units[item + 1]) if item + 1 < len(units) else None
        rows = slice(block * FORWARD_ROWS, (block + 1) * FORWARD_ROWS)
        largest = jnp.max(scores, axis=0, keepdims=True)
        raised = jnp.exp(scores - largest)
        summed = jnp.sum(raised, axis=0, keepdims=True)
        turned = values_turned[head * HEAD : (head + 1) * HEAD, : scores.shape[0]]
        outs.append(dot(turned, raised.astype(BF16)) / summed)
        log_ref[0, head : head + 1, rows] = largest + jnp.log(summed)
        if head == 1:
            out_ref[rows, :] = jnp.concatenate(outs, axis=0).T.astype(BF16)
            outs = []
        scores = later


def attention_backward_kernel(*refs, causal):
    _, q_ref, k_ref, v_ref, grad_ref, out_ref, log_ref = refs[:7]
    bias_ref = None if causal else refs[7]
    dq_ref, dk_ref, dv_ref, sums_ref, dq_half, dk_half, dv_half, chance_ref, score_ref = refs[-9:]
    query_sum = jnp.zeros((1, LANES), F32)
    value_sums = []
    keys = k_ref[...]
    values = v_ref[...]
    key_count = keys.shape[0]
    row_count = q_ref.shape[0]
    keys_turned = keys.T
    product = (grad_ref[...].astype(F32) * out_ref[...].astype(F32)).T
    inner = [
        jnp.sum(product[head * HEAD : (head + 1) * HEAD], axis=0, keepdims=True)
        for head in range(2)
    ]
    slots_of = chance_ref.shape[0]
    key_rows = chance_ref.shape[1]
    lane_head = head_of_lane((key_rows, LANES))
    blocks = row_count // QUERY_ROWS
    units = [
        (piece, head, block)
        for piece in range(key_count // key_rows)
        for head in range(2)
        for block in range(piece * key_rows // QUERY_ROWS if causal else 0, blocks)
    ]

    def products_of(unit):
        piece, head, block = unit
        slots = slice(piece * key_rows, (piece + 1) * key_rows)
        rows = slice(block * QUERY_ROWS, (block + 1) * QUERY_ROWS)
        return (
            dot_last(one_head(keys[slots], lane_head, head), q_ref[rows, :]),
            dot_last(one_head(values[slots], lane_head, head), grad_ref[rows, :]),
        )

    even_heads = {}

    def finish(piece, head):
        slots = slice(piece * key_rows, (piece + 1) * key_rows)
        first = piece * key_rows if causal else 0
        kept = chance_ref[(2 * piece + head) % slots_of, :, first:]
        grad_value = dot(kept, grad_ref[first:, :])
        grad_key = dot(score_ref[head, slots, first:], q_ref[first:, :])
        if head == 0:
            even_heads[piece] = (grad_key, grad_value)
            return
        even_key, even_value = even_heads.pop(piece)
        grad_key = jnp.where(lane_head == 0, even_key, grad_key).astype(BF16)
        grad_value = jnp.where(lane_head == 0, even_value, grad_value).astype(BF16)
        dk_ref[slots, :] = grad_key
        dk_half[slots, :] = grad_key
        dv_ref[slots, :] = grad_value
        dv_half[slots, :] = grad_value
        value_sums.append(jnp.sum(grad_value.astype(F32), axis=0, keepdims=True))

    current = products_of(units[0])
    ended = None
    for item, (piece, head, block) in enumerate(units):
        later = products_of(units[item + 1]) if item + 1 < len(units) else None
        if ended is not None:
            finish(*ended)
            ended = None
        scores, grad_chance = current
        slots = slice(piece * key_rows, (piece + 1) * key_rows)
        rows = slice(block * QUERY_ROWS, (block + 1) * QUERY_ROWS)
        if not causal:
            scores = scores + widen(bias_ref[slots, :], QUERY_ROWS)
        elif (piece + 1) * key_rows > block * QUERY_ROWS:
            scores = causal_mask(scores, piece * key_rows, block * QUERY_ROWS)
        chance = jnp.exp(scores - log_ref[0, head : head + 1, rows])
        chance_ref[(2 * piece + head) % slots_of, :, rows] = chance.astype(BF16)
        score_ref[head, slots, rows] = (chance * (grad_chance - inner[head][:, rows])).astype(BF16)
        if block == blocks - 1:
            ended = (piece, head)
        current = later
    finish(*ended)
    for block in range(blocks):
        rows = slice(block * QUERY_ROWS, (block + 1) * QUERY_ROWS)
        seen = (block + 1) * QUERY_ROWS if causal else key_count
        parts = [
            dot(
                keys_turned[head * HEAD : (head + 1) * HEAD, :seen],
                score_ref[head, :seen, rows],
            )
            for head in range(2)
        ]
        grad_query = jnp.concatenate(parts, axis=0).T.astype(BF16)
        grad_query = (grad_query.astype(F32) * HEAD ** (-0.5)).astype(BF16)
        dq_ref[rows, :] = grad_query
        dq_half[rows, :] = grad_query
        query_sum = query_sum + jnp.sum(grad_query.astype(F32), axis=0, keepdims=True)
    sums_ref[0:1, :] = query_sum
    sums_ref[1:2, :] = sum(value_sums[1:], value_sums[0])


def head_pair(row_count, first):
    return pl.BlockSpec((row_count, LANES), lambda pair: (0, first + pair))


def attention_forward(queries, keys, values, firsts, bias=None):
    causal = bias is None
    row_count = queries.shape[0]
    key_count = keys.shape[0]
    pairs = HEADS // 2
    in_specs = [
        head_pair(row_count, firsts[0]),
        head_pair(key_count, firsts[1]),
        head_pair(key_count, firsts[2]),
    ]
    operands = [queries, keys, values]
    if not causal:
        in_specs.append(pl.BlockSpec((key_count, LANES), lambda pair: (0, 0)))
        operands.append(bias)
    return pl.pallas_call(
        functools.partial(attention_forward_kernel, causal=causal),
        grid=(pairs,),
        in_specs=in_specs,
        out_specs=[
            head_pair(row_count, 0),
            pl.BlockSpec((1, 8, row_count), lambda pair: (pair, 0, 0)),
        ],
        out_shape=[
            jax.ShapeDtypeStruct((row_count, pairs * LANES), BF16),
            jax.ShapeDtypeStruct((pairs, 8, row_count), F32),
        ],
        compiler_params=pltpu.CompilerParams(vmem_limit_bytes=60 << 20),
        cost_estimate=SMALL,
    )(*operands)


def attention_backward(
    half, width, queries, keys, values, firsts, grads, outs, log_total, bias, whole
):
    causal = bias is None
    row_count, model = grads.shape
    key_count = keys.shape[0]
    key_rows = QUERY_ROWS if causal else key_count // 2
    per_unit = width // LANES
    steps = HEADS // 4

    def chosen(step, side):
        return (2 * (step // per_unit) + side[0]) * per_unit + step % per_unit

    def in_whole(count, first=0):
        return pl.BlockSpec((count, LANES), lambda step, side: (0, first + chosen(step, side)))

    def alone(count):
        return pl.BlockSpec((count, LANES), lambda step, side: (0, step))

    in_specs = [
        in_whole(row_count, firsts[0]),
        in_whole(key_count, firsts[1]),
        in_whole(key_count, firsts[2]),
        in_whole(row_count),
        in_whole(row_count),
        pl.BlockSpec((1, 8, row_count), lambda step, side: (chosen(step, side), 0, 0)),
    ]
    operands = [queries, keys, values, grads, outs, log_total]
    if not causal:
        in_specs.append(pl.BlockSpec((key_count, LANES), lambda step, side: (0, 0)))
        operands.append(bias)
    aliases = {}
    if whole is not None:
        for item, array in enumerate(whole):
            aliases[1 + len(operands)] = item
            in_specs.append(pl.BlockSpec(memory_space=pl.ANY))
            operands.append(array)
    counts = (row_count, key_count, key_count)
    results = pl.pallas_call(
        functools.partial(attention_backward_kernel, causal=causal),
        grid_spec=pltpu.PrefetchScalarGridSpec(
            num_scalar_prefetch=1,
            grid=(steps,),
            in_specs=in_specs,
            out_specs=[in_whole(count) for count in counts]
            + [in_whole(8)]
            + [alone(count) for count in counts],
            scratch_shapes=[
                pltpu.VMEM((4, key_rows, row_count), BF16),
                pltpu.VMEM((2, key_count, row_count), BF16),
            ],
        ),
        out_shape=[jax.ShapeDtypeStruct((count, model), BF16) for count in counts]
        + [jax.ShapeDtypeStruct((8, model), F32)]
        + [jax.ShapeDtypeStruct((count, model // 2), BF16) for count in counts],
        input_output_aliases=aliases,
        compiler_params=pltpu.CompilerParams(vmem_limit_bytes=60 << 20),
        cost_estimate=SMALL,
    )(half, *operands)
    return results[:4], results[4:]


PLACE_PLANE = 3
VECTOR_ROWS = 24


def holders(group, plane):
    if group == 0:
        return ((1, plane != 0), (0, plane == 0))
    if group == 1:
        return ((2, plane > 1), (0, plane == 1), (1, plane == 0))
    if group == 2:
        return ((2, plane < 2), (0, plane == 2), (3, plane == 3))
    return ((3, plane != 3), (0, plane == 3))


class Source:
    def __init__(self, slots, group, sides):
        self.group = group
        self.sides = sides
        self.which = [slot for slot, _ in holders(group, 0)]
        self.operands = [
            array for slot in self.which for side in sides for array in slots[slot][side]
        ]
        self.shape = self.operands[0].shape
        self.dtype = self.operands[0].dtype

    def chunks(self):
        return 2 * self.shape[0]

    def specs(self):
        return [pl.BlockSpec(memory_space=pl.ANY)] * len(self.operands)

    def scratch(self):
        return [
            pltpu.VMEM((2, 2 * self.shape[1], self.shape[2]), self.dtype),
            pltpu.SemaphoreType.DMA((2, 2)),
        ]


def start_fetch(source, refs, buffer, semaphores, plane, side, chunk, turn):
    top, half = source.shape[:2]
    lower_place = 0
    rest = chunk // 2
    size = top
    while size > 1:
        lower_place = lower_place * 2 + rest % 2
        rest = rest // 2
        size //= 2
    item = 0
    for _, chosen in holders(source.group, plane):
        for number in range(len(source.sides)):
            wanted = chosen & (side == number)
            lows, highs, evens, odds = refs[item : item + 4]
            item += 4
            copies = (
                (chunk < top, lows, chunk, 0),
                (chunk >= top, highs, chunk - top, 0),
                (chunk % 2 == 0, evens, lower_place, 1),
                (chunk % 2 == 1, odds, lower_place, 1),
            )
            for condition, array, index, part in copies:

                @pl.when(wanted & condition)
                def _(array=array, index=index, part=part):
                    pltpu.make_async_copy(
                        array.at[index],
                        buffer.at[turn, pl.ds(part * half, half), :],
                        semaphores.at[turn, part],
                    ).start()


def wait_fetch(source, refs, buffer, semaphores, turn):
    half = source.shape[1]
    for part in range(2):
        pltpu.make_async_copy(
            refs[0].at[0],
            buffer.at[turn, pl.ds(part * half, half), :],
            semaphores.at[turn, part],
        ).wait()


def fetched(source, refs, buffer, semaphores, plane, order, item, count):
    turn = item % 2

    @pl.when(item == 0)
    def _():
        side, chunk = order(0)
        start_fetch(source, refs, buffer, semaphores, plane, side, chunk, 0)

    @pl.when(item + 1 < count)
    def _():
        side, chunk = order(item + 1)
        start_fetch(source, refs, buffer, semaphores, plane, side, chunk, (item + 1) % 2)

    wait_fetch(source, refs, buffer, semaphores, turn)
    return buffer.at[turn]


def vector_part(vectors_ref, row, first, width):
    return vectors_ref[row : row + 1, pl.ds(pl.multiple_of(first, width), width)]


def gelu_parts(values):
    slope = 0.7978845608028654
    square = values * values
    turned = jnp.tanh(slope * values * (1.0 + 0.044715 * square))
    weight = 0.5 * (1.0 + turned)
    derivative = weight + 0.5 * values * (1.0 - turned * turned) * (
        slope + (3.0 * 0.044715 * slope) * square
    )
    return values * weight, derivative


def feed_kernel(*refs, norm, up_source, down_source):
    refs = list(refs)
    place_ref = refs.pop(0)
    values_ref = refs.pop(0)
    grad_ref = refs.pop(0)
    vectors_ref = refs.pop(0)
    bias_ref = refs.pop(0)
    up_refs = refs[: len(up_source.operands)]
    refs = refs[len(up_refs) :]
    down_refs = refs[: len(down_source.operands)]
    refs = refs[len(down_refs) :]
    out_ref, back_ref, grad_up_ref, grad_down_ref, grad_bias_ref = refs[:5]
    low_ref = refs[5] if norm else values_ref
    low_turned, grad_turned, active_ref, hidden_ref = refs[-8:-4]
    up_buffer, up_semaphores, down_buffer, down_semaphores = refs[-4:]
    plane = place_ref[PLACE_PLANE]
    step = pl.program_id(0)
    count = up_source.chunks()

    def order(item):
        return 0, item

    up_chunk = fetched(up_source, up_refs, up_buffer, up_semaphores, plane, order, step, count)
    down_chunk = fetched(
        down_source, down_refs, down_buffer, down_semaphores, plane, order, step, count
    )

    @pl.when(step == 0)
    def _():
        if norm:
            for first in range(0, values_ref.shape[0], QUERY_ROWS):
                rows = slice(first, first + QUERY_ROWS)
                low_ref[rows, :] = normalize(
                    values_ref[rows, :], vectors_ref[4:5, :], vectors_ref[5:6, :]
                ).astype(BF16)
        low_turned[...] = low_ref[...].T
        grad_turned[...] = grad_ref[...].T
        out_ref[...] = jnp.zeros_like(out_ref)
        back_ref[...] = jnp.zeros_like(back_ref)

    up = up_chunk[...]
    down = down_chunk[...]
    total = jnp.zeros((1, up.shape[1]), F32)
    pieces = low_ref.shape[0] // FEED_ROWS
    for piece in range(pieces):
        rows = slice(piece * FEED_ROWS, (piece + 1) * FEED_ROWS)
        active, derivative = gelu_parts(dot(low_ref[rows, :], up) + bias_ref[0])
        active_low = active.astype(BF16)
        hidden_low = (derivative * dot(grad_ref[rows, :], down)).astype(BF16)
        active_ref[rows, :] = active_low
        hidden_ref[rows, :] = hidden_low
        total = total + jnp.sum(hidden_low.astype(F32), axis=0, keepdims=True)
        out_ref[rows, :] += dot_last(active_low, down)
        back_ref[rows, :] += dot_last(hidden_low, up)
    grad_bias_ref[0] = total
    for piece in range(low_turned.shape[0] // FEED_ROWS):
        rows = slice(piece * FEED_ROWS, (piece + 1) * FEED_ROWS)
        grad_down_ref[0, rows, :] = dot(grad_turned[rows, :], active_ref[...]).astype(BF16)
        grad_up_ref[0, rows, :] = dot(low_turned[rows, :], hidden_ref[...]).astype(BF16)


def feed_half(place, values, grad, vectors, bias, slots, side, norm):
    row_count, model = values.shape
    up_source = Source(slots, 2, (side,))
    down_source = Source(slots, 3, (side,))
    steps = up_source.chunks()
    width = up_source.shape[2]

    def whole(shape):
        return pl.BlockSpec(shape, lambda step, place: (0, 0), pipeline_mode=pl.Buffered(1))

    total = pl.BlockSpec((row_count, model), lambda step, place: (0, 0))
    chunk = pl.BlockSpec((1, model, width), lambda step, place: (step, 0, 0))
    out_specs = [
        total,
        total,
        chunk,
        chunk,
        pl.BlockSpec((1, 1, width), lambda step, place: (step ^ place[1], 0, 0)),
    ]
    out_shape = [
        jax.ShapeDtypeStruct((row_count, model), F32),
        jax.ShapeDtypeStruct((row_count, model), F32),
        jax.ShapeDtypeStruct((steps, model, width), BF16),
        jax.ShapeDtypeStruct((steps, model, width), BF16),
        jax.ShapeDtypeStruct((steps, 1, width), F32),
    ]
    if norm:
        out_specs.append(total)
        out_shape.append(jax.ShapeDtypeStruct((row_count, model), BF16))
    return pl.pallas_call(
        functools.partial(
            feed_kernel, norm=norm, up_source=up_source, down_source=down_source
        ),
        grid_spec=pltpu.PrefetchScalarGridSpec(
            num_scalar_prefetch=1,
            grid=(steps,),
            in_specs=[
                whole((row_count, model)),
                whole((row_count, model)),
                whole((VECTOR_ROWS, model)),
                pl.BlockSpec(
                    (1, 1, width), lambda step, place: (2 * (step ^ place[1]) + place[0], 0, 0)
                ),
            ]
            + up_source.specs()
            + down_source.specs(),
            out_specs=out_specs,
            scratch_shapes=[
                pltpu.VMEM((model, row_count), BF16),
                pltpu.VMEM((model, row_count), BF16),
                pltpu.VMEM((row_count, width), BF16),
                pltpu.VMEM((row_count, width), BF16),
            ]
            + up_source.scratch()
            + down_source.scratch(),
        ),
        out_shape=out_shape,
        compiler_params=pltpu.CompilerParams(vmem_limit_bytes=60 << 20),
        cost_estimate=SMALL,
    )(place, values, grad, vectors, bias, *up_source.operands, *down_source.operands)


def norm_back_rows(values, grad, gain, stream):
    values = values.astype(F32)
    centred = values - jnp.mean(values, axis=-1, keepdims=True)
    inverse = lax.rsqrt(jnp.mean(centred * centred, axis=-1, keepdims=True) + NORM_EPS)
    normal = centred * inverse
    scaled = grad * gain
    product = scaled * normal
    back = inverse * (
        scaled
        - jnp.mean(scaled, axis=-1, keepdims=True)
        - normal * jnp.mean(product, axis=-1, keepdims=True)
    )
    return stream.astype(F32) + back, normal


def row_sums(grad, normal, low, stream):
    parts = (grad * normal, grad, low.astype(F32), stream.astype(F32))
    return [jnp.sum(part, axis=0, keepdims=True) for part in parts]


def norm_back_kernel(*refs, count, row):
    values_ref, vectors_ref, stream_ref = refs[:3]
    grad_refs = refs[3 : 3 + count]
    out_ref, low_ref, sums_ref = refs[3 + count :]
    grad = grad_refs[0][...]
    for grad_ref in grad_refs[1:]:
        grad = grad + grad_ref[...]
    result, normal = norm_back_rows(
        values_ref[...], grad, vectors_ref[row : row + 1, :], stream_ref[...]
    )
    low = result.astype(BF16)
    out_ref[...] = result
    low_ref[...] = low

    @pl.when(pl.program_id(0) == 0)
    def _():
        sums_ref[...] = jnp.zeros_like(sums_ref)

    for number, part in enumerate(row_sums(grad, normal, low, stream_ref[...])):
        sums_ref[number : number + 1, :] += part


def norm_back(values, vectors, row, stream, grads):
    row_count, model = values.shape
    panel = pl.BlockSpec((QUERY_ROWS // 2, model), lambda step: (step, 0))
    return pl.pallas_call(
        functools.partial(norm_back_kernel, count=len(grads), row=row),
        grid=(2 * row_count // QUERY_ROWS,),
        in_specs=[panel, pl.BlockSpec((VECTOR_ROWS, model), lambda step: (0, 0)), panel]
        + [panel] * len(grads),
        out_specs=[panel, panel, pl.BlockSpec((8, model), lambda step: (0, 0))],
        out_shape=[
            jax.ShapeDtypeStruct((row_count, model), F32),
            jax.ShapeDtypeStruct((row_count, model), BF16),
            jax.ShapeDtypeStruct((8, model), F32),
        ],
        compiler_params=pltpu.CompilerParams(vmem_limit_bytes=60 << 20),
        cost_estimate=SMALL,
    )(values, vectors, stream, *grads)


def project_kernel(*refs, source, block, lines, norm, residual):
    refs = list(refs)
    place_ref = refs.pop(0)
    values_ref = refs.pop(0)
    vectors_ref = refs.pop(0)
    residual_ref = refs.pop(0) if residual else None
    source_refs = refs[: len(source.operands)]
    refs = refs[len(source_refs) :]
    out_ref = refs.pop(0)
    low_ref = refs.pop(0) if norm is not None else values_ref
    buffer, semaphores = refs
    model = values_ref.shape[1]
    width = out_ref.shape[1]
    parts = model // (2 * width)
    item = pl.program_id(0)
    count = 2 * parts * len(lines)

    def order(item):
        return item % 2, (block * parts + item // 2) ^ place_ref[1]

    columns_ref = fetched(
        source, source_refs, buffer, semaphores, place_ref[PLACE_PLANE], order, item, count
    )
    if norm is not None:

        @pl.when(item == 0)
        def _():
            for first in range(0, values_ref.shape[0], QUERY_ROWS):
                rows = slice(first, first + QUERY_ROWS)
                low_ref[rows, :] = normalize(
                    values_ref[rows, :].astype(F32),
                    vectors_ref[norm : norm + 1, :],
                    vectors_ref[norm + 1 : norm + 2, :],
                ).astype(BF16)

    inside = item // 2 % parts
    column = (2 * inside + (item % 2 ^ place_ref[0])) * width
    row_count = values_ref.shape[0]
    step = row_count // 2
    for number, (line, scale) in enumerate(lines):

        @pl.when(item // (2 * parts) == number)
        def _(line=line, scale=scale):
            columns = columns_ref[...]
            for first in range(0, row_count, step):
                rows = slice(first, first + step)
                made = dot(low_ref[rows, :], columns)
                if line is not None:
                    made = made + vector_part(vectors_ref, line, column, width)
                if scale != 1.0:
                    made = made * scale
                if residual:
                    made = residual_ref[rows, :].astype(F32) + made
                out_ref[rows, :] = made.astype(out_ref.dtype)


def project(
    place, values, vectors, slots, group, block, lines, norm=None, residual=None, out_type=BF16
):
    row_count, model = values.shape
    source = Source(slots, group, (0, 1))
    width = source.shape[2]
    parts = model // (2 * width)

    def whole(shape):
        return pl.BlockSpec(shape, lambda *_: (0, 0), pipeline_mode=pl.Buffered(1))

    panel = pl.BlockSpec(
        (row_count, width),
        lambda item, place: (0, 2 * (item // 2) + (item % 2 ^ place[0])),
    )
    in_specs = [whole((row_count, model)), whole((VECTOR_ROWS, model))]
    operands = [values, vectors]
    if residual is not None:
        in_specs.append(panel)
        operands.append(residual)
    out_specs = [panel]
    out_shape = [jax.ShapeDtypeStruct((row_count, len(lines) * model), out_type)]
    if norm is not None:
        out_specs.append(pl.BlockSpec((row_count, model), lambda *_: (0, 0)))
        out_shape.append(jax.ShapeDtypeStruct((row_count, model), BF16))
    results = pl.pallas_call(
        functools.partial(
            project_kernel,
            source=source,
            block=block,
            lines=lines,
            norm=norm,
            residual=residual is not None,
        ),
        grid_spec=pltpu.PrefetchScalarGridSpec(
            num_scalar_prefetch=1,
            grid=(2 * parts * len(lines),),
            in_specs=in_specs + source.specs(),
            out_specs=out_specs,
            scratch_shapes=source.scratch(),
        ),
        out_shape=out_shape,
        compiler_params=pltpu.CompilerParams(vmem_limit_bytes=60 << 20),
        cost_estimate=SMALL,
    )(place, *operands, *source.operands)
    return results if norm is not None else results[0]


def project_back_kernel(*refs, source, block, count, row):
    refs = list(refs)
    place_ref = refs.pop(0)
    grad_refs = refs[:count]
    refs = refs[count:]
    if row is not None:
        values_hbm, stream_hbm, vectors_ref = refs[:3]
        refs = refs[3:]
    source_refs = refs[: len(source.operands)]
    refs = refs[len(source.operands) :]
    if row is None:
        out_ref, total_ref, buffer, semaphores = refs
    else:
        out_hbm, low_hbm, sums_ref, total_ref, buffer, semaphores = refs[:6]
        values_ref, stream_ref, low_ref, load_semaphores, store_semaphores = refs[6:]
    row_count, model = total_ref.shape
    width = grad_refs[0].shape[1]
    parts = model // (2 * width)
    item = pl.program_id(0)
    steps = 2 * parts * count

    def order(item):
        return item % 2, (block * parts + item // 2) ^ place_ref[1]

    columns_ref = fetched(
        source, source_refs, buffer, semaphores, place_ref[PLACE_PLANE], order, item, steps
    )
    if row is not None:
        loads = [
            pltpu.make_async_copy(values_hbm, values_ref, load_semaphores.at[0]),
            pltpu.make_async_copy(stream_hbm, stream_ref, load_semaphores.at[1]),
        ]

    @pl.when(item == 0)
    def _():
        if row is not None:
            for load in loads:
                load.start()
        total_ref[...] = jnp.zeros_like(total_ref)

    for number, grad_ref in enumerate(grad_refs):

        @pl.when(item // (2 * parts) == number)
        def _(grad_ref=grad_ref):
            columns = columns_ref[...]
            size = row_count // 2
            for first in range(0, row_count, size):
                rows = slice(first, first + size)
                total_ref[rows, :] += dot_last(grad_ref[rows, :], columns)

    @pl.when(item == steps - 1)
    def _():
        if row is None:
            out_ref[...] = total_ref[...].astype(out_ref.dtype)
            return
        for load in loads:
            load.wait()
        stores = []
        sums = None
        for number in range(row_count // QUERY_ROWS):
            rows = slice(number * QUERY_ROWS, (number + 1) * QUERY_ROWS)
            grad = total_ref[rows, :]
            stream = stream_ref[rows, :]
            result, normal = norm_back_rows(
                values_ref[rows, :], grad, vectors_ref[row : row + 1, :], stream
            )
            low = result.astype(BF16)
            made = row_sums(grad, normal, low, stream)
            sums = made if sums is None else [a + b for a, b in zip(sums, made, strict=True)]
            total_ref[rows, :] = result
            low_ref[rows, :] = low
            for kind, (held, target) in enumerate(((total_ref, out_hbm), (low_ref, low_hbm))):
                store = pltpu.make_async_copy(
                    held.at[rows, :], target.at[rows, :], store_semaphores.at[kind, number]
                )
                store.start()
                stores.append(store)
        for number, part in enumerate(sums):
            sums_ref[number : number + 1, :] = part
        for store in stores:
            store.wait()


def project_back(place, grads, slots, group, block, out_type, norm=None):
    row_count, model = grads[0].shape
    source = Source(slots, group, (0, 1))
    width = source.shape[2]
    parts = model // (2 * width)

    def grad_panel(number):
        def index(item, place):
            column = 2 * (item // 2 % parts) + (item % 2 ^ place[0])
            last = 2 * (parts - 1) + (1 ^ place[0])
            done = item // (2 * parts) > number
            return 0, jnp.where(item // (2 * parts) == number, column, jnp.where(done, last, place[0]))

        return pl.BlockSpec((row_count, width), index)

    anywhere = pl.BlockSpec(memory_space=pl.ANY)
    in_specs = [grad_panel(number) for number in range(len(grads))]
    operands = list(grads)
    out_specs = [pl.BlockSpec((row_count, model), lambda *_: (0, 0))]
    out_shape = [jax.ShapeDtypeStruct((row_count, model), out_type)]
    scratch = [pltpu.VMEM((row_count, model), F32)] + source.scratch()
    row = None
    if norm is not None:
        values, stream, vectors, row = norm
        in_specs += [
            anywhere,
            anywhere,
            pl.BlockSpec((VECTOR_ROWS, model), lambda *_: (0, 0)),
        ]
        operands += [values, stream, vectors]
        out_specs = [anywhere, anywhere, pl.BlockSpec((8, model), lambda *_: (0, 0))]
        out_shape += [
            jax.ShapeDtypeStruct((row_count, model), BF16),
            jax.ShapeDtypeStruct((8, model), F32),
        ]
        scratch += [
            pltpu.VMEM(values.shape, values.dtype),
            pltpu.VMEM(stream.shape, stream.dtype),
            pltpu.VMEM((row_count, model), BF16),
            pltpu.SemaphoreType.DMA((2,)),
            pltpu.SemaphoreType.DMA((2, row_count // QUERY_ROWS)),
        ]
    results = pl.pallas_call(
        functools.partial(
            project_back_kernel, source=source, block=block, count=len(grads), row=row
        ),
        grid_spec=pltpu.PrefetchScalarGridSpec(
            num_scalar_prefetch=1,
            grid=(2 * parts * len(grads),),
            in_specs=in_specs + source.specs(),
            out_specs=out_specs,
            scratch_shapes=scratch,
        ),
        out_shape=out_shape,
        compiler_params=pltpu.CompilerParams(vmem_limit_bytes=60 << 20),
        cost_estimate=SMALL,
    )(place, *operands, *source.operands)
    return results[0] if norm is None else results


NEAR = ((0, 1), (1, 0), (2, 3), (3, 2))


def pinned(*values):
    return lax.optimization_barrier(values)


def swap_bit(values, device_count, bit):
    return lax.ppermute(values, AXES, [(item, item ^ bit) for item in range(device_count)])


def move_planes(values, moves, plane_size):
    pairs = [
        (source * plane_size + inner, target * plane_size + inner)
        for source, target in moves
        for inner in range(plane_size)
    ]
    return lax.ppermute(values, AXES, pairs)


def by_member(values, member):
    count = values.shape[0]
    bit = 1
    while bit < count:
        pairs = values.reshape((count // (2 * bit), 2, bit) + values.shape[1:])
        turned = jnp.where((member // bit) % 2 == 1, pairs[:, ::-1], pairs)
        values = turned.reshape(values.shape)
        bit *= 2
    return values


def exchange_members(items, device_count):
    return [items[0]] + [swap_bit(item, device_count, k) for k, item in enumerate(items) if k > 0]


def inner_bits(device_count):
    bits = []
    bit = device_count // GROUPS // 2
    while bit > 1:
        bits.append(bit)
        bit //= 2
    return bits


def spread_begin(own):
    rows = own.shape[-2] // 2
    return [own[..., :rows, :], own[..., rows:, :]]


def spread_swaps(parts, stage, device_count):
    bits = inner_bits(device_count)
    return [
        swap_bit(parts[0], device_count, bits[len(bits) - 1 - stage]),
        swap_bit(parts[1], device_count, bits[stage]),
    ]


def spread_on(parts, got, device_count):
    for stage in range(1, len(inner_bits(device_count))):
        parts = [jnp.stack([part, item]) for part, item in zip(parts, got, strict=True)]
        got = spread_swaps(parts, stage, device_count)
    return parts, got


def swap_cores(items, device_count):
    return [swap_bit(item, device_count, 1) for item in items]


def flat_slot(parts, got):
    shape = (-1,) + parts[0].shape[-2:]
    return tuple(item.reshape(shape) for item in (parts[0], got[0], parts[1], got[1]))


class Sum:
    def __init__(self, kept, got, absolute, swaps=()):
        self.kept = kept
        self.got = got
        self.absolute = absolute
        self.swaps = list(swaps)

    def joined(self, got):
        return Sum(self.kept, self.got, self.absolute, self.swaps + [got])


def stage_kernel(*refs, members, terms, parts):
    ins = refs[1:-parts]
    outs = refs[-parts:]
    per_part = 2 * members + terms
    for part, out_ref in enumerate(outs):
        mine = ins[part * per_part : (part + 1) * per_part]
        for member in range(members):
            total = mine[2 * member][0].astype(F32) + mine[2 * member + 1][0].astype(F32)
            for swap_ref in mine[2 * members :]:
                total = total + swap_ref[member, 0].astype(F32)
            out_ref[member, 0] = total.astype(BF16)


def stage_sends(place, pending, device_count):
    levels = len(inner_bits(device_count))
    stage = len(pending.swaps)
    chunks, rows, width = pending.kept[0].shape
    half = rows // 2
    count = chunks >> (stage + 1)
    members = len(pending.kept)

    def relative(part, step):
        if part == 0:
            return count + step
        return (step << (stage + 1)) + (1 << stage)

    def stored(part):
        def index(step, place):
            chunk = relative(part, step)
            return (chunk ^ place[1] if pending.absolute else chunk), part, 0

        return pl.BlockSpec((1, half, width), index)

    def swapped(part, earlier):
        def index(step, place):
            chunk = relative(part, step)
            return 0, (chunk if part == 0 else chunk >> (earlier + 1)), 0, 0

        return pl.BlockSpec((members, 1, half, width), index)

    in_specs = []
    operands = []
    for part in range(2):
        for kept, got in zip(pending.kept, pending.got, strict=True):
            in_specs += [stored(part)] * 2
            operands += [kept, got]
        for earlier, items in enumerate(pending.swaps):
            in_specs.append(swapped(part, earlier))
            operands.append(items[part])
    assert stage < levels
    return pl.pallas_call(
        functools.partial(stage_kernel, members=members, terms=stage, parts=2),
        grid_spec=pltpu.PrefetchScalarGridSpec(
            num_scalar_prefetch=1,
            grid=(count,),
            in_specs=in_specs,
            out_specs=[pl.BlockSpec((members, 1, half, width), lambda step, place: (0, step, 0, 0))]
            * 2,
        ),
        out_shape=[jax.ShapeDtypeStruct((members, count, half, width), BF16)] * 2,
        compiler_params=pltpu.CompilerParams(vmem_limit_bytes=60 << 20),
        cost_estimate=SMALL,
    )(place, *operands)


def stage_swaps(sends, pending, device_count):
    bits = inner_bits(device_count)
    stage = len(pending.swaps)
    return [
        swap_bit(sends[0], device_count, bits[stage]),
        swap_bit(sends[1], device_count, bits[len(bits) - 1 - stage]),
    ]


def finish_stages(place, pending, device_count):
    while len(pending.swaps) < len(inner_bits(device_count)):
        sends = stage_sends(place, pending, device_count)
        pending = pending.joined(stage_swaps(sends, pending, device_count))
    return pending


def total_kernel(*refs, members, stages):
    place_ref = refs[0]
    stored = refs[1 : 1 + 2 * members]
    swaps = refs[1 + 2 * members : 1 + 2 * members + 2 * stages]
    kept_ref, sent_ref = refs[1 + 2 * members + 2 * stages :]

    def total(part, member):
        result = stored[2 * member][0].astype(F32) + stored[2 * member + 1][0].astype(F32)
        for stage in range(stages):
            result = result + swaps[2 * stage + part][member, 0].astype(F32)
        return result

    for part in range(2):

        @pl.when(pl.program_id(0) // 2 == part)
        def _(part=part):
            if members == 1:
                made = total(part, 0)
                kept_ref[...] = made
                sent_ref[...] = made.astype(BF16)
            else:
                low = total(part, 0)
                high = total(part, 1)
                even = place_ref[2] == 0
                kept_ref[...] = jnp.where(even, low, high)
                sent_ref[...] = jnp.where(even, high, low).astype(BF16)


def plane_totals(place, pending):
    chunks, rows, width = pending.kept[0].shape
    quarter = rows // 4
    members = len(pending.kept)

    def stored(step, place):
        return (place[1] if pending.absolute else 0), step, 0

    in_specs = []
    operands = []
    for kept, got in zip(pending.kept, pending.got, strict=True):
        in_specs += [pl.BlockSpec((1, quarter, width), stored)] * 2
        operands += [kept, got]
    for items in pending.swaps:
        for part in range(2):
            in_specs.append(
                pl.BlockSpec(
                    (members, 1, quarter, width),
                    (lambda step, place: (0, 0, jnp.minimum(step, 1), 0))
                    if part == 0
                    else (lambda step, place: (0, 0, jnp.maximum(step - 2, 0), 0)),
                )
            )
            operands.append(items[part])
    panel = pl.BlockSpec((quarter, width), lambda step, place: (step, 0))
    return pl.pallas_call(
        functools.partial(total_kernel, members=members, stages=len(pending.swaps)),
        grid_spec=pltpu.PrefetchScalarGridSpec(
            num_scalar_prefetch=1,
            grid=(4,),
            in_specs=in_specs,
            out_specs=[panel, panel],
        ),
        out_shape=[
            jax.ShapeDtypeStruct((rows, width), F32),
            jax.ShapeDtypeStruct((rows, width), BF16),
        ],
        compiler_params=pltpu.CompilerParams(vmem_limit_bytes=60 << 20),
        cost_estimate=SMALL,
    )(place, *operands)


def column_half(values, half, width):
    rows, columns = values.shape
    if columns == 2 * width:
        return lax.dynamic_slice_in_dim(values, half * width, width, 1)
    pieces = values.reshape(rows, -1, 2, width)
    return lax.dynamic_index_in_dim(pieces, half, 2, keepdims=False).reshape(rows, -1)


def weight_half(pairs, width):
    terms = []
    for left, right in pairs:
        product = dot_rows(left, right).astype(BF16)
        if product.shape[1] == width:
            terms.append(product[None])
        else:
            terms.append(jnp.swapaxes(product.reshape(product.shape[0], -1, width), 0, 1))
    return jnp.concatenate(terms, axis=0)


def dot_high(left, right, dims):
    return lax.dot_general(
        left, right, (dims, ((), ())), precision=HIGHEST, preferred_element_type=F32
    )


def update_kernel(
    place_ref,
    total_ref,
    near_ref,
    far_ref,
    other_ref,
    weight_ref,
    average_ref,
    moment1_ref,
    moment2_ref,
    stats_ref,
    bases_ref,
    grad_ref,
    first_ref,
    second_ref,
    new_ref,
    new_average_ref,
    copy_ref,
    new_stats_ref,
    new_bases_ref,
    state_ref,
    solved_ref,
    *,
    chunks,
):
    blocks = stats_ref.shape[0]
    step = pl.program_id(0)
    rows = weight_ref.shape[0]

    @pl.when(step == 0)
    def _():
        @pl.when(place_ref[PLACE_PLANE] == 0)
        def _():
            grad_ref[...] = total_ref[...] + near_ref[...].astype(F32) + far_ref[...].astype(F32)

        @pl.when(place_ref[PLACE_PLANE] != 0)
        def _():
            grad_ref[...] = other_ref[...]

        for block in range(blocks):
            grad = grad_ref[:, block * BLK : (block + 1) * BLK]
            square = dot_high(grad, grad, ((0,), (0,)))
            renewed = BETA_TWO * stats_ref[block] + (1.0 - BETA_TWO) * square
            new_stats_ref[block] = renewed
            product = dot_high(renewed, bases_ref[block], ((1,), (0,)))
            gram = dot_high(product, product, ((0,), (0,)))
            state_ref[block] = jnp.concatenate([gram, product.T], axis=1)

    def rotate(chunk):
        for block in range(blocks):
            columns = slice(block * BLK, (block + 1) * BLK)
            basis = bases_ref[block]
            turned = dot_high(
                grad_ref[chunk * rows : (chunk + 1) * rows, columns], basis, ((1,), (0,))
            )
            first = BETA_ONE * moment1_ref[:, columns] + (1.0 - BETA_ONE) * turned
            second = BETA_TWO * moment2_ref[:, columns] + (1.0 - BETA_TWO) * turned * turned
            first_ref[:, columns] = first
            second_ref[:, columns] = second
            direction = (
                first
                / (1.0 - BETA_ONE**STEP)
                / (jnp.sqrt(second / (1.0 - BETA_TWO**STEP)) + ADAM_EPS)
            )
            returned = dot_high(direction, basis, ((1,), (1,)))
            weight = weight_ref[:, columns]
            updated = weight - RATE * (returned + DECAY * weight)
            new_ref[:, columns] = updated
            new_average_ref[:, columns] = (
                AVERAGE * average_ref[:, columns] + (1.0 - AVERAGE) * updated
            )
            copy_ref[:, columns] = updated.astype(BF16)

    row_index = lax.broadcasted_iota(jnp.int32, (PANEL, 2 * BLK), 0)
    panels = BLK // PANEL

    def eliminate(panel):
        top_rows = slice(panel * PANEL, (panel + 1) * PANEL)
        tops = [state_ref[block, top_rows, :] for block in range(blocks)]
        for row in range(PANEL):
            lane = panel * PANEL + row
            for block in range(blocks):
                top = tops[block]
                pivot = top[row : row + 1, lane : lane + 1]
                inverse = lax.rsqrt(pivot)
                inverse = inverse * (1.5 - 0.5 * pivot * inverse * inverse)
                scaled = top[row : row + 1] * inverse
                reduced = top - (top[:, lane : lane + 1] * inverse) * scaled
                tops[block] = jnp.where(
                    row_index == row, scaled, jnp.where(row_index > row, reduced, top)
                )
        for block in range(blocks):
            solved_ref[block, top_rows, :] = tops[block][:, BLK:]
            if panel + 1 < panels:
                rest = slice((panel + 1) * PANEL, BLK)
                state_ref[block, rest, :] -= dot_high(
                    tops[block][:, rest], tops[block], ((0,), (0,))
                )

    for chunk in range(chunks):

        @pl.when(step == chunk)
        def _(chunk=chunk):
            rotate(chunk)
            for panel in range(panels * chunk // chunks, panels * (chunk + 1) // chunks):
                eliminate(panel)
            if chunk == chunks - 1:
                for block in range(blocks):
                    new_bases_ref[block] = solved_ref[block].T


def rotated_update(
    place, total, near, far, other, weights, average, moment1, moment2, stats, bases
):
    rows, width = weights.shape
    chunks = rows // QUERY_ROWS
    whole = pl.BlockSpec(
        (rows, width), lambda step, place: (0, 0), pipeline_mode=pl.Buffered(1)
    )
    big = pl.BlockSpec((QUERY_ROWS, width), lambda step, place: (step, 0))
    small = pl.BlockSpec(stats.shape, lambda step, place: (0, 0, 0))
    wide = jax.ShapeDtypeStruct(weights.shape, F32)
    return pl.pallas_call(
        functools.partial(update_kernel, chunks=chunks),
        grid_spec=pltpu.PrefetchScalarGridSpec(
            num_scalar_prefetch=1,
            grid=(chunks,),
            in_specs=[whole] * 4 + [big] * 4 + [small] * 2,
            out_specs=[pl.BlockSpec((rows, width), lambda step, place: (0, 0))]
            + [big] * 5
            + [small] * 2,
            scratch_shapes=[
                pltpu.VMEM(stats.shape[:2] + (2 * BLK,), F32),
                pltpu.VMEM(stats.shape, F32),
            ],
        ),
        out_shape=[wide] * 5
        + [jax.ShapeDtypeStruct(weights.shape, BF16)]
        + [jax.ShapeDtypeStruct(stats.shape, F32)] * 2,
        compiler_params=pltpu.CompilerParams(vmem_limit_bytes=60 << 20),
        cost_estimate=SMALL,
    )(place, total, near, far, other, weights, average, moment1, moment2, stats, bases)


def adam_update(grad, values, moment1, moment2):
    first_moment = BETA_ONE * moment1 + (1.0 - BETA_ONE) * grad
    second_moment = BETA_TWO * moment2 + (1.0 - BETA_TWO) * grad * grad
    updated = values - VECTOR_RATE * (first_moment / (1.0 - BETA_ONE**STEP)) / (
        jnp.sqrt(second_moment / (1.0 - BETA_TWO**STEP)) + ADAM_EPS
    )
    return (first_moment, second_moment, updated)


def exchange_vectors(pieces, rows, width):
    device_count = pieces.shape[0]
    size = rows * width
    padded = pad_vectors(pieces, 16)
    got = lax.all_to_all(padded, AXES, split_axis=0, concat_axis=0, tiled=True)
    return got.reshape(device_count, -1)[:, :size].reshape(device_count, rows, width)


def pad_vectors(pieces, sublanes):
    device_count, size = pieces.shape
    room = sublanes * LANES
    tiles = -(-size // room)
    padded = jnp.pad(pieces, ((0, 0), (0, tiles * room - size)))
    return padded.reshape(device_count, tiles * sublanes, LANES)


def vector_send(pieces, device, bit):
    halves = pieces.reshape((2, -1) + pieces.shape[1:])
    mine = (device // bit) % 2
    kept = lax.dynamic_index_in_dim(halves, mine, 0, keepdims=False)
    sent = lax.dynamic_index_in_dim(halves, 1 - mine, 0, keepdims=False)
    return kept, sent


def local(
    tokens,
    memory,
    page_lengths,
    slot_masks,
    upstream,
    weights,
    weight_average,
    weight_moment1,
    weight_moment2,
    stats,
    bases,
    vectors,
    vector_average,
    vector_moment1,
    vector_moment2,
):
    row_count, model = tokens.shape
    width = weights.shape[1]
    group_size = lax.axis_size("mem")
    device_count = lax.axis_size("seq") * group_size
    device = lax.axis_index(AXES)
    member = lax.axis_index("mem")
    core = device % 2
    quarter = memory.shape[1]
    scale_q = HEAD ** (-0.5)
    plane_size = device_count // GROUPS
    plane = device // plane_size
    inner = (device % plane_size) // 2
    here = jnp.stack([core, inner, plane % 2, plane]).astype(jnp.int32)
    away = jnp.stack([1 - core, inner, plane % 2, plane]).astype(jnp.int32)

    vector_shape = vectors.shape
    own = weights.astype(BF16)
    first = move_planes(own, ((0, 2), (1, 0), (2, 3), (3, 1)), plane_size)
    pieces = jnp.broadcast_to(
        vectors.astype(BF16).reshape(1, -1), (device_count, vectors.size)
    )
    vector_pieces = exchange_vectors(pieces, *vector_shape)
    memory_padded = jnp.pad(memory, ((0, 0), (0, SLOT_PAD - quarter), (0, 0)))
    memory_parts = exchange_members(
        [
            lax.dynamic_index_in_dim(memory_padded, member ^ item, 0, keepdims=False)
            for item in range(group_size)
        ],
        device_count,
    )
    parts = spread_begin(own)
    got = spread_swaps(parts, 0, device_count)
    first, got, vector_pieces, own = pinned(first, got, vector_pieces, own)
    held = jnp.where((plane == 0) | (plane == 3), own, first)
    near = move_planes(held, NEAR, plane_size)
    middle = move_planes(own, ((1, 2), (2, 1)), plane_size)
    parts, got = spread_on(parts, got, device_count)
    near, middle, first, got, memory_parts = pinned(near, middle, first, got, memory_parts)
    slot_zero = flat_slot(parts, got)
    even = plane % 2 == 0
    parts_one = spread_begin(jnp.where(even, first, near))
    got_one = spread_swaps(parts_one, 0, device_count)
    last = move_planes(middle, ((1, 0), (2, 3)), plane_size)
    zero_away = swap_cores(slot_zero, device_count)
    got_one, zero_away = pinned(got_one, zero_away)
    vector_rows = jnp.swapaxes(vector_pieces, 0, 1).reshape(vector_shape[0], model).astype(F32)
    table = jnp.pad(vector_rows, ((0, VECTOR_ROWS - vector_shape[0]), (0, 0)))
    parts_one, got_one = spread_on(parts_one, got_one, device_count)
    one_away = swap_cores(parts_one, device_count)
    got_one, one_away, last, vector_rows, table = pinned(
        got_one, one_away, last, vector_rows, table
    )
    got_one_away = swap_cores(got_one, device_count)
    parts_two = spread_begin(jnp.where((plane == 1) | (plane == 2), middle, last))
    got_two = spread_swaps(parts_two, 0, device_count)
    slots = [
        (slot_zero, tuple(zero_away)),
        (flat_slot(parts_one, got_one), flat_slot(one_away, got_one_away)),
    ]

    memory_here = jnp.concatenate(memory_parts, axis=0)
    live_rows = (jnp.arange(row_count) < page_lengths[0]).astype(F32)[:, None]
    slots_here = lax.dynamic_slice_in_dim(slot_masks, member, 1, 0).reshape(group_size, quarter)
    slots_here = by_member(slots_here, member)
    slots_here = jnp.pad(slots_here, ((0, 0), (0, SLOT_PAD - quarter))).reshape(-1, 1)
    slot_bias = jnp.broadcast_to(
        jnp.where(slots_here > 0, 0.0, MASKED).astype(F32), (group_size * SLOT_PAD, LANES)
    )
    pairs = HEADS // 2
    self_firsts = (0, pairs, 2 * pairs)
    cross_firsts = (0, 0, pairs)

    self_low, low_one = project(
        here, tokens, table, slots, 0, 0, ((6, scale_q), (None, 1.0), (7, 1.0)), norm=0
    )
    got_two, self_low = pinned(got_two, self_low)
    parts_two, got_two = spread_on(parts_two, got_two, device_count)
    two_away = swap_cores(parts_two, device_count)
    attended, self_log = attention_forward(self_low, self_low, self_low, self_firsts)
    got_two, two_away, attended = pinned(got_two, two_away, attended)
    got_two_away = swap_cores(got_two, device_count)
    parts_three = spread_begin(jnp.where(even, near, first))
    got_three = spread_swaps(parts_three, 0, device_count)
    after_self = project(
        here, attended, table, slots, 0, 3, ((8, 1.0),), residual=tokens, out_type=F32
    )
    got_two_away, after_self = pinned(got_two_away, after_self)
    slots.append((flat_slot(parts_two, got_two), flat_slot(two_away, got_two_away)))
    queries_cross, low_two = project(
        here, after_self, table, slots, 1, 0, ((9, scale_q),), norm=2
    )
    got_three, queries_cross, memory_here = pinned(got_three, queries_cross, memory_here)
    parts_three, got_three = spread_on(parts_three, got_three, device_count)
    three_away = swap_cores(parts_three, device_count)
    cross_low = project(here, memory_here, table, slots, 1, 1, ((None, 1.0), (10, 1.0)))
    merged, cross_log = attention_forward(
        queries_cross, cross_low, cross_low, cross_firsts, slot_bias
    )
    got_three, three_away, merged = pinned(got_three, three_away, merged)
    got_three_away = swap_cores(got_three, device_count)
    after_cross = project(
        here, merged, table, slots, 1, 3, ((11, 1.0),), residual=after_self, out_type=F32
    )
    grad_low_three = (upstream.astype(F32) * live_rows).astype(BF16)
    got_three_away, after_cross, grad_low_three = pinned(
        got_three_away, after_cross, grad_low_three
    )
    slots.append((flat_slot(parts_three, got_three), flat_slot(three_away, got_three_away)))

    bias_up = vector_rows[13:17].reshape(-1, 1, width)
    out_a, back_a, up_sent, down_sent, bias_sent, low_three = feed_half(
        away, after_cross, grad_low_three, table, bias_up, slots, 1, True
    )
    up_got = swap_bit(up_sent, device_count, 1)
    down_got = swap_bit(down_sent, device_count, 1)
    low_three, up_sent, down_sent = pinned(low_three, up_sent, down_sent)
    out_b, back_b, up_kept, down_kept, bias_kept = feed_half(
        here, low_three, grad_low_three, table, bias_up, slots, 0, False
    )
    up_got, down_got, out_b, back_b, up_kept, down_kept = pinned(
        up_got, down_got, out_b, back_b, up_kept, down_kept
    )
    feed_sum = Sum((up_kept, down_kept), (up_got, down_got), False)
    feed_sends = stage_sends(here, feed_sum, device_count)
    feed_sends, back_b = pinned(feed_sends, back_b)
    feed_swaps = stage_swaps(feed_sends, feed_sum, device_count)

    bias_even = jnp.where(core == 0, bias_kept, bias_sent)
    bias_odd = jnp.where(core == 0, bias_sent, bias_kept)
    grad_bias_up = jnp.concatenate([bias_even, bias_odd], axis=1).reshape(4, model)

    grad_two, grad_low_two, sums_three = norm_back(
        after_cross, table, 4, grad_low_three, (back_a, back_b)
    )
    grad_merged = project_back(here, (grad_low_two,), slots, 1, 3, BF16)
    cross_operands = (
        queries_cross,
        cross_low,
        cross_low,
        cross_firsts,
        grad_merged,
        merged,
        cross_log,
        slot_bias,
    )
    cross_whole, (queries_part, keys_part, values_part) = attention_backward(
        away, width, *cross_operands, None
    )
    cross_whole, (queries_own, keys_own, values_own) = attention_backward(
        here, width, *cross_operands, cross_whole
    )
    grad_queries_cross, grad_keys_cross, grad_values_cross, cross_sums = cross_whole
    feed_swaps, queries_part, queries_own, grad_queries_cross = pinned(
        feed_swaps, queries_part, queries_own, grad_queries_cross
    )
    feed_sum = feed_sum.joined(feed_swaps)
    feed_sends = stage_sends(here, feed_sum, device_count)
    feed_sends, queries_part, queries_own, grad_queries_cross = pinned(
        feed_sends, queries_part, queries_own, grad_queries_cross
    )
    feed_swaps = stage_swaps(feed_sends, feed_sum, device_count)
    cross_sent = weight_half(
        (
            (low_two, queries_part),
            (memory_here, keys_part),
            (memory_here, values_part),
            (merged, column_half(grad_low_two, 1 - core, width)),
        ),
        width,
    )
    cross_sent, queries_own, grad_queries_cross = pinned(
        cross_sent, queries_own, grad_queries_cross
    )
    cross_got = swap_bit(cross_sent, device_count, 1)
    cross_kept = weight_half(
        (
            (low_two, queries_own),
            (memory_here, keys_own),
            (memory_here, values_own),
            (merged, column_half(grad_low_two, core, width)),
        ),
        width,
    )

    grad_one, grad_low_one, sums_two = project_back(
        here, (grad_queries_cross,), slots, 1, 0, F32, (after_self, grad_two, table, 2)
    )
    grad_attended = project_back(here, (grad_low_one,), slots, 0, 3, BF16)
    memory_back = project_back(here, (grad_keys_cross, grad_values_cross), slots, 1, 1, BF16)
    memory_back = memory_back.reshape(group_size, SLOT_PAD, model)
    memory_back = exchange_members([memory_back[item] for item in range(group_size)], device_count)
    feed_swaps, cross_got, cross_kept, grad_attended = pinned(
        feed_swaps, cross_got, cross_kept, grad_attended
    )
    feed_sum = finish_stages(here, feed_sum.joined(feed_swaps), device_count)
    feed_kept, feed_sent = plane_totals(here, feed_sum)
    cross_sum = Sum((cross_kept,), (cross_got,), True)
    cross_sends = stage_sends(here, cross_sum, device_count)
    feed_sent, cross_sends, grad_attended = pinned(feed_sent, cross_sends, grad_attended)
    feed_got = move_planes(feed_sent, NEAR, plane_size)
    cross_swaps = stage_swaps(cross_sends, cross_sum, device_count)
    self_operands = (
        self_low,
        self_low,
        self_low,
        self_firsts,
        grad_attended,
        attended,
        self_log,
        None,
    )
    self_whole, (queries_part, keys_part, values_part) = attention_backward(
        away, width, *self_operands, None
    )
    self_sent = weight_half(
        (
            (low_one, queries_part),
            (low_one, keys_part),
            (low_one, values_part),
            (attended, column_half(grad_low_one, 1 - core, width)),
        ),
        width,
    )
    feed_got, cross_swaps, self_sent, self_whole, memory_back = pinned(
        feed_got, cross_swaps, self_sent, self_whole, memory_back
    )
    self_got = swap_bit(self_sent, device_count, 1)
    feed_kept = feed_kept + feed_got.astype(F32)
    cross_sum = cross_sum.joined(cross_swaps)
    cross_sends = stage_sends(here, cross_sum, device_count)
    feed_sent, cross_sends, self_whole = pinned(
        feed_kept.astype(BF16), cross_sends, self_whole
    )
    feed_got = move_planes(feed_sent, ((0, 2), (1, 3)), plane_size)
    cross_swaps = stage_swaps(cross_sends, cross_sum, device_count)
    self_whole, (queries_own, keys_own, values_own) = attention_backward(
        here, width, *self_operands, self_whole
    )
    grad_queries_self, grad_keys_self, grad_values_self, self_sums = self_whole
    self_kept = weight_half(
        (
            (low_one, queries_own),
            (low_one, keys_own),
            (low_one, values_own),
            (attended, column_half(grad_low_one, core, width)),
        ),
        width,
    )
    self_got, cross_swaps, self_kept = pinned(self_got, cross_swaps, self_kept)
    self_sum = Sum((self_kept,), (self_got,), True)
    self_sends = stage_sends(here, self_sum, device_count)
    self_sends, grad_queries_self, cross_swaps = pinned(
        self_sends, grad_queries_self, cross_swaps
    )
    self_swaps = stage_swaps(self_sends, self_sum, device_count)
    cross_sum = finish_stages(here, cross_sum.joined(cross_swaps), device_count)
    input_grad, _, sums_one = project_back(
        here,
        (grad_queries_self, grad_keys_self, grad_values_self),
        slots,
        0,
        0,
        F32,
        (tokens, grad_one, table, 0),
    )
    sums_one, cross_swaps = pinned(sums_one, cross_sum.swaps)
    cross_sum.swaps = list(cross_swaps)
    cross_total, cross_sent = plane_totals(here, cross_sum)
    self_swaps, cross_sent, sums_one = pinned(self_swaps, cross_sent, sums_one)
    cross_got = move_planes(cross_sent, ((0, 1), (3, 2)), plane_size)
    self_sum = self_sum.joined(self_swaps)
    self_sends = stage_sends(here, self_sum, device_count)
    self_sends, sums_one = pinned(self_sends, sums_one)
    self_swaps = stage_swaps(self_sends, self_sum, device_count)
    vector_head = jnp.stack(
        [
            sums_one[0],
            sums_one[1],
            sums_two[0],
            sums_two[1],
            sums_three[0],
            sums_three[1],
            self_sums[0],
            self_sums[1],
            sums_two[2],
            cross_sums[0],
            cross_sums[1],
            sums_three[2],
            sums_three[3],
        ],
        axis=0,
    )
    vector_terms = jnp.concatenate([vector_head, grad_bias_up], axis=0)
    vector_terms = jnp.swapaxes(
        vector_terms.reshape(vector_shape[0], device_count, vector_shape[1]), 0, 1
    )
    vector_bits = [1 << number for number in reversed(range(device_count.bit_length() - 1))]
    vector_terms = pad_vectors(vector_terms.reshape(device_count, -1), 8)
    vector_kept, vector_sent = vector_send(vector_terms, device, vector_bits[0])
    vector_got = swap_bit(vector_sent, device_count, vector_bits[0])

    def vector_next(kept, got, number):
        kept, sent = vector_send(kept + got, device, vector_bits[number])
        return kept, swap_bit(sent, device_count, vector_bits[number])

    self_swaps, vector_got = pinned(self_swaps, vector_got)
    self_sum = finish_stages(here, self_sum.joined(self_swaps), device_count)
    self_total, self_sent = plane_totals(here, self_sum)
    self_sent, vector_got = pinned(self_sent, vector_got)
    self_got = move_planes(self_sent, ((1, 0), (3, 2)), plane_size)
    vector_kept, vector_got = vector_next(vector_kept, vector_got, 1)
    result = (after_cross + (out_a + out_b) + vector_rows[12]) * live_rows
    mixed = result.astype(BF16)
    mixed, vector_got = pinned(mixed, vector_got)
    vector_kept, vector_got = vector_next(vector_kept, vector_got, 2)
    cross_total = cross_total + cross_got.astype(F32)
    cross_got = move_planes(cross_total.astype(BF16), ((2, 1),), plane_size)

    self_got, cross_got, feed_got, vector_got = pinned(
        self_got, cross_got, feed_got, vector_got
    )
    self_sent = (self_total + self_got.astype(F32)).astype(BF16)
    self_sent, cross_got, feed_got, memory_back, vector_got = pinned(
        self_sent, cross_got, feed_got, memory_back, vector_got
    )
    self_far = move_planes(self_sent, ((2, 0),), plane_size)
    group_other = jnp.where(
        plane < 2,
        cross_total + cross_got.astype(F32),
        feed_kept + feed_got.astype(F32),
    )
    memory_back = jnp.stack([item[:quarter] for item in memory_back])
    memory_back = by_member(memory_back, member).astype(F32)
    vector_kept, vector_got = vector_next(vector_kept, vector_got, 3)
    group_other, vector_got = pinned(group_other, vector_got)
    for number in range(4, len(vector_bits)):
        vector_kept, vector_got = vector_next(vector_kept, vector_got, number)
    group_other, self_far, vector_got = pinned(group_other, self_far, vector_got)
    vector_grad = (vector_kept + vector_got).reshape(-1)[: vectors.size].reshape(vector_shape)
    (
        weight_grad,
        weight_first,
        weight_second,
        new_weights,
        new_average,
        weights_copy,
        new_stats,
        new_bases,
    ) = rotated_update(
        here,
        self_total,
        self_got,
        self_far,
        group_other,
        weights,
        weight_average,
        weight_moment1,
        weight_moment2,
        stats,
        bases,
    )
    vector_first, vector_second, new_vectors = adam_update(
        vector_grad, vectors, vector_moment1, vector_moment2
    )
    new_vector_average = AVERAGE * vector_average + (1.0 - AVERAGE) * new_vectors
    return (
        mixed,
        input_grad,
        memory_back,
        weight_grad,
        weight_first,
        weight_second,
        new_weights,
        new_average,
        weights_copy,
        new_stats,
        new_bases,
        vector_grad,
        vector_first,
        vector_second,
        new_vectors,
        new_vector_average,
        new_vectors.astype(BF16),
        vector_grad[12],
    )


def solution(mesh):
    return jax.shard_map(
        local,
        mesh=mesh,
        in_specs=(
            P(("seq", "mem"), None),
            P("seq", "mem", None),
            P(("seq", "mem")),
            P("seq", None),
            P(("seq", "mem"), None),
            P(None, ("seq", "mem")),
            P(None, ("seq", "mem")),
            P(None, ("seq", "mem")),
            P(None, ("seq", "mem")),
            P(("seq", "mem"), None, None),
            P(("seq", "mem"), None, None),
            P(None, ("seq", "mem")),
            P(None, ("seq", "mem")),
            P(None, ("seq", "mem")),
            P(None, ("seq", "mem")),
        ),
        out_specs=(
            P(("seq", "mem"), None),
            P(("seq", "mem"), None),
            P("seq", "mem", None),
            P(None, ("seq", "mem")),
            P(None, ("seq", "mem")),
            P(None, ("seq", "mem")),
            P(None, ("seq", "mem")),
            P(None, ("seq", "mem")),
            P(None, ("seq", "mem")),
            P(("seq", "mem"), None, None),
            P(("seq", "mem"), None, None),
            P(None, ("seq", "mem")),
            P(None, ("seq", "mem")),
            P(None, ("seq", "mem")),
            P(None, ("seq", "mem")),
            P(None, ("seq", "mem")),
            P(None, ("seq", "mem")),
            P(("seq", "mem")),
        ),
        check_vma=False,
    )
```

```python
import functools

import jax
import jax.numpy as jnp
from jax import lax
from jax.experimental import pallas as pl
from jax.experimental.pallas import tpu as pltpu
from jax.sharding import PartitionSpec as P

HEADS = 16
HEAD = 64
BLK = 128
STEP = 10
LANES = 128
QUERY_ROWS = 256
FORWARD_ROWS = 512
FEED_ROWS = 1024
SLOT_PAD = 160
PANEL = 32
GROUPS = 4
AXES = ("seq", "mem")
SMALL = pl.CostEstimate(flops=1 << 20, bytes_accessed=1 << 16, transcendentals=0)

F32 = jnp.float32
BF16 = jnp.bfloat16
HIGHEST = lax.Precision.HIGHEST
NORM_EPS = 1e-05
ADAM_EPS = 1e-08
BETA_ONE = 0.9
BETA_TWO = 0.95
RATE = 0.04
VECTOR_RATE = 0.4
DECAY = 0.01
AVERAGE = 0.999
MASKED = -1e30
CONTRACT_ROWS = (((0,), (0,)), ((), ()))
CONTRACT_LAST = (((1,), (1,)), ((), ()))


def dot(left, right):
    return jnp.dot(left, right, preferred_element_type=F32)


def dot_last(left, right):
    return lax.dot_general(left, right, CONTRACT_LAST, preferred_element_type=F32)


def dot_rows(left, right):
    return lax.dot_general(left, right, CONTRACT_ROWS, preferred_element_type=F32)


def normalize(values, scale_gain, offset):
    centre = jnp.mean(values, axis=-1, keepdims=True)
    centred = values - centre
    variance = jnp.mean(centred * centred, axis=-1, keepdims=True)
    return centred * lax.rsqrt(variance + NORM_EPS) * scale_gain + offset


def causal_mask(scores, first_key, first_query):
    key_pos = lax.broadcasted_iota(jnp.int32, scores.shape, 0) + first_key
    query_pos = lax.broadcasted_iota(jnp.int32, scores.shape, 1) + first_query
    return jnp.where(key_pos <= query_pos, scores, MASKED)


def head_of_lane(shape):
    return lax.broadcasted_iota(jnp.int32, shape, 1) // HEAD


def one_head(values, lane_head, head):
    return jnp.where(lane_head == head, values, jnp.zeros_like(values))


def widen(bias, columns):
    return jnp.concatenate([bias] * (columns // LANES), axis=1)


def attention_forward_kernel(*refs, causal):
    if causal:
        q_ref, k_ref, v_ref, out_ref, log_ref = refs
    else:
        q_ref, k_ref, v_ref, bias_ref, out_ref, log_ref = refs
    keys = k_ref[...]
    key_count = keys.shape[0]
    values_turned = v_ref[...].T
    lane_head = head_of_lane(keys.shape)
    key_heads = [one_head(keys, lane_head, head) for head in range(2)]
    units = [
        (block, head) for block in range(q_ref.shape[0] // FORWARD_ROWS) for head in range(2)
    ]

    def scores_of(unit):
        block, head = unit
        seen = (block + 1) * FORWARD_ROWS if causal else key_count
        queries = q_ref[block * FORWARD_ROWS : (block + 1) * FORWARD_ROWS, :]
        scores = dot_last(key_heads[head][:seen], queries)
        if not causal:
            return scores + widen(bias_ref[...], FORWARD_ROWS)
        last = causal_mask(scores[seen - FORWARD_ROWS :], 0, 0)
        if seen == FORWARD_ROWS:
            return last
        return jnp.concatenate([scores[: seen - FORWARD_ROWS], last], axis=0)

    scores = scores_of(units[0])
    outs = []
    for item, (block, head) in enumerate(units):
        later = scores_of(units[item + 1]) if item + 1 < len(units) else None
        rows = slice(block * FORWARD_ROWS, (block + 1) * FORWARD_ROWS)
        largest = jnp.max(scores, axis=0, keepdims=True)
        raised = jnp.exp(scores - largest)
        summed = jnp.sum(raised, axis=0, keepdims=True)
        turned = values_turned[head * HEAD : (head + 1) * HEAD, : scores.shape[0]]
        outs.append(dot(turned, raised.astype(BF16)) / summed)
        log_ref[0, head : head + 1, rows] = largest + jnp.log(summed)
        if head == 1:
            out_ref[rows, :] = jnp.concatenate(outs, axis=0).T.astype(BF16)
            outs = []
        scores = later


def attention_backward_kernel(*refs, causal):
    _, q_ref, k_ref, v_ref, grad_ref, out_ref, log_ref = refs[:7]
    bias_ref = None if causal else refs[7]
    dq_ref, dk_ref, dv_ref, sums_ref, dq_half, dk_half, dv_half, chance_ref, score_ref = refs[-9:]
    query_sum = jnp.zeros((1, LANES), F32)
    value_sums = []
    keys = k_ref[...]
    values = v_ref[...]
    key_count = keys.shape[0]
    row_count = q_ref.shape[0]
    keys_turned = keys.T
    product = (grad_ref[...].astype(F32) * out_ref[...].astype(F32)).T
    inner = [
        jnp.sum(product[head * HEAD : (head + 1) * HEAD], axis=0, keepdims=True)
        for head in range(2)
    ]
    slots_of = chance_ref.shape[0]
    key_rows = chance_ref.shape[1]
    lane_head = head_of_lane((key_rows, LANES))
    blocks = row_count // QUERY_ROWS
    units = [
        (piece, head, block)
        for piece in range(key_count // key_rows)
        for head in range(2)
        for block in range(piece * key_rows // QUERY_ROWS if causal else 0, blocks)
    ]

    def products_of(unit):
        piece, head, block = unit
        slots = slice(piece * key_rows, (piece + 1) * key_rows)
        rows = slice(block * QUERY_ROWS, (block + 1) * QUERY_ROWS)
        return (
            dot_last(one_head(keys[slots], lane_head, head), q_ref[rows, :]),
            dot_last(one_head(values[slots], lane_head, head), grad_ref[rows, :]),
        )

    even_heads = {}

    def finish(piece, head):
        slots = slice(piece * key_rows, (piece + 1) * key_rows)
        first = piece * key_rows if causal else 0
        kept = chance_ref[(2 * piece + head) % slots_of, :, first:]
        grad_value = dot(kept, grad_ref[first:, :])
        grad_key = dot(score_ref[head, slots, first:], q_ref[first:, :])
        if head == 0:
            even_heads[piece] = (grad_key, grad_value)
            return
        even_key, even_value = even_heads.pop(piece)
        grad_key = jnp.where(lane_head == 0, even_key, grad_key).astype(BF16)
        grad_value = jnp.where(lane_head == 0, even_value, grad_value).astype(BF16)
        dk_ref[slots, :] = grad_key
        dk_half[slots, :] = grad_key
        dv_ref[slots, :] = grad_value
        dv_half[slots, :] = grad_value
        value_sums.append(jnp.sum(grad_value.astype(F32), axis=0, keepdims=True))

    current = products_of(units[0])
    ended = None
    for item, (piece, head, block) in enumerate(units):
        later = products_of(units[item + 1]) if item + 1 < len(units) else None
        if ended is not None:
            finish(*ended)
            ended = None
        scores, grad_chance = current
        slots = slice(piece * key_rows, (piece + 1) * key_rows)
        rows = slice(block * QUERY_ROWS, (block + 1) * QUERY_ROWS)
        if not causal:
            scores = scores + widen(bias_ref[slots, :], QUERY_ROWS)
        elif (piece + 1) * key_rows > block * QUERY_ROWS:
            scores = causal_mask(scores, piece * key_rows, block * QUERY_ROWS)
        chance = jnp.exp(scores - log_ref[0, head : head + 1, rows])
        chance_ref[(2 * piece + head) % slots_of, :, rows] = chance.astype(BF16)
        score_ref[head, slots, rows] = (chance * (grad_chance - inner[head][:, rows])).astype(BF16)
        if block == blocks - 1:
            ended = (piece, head)
        current = later
    finish(*ended)
    for block in range(blocks):
        rows = slice(block * QUERY_ROWS, (block + 1) * QUERY_ROWS)
        seen = (block + 1) * QUERY_ROWS if causal else key_count
        parts = [
            dot(
                keys_turned[head * HEAD : (head + 1) * HEAD, :seen],
                score_ref[head, :seen, rows],
            )
            for head in range(2)
        ]
        grad_query = jnp.concatenate(parts, axis=0).T.astype(BF16)
        grad_query = (grad_query.astype(F32) * HEAD ** (-0.5)).astype(BF16)
        dq_ref[rows, :] = grad_query
        dq_half[rows, :] = grad_query
        query_sum = query_sum + jnp.sum(grad_query.astype(F32), axis=0, keepdims=True)
    sums_ref[0:1, :] = query_sum
    sums_ref[1:2, :] = sum(value_sums[1:], value_sums[0])


def head_pair(row_count, first):
    return pl.BlockSpec((row_count, LANES), lambda pair: (0, first + pair))


def attention_forward(queries, keys, values, firsts, bias=None):
    causal = bias is None
    row_count = queries.shape[0]
    key_count = keys.shape[0]
    pairs = HEADS // 2
    in_specs = [
        head_pair(row_count, firsts[0]),
        head_pair(key_count, firsts[1]),
        head_pair(key_count, firsts[2]),
    ]
    operands = [queries, keys, values]
    if not causal:
        in_specs.append(pl.BlockSpec((key_count, LANES), lambda pair: (0, 0)))
        operands.append(bias)
    return pl.pallas_call(
        functools.partial(attention_forward_kernel, causal=causal),
        grid=(pairs,),
        in_specs=in_specs,
        out_specs=[
            head_pair(row_count, 0),
            pl.BlockSpec((1, 8, row_count), lambda pair: (pair, 0, 0)),
        ],
        out_shape=[
            jax.ShapeDtypeStruct((row_count, pairs * LANES), BF16),
            jax.ShapeDtypeStruct((pairs, 8, row_count), F32),
        ],
        compiler_params=pltpu.CompilerParams(vmem_limit_bytes=60 << 20),
        cost_estimate=SMALL,
    )(*operands)


def attention_backward(
    half, width, queries, keys, values, firsts, grads, outs, log_total, bias, whole
):
    causal = bias is None
    row_count, model = grads.shape
    key_count = keys.shape[0]
    key_rows = QUERY_ROWS if causal else key_count // 2
    per_unit = width // LANES
    steps = HEADS // 4

    def chosen(step, side):
        return (2 * (step // per_unit) + side[0]) * per_unit + step % per_unit

    def in_whole(count, first=0):
        return pl.BlockSpec((count, LANES), lambda step, side: (0, first + chosen(step, side)))

    def alone(count):
        return pl.BlockSpec((count, LANES), lambda step, side: (0, step))

    in_specs = [
        in_whole(row_count, firsts[0]),
        in_whole(key_count, firsts[1]),
        in_whole(key_count, firsts[2]),
        in_whole(row_count),
        in_whole(row_count),
        pl.BlockSpec((1, 8, row_count), lambda step, side: (chosen(step, side), 0, 0)),
    ]
    operands = [queries, keys, values, grads, outs, log_total]
    if not causal:
        in_specs.append(pl.BlockSpec((key_count, LANES), lambda step, side: (0, 0)))
        operands.append(bias)
    aliases = {}
    if whole is not None:
        for item, array in enumerate(whole):
            aliases[1 + len(operands)] = item
            in_specs.append(pl.BlockSpec(memory_space=pl.ANY))
            operands.append(array)
    counts = (row_count, key_count, key_count)
    results = pl.pallas_call(
        functools.partial(attention_backward_kernel, causal=causal),
        grid_spec=pltpu.PrefetchScalarGridSpec(
            num_scalar_prefetch=1,
            grid=(steps,),
            in_specs=in_specs,
            out_specs=[in_whole(count) for count in counts]
            + [in_whole(8)]
            + [alone(count) for count in counts],
            scratch_shapes=[
                pltpu.VMEM((4, key_rows, row_count), BF16),
                pltpu.VMEM((2, key_count, row_count), BF16),
            ],
        ),
        out_shape=[jax.ShapeDtypeStruct((count, model), BF16) for count in counts]
        + [jax.ShapeDtypeStruct((8, model), F32)]
        + [jax.ShapeDtypeStruct((count, model // 2), BF16) for count in counts],
        input_output_aliases=aliases,
        compiler_params=pltpu.CompilerParams(vmem_limit_bytes=60 << 20),
        cost_estimate=SMALL,
    )(half, *operands)
    return results[:4], results[4:]


PLACE_PLANE = 3
VECTOR_ROWS = 24


def holders(group, plane):
    if group == 0:
        return ((1, plane != 0), (0, plane == 0))
    if group == 1:
        return ((2, plane > 1), (0, plane == 1), (1, plane == 0))
    if group == 2:
        return ((2, plane < 2), (0, plane == 2), (3, plane == 3))
    return ((3, plane != 3), (0, plane == 3))


class Source:
    def __init__(self, slots, group, sides):
        self.group = group
        self.sides = sides
        self.which = [slot for slot, _ in holders(group, 0)]
        self.operands = [
            array for slot in self.which for side in sides for array in slots[slot][side]
        ]
        self.shape = self.operands[0].shape
        self.dtype = self.operands[0].dtype

    def chunks(self):
        return 2 * self.shape[0]

    def specs(self):
        return [pl.BlockSpec(memory_space=pl.ANY)] * len(self.operands)

    def scratch(self):
        return [
            pltpu.VMEM((2, 2 * self.shape[1], self.shape[2]), self.dtype),
            pltpu.SemaphoreType.DMA((2, 2)),
        ]


def start_fetch(source, refs, buffer, semaphores, plane, side, chunk, turn):
    top, half = source.shape[:2]
    lower_place = 0
    rest = chunk // 2
    size = top
    while size > 1:
        lower_place = lower_place * 2 + rest % 2
        rest = rest // 2
        size //= 2
    item = 0
    for _, chosen in holders(source.group, plane):
        for number in range(len(source.sides)):
            wanted = chosen & (side == number)
            lows, highs, evens, odds = refs[item : item + 4]
            item += 4
            copies = (
                (chunk < top, lows, chunk, 0),
                (chunk >= top, highs, chunk - top, 0),
                (chunk % 2 == 0, evens, lower_place, 1),
                (chunk % 2 == 1, odds, lower_place, 1),
            )

            @pl.when(wanted)
            def _(copies=copies):
                for condition, array, index, part in copies:

                    @pl.when(condition)
                    def _(array=array, index=index, part=part):
                        pltpu.make_async_copy(
                            array.at[index],
                            buffer.at[turn, pl.ds(part * half, half), :],
                            semaphores.at[turn, part],
                        ).start()


def wait_fetch(source, refs, buffer, semaphores, turn):
    half = source.shape[1]
    for part in range(2):
        pltpu.make_async_copy(
            refs[0].at[0],
            buffer.at[turn, pl.ds(part * half, half), :],
            semaphores.at[turn, part],
        ).wait()


def start_fetches(source, refs, buffer, semaphores, plane, order, item, count):
    @pl.when(item == 0)
    def _():
        side, chunk = order(0)
        start_fetch(source, refs, buffer, semaphores, plane, side, chunk, 0)

    @pl.when(item + 1 < count)
    def _():
        side, chunk = order(item + 1)
        start_fetch(source, refs, buffer, semaphores, plane, side, chunk, (item + 1) % 2)


def fetched(source, refs, buffer, semaphores, item):
    wait_fetch(source, refs, buffer, semaphores, item % 2)
    return buffer.at[item % 2]


def vector_part(vectors_ref, row, first, width):
    return vectors_ref[row : row + 1, pl.ds(pl.multiple_of(first, width), width)]


def gelu_parts(values):
    slope = 0.7978845608028654
    square = values * values
    turned = jnp.tanh(slope * values * (1.0 + 0.044715 * square))
    weight = 0.5 * (1.0 + turned)
    derivative = weight + 0.5 * values * (1.0 - turned * turned) * (
        slope + (3.0 * 0.044715 * slope) * square
    )
    return values * weight, derivative


def feed_kernel(*refs, norm, up_source, down_source):
    refs = list(refs)
    place_ref = refs.pop(0)
    values_ref = refs.pop(0)
    grad_ref = refs.pop(0)
    vectors_ref = refs.pop(0)
    bias_ref = refs.pop(0)
    up_refs = refs[: len(up_source.operands)]
    refs = refs[len(up_refs) :]
    down_refs = refs[: len(down_source.operands)]
    refs = refs[len(down_refs) :]
    out_ref, back_ref, grad_up_ref, grad_down_ref, grad_bias_ref = refs[:5]
    low_ref = refs[5] if norm else values_ref
    out_total, back_total, low_turned, grad_turned, active_ref, hidden_ref = refs[-10:-4]
    up_buffer, up_semaphores, down_buffer, down_semaphores = refs[-4:]
    plane = place_ref[PLACE_PLANE]
    step = pl.program_id(0)
    count = up_source.chunks()

    def order(item):
        return 0, item

    start_fetches(up_source, up_refs, up_buffer, up_semaphores, plane, order, step, count)
    start_fetches(
        down_source, down_refs, down_buffer, down_semaphores, plane, order, step, count
    )

    @pl.when(step == 0)
    def _():
        if norm:
            for first in range(0, values_ref.shape[0], QUERY_ROWS):
                rows = slice(first, first + QUERY_ROWS)
                low_ref[rows, :] = normalize(
                    values_ref[rows, :], vectors_ref[4:5, :], vectors_ref[5:6, :]
                ).astype(BF16)
        low_turned[...] = low_ref[...].T
        grad_turned[...] = grad_ref[...].T
        out_total[...] = jnp.zeros_like(out_total)
        back_total[...] = jnp.zeros_like(back_total)

    up = fetched(up_source, up_refs, up_buffer, up_semaphores, step)[...]
    down = fetched(down_source, down_refs, down_buffer, down_semaphores, step)[...]
    total = jnp.zeros((1, up.shape[1]), F32)
    pieces = low_ref.shape[0] // FEED_ROWS
    for piece in range(pieces):
        rows = slice(piece * FEED_ROWS, (piece + 1) * FEED_ROWS)
        active, derivative = gelu_parts(dot(low_ref[rows, :], up) + bias_ref[0])
        active_low = active.astype(BF16)
        hidden_low = (derivative * dot(grad_ref[rows, :], down)).astype(BF16)
        active_ref[rows, :] = active_low
        hidden_ref[rows, :] = hidden_low
        total = total + jnp.sum(hidden_low.astype(F32), axis=0, keepdims=True)
        out_total[rows, :] += dot_last(active_low, down)
        back_total[rows, :] += dot_last(hidden_low, up)
    grad_bias_ref[0] = total
    for piece in range(low_turned.shape[0] // FEED_ROWS):
        rows = slice(piece * FEED_ROWS, (piece + 1) * FEED_ROWS)
        grad_down_ref[0, rows, :] = dot(grad_turned[rows, :], active_ref[...]).astype(BF16)
        grad_up_ref[0, rows, :] = dot(low_turned[rows, :], hidden_ref[...]).astype(BF16)

    @pl.when(step == count - 1)
    def _():
        out_ref[...] = out_total[...].astype(BF16)
        back_ref[...] = back_total[...].astype(BF16)


def feed_half(place, values, grad, vectors, bias, slots, side, norm):
    row_count, model = values.shape
    up_source = Source(slots, 2, (side,))
    down_source = Source(slots, 3, (side,))
    steps = up_source.chunks()
    width = up_source.shape[2]

    def whole(shape):
        return pl.BlockSpec(shape, lambda step, place: (0, 0), pipeline_mode=pl.Buffered(1))

    total = pl.BlockSpec((row_count, model), lambda step, place: (0, 0))
    chunk = pl.BlockSpec((1, model, width), lambda step, place: (step, 0, 0))
    out_specs = [
        total,
        total,
        chunk,
        chunk,
        pl.BlockSpec((1, 1, width), lambda step, place: (step ^ place[1], 0, 0)),
    ]
    out_shape = [
        jax.ShapeDtypeStruct((row_count, model), BF16),
        jax.ShapeDtypeStruct((row_count, model), BF16),
        jax.ShapeDtypeStruct((steps, model, width), BF16),
        jax.ShapeDtypeStruct((steps, model, width), BF16),
        jax.ShapeDtypeStruct((steps, 1, width), F32),
    ]
    if norm:
        out_specs.append(total)
        out_shape.append(jax.ShapeDtypeStruct((row_count, model), BF16))
    return pl.pallas_call(
        functools.partial(
            feed_kernel, norm=norm, up_source=up_source, down_source=down_source
        ),
        grid_spec=pltpu.PrefetchScalarGridSpec(
            num_scalar_prefetch=1,
            grid=(steps,),
            in_specs=[
                whole((row_count, model)),
                whole((row_count, model)),
                whole((VECTOR_ROWS, model)),
                pl.BlockSpec(
                    (1, 1, width), lambda step, place: (2 * (step ^ place[1]) + place[0], 0, 0)
                ),
            ]
            + up_source.specs()
            + down_source.specs(),
            out_specs=out_specs,
            scratch_shapes=[
                pltpu.VMEM((row_count, model), F32),
                pltpu.VMEM((row_count, model), F32),
                pltpu.VMEM((model, row_count), BF16),
                pltpu.VMEM((model, row_count), BF16),
                pltpu.VMEM((row_count, width), BF16),
                pltpu.VMEM((row_count, width), BF16),
            ]
            + up_source.scratch()
            + down_source.scratch(),
        ),
        out_shape=out_shape,
        compiler_params=pltpu.CompilerParams(vmem_limit_bytes=60 << 20),
        cost_estimate=SMALL,
    )(place, values, grad, vectors, bias, *up_source.operands, *down_source.operands)


def norm_back_rows(values, grad, gain, stream):
    values = values.astype(F32)
    centred = values - jnp.mean(values, axis=-1, keepdims=True)
    inverse = lax.rsqrt(jnp.mean(centred * centred, axis=-1, keepdims=True) + NORM_EPS)
    normal = centred * inverse
    scaled = grad * gain
    product = scaled * normal
    back = inverse * (
        scaled
        - jnp.mean(scaled, axis=-1, keepdims=True)
        - normal * jnp.mean(product, axis=-1, keepdims=True)
    )
    return stream.astype(F32) + back, normal


def row_sums(grad, normal, low, stream):
    parts = (grad * normal, grad, low.astype(F32), stream.astype(F32))
    return [jnp.sum(part, axis=0, keepdims=True) for part in parts]


def norm_back_kernel(*refs, count, row):
    values_ref, vectors_ref, stream_ref = refs[:3]
    grad_refs = refs[3 : 3 + count]
    out_ref, low_ref, sums_ref = refs[3 + count :]
    grad = grad_refs[0][...].astype(F32)
    for grad_ref in grad_refs[1:]:
        grad = grad + grad_ref[...].astype(F32)
    result, normal = norm_back_rows(
        values_ref[...], grad, vectors_ref[row : row + 1, :], stream_ref[...]
    )
    low = result.astype(BF16)
    out_ref[...] = result
    low_ref[...] = low

    @pl.when(pl.program_id(0) == 0)
    def _():
        sums_ref[...] = jnp.zeros_like(sums_ref)

    for number, part in enumerate(row_sums(grad, normal, low, stream_ref[...])):
        sums_ref[number : number + 1, :] += part


def norm_back(values, vectors, row, stream, grads):
    row_count, model = values.shape
    panel = pl.BlockSpec((QUERY_ROWS // 2, model), lambda step: (step, 0))
    return pl.pallas_call(
        functools.partial(norm_back_kernel, count=len(grads), row=row),
        grid=(2 * row_count // QUERY_ROWS,),
        in_specs=[panel, pl.BlockSpec((VECTOR_ROWS, model), lambda step: (0, 0)), panel]
        + [panel] * len(grads),
        out_specs=[panel, panel, pl.BlockSpec((8, model), lambda step: (0, 0))],
        out_shape=[
            jax.ShapeDtypeStruct((row_count, model), F32),
            jax.ShapeDtypeStruct((row_count, model), BF16),
            jax.ShapeDtypeStruct((8, model), F32),
        ],
        compiler_params=pltpu.CompilerParams(vmem_limit_bytes=60 << 20),
        cost_estimate=SMALL,
    )(values, vectors, stream, *grads)


def project_kernel(*refs, source, block, lines, norm, residual):
    refs = list(refs)
    place_ref = refs.pop(0)
    values_ref = refs.pop(0)
    vectors_ref = refs.pop(0)
    residual_ref = refs.pop(0) if residual else None
    source_refs = refs[: len(source.operands)]
    refs = refs[len(source_refs) :]
    out_ref = refs.pop(0)
    low_ref = refs.pop(0) if norm is not None else None
    buffer, semaphores, held_ref, load_semaphore = refs
    load = pltpu.make_async_copy(values_ref, held_ref, load_semaphore)
    values_ref = held_ref
    low_ref = held_ref if low_ref is None else low_ref
    model = values_ref.shape[1]
    width = out_ref.shape[1]
    parts = model // (2 * width)
    item = pl.program_id(0)
    count = 2 * parts * len(lines)

    def order(item):
        return item % 2, (block * parts + item // 2) ^ place_ref[1]

    @pl.when(item == 0)
    def _():
        load.start()

    start_fetches(
        source, source_refs, buffer, semaphores, place_ref[PLACE_PLANE], order, item, count
    )

    @pl.when(item == 0)
    def _():
        load.wait()
        if norm is not None:
            for first in range(0, values_ref.shape[0], QUERY_ROWS):
                rows = slice(first, first + QUERY_ROWS)
                low_ref[rows, :] = normalize(
                    values_ref[rows, :].astype(F32),
                    vectors_ref[norm : norm + 1, :],
                    vectors_ref[norm + 1 : norm + 2, :],
                ).astype(BF16)

    columns_ref = fetched(source, source_refs, buffer, semaphores, item)
    inside = item // 2 % parts
    column = (2 * inside + (item % 2 ^ place_ref[0])) * width
    row_count = values_ref.shape[0]
    step = row_count // 2
    for number, (line, scale) in enumerate(lines):

        @pl.when(item // (2 * parts) == number)
        def _(line=line, scale=scale):
            columns = columns_ref[...]
            for first in range(0, row_count, step):
                rows = slice(first, first + step)
                made = dot(low_ref[rows, :], columns)
                if line is not None:
                    made = made + vector_part(vectors_ref, line, column, width)
                if scale != 1.0:
                    made = made * scale
                if residual:
                    made = residual_ref[rows, :].astype(F32) + made
                out_ref[rows, :] = made.astype(out_ref.dtype)


def project(
    place, values, vectors, slots, group, block, lines, norm=None, residual=None, out_type=BF16
):
    row_count, model = values.shape
    source = Source(slots, group, (0, 1))
    width = source.shape[2]
    parts = model // (2 * width)

    def whole(shape):
        return pl.BlockSpec(shape, lambda *_: (0, 0), pipeline_mode=pl.Buffered(1))

    panel = pl.BlockSpec(
        (row_count, width),
        lambda item, place: (0, 2 * (item // 2) + (item % 2 ^ place[0])),
    )
    in_specs = [pl.BlockSpec(memory_space=pl.ANY), whole((VECTOR_ROWS, model))]
    operands = [values, vectors]
    if residual is not None:
        in_specs.append(panel)
        operands.append(residual)
    out_specs = [panel]
    out_shape = [jax.ShapeDtypeStruct((row_count, len(lines) * model), out_type)]
    if norm is not None:
        out_specs.append(pl.BlockSpec((row_count, model), lambda *_: (0, 0)))
        out_shape.append(jax.ShapeDtypeStruct((row_count, model), BF16))
    results = pl.pallas_call(
        functools.partial(
            project_kernel,
            source=source,
            block=block,
            lines=lines,
            norm=norm,
            residual=residual is not None,
        ),
        grid_spec=pltpu.PrefetchScalarGridSpec(
            num_scalar_prefetch=1,
            grid=(2 * parts * len(lines),),
            in_specs=in_specs + source.specs(),
            out_specs=out_specs,
            scratch_shapes=source.scratch()
            + [pltpu.VMEM(values.shape, values.dtype), pltpu.SemaphoreType.DMA],
        ),
        out_shape=out_shape,
        compiler_params=pltpu.CompilerParams(vmem_limit_bytes=60 << 20),
        cost_estimate=SMALL,
    )(place, *operands, *source.operands)
    return results if norm is not None else results[0]


def project_back_kernel(*refs, source, block, count, row):
    refs = list(refs)
    place_ref = refs.pop(0)
    grad_refs = refs[:count]
    refs = refs[count:]
    if row is not None:
        values_hbm, stream_hbm, vectors_ref = refs[:3]
        refs = refs[3:]
    source_refs = refs[: len(source.operands)]
    refs = refs[len(source.operands) :]
    if row is None:
        out_ref, total_ref, buffer, semaphores = refs
    else:
        out_hbm, low_hbm, sums_ref, total_ref, buffer, semaphores = refs[:6]
        values_ref, stream_ref, low_ref, load_semaphores, store_semaphores = refs[6:]
    row_count, model = total_ref.shape
    width = grad_refs[0].shape[1]
    parts = model // (2 * width)
    item = pl.program_id(0)
    steps = 2 * parts * count

    def order(item):
        return item % 2, (block * parts + item // 2) ^ place_ref[1]

    start_fetches(
        source, source_refs, buffer, semaphores, place_ref[PLACE_PLANE], order, item, steps
    )
    if row is not None:
        loads = [
            pltpu.make_async_copy(values_hbm, values_ref, load_semaphores.at[0]),
            pltpu.make_async_copy(stream_hbm, stream_ref, load_semaphores.at[1]),
        ]

    @pl.when(item == 0)
    def _():
        if row is not None:
            for load in loads:
                load.start()
        total_ref[...] = jnp.zeros_like(total_ref)

    columns_ref = fetched(source, source_refs, buffer, semaphores, item)
    for number, grad_ref in enumerate(grad_refs):

        @pl.when(item // (2 * parts) == number)
        def _(grad_ref=grad_ref):
            columns = columns_ref[...]
            size = row_count // 2
            for first in range(0, row_count, size):
                rows = slice(first, first + size)
                total_ref[rows, :] += dot_last(grad_ref[rows, :], columns)

    @pl.when(item == steps - 1)
    def _():
        if row is None:
            out_ref[...] = total_ref[...].astype(out_ref.dtype)
            return
        for load in loads:
            load.wait()
        stores = []
        sums = None
        for number in range(row_count // QUERY_ROWS):
            rows = slice(number * QUERY_ROWS, (number + 1) * QUERY_ROWS)
            grad = total_ref[rows, :]
            stream = stream_ref[rows, :]
            result, normal = norm_back_rows(
                values_ref[rows, :], grad, vectors_ref[row : row + 1, :], stream
            )
            low = result.astype(BF16)
            made = row_sums(grad, normal, low, stream)
            sums = made if sums is None else [a + b for a, b in zip(sums, made, strict=True)]
            total_ref[rows, :] = result
            low_ref[rows, :] = low
            for kind, (held, target) in enumerate(((total_ref, out_hbm), (low_ref, low_hbm))):
                store = pltpu.make_async_copy(
                    held.at[rows, :], target.at[rows, :], store_semaphores.at[kind, number]
                )
                store.start()
                stores.append(store)
        for number, part in enumerate(sums):
            sums_ref[number : number + 1, :] = part
        for store in stores:
            store.wait()


def project_back(place, grads, slots, group, block, out_type, norm=None):
    row_count, model = grads[0].shape
    source = Source(slots, group, (0, 1))
    width = source.shape[2]
    parts = model // (2 * width)

    def grad_panel(number):
        def index(item, place):
            column = 2 * (item // 2 % parts) + (item % 2 ^ place[0])
            last = 2 * (parts - 1) + (1 ^ place[0])
            done = item // (2 * parts) > number
            return 0, jnp.where(item // (2 * parts) == number, column, jnp.where(done, last, place[0]))

        return pl.BlockSpec((row_count, width), index)

    anywhere = pl.BlockSpec(memory_space=pl.ANY)
    in_specs = [grad_panel(number) for number in range(len(grads))]
    operands = list(grads)
    out_specs = [pl.BlockSpec((row_count, model), lambda *_: (0, 0))]
    out_shape = [jax.ShapeDtypeStruct((row_count, model), out_type)]
    scratch = [pltpu.VMEM((row_count, model), F32)] + source.scratch()
    row = None
    if norm is not None:
        values, stream, vectors, row = norm
        in_specs += [
            anywhere,
            anywhere,
            pl.BlockSpec((VECTOR_ROWS, model), lambda *_: (0, 0)),
        ]
        operands += [values, stream, vectors]
        out_specs = [anywhere, anywhere, pl.BlockSpec((8, model), lambda *_: (0, 0))]
        out_shape += [
            jax.ShapeDtypeStruct((row_count, model), BF16),
            jax.ShapeDtypeStruct((8, model), F32),
        ]
        scratch += [
            pltpu.VMEM(values.shape, values.dtype),
            pltpu.VMEM(stream.shape, stream.dtype),
            pltpu.VMEM((row_count, model), BF16),
            pltpu.SemaphoreType.DMA((2,)),
            pltpu.SemaphoreType.DMA((2, row_count // QUERY_ROWS)),
        ]
    results = pl.pallas_call(
        functools.partial(
            project_back_kernel, source=source, block=block, count=len(grads), row=row
        ),
        grid_spec=pltpu.PrefetchScalarGridSpec(
            num_scalar_prefetch=1,
            grid=(2 * parts * len(grads),),
            in_specs=in_specs + source.specs(),
            out_specs=out_specs,
            scratch_shapes=scratch,
        ),
        out_shape=out_shape,
        compiler_params=pltpu.CompilerParams(vmem_limit_bytes=60 << 20),
        cost_estimate=SMALL,
    )(place, *operands, *source.operands)
    return results[0] if norm is None else results


NEAR = ((0, 1), (1, 0), (2, 3), (3, 2))


def pinned(*values):
    return lax.optimization_barrier(values)


def swap_bit(values, device_count, bit):
    return lax.ppermute(values, AXES, [(item, item ^ bit) for item in range(device_count)])


def move_planes(values, moves, plane_size):
    pairs = [
        (source * plane_size + inner, target * plane_size + inner)
        for source, target in moves
        for inner in range(plane_size)
    ]
    return lax.ppermute(values, AXES, pairs)


def by_member(values, member):
    count = values.shape[0]
    bit = 1
    while bit < count:
        pairs = values.reshape((count // (2 * bit), 2, bit) + values.shape[1:])
        turned = jnp.where((member // bit) % 2 == 1, pairs[:, ::-1], pairs)
        values = turned.reshape(values.shape)
        bit *= 2
    return values


def exchange_members(items, device_count):
    return [items[0]] + [swap_bit(item, device_count, k) for k, item in enumerate(items) if k > 0]


def inner_bits(device_count):
    bits = []
    bit = device_count // GROUPS // 2
    while bit > 1:
        bits.append(bit)
        bit //= 2
    return bits


def spread_begin(own):
    rows = own.shape[-2] // 2
    return [own[..., :rows, :], own[..., rows:, :]]


def spread_swaps(parts, stage, device_count):
    bits = inner_bits(device_count)
    return [
        swap_bit(parts[0], device_count, bits[len(bits) - 1 - stage]),
        swap_bit(parts[1], device_count, bits[stage]),
    ]


def spread_on(parts, got, device_count):
    for stage in range(1, len(inner_bits(device_count))):
        parts = [jnp.stack([part, item]) for part, item in zip(parts, got, strict=True)]
        got = spread_swaps(parts, stage, device_count)
    return parts, got


def swap_cores(items, device_count):
    return [swap_bit(item, device_count, 1) for item in items]


def flat_slot(parts, got):
    shape = (-1,) + parts[0].shape[-2:]
    return tuple(item.reshape(shape) for item in (parts[0], got[0], parts[1], got[1]))


class Sum:
    def __init__(self, kept, got, absolute, swaps=()):
        self.kept = kept
        self.got = got
        self.absolute = absolute
        self.swaps = list(swaps)

    def joined(self, got):
        return Sum(self.kept, self.got, self.absolute, self.swaps + [got])


def stage_kernel(*refs, members, terms, parts):
    ins = refs[1:-parts]
    outs = refs[-parts:]
    per_part = 2 * members + terms
    for part, out_ref in enumerate(outs):
        mine = ins[part * per_part : (part + 1) * per_part]
        for member in range(members):
            total = mine[2 * member][0].astype(F32) + mine[2 * member + 1][0].astype(F32)
            for swap_ref in mine[2 * members :]:
                total = total + swap_ref[member, 0].astype(F32)
            out_ref[member, 0] = total.astype(BF16)


def stage_sends(place, pending, device_count):
    levels = len(inner_bits(device_count))
    stage = len(pending.swaps)
    chunks, rows, width = pending.kept[0].shape
    half = rows // 2
    count = chunks >> (stage + 1)
    members = len(pending.kept)

    def relative(part, step):
        if part == 0:
            return count + step
        return (step << (stage + 1)) + (1 << stage)

    def stored(part):
        def index(step, place):
            chunk = relative(part, step)
            return (chunk ^ place[1] if pending.absolute else chunk), part, 0

        return pl.BlockSpec((1, half, width), index)

    def swapped(part, earlier):
        def index(step, place):
            chunk = relative(part, step)
            return 0, (chunk if part == 0 else chunk >> (earlier + 1)), 0, 0

        return pl.BlockSpec((members, 1, half, width), index)

    in_specs = []
    operands = []
    for part in range(2):
        for kept, got in zip(pending.kept, pending.got, strict=True):
            in_specs += [stored(part)] * 2
            operands += [kept, got]
        for earlier, items in enumerate(pending.swaps):
            in_specs.append(swapped(part, earlier))
            operands.append(items[part])
    assert stage < levels
    return pl.pallas_call(
        functools.partial(stage_kernel, members=members, terms=stage, parts=2),
        grid_spec=pltpu.PrefetchScalarGridSpec(
            num_scalar_prefetch=1,
            grid=(count,),
            in_specs=in_specs,
            out_specs=[pl.BlockSpec((members, 1, half, width), lambda step, place: (0, step, 0, 0))]
            * 2,
        ),
        out_shape=[jax.ShapeDtypeStruct((members, count, half, width), BF16)] * 2,
        compiler_params=pltpu.CompilerParams(vmem_limit_bytes=60 << 20),
        cost_estimate=SMALL,
    )(place, *operands)


def stage_swaps(sends, pending, device_count):
    bits = inner_bits(device_count)
    stage = len(pending.swaps)
    return [
        swap_bit(sends[0], device_count, bits[stage]),
        swap_bit(sends[1], device_count, bits[len(bits) - 1 - stage]),
    ]


def finish_stages(place, pending, device_count):
    while len(pending.swaps) < len(inner_bits(device_count)):
        sends = stage_sends(place, pending, device_count)
        pending = pending.joined(stage_swaps(sends, pending, device_count))
    return pending


def total_kernel(*refs, members, stages):
    place_ref = refs[0]
    stored = refs[1 : 1 + 2 * members]
    swaps = refs[1 + 2 * members : 1 + 2 * members + 2 * stages]
    kept_ref, sent_ref = refs[1 + 2 * members + 2 * stages :]

    def total(part, member):
        result = stored[2 * member][0].astype(F32) + stored[2 * member + 1][0].astype(F32)
        for stage in range(stages):
            result = result + swaps[2 * stage + part][member, 0].astype(F32)
        return result

    for part in range(2):

        @pl.when(pl.program_id(0) // 2 == part)
        def _(part=part):
            if members == 1:
                made = total(part, 0)
                kept_ref[...] = made
                sent_ref[...] = made.astype(BF16)
            else:
                low = total(part, 0)
                high = total(part, 1)
                even = place_ref[2] == 0
                kept_ref[...] = jnp.where(even, low, high)
                sent_ref[...] = jnp.where(even, high, low).astype(BF16)


def plane_totals(place, pending):
    chunks, rows, width = pending.kept[0].shape
    quarter = rows // 4
    members = len(pending.kept)

    def stored(step, place):
        return (place[1] if pending.absolute else 0), step, 0

    in_specs = []
    operands = []
    for kept, got in zip(pending.kept, pending.got, strict=True):
        in_specs += [pl.BlockSpec((1, quarter, width), stored)] * 2
        operands += [kept, got]
    for items in pending.swaps:
        for part in range(2):
            in_specs.append(
                pl.BlockSpec(
                    (members, 1, quarter, width),
                    (lambda step, place: (0, 0, jnp.minimum(step, 1), 0))
                    if part == 0
                    else (lambda step, place: (0, 0, jnp.maximum(step - 2, 0), 0)),
                )
            )
            operands.append(items[part])
    panel = pl.BlockSpec((quarter, width), lambda step, place: (step, 0))
    return pl.pallas_call(
        functools.partial(total_kernel, members=members, stages=len(pending.swaps)),
        grid_spec=pltpu.PrefetchScalarGridSpec(
            num_scalar_prefetch=1,
            grid=(4,),
            in_specs=in_specs,
            out_specs=[panel, panel],
        ),
        out_shape=[
            jax.ShapeDtypeStruct((rows, width), F32),
            jax.ShapeDtypeStruct((rows, width), BF16),
        ],
        compiler_params=pltpu.CompilerParams(vmem_limit_bytes=60 << 20),
        cost_estimate=SMALL,
    )(place, *operands)


def column_half(values, half, width):
    rows, columns = values.shape
    if columns == 2 * width:
        return lax.dynamic_slice_in_dim(values, half * width, width, 1)
    pieces = values.reshape(rows, -1, 2, width)
    return lax.dynamic_index_in_dim(pieces, half, 2, keepdims=False).reshape(rows, -1)


def weight_half(pairs, width):
    terms = []
    for left, right in pairs:
        product = dot_rows(left, right).astype(BF16)
        if product.shape[1] == width:
            terms.append(product[None])
        else:
            terms.append(jnp.swapaxes(product.reshape(product.shape[0], -1, width), 0, 1))
    return jnp.concatenate(terms, axis=0)


def dot_high(left, right, dims):
    return lax.dot_general(
        left, right, (dims, ((), ())), precision=HIGHEST, preferred_element_type=F32
    )


def update_kernel(
    place_ref,
    total_ref,
    near_ref,
    far_ref,
    other_ref,
    weight_ref,
    average_ref,
    moment1_ref,
    moment2_ref,
    stats_ref,
    bases_ref,
    grad_ref,
    first_ref,
    second_ref,
    new_ref,
    new_average_ref,
    copy_ref,
    new_stats_ref,
    new_bases_ref,
    state_ref,
    solved_ref,
    *,
    chunks,
):
    blocks = stats_ref.shape[0]
    step = pl.program_id(0)
    rows = weight_ref.shape[0]

    @pl.when(step == 0)
    def _():
        @pl.when(place_ref[PLACE_PLANE] == 0)
        def _():
            grad_ref[...] = total_ref[...] + near_ref[...].astype(F32) + far_ref[...].astype(F32)

        @pl.when(place_ref[PLACE_PLANE] != 0)
        def _():
            grad_ref[...] = other_ref[...]

        for block in range(blocks):
            grad = grad_ref[:, block * BLK : (block + 1) * BLK]
            square = dot_high(grad, grad, ((0,), (0,)))
            renewed = BETA_TWO * stats_ref[block] + (1.0 - BETA_TWO) * square
            new_stats_ref[block] = renewed
            product = dot_high(renewed, bases_ref[block], ((1,), (0,)))
            gram = dot_high(product, product, ((0,), (0,)))
            state_ref[block] = jnp.concatenate([gram, product.T], axis=1)

    def rotate(chunk):
        for block in range(blocks):
            columns = slice(block * BLK, (block + 1) * BLK)
            basis = bases_ref[block]
            turned = dot_high(
                grad_ref[chunk * rows : (chunk + 1) * rows, columns], basis, ((1,), (0,))
            )
            first = BETA_ONE * moment1_ref[:, columns] + (1.0 - BETA_ONE) * turned
            second = BETA_TWO * moment2_ref[:, columns] + (1.0 - BETA_TWO) * turned * turned
            first_ref[:, columns] = first
            second_ref[:, columns] = second
            direction = (
                first
                / (1.0 - BETA_ONE**STEP)
                / (jnp.sqrt(second / (1.0 - BETA_TWO**STEP)) + ADAM_EPS)
            )
            returned = dot_high(direction, basis, ((1,), (1,)))
            weight = weight_ref[:, columns]
            updated = weight - RATE * (returned + DECAY * weight)
            new_ref[:, columns] = updated
            new_average_ref[:, columns] = (
                AVERAGE * average_ref[:, columns] + (1.0 - AVERAGE) * updated
            )
            copy_ref[:, columns] = updated.astype(BF16)

    row_index = lax.broadcasted_iota(jnp.int32, (PANEL, 2 * BLK), 0)
    panels = BLK // PANEL

    def eliminate(panel):
        top_rows = slice(panel * PANEL, (panel + 1) * PANEL)
        tops = [state_ref[block, top_rows, :] for block in range(blocks)]
        for row in range(PANEL):
            lane = panel * PANEL + row
            for block in range(blocks):
                top = tops[block]
                pivot = top[row : row + 1, lane : lane + 1]
                inverse = lax.rsqrt(pivot)
                inverse = inverse * (1.5 - 0.5 * pivot * inverse * inverse)
                scaled = top[row : row + 1] * inverse
                reduced = top - (top[:, lane : lane + 1] * inverse) * scaled
                tops[block] = jnp.where(
                    row_index == row, scaled, jnp.where(row_index > row, reduced, top)
                )
        for block in range(blocks):
            solved_ref[block, top_rows, :] = tops[block][:, BLK:]
            if panel + 1 < panels:
                rest = slice((panel + 1) * PANEL, BLK)
                state_ref[block, rest, :] -= dot_high(
                    tops[block][:, rest], tops[block], ((0,), (0,))
                )

    for chunk in range(chunks):

        @pl.when(step == chunk)
        def _(chunk=chunk):
            rotate(chunk)
            for panel in range(panels * chunk // chunks, panels * (chunk + 1) // chunks):
                eliminate(panel)
            if chunk == chunks - 1:
                for block in range(blocks):
                    new_bases_ref[block] = solved_ref[block].T


def rotated_update(
    place, total, near, far, other, weights, average, moment1, moment2, stats, bases
):
    rows, width = weights.shape
    chunks = rows // QUERY_ROWS
    whole = pl.BlockSpec(
        (rows, width), lambda step, place: (0, 0), pipeline_mode=pl.Buffered(1)
    )
    big = pl.BlockSpec((QUERY_ROWS, width), lambda step, place: (step, 0))
    small = pl.BlockSpec(stats.shape, lambda step, place: (0, 0, 0))
    wide = jax.ShapeDtypeStruct(weights.shape, F32)
    return pl.pallas_call(
        functools.partial(update_kernel, chunks=chunks),
        grid_spec=pltpu.PrefetchScalarGridSpec(
            num_scalar_prefetch=1,
            grid=(chunks,),
            in_specs=[whole] * 4 + [big] * 4 + [small] * 2,
            out_specs=[pl.BlockSpec((rows, width), lambda step, place: (0, 0))]
            + [big] * 5
            + [small] * 2,
            scratch_shapes=[
                pltpu.VMEM(stats.shape[:2] + (2 * BLK,), F32),
                pltpu.VMEM(stats.shape, F32),
            ],
        ),
        out_shape=[wide] * 5
        + [jax.ShapeDtypeStruct(weights.shape, BF16)]
        + [jax.ShapeDtypeStruct(stats.shape, F32)] * 2,
        compiler_params=pltpu.CompilerParams(vmem_limit_bytes=60 << 20),
        cost_estimate=SMALL,
    )(place, total, near, far, other, weights, average, moment1, moment2, stats, bases)


def adam_update(grad, values, moment1, moment2):
    first_moment = BETA_ONE * moment1 + (1.0 - BETA_ONE) * grad
    second_moment = BETA_TWO * moment2 + (1.0 - BETA_TWO) * grad * grad
    updated = values - VECTOR_RATE * (first_moment / (1.0 - BETA_ONE**STEP)) / (
        jnp.sqrt(second_moment / (1.0 - BETA_TWO**STEP)) + ADAM_EPS
    )
    return (first_moment, second_moment, updated)


def exchange_vectors(pieces, rows, width):
    device_count = pieces.shape[0]
    size = rows * width
    padded = pad_vectors(pieces, 16)
    got = lax.all_to_all(padded, AXES, split_axis=0, concat_axis=0, tiled=True)
    return got.reshape(device_count, -1)[:, :size].reshape(device_count, rows, width)


def pad_vectors(pieces, sublanes):
    device_count, size = pieces.shape
    room = sublanes * LANES
    tiles = -(-size // room)
    padded = jnp.pad(pieces, ((0, 0), (0, tiles * room - size)))
    return padded.reshape(device_count, tiles * sublanes, LANES)


def vector_kernel(one_ref, two_ref, three_ref, self_ref, cross_ref, up_ref, out_ref):
    rows = (
        (one_ref, 0),
        (one_ref, 1),
        (two_ref, 0),
        (two_ref, 1),
        (three_ref, 0),
        (three_ref, 1),
        (self_ref, 0),
        (self_ref, 1),
        (two_ref, 2),
        (cross_ref, 0),
        (cross_ref, 1),
        (three_ref, 2),
        (three_ref, 3),
        (up_ref, 0),
        (up_ref, 1),
        (up_ref, 2),
        (up_ref, 3),
    )
    out_ref[...] = jnp.zeros_like(out_ref)
    for number, (source, row) in enumerate(rows):
        out_ref[number : number + 1, :] = source[row : row + 1, :]


def vector_table(sums_one, sums_two, sums_three, self_sums, cross_sums, up_bias):
    return pl.pallas_call(
        vector_kernel,
        out_shape=jax.ShapeDtypeStruct((VECTOR_ROWS, sums_one.shape[1]), F32),
        compiler_params=pltpu.CompilerParams(vmem_limit_bytes=60 << 20),
        cost_estimate=SMALL,
    )(sums_one, sums_two, sums_three, self_sums, cross_sums, up_bias)


def vector_send(terms, device, bit):
    half = terms.shape[1] // 2
    mine = (device // bit) % 2
    kept = lax.dynamic_slice_in_dim(terms, mine * half, half, 1)
    sent = lax.dynamic_slice_in_dim(terms, (1 - mine) * half, half, 1)
    return kept, sent


def local(
    tokens,
    memory,
    page_lengths,
    slot_masks,
    upstream,
    weights,
    weight_average,
    weight_moment1,
    weight_moment2,
    stats,
    bases,
    vectors,
    vector_average,
    vector_moment1,
    vector_moment2,
):
    row_count, model = tokens.shape
    width = weights.shape[1]
    group_size = lax.axis_size("mem")
    device_count = lax.axis_size("seq") * group_size
    device = lax.axis_index(AXES)
    member = lax.axis_index("mem")
    core = device % 2
    quarter = memory.shape[1]
    scale_q = HEAD ** (-0.5)
    plane_size = device_count // GROUPS
    plane = device // plane_size
    inner = (device % plane_size) // 2
    here = jnp.stack([core, inner, plane % 2, plane]).astype(jnp.int32)
    away = jnp.stack([1 - core, inner, plane % 2, plane]).astype(jnp.int32)

    vector_shape = vectors.shape
    own = weights.astype(BF16)
    first = move_planes(own, ((0, 2), (1, 0), (2, 3), (3, 1)), plane_size)
    pieces = jnp.broadcast_to(
        vectors.astype(BF16).reshape(1, -1), (device_count, vectors.size)
    )
    vector_pieces = exchange_vectors(pieces, *vector_shape)
    memory_padded = jnp.pad(memory, ((0, 0), (0, SLOT_PAD - quarter), (0, 0)))
    memory_parts = exchange_members(
        [
            lax.dynamic_index_in_dim(memory_padded, member ^ item, 0, keepdims=False)
            for item in range(group_size)
        ],
        device_count,
    )
    parts = spread_begin(own)
    got = spread_swaps(parts, 0, device_count)
    first, got, vector_pieces, own, memory_parts = pinned(
        first, got, vector_pieces, own, memory_parts
    )
    held = jnp.where((plane == 0) | (plane == 3), own, first)
    near = move_planes(held, NEAR, plane_size)
    middle = move_planes(own, ((1, 2), (2, 1)), plane_size)
    parts, got = spread_on(parts, got, device_count)
    near, middle, first, got = pinned(near, middle, first, got)
    slot_zero = flat_slot(parts, got)
    even = plane % 2 == 0
    parts_one = spread_begin(jnp.where(even, first, near))
    got_one = spread_swaps(parts_one, 0, device_count)
    last = move_planes(middle, ((1, 0), (2, 3)), plane_size)
    zero_away = swap_cores(slot_zero, device_count)
    got_one, zero_away, memory_parts, near, first, upstream, slot_masks = pinned(
        got_one, zero_away, memory_parts, near, first, upstream, slot_masks
    )
    parts_three = spread_begin(jnp.where(even, near, first))
    memory_here = jnp.concatenate(memory_parts, axis=0)
    live_rows = (jnp.arange(row_count) < page_lengths[0]).astype(F32)[:, None]
    slots_here = lax.dynamic_slice_in_dim(slot_masks, member, 1, 0).reshape(group_size, quarter)
    slots_here = by_member(slots_here, member)
    slots_here = jnp.pad(slots_here, ((0, 0), (0, SLOT_PAD - quarter))).reshape(-1, 1)
    slot_bias = jnp.broadcast_to(
        jnp.where(slots_here > 0, 0.0, MASKED).astype(F32), (group_size * SLOT_PAD, LANES)
    )
    grad_low_three = (upstream.astype(F32) * live_rows).astype(BF16)
    vector_rows = jnp.swapaxes(vector_pieces, 0, 1).reshape(vector_shape[0], model).astype(F32)
    table = jnp.pad(vector_rows, ((0, VECTOR_ROWS - vector_shape[0]), (0, 0)))
    parts_one, got_one = spread_on(parts_one, got_one, device_count)
    one_away = swap_cores(parts_one, device_count)
    bias_up = vector_rows[13:17].reshape(-1, 1, width)
    last, table, bias_up, slot_bias, grad_low_three, memory_here, parts_three = pinned(
        last, table, bias_up, slot_bias, grad_low_three, memory_here, parts_three
    )
    parts_two = spread_begin(jnp.where((plane == 1) | (plane == 2), middle, last))
    got_one, one_away, parts_two, table = pinned(got_one, one_away, parts_two, table)
    got_one_away = swap_cores(got_one, device_count)
    got_two = spread_swaps(parts_two, 0, device_count)
    slots = [
        (slot_zero, tuple(zero_away)),
        (flat_slot(parts_one, got_one), flat_slot(one_away, got_one_away)),
    ]

    pairs = HEADS // 2
    self_firsts = (0, pairs, 2 * pairs)
    cross_firsts = (0, 0, pairs)

    self_low, low_one = project(
        here, tokens, table, slots, 0, 0, ((6, scale_q), (None, 1.0), (7, 1.0)), norm=0
    )
    got_two, self_low = pinned(got_two, self_low)
    parts_two, got_two = spread_on(parts_two, got_two, device_count)
    two_away = swap_cores(parts_two, device_count)
    attended, self_log = attention_forward(self_low, self_low, self_low, self_firsts)
    got_two, two_away, attended = pinned(got_two, two_away, attended)
    got_two_away = swap_cores(got_two, device_count)
    got_three = spread_swaps(parts_three, 0, device_count)
    after_self = project(
        here, attended, table, slots, 0, 3, ((8, 1.0),), residual=tokens, out_type=F32
    )
    got_two_away, after_self = pinned(got_two_away, after_self)
    slots.append((flat_slot(parts_two, got_two), flat_slot(two_away, got_two_away)))
    queries_cross, low_two = project(
        here, after_self, table, slots, 1, 0, ((9, scale_q),), norm=2
    )
    got_three, queries_cross, memory_here = pinned(got_three, queries_cross, memory_here)
    parts_three, got_three = spread_on(parts_three, got_three, device_count)
    three_away = swap_cores(parts_three, device_count)
    cross_low = project(here, memory_here, table, slots, 1, 1, ((None, 1.0), (10, 1.0)))
    merged, cross_log = attention_forward(
        queries_cross, cross_low, cross_low, cross_firsts, slot_bias
    )
    got_three, three_away, merged = pinned(got_three, three_away, merged)
    got_three_away = swap_cores(got_three, device_count)
    after_cross = project(
        here, merged, table, slots, 1, 3, ((11, 1.0),), residual=after_self, out_type=F32
    )
    got_three_away, after_cross, grad_low_three = pinned(
        got_three_away, after_cross, grad_low_three
    )
    slots.append((flat_slot(parts_three, got_three), flat_slot(three_away, got_three_away)))

    out_a, back_a, up_sent, down_sent, bias_sent, low_three = feed_half(
        away, after_cross, grad_low_three, table, bias_up, slots, 1, True
    )
    up_got = swap_bit(up_sent, device_count, 1)
    down_got = swap_bit(down_sent, device_count, 1)
    low_three, up_sent, down_sent = pinned(low_three, up_sent, down_sent)
    out_b, back_b, up_kept, down_kept, bias_kept = feed_half(
        here, low_three, grad_low_three, table, bias_up, slots, 0, False
    )
    up_got, down_got, out_b, back_b, up_kept, down_kept = pinned(
        up_got, down_got, out_b, back_b, up_kept, down_kept
    )
    feed_sum = Sum((up_kept, down_kept), (up_got, down_got), False)
    feed_sends = stage_sends(here, feed_sum, device_count)
    feed_sends, back_b = pinned(feed_sends, back_b)
    feed_swaps = stage_swaps(feed_sends, feed_sum, device_count)

    bias_even = jnp.where(core == 0, bias_kept, bias_sent)
    bias_odd = jnp.where(core == 0, bias_sent, bias_kept)
    grad_bias_up = jnp.concatenate([bias_even, bias_odd], axis=1).reshape(4, model)

    grad_two, grad_low_two, sums_three = norm_back(
        after_cross, table, 4, grad_low_three, (back_a, back_b)
    )
    grad_merged = project_back(here, (grad_low_two,), slots, 1, 3, BF16)
    cross_operands = (
        queries_cross,
        cross_low,
        cross_low,
        cross_firsts,
        grad_merged,
        merged,
        cross_log,
        slot_bias,
    )
    cross_whole, (queries_part, keys_part, values_part) = attention_backward(
        away, width, *cross_operands, None
    )
    cross_whole, (queries_own, keys_own, values_own) = attention_backward(
        here, width, *cross_operands, cross_whole
    )
    grad_queries_cross, grad_keys_cross, grad_values_cross, cross_sums = cross_whole
    feed_swaps, queries_part, queries_own, grad_queries_cross = pinned(
        feed_swaps, queries_part, queries_own, grad_queries_cross
    )
    feed_sum = feed_sum.joined(feed_swaps)
    feed_sends = stage_sends(here, feed_sum, device_count)
    feed_sends, queries_part, queries_own, grad_queries_cross = pinned(
        feed_sends, queries_part, queries_own, grad_queries_cross
    )
    feed_swaps = stage_swaps(feed_sends, feed_sum, device_count)
    cross_sent = weight_half(
        (
            (low_two, queries_part),
            (memory_here, keys_part),
            (memory_here, values_part),
            (merged, column_half(grad_low_two, 1 - core, width)),
        ),
        width,
    )
    cross_sent, queries_own, grad_queries_cross = pinned(
        cross_sent, queries_own, grad_queries_cross
    )
    cross_got = swap_bit(cross_sent, device_count, 1)
    cross_kept = weight_half(
        (
            (low_two, queries_own),
            (memory_here, keys_own),
            (memory_here, values_own),
            (merged, column_half(grad_low_two, core, width)),
        ),
        width,
    )

    grad_one, grad_low_one, sums_two = project_back(
        here, (grad_queries_cross,), slots, 1, 0, F32, (after_self, grad_two, table, 2)
    )
    grad_attended = project_back(here, (grad_low_one,), slots, 0, 3, BF16)
    memory_back = project_back(here, (grad_keys_cross, grad_values_cross), slots, 1, 1, BF16)
    memory_back = memory_back.reshape(group_size, SLOT_PAD, model)
    memory_back = exchange_members([memory_back[item] for item in range(group_size)], device_count)
    feed_swaps, cross_got, cross_kept, grad_attended = pinned(
        feed_swaps, cross_got, cross_kept, grad_attended
    )
    feed_sum = finish_stages(here, feed_sum.joined(feed_swaps), device_count)
    feed_kept, feed_sent = plane_totals(here, feed_sum)
    cross_sum = Sum((cross_kept,), (cross_got,), True)
    cross_sends = stage_sends(here, cross_sum, device_count)
    feed_sent, cross_sends, grad_attended = pinned(feed_sent, cross_sends, grad_attended)
    feed_got = move_planes(feed_sent, NEAR, plane_size)
    cross_swaps = stage_swaps(cross_sends, cross_sum, device_count)
    self_operands = (
        self_low,
        self_low,
        self_low,
        self_firsts,
        grad_attended,
        attended,
        self_log,
        None,
    )
    self_whole, (queries_part, keys_part, values_part) = attention_backward(
        away, width, *self_operands, None
    )
    self_sent = weight_half(
        (
            (low_one, queries_part),
            (low_one, keys_part),
            (low_one, values_part),
            (attended, column_half(grad_low_one, 1 - core, width)),
        ),
        width,
    )
    feed_got, cross_swaps, self_sent, self_whole, memory_back = pinned(
        feed_got, cross_swaps, self_sent, self_whole, memory_back
    )
    self_got = swap_bit(self_sent, device_count, 1)
    feed_kept = feed_kept + feed_got.astype(F32)
    cross_sum = cross_sum.joined(cross_swaps)
    cross_sends = stage_sends(here, cross_sum, device_count)
    feed_sent, cross_sends, self_whole = pinned(
        feed_kept.astype(BF16), cross_sends, self_whole
    )
    feed_middle = model // 2
    feed_upper = move_planes(feed_sent[:feed_middle], ((0, 2), (1, 3)), plane_size)
    cross_swaps = stage_swaps(cross_sends, cross_sum, device_count)
    self_whole, (queries_own, keys_own, values_own) = attention_backward(
        here, width, *self_operands, self_whole
    )
    grad_queries_self, grad_keys_self, grad_values_self, self_sums = self_whole
    self_kept = weight_half(
        (
            (low_one, queries_own),
            (low_one, keys_own),
            (low_one, values_own),
            (attended, column_half(grad_low_one, core, width)),
        ),
        width,
    )
    self_got, cross_swaps, self_kept = pinned(self_got, cross_swaps, self_kept)
    self_sum = Sum((self_kept,), (self_got,), True)
    self_sends = stage_sends(here, self_sum, device_count)
    self_sends, grad_queries_self, cross_swaps = pinned(
        self_sends, grad_queries_self, cross_swaps
    )
    self_swaps = stage_swaps(self_sends, self_sum, device_count)
    cross_sum = finish_stages(here, cross_sum.joined(cross_swaps), device_count)
    input_grad, _, sums_one = project_back(
        here,
        (grad_queries_self, grad_keys_self, grad_values_self),
        slots,
        0,
        0,
        F32,
        (tokens, grad_one, table, 0),
    )
    sums_one, cross_swaps = pinned(sums_one, cross_sum.swaps)
    cross_sum.swaps = list(cross_swaps)
    cross_total, cross_sent = plane_totals(here, cross_sum)
    self_swaps, cross_sent, sums_one, feed_upper, feed_sent = pinned(
        self_swaps, cross_sent, sums_one, feed_upper, feed_sent
    )
    feed_lower = move_planes(feed_sent[feed_middle:], ((0, 2), (1, 3)), plane_size)
    cross_got = move_planes(cross_sent, ((0, 1), (3, 2)), plane_size)
    self_sum = self_sum.joined(self_swaps)
    self_sends = stage_sends(here, self_sum, device_count)
    self_sends, sums_one = pinned(self_sends, sums_one)
    self_swaps = stage_swaps(self_sends, self_sum, device_count)
    vector_terms = vector_table(
        sums_one, sums_two, sums_three, self_sums, cross_sums, grad_bias_up
    )
    vector_bits = [1 << number for number in reversed(range(device_count.bit_length() - 1))]
    vector_kept, vector_sent = vector_send(vector_terms, device, vector_bits[0])
    vector_got = swap_bit(vector_sent, device_count, vector_bits[0])

    def vector_next(kept, got, number):
        kept, sent = vector_send(kept + got, device, vector_bits[number])
        return kept, swap_bit(sent, device_count, vector_bits[number])

    self_swaps, vector_got = pinned(self_swaps, vector_got)
    self_sum = finish_stages(here, self_sum.joined(self_swaps), device_count)
    self_total, self_sent = plane_totals(here, self_sum)
    self_sent, vector_got = pinned(self_sent, vector_got)
    self_got = move_planes(self_sent, ((1, 0), (3, 2)), plane_size)
    vector_kept, vector_got = vector_next(vector_kept, vector_got, 1)
    branch = out_a.astype(F32) + out_b.astype(F32)
    result = (after_cross + branch + vector_rows[12]) * live_rows
    mixed = result.astype(BF16)
    mixed, vector_got = pinned(mixed, vector_got)
    vector_kept, vector_got = vector_next(vector_kept, vector_got, 2)
    cross_total = cross_total + cross_got.astype(F32)
    cross_got = move_planes(cross_total.astype(BF16), ((2, 1),), plane_size)

    self_got, cross_got, feed_lower, vector_got = pinned(
        self_got, cross_got, feed_lower, vector_got
    )
    feed_got = jnp.concatenate([feed_upper, feed_lower], axis=0)
    self_sent = (self_total + self_got.astype(F32)).astype(BF16)
    self_sent, cross_got, feed_got, memory_back, vector_got = pinned(
        self_sent, cross_got, feed_got, memory_back, vector_got
    )
    self_far = move_planes(self_sent, ((2, 0),), plane_size)
    group_other = jnp.where(
        plane < 2,
        cross_total + cross_got.astype(F32),
        feed_kept + feed_got.astype(F32),
    )
    memory_back = jnp.stack([item[:quarter] for item in memory_back])
    memory_back = by_member(memory_back, member).astype(F32)
    vector_kept, vector_got = vector_next(vector_kept, vector_got, 3)
    group_other, vector_got = pinned(group_other, vector_got)
    for number in range(4, len(vector_bits)):
        vector_kept, vector_got = vector_next(vector_kept, vector_got, number)
    group_other, self_far, vector_got = pinned(group_other, self_far, vector_got)
    vector_grad = (vector_kept + vector_got)[: vector_shape[0]]
    (
        weight_grad,
        weight_first,
        weight_second,
        new_weights,
        new_average,
        weights_copy,
        new_stats,
        new_bases,
    ) = rotated_update(
        here,
        self_total,
        self_got,
        self_far,
        group_other,
        weights,
        weight_average,
        weight_moment1,
        weight_moment2,
        stats,
        bases,
    )
    vector_first, vector_second, new_vectors = adam_update(
        vector_grad, vectors, vector_moment1, vector_moment2
    )
    new_vector_average = AVERAGE * vector_average + (1.0 - AVERAGE) * new_vectors
    return (
        mixed,
        input_grad,
        memory_back,
        weight_grad,
        weight_first,
        weight_second,
        new_weights,
        new_average,
        weights_copy,
        new_stats,
        new_bases,
        vector_grad,
        vector_first,
        vector_second,
        new_vectors,
        new_vector_average,
        new_vectors.astype(BF16),
        vector_grad[12],
    )


def solution(mesh):
    return jax.shard_map(
        local,
        mesh=mesh,
        in_specs=(
            P(("seq", "mem"), None),
            P("seq", "mem", None),
            P(("seq", "mem")),
            P("seq", None),
            P(("seq", "mem"), None),
            P(None, ("seq", "mem")),
            P(None, ("seq", "mem")),
            P(None, ("seq", "mem")),
            P(None, ("seq", "mem")),
            P(("seq", "mem"), None, None),
            P(("seq", "mem"), None, None),
            P(None, ("seq", "mem")),
            P(None, ("seq", "mem")),
            P(None, ("seq", "mem")),
            P(None, ("seq", "mem")),
        ),
        out_specs=(
            P(("seq", "mem"), None),
            P(("seq", "mem"), None),
            P("seq", "mem", None),
            P(None, ("seq", "mem")),
            P(None, ("seq", "mem")),
            P(None, ("seq", "mem")),
            P(None, ("seq", "mem")),
            P(None, ("seq", "mem")),
            P(None, ("seq", "mem")),
            P(("seq", "mem"), None, None),
            P(("seq", "mem"), None, None),
            P(None, ("seq", "mem")),
            P(None, ("seq", "mem")),
            P(None, ("seq", "mem")),
            P(None, ("seq", "mem")),
            P(None, ("seq", "mem")),
            P(None, ("seq", "mem")),
            P(("seq", "mem")),
        ),
        check_vma=False,
    )
```

```python
import functools

import jax
import jax.numpy as jnp
from jax import lax
from jax.experimental import pallas as pl
from jax.experimental.pallas import tpu as pltpu
from jax.sharding import PartitionSpec as P

HEADS = 16
HEAD = 64
BLK = 128
STEP = 10
LANES = 128
QUERY_ROWS = 256
FORWARD_ROWS = 512
FEED_ROWS = 1024
SLOT_PAD = 160
PANEL = 32
GROUPS = 4
AXES = ("seq", "mem")
SMALL = pl.CostEstimate(flops=1 << 20, bytes_accessed=1 << 16, transcendentals=0)

F32 = jnp.float32
BF16 = jnp.bfloat16
HIGHEST = lax.Precision.HIGHEST
NORM_EPS = 1e-05
ADAM_EPS = 1e-08
BETA_ONE = 0.9
BETA_TWO = 0.95
RATE = 0.04
VECTOR_RATE = 0.4
DECAY = 0.01
AVERAGE = 0.999
MASKED = -1e30
CONTRACT_ROWS = (((0,), (0,)), ((), ()))
CONTRACT_LAST = (((1,), (1,)), ((), ()))


def dot(left, right):
    return jnp.dot(left, right, preferred_element_type=F32)


def dot_last(left, right):
    return lax.dot_general(left, right, CONTRACT_LAST, preferred_element_type=F32)


def dot_rows(left, right):
    return lax.dot_general(left, right, CONTRACT_ROWS, preferred_element_type=F32)


def normalize(values, scale_gain, offset):
    centre = jnp.mean(values, axis=-1, keepdims=True)
    centred = values - centre
    variance = jnp.mean(centred * centred, axis=-1, keepdims=True)
    return centred * lax.rsqrt(variance + NORM_EPS) * scale_gain + offset


def causal_mask(scores, first_key, first_query):
    key_pos = lax.broadcasted_iota(jnp.int32, scores.shape, 0) + first_key
    query_pos = lax.broadcasted_iota(jnp.int32, scores.shape, 1) + first_query
    return jnp.where(key_pos <= query_pos, scores, MASKED)


def head_of_lane(shape):
    return lax.broadcasted_iota(jnp.int32, shape, 1) // HEAD


def one_head(values, lane_head, head):
    return jnp.where(lane_head == head, values, jnp.zeros_like(values))


def widen(bias, columns):
    return jnp.concatenate([bias] * (columns // LANES), axis=1)


def attention_forward_kernel(*refs, causal):
    if causal:
        q_ref, k_ref, v_ref, out_ref, log_ref = refs
    else:
        q_ref, k_ref, v_ref, bias_ref, out_ref, log_ref = refs
    keys = k_ref[...]
    key_count = keys.shape[0]
    values_turned = v_ref[...].T
    lane_head = head_of_lane(keys.shape)
    key_heads = [one_head(keys, lane_head, head) for head in range(2)]
    units = [
        (block, head) for block in range(q_ref.shape[0] // FORWARD_ROWS) for head in range(2)
    ]

    def scores_of(unit):
        block, head = unit
        seen = (block + 1) * FORWARD_ROWS if causal else key_count
        queries = q_ref[block * FORWARD_ROWS : (block + 1) * FORWARD_ROWS, :]
        scores = dot_last(key_heads[head][:seen], queries)
        if not causal:
            return scores + widen(bias_ref[...], FORWARD_ROWS)
        last = causal_mask(scores[seen - FORWARD_ROWS :], 0, 0)
        if seen == FORWARD_ROWS:
            return last
        return jnp.concatenate([scores[: seen - FORWARD_ROWS], last], axis=0)

    scores = scores_of(units[0])
    outs = []
    for item, (block, head) in enumerate(units):
        later = scores_of(units[item + 1]) if item + 1 < len(units) else None
        rows = slice(block * FORWARD_ROWS, (block + 1) * FORWARD_ROWS)
        largest = jnp.max(scores, axis=0, keepdims=True)
        raised = jnp.exp(scores - largest)
        summed = jnp.sum(raised, axis=0, keepdims=True)
        turned = values_turned[head * HEAD : (head + 1) * HEAD, : scores.shape[0]]
        outs.append(dot(turned, raised.astype(BF16)) / summed)
        log_ref[0, head : head + 1, rows] = largest + jnp.log(summed)
        if head == 1:
            out_ref[rows, :] = jnp.concatenate(outs, axis=0).T.astype(BF16)
            outs = []
        scores = later


def attention_backward_kernel(*refs, causal):
    _, q_ref, k_ref, v_ref, grad_ref, out_ref, log_ref = refs[:7]
    bias_ref = None if causal else refs[7]
    dq_ref, dk_ref, dv_ref, sums_ref, dq_half, dk_half, dv_half, chance_ref, score_ref = refs[-9:]
    query_sum = jnp.zeros((1, LANES), F32)
    value_sums = []
    keys = k_ref[...]
    values = v_ref[...]
    key_count = keys.shape[0]
    row_count = q_ref.shape[0]
    keys_turned = keys.T
    product = (grad_ref[...].astype(F32) * out_ref[...].astype(F32)).T
    inner = [
        jnp.sum(product[head * HEAD : (head + 1) * HEAD], axis=0, keepdims=True)
        for head in range(2)
    ]
    slots_of = chance_ref.shape[0]
    key_rows = chance_ref.shape[1]
    lane_head = head_of_lane((key_rows, LANES))
    blocks = row_count // QUERY_ROWS
    units = [
        (piece, head, block)
        for piece in range(key_count // key_rows)
        for head in range(2)
        for block in range(piece * key_rows // QUERY_ROWS if causal else 0, blocks)
    ]

    def products_of(unit):
        piece, head, block = unit
        slots = slice(piece * key_rows, (piece + 1) * key_rows)
        rows = slice(block * QUERY_ROWS, (block + 1) * QUERY_ROWS)
        return (
            dot_last(one_head(keys[slots], lane_head, head), q_ref[rows, :]),
            dot_last(one_head(values[slots], lane_head, head), grad_ref[rows, :]),
        )

    even_heads = {}

    def finish(piece, head):
        slots = slice(piece * key_rows, (piece + 1) * key_rows)
        first = piece * key_rows if causal else 0
        kept = chance_ref[(2 * piece + head) % slots_of, :, first:]
        grad_value = dot(kept, grad_ref[first:, :])
        grad_key = dot(score_ref[head, slots, first:], q_ref[first:, :])
        if head == 0:
            even_heads[piece] = (grad_key, grad_value)
            return
        even_key, even_value = even_heads.pop(piece)
        grad_key = jnp.where(lane_head == 0, even_key, grad_key).astype(BF16)
        grad_value = jnp.where(lane_head == 0, even_value, grad_value).astype(BF16)
        dk_ref[slots, :] = grad_key
        dk_half[slots, :] = grad_key
        dv_ref[slots, :] = grad_value
        dv_half[slots, :] = grad_value
        value_sums.append(jnp.sum(grad_value.astype(F32), axis=0, keepdims=True))

    current = products_of(units[0])
    ended = None
    for item, (piece, head, block) in enumerate(units):
        later = products_of(units[item + 1]) if item + 1 < len(units) else None
        if ended is not None:
            finish(*ended)
            ended = None
        scores, grad_chance = current
        slots = slice(piece * key_rows, (piece + 1) * key_rows)
        rows = slice(block * QUERY_ROWS, (block + 1) * QUERY_ROWS)
        if not causal:
            scores = scores + widen(bias_ref[slots, :], QUERY_ROWS)
        elif (piece + 1) * key_rows > block * QUERY_ROWS:
            scores = causal_mask(scores, piece * key_rows, block * QUERY_ROWS)
        chance = jnp.exp(scores - log_ref[0, head : head + 1, rows])
        chance_ref[(2 * piece + head) % slots_of, :, rows] = chance.astype(BF16)
        score_ref[head, slots, rows] = (chance * (grad_chance - inner[head][:, rows])).astype(BF16)
        if block == blocks - 1:
            ended = (piece, head)
        current = later
    finish(*ended)
    for block in range(blocks):
        rows = slice(block * QUERY_ROWS, (block + 1) * QUERY_ROWS)
        seen = (block + 1) * QUERY_ROWS if causal else key_count
        parts = [
            dot(
                keys_turned[head * HEAD : (head + 1) * HEAD, :seen],
                score_ref[head, :seen, rows],
            )
            for head in range(2)
        ]
        grad_query = jnp.concatenate(parts, axis=0).T.astype(BF16)
        grad_query = (grad_query.astype(F32) * HEAD ** (-0.5)).astype(BF16)
        dq_ref[rows, :] = grad_query
        dq_half[rows, :] = grad_query
        query_sum = query_sum + jnp.sum(grad_query.astype(F32), axis=0, keepdims=True)
    sums_ref[0:1, :] = query_sum
    sums_ref[1:2, :] = sum(value_sums[1:], value_sums[0])


def head_pair(row_count, first):
    return pl.BlockSpec((row_count, LANES), lambda pair: (0, first + pair))


def attention_forward(queries, keys, values, firsts, bias=None):
    causal = bias is None
    row_count = queries.shape[0]
    key_count = keys.shape[0]
    pairs = HEADS // 2
    in_specs = [
        head_pair(row_count, firsts[0]),
        head_pair(key_count, firsts[1]),
        head_pair(key_count, firsts[2]),
    ]
    operands = [queries, keys, values]
    if not causal:
        in_specs.append(pl.BlockSpec((key_count, LANES), lambda pair: (0, 0)))
        operands.append(bias)
    return pl.pallas_call(
        functools.partial(attention_forward_kernel, causal=causal),
        grid=(pairs,),
        in_specs=in_specs,
        out_specs=[
            head_pair(row_count, 0),
            pl.BlockSpec((1, 8, row_count), lambda pair: (pair, 0, 0)),
        ],
        out_shape=[
            jax.ShapeDtypeStruct((row_count, pairs * LANES), BF16),
            jax.ShapeDtypeStruct((pairs, 8, row_count), F32),
        ],
        compiler_params=pltpu.CompilerParams(vmem_limit_bytes=60 << 20),
        cost_estimate=SMALL,
    )(*operands)


def attention_backward(
    half, width, queries, keys, values, firsts, grads, outs, log_total, bias, whole
):
    causal = bias is None
    row_count, model = grads.shape
    key_count = keys.shape[0]
    key_rows = QUERY_ROWS if causal else key_count // 2
    per_unit = width // LANES
    steps = HEADS // 4

    def chosen(step, side):
        return (2 * (step // per_unit) + side[0]) * per_unit + step % per_unit

    def in_whole(count, first=0):
        return pl.BlockSpec((count, LANES), lambda step, side: (0, first + chosen(step, side)))

    def alone(count):
        return pl.BlockSpec((count, LANES), lambda step, side: (0, step))

    in_specs = [
        in_whole(row_count, firsts[0]),
        in_whole(key_count, firsts[1]),
        in_whole(key_count, firsts[2]),
        in_whole(row_count),
        in_whole(row_count),
        pl.BlockSpec((1, 8, row_count), lambda step, side: (chosen(step, side), 0, 0)),
    ]
    operands = [queries, keys, values, grads, outs, log_total]
    if not causal:
        in_specs.append(pl.BlockSpec((key_count, LANES), lambda step, side: (0, 0)))
        operands.append(bias)
    aliases = {}
    if whole is not None:
        for item, array in enumerate(whole):
            aliases[1 + len(operands)] = item
            in_specs.append(pl.BlockSpec(memory_space=pl.ANY))
            operands.append(array)
    counts = (row_count, key_count, key_count)
    results = pl.pallas_call(
        functools.partial(attention_backward_kernel, causal=causal),
        grid_spec=pltpu.PrefetchScalarGridSpec(
            num_scalar_prefetch=1,
            grid=(steps,),
            in_specs=in_specs,
            out_specs=[in_whole(count) for count in counts]
            + [in_whole(8)]
            + [alone(count) for count in counts],
            scratch_shapes=[
                pltpu.VMEM((4, key_rows, row_count), BF16),
                pltpu.VMEM((2, key_count, row_count), BF16),
            ],
        ),
        out_shape=[jax.ShapeDtypeStruct((count, model), BF16) for count in counts]
        + [jax.ShapeDtypeStruct((8, model), F32)]
        + [jax.ShapeDtypeStruct((count, model // 2), BF16) for count in counts],
        input_output_aliases=aliases,
        compiler_params=pltpu.CompilerParams(vmem_limit_bytes=60 << 20),
        cost_estimate=SMALL,
    )(half, *operands)
    return results[:4], results[4:]


PLACE_PLANE = 3
VECTOR_ROWS = 24


def holders(group, plane):
    if group == 0:
        return ((1, plane != 0), (0, plane == 0))
    if group == 1:
        return ((2, plane > 1), (0, plane == 1), (1, plane == 0))
    if group == 2:
        return ((2, plane < 2), (0, plane == 2), (3, plane == 3))
    return ((3, plane != 3), (0, plane == 3))


class Source:
    def __init__(self, slots, group, sides):
        self.group = group
        self.sides = sides
        self.which = [slot for slot, _ in holders(group, 0)]
        self.operands = [
            array for slot in self.which for side in sides for array in slots[slot][side]
        ]
        self.shape = self.operands[0].shape
        self.dtype = self.operands[0].dtype

    def chunks(self):
        return 2 * self.shape[0]

    def specs(self):
        return [pl.BlockSpec(memory_space=pl.ANY)] * len(self.operands)

    def scratch(self):
        return [
            pltpu.VMEM((2, 2 * self.shape[1], self.shape[2]), self.dtype),
            pltpu.SemaphoreType.DMA((2, 2)),
        ]


def start_fetch(source, refs, buffer, semaphores, plane, side, chunk, turn):
    top, half = source.shape[:2]
    lower_place = 0
    rest = chunk // 2
    size = top
    while size > 1:
        lower_place = lower_place * 2 + rest % 2
        rest = rest // 2
        size //= 2
    item = 0
    for _, chosen in holders(source.group, plane):
        for number in range(len(source.sides)):
            wanted = chosen & (side == number)
            lows, highs, evens, odds = refs[item : item + 4]
            item += 4
            copies = (
                (chunk < top, lows, chunk, 0),
                (chunk >= top, highs, chunk - top, 0),
                (chunk % 2 == 0, evens, lower_place, 1),
                (chunk % 2 == 1, odds, lower_place, 1),
            )

            @pl.when(wanted)
            def _(copies=copies):
                for condition, array, index, part in copies:

                    @pl.when(condition)
                    def _(array=array, index=index, part=part):
                        pltpu.make_async_copy(
                            array.at[index],
                            buffer.at[turn, pl.ds(part * half, half), :],
                            semaphores.at[turn, part],
                        ).start()


def wait_fetch(source, refs, buffer, semaphores, turn):
    half = source.shape[1]
    for part in range(2):
        pltpu.make_async_copy(
            refs[0].at[0],
            buffer.at[turn, pl.ds(part * half, half), :],
            semaphores.at[turn, part],
        ).wait()


def start_fetches(source, refs, buffer, semaphores, plane, order, item, count):
    @pl.when(item == 0)
    def _():
        side, chunk = order(0)
        start_fetch(source, refs, buffer, semaphores, plane, side, chunk, 0)

    @pl.when(item + 1 < count)
    def _():
        side, chunk = order(item + 1)
        start_fetch(source, refs, buffer, semaphores, plane, side, chunk, (item + 1) % 2)


def fetched(source, refs, buffer, semaphores, item):
    wait_fetch(source, refs, buffer, semaphores, item % 2)
    return buffer.at[item % 2]


def vector_part(vectors_ref, row, first, width):
    return vectors_ref[row : row + 1, pl.ds(pl.multiple_of(first, width), width)]


def gelu_parts(values):
    slope = 0.7978845608028654
    square = values * values
    turned = jnp.tanh(slope * values * (1.0 + 0.044715 * square))
    weight = 0.5 * (1.0 + turned)
    derivative = weight + 0.5 * values * (1.0 - turned * turned) * (
        slope + (3.0 * 0.044715 * slope) * square
    )
    return values * weight, derivative


def feed_kernel(*refs, norm, up_source, down_source):
    refs = list(refs)
    place_ref = refs.pop(0)
    values_ref = refs.pop(0)
    grad_ref = refs.pop(0)
    vectors_ref = refs.pop(0)
    bias_ref = refs.pop(0)
    up_refs = refs[: len(up_source.operands)]
    refs = refs[len(up_refs) :]
    down_refs = refs[: len(down_source.operands)]
    refs = refs[len(down_refs) :]
    out_ref, back_ref, grad_up_ref, grad_down_ref, grad_bias_ref = refs[:5]
    low_ref = refs[5] if norm else values_ref
    out_total, back_total, low_turned, grad_turned, active_ref, hidden_ref = refs[-10:-4]
    up_buffer, up_semaphores, down_buffer, down_semaphores = refs[-4:]
    plane = place_ref[PLACE_PLANE]
    step = pl.program_id(0)
    count = up_source.chunks()

    def order(item):
        return 0, item

    start_fetches(up_source, up_refs, up_buffer, up_semaphores, plane, order, step, count)
    start_fetches(
        down_source, down_refs, down_buffer, down_semaphores, plane, order, step, count
    )

    @pl.when(step == 0)
    def _():
        if norm:
            for first in range(0, values_ref.shape[0], QUERY_ROWS):
                rows = slice(first, first + QUERY_ROWS)
                low_ref[rows, :] = normalize(
                    values_ref[rows, :], vectors_ref[4:5, :], vectors_ref[5:6, :]
                ).astype(BF16)
        low_turned[...] = low_ref[...].T
        grad_turned[...] = grad_ref[...].T
        out_total[...] = jnp.zeros_like(out_total)
        back_total[...] = jnp.zeros_like(back_total)

    up = fetched(up_source, up_refs, up_buffer, up_semaphores, step)[...]
    down = fetched(down_source, down_refs, down_buffer, down_semaphores, step)[...]
    total = jnp.zeros((1, up.shape[1]), F32)
    pieces = low_ref.shape[0] // FEED_ROWS
    for piece in range(pieces):
        rows = slice(piece * FEED_ROWS, (piece + 1) * FEED_ROWS)
        active, derivative = gelu_parts(dot(low_ref[rows, :], up) + bias_ref[0])
        active_low = active.astype(BF16)
        hidden_low = (derivative * dot(grad_ref[rows, :], down)).astype(BF16)
        active_ref[rows, :] = active_low
        hidden_ref[rows, :] = hidden_low
        total = total + jnp.sum(hidden_low.astype(F32), axis=0, keepdims=True)
        out_total[rows, :] += dot_last(active_low, down)
        back_total[rows, :] += dot_last(hidden_low, up)
    grad_bias_ref[0] = total
    for piece in range(low_turned.shape[0] // FEED_ROWS):
        rows = slice(piece * FEED_ROWS, (piece + 1) * FEED_ROWS)
        grad_down_ref[0, rows, :] = dot(grad_turned[rows, :], active_ref[...]).astype(BF16)
        grad_up_ref[0, rows, :] = dot(low_turned[rows, :], hidden_ref[...]).astype(BF16)

    @pl.when(step == count - 1)
    def _():
        out_ref[...] = out_total[...].astype(BF16)
        back_ref[...] = back_total[...].astype(BF16)


def feed_half(place, values, grad, vectors, bias, slots, side, norm):
    row_count, model = values.shape
    up_source = Source(slots, 2, (side,))
    down_source = Source(slots, 3, (side,))
    steps = up_source.chunks()
    width = up_source.shape[2]

    def whole(shape):
        return pl.BlockSpec(shape, lambda step, place: (0, 0), pipeline_mode=pl.Buffered(1))

    total = pl.BlockSpec((row_count, model), lambda step, place: (0, 0))
    chunk = pl.BlockSpec((1, model, width), lambda step, place: (step, 0, 0))
    out_specs = [
        total,
        total,
        chunk,
        chunk,
        pl.BlockSpec((1, 1, width), lambda step, place: (step ^ place[1], 0, 0)),
    ]
    out_shape = [
        jax.ShapeDtypeStruct((row_count, model), BF16),
        jax.ShapeDtypeStruct((row_count, model), BF16),
        jax.ShapeDtypeStruct((steps, model, width), BF16),
        jax.ShapeDtypeStruct((steps, model, width), BF16),
        jax.ShapeDtypeStruct((steps, 1, width), F32),
    ]
    if norm:
        out_specs.append(total)
        out_shape.append(jax.ShapeDtypeStruct((row_count, model), BF16))
    return pl.pallas_call(
        functools.partial(
            feed_kernel, norm=norm, up_source=up_source, down_source=down_source
        ),
        grid_spec=pltpu.PrefetchScalarGridSpec(
            num_scalar_prefetch=1,
            grid=(steps,),
            in_specs=[
                whole((row_count, model)),
                whole((row_count, model)),
                whole((VECTOR_ROWS, model)),
                pl.BlockSpec(
                    (1, 1, width), lambda step, place: (2 * (step ^ place[1]) + place[0], 0, 0)
                ),
            ]
            + up_source.specs()
            + down_source.specs(),
            out_specs=out_specs,
            scratch_shapes=[
                pltpu.VMEM((row_count, model), F32),
                pltpu.VMEM((row_count, model), F32),
                pltpu.VMEM((model, row_count), BF16),
                pltpu.VMEM((model, row_count), BF16),
                pltpu.VMEM((row_count, width), BF16),
                pltpu.VMEM((row_count, width), BF16),
            ]
            + up_source.scratch()
            + down_source.scratch(),
        ),
        out_shape=out_shape,
        compiler_params=pltpu.CompilerParams(vmem_limit_bytes=60 << 20),
        cost_estimate=SMALL,
    )(place, values, grad, vectors, bias, *up_source.operands, *down_source.operands)


def norm_back_rows(values, grad, gain, stream):
    values = values.astype(F32)
    centred = values - jnp.mean(values, axis=-1, keepdims=True)
    inverse = lax.rsqrt(jnp.mean(centred * centred, axis=-1, keepdims=True) + NORM_EPS)
    normal = centred * inverse
    scaled = grad * gain
    product = scaled * normal
    back = inverse * (
        scaled
        - jnp.mean(scaled, axis=-1, keepdims=True)
        - normal * jnp.mean(product, axis=-1, keepdims=True)
    )
    return stream.astype(F32) + back, normal


def row_sums(grad, normal, low, stream):
    parts = (grad * normal, grad, low.astype(F32), stream.astype(F32))
    return [jnp.sum(part, axis=0, keepdims=True) for part in parts]


def norm_back_kernel(*refs, count, row):
    values_ref, vectors_ref, stream_ref = refs[:3]
    grad_refs = refs[3 : 3 + count]
    out_ref, low_ref, sums_ref = refs[3 + count :]
    grad = grad_refs[0][...].astype(F32)
    for grad_ref in grad_refs[1:]:
        grad = grad + grad_ref[...].astype(F32)
    result, normal = norm_back_rows(
        values_ref[...], grad, vectors_ref[row : row + 1, :], stream_ref[...]
    )
    low = result.astype(BF16)
    out_ref[...] = result
    low_ref[...] = low

    @pl.when(pl.program_id(0) == 0)
    def _():
        sums_ref[...] = jnp.zeros_like(sums_ref)

    for number, part in enumerate(row_sums(grad, normal, low, stream_ref[...])):
        sums_ref[number : number + 1, :] += part


def norm_back(values, vectors, row, stream, grads):
    row_count, model = values.shape
    panel = pl.BlockSpec((QUERY_ROWS // 2, model), lambda step: (step, 0))
    return pl.pallas_call(
        functools.partial(norm_back_kernel, count=len(grads), row=row),
        grid=(2 * row_count // QUERY_ROWS,),
        in_specs=[panel, pl.BlockSpec((VECTOR_ROWS, model), lambda step: (0, 0)), panel]
        + [panel] * len(grads),
        out_specs=[panel, panel, pl.BlockSpec((8, model), lambda step: (0, 0))],
        out_shape=[
            jax.ShapeDtypeStruct((row_count, model), F32),
            jax.ShapeDtypeStruct((row_count, model), BF16),
            jax.ShapeDtypeStruct((8, model), F32),
        ],
        compiler_params=pltpu.CompilerParams(vmem_limit_bytes=60 << 20),
        cost_estimate=SMALL,
    )(values, vectors, stream, *grads)


def project_kernel(*refs, source, block, lines, norm, residual):
    refs = list(refs)
    place_ref = refs.pop(0)
    values_ref = refs.pop(0)
    vectors_ref = refs.pop(0)
    residual_ref = refs.pop(0) if residual else None
    source_refs = refs[: len(source.operands)]
    refs = refs[len(source_refs) :]
    out_ref = refs.pop(0)
    low_ref = refs.pop(0) if norm is not None else None
    buffer, semaphores, held_ref, load_semaphore = refs
    load = pltpu.make_async_copy(values_ref, held_ref, load_semaphore)
    values_ref = held_ref
    low_ref = held_ref if low_ref is None else low_ref
    model = values_ref.shape[1]
    width = out_ref.shape[1]
    parts = model // (2 * width)
    item = pl.program_id(0)
    count = 2 * parts * len(lines)

    def order(item):
        return item % 2, (block * parts + item // 2) ^ place_ref[1]

    @pl.when(item == 0)
    def _():
        load.start()

    start_fetches(
        source, source_refs, buffer, semaphores, place_ref[PLACE_PLANE], order, item, count
    )

    @pl.when(item == 0)
    def _():
        load.wait()
        if norm is not None:
            for first in range(0, values_ref.shape[0], QUERY_ROWS):
                rows = slice(first, first + QUERY_ROWS)
                low_ref[rows, :] = normalize(
                    values_ref[rows, :].astype(F32),
                    vectors_ref[norm : norm + 1, :],
                    vectors_ref[norm + 1 : norm + 2, :],
                ).astype(BF16)

    columns_ref = fetched(source, source_refs, buffer, semaphores, item)
    inside = item // 2 % parts
    column = (2 * inside + (item % 2 ^ place_ref[0])) * width
    row_count = values_ref.shape[0]
    step = row_count // 2
    for number, (line, scale) in enumerate(lines):

        @pl.when(item // (2 * parts) == number)
        def _(line=line, scale=scale):
            columns = columns_ref[...]
            for first in range(0, row_count, step):
                rows = slice(first, first + step)
                made = dot(low_ref[rows, :], columns)
                if line is not None:
                    made = made + vector_part(vectors_ref, line, column, width)
                if scale != 1.0:
                    made = made * scale
                if residual:
                    made = residual_ref[rows, :].astype(F32) + made
                out_ref[rows, :] = made.astype(out_ref.dtype)


def project(
    place, values, vectors, slots, group, block, lines, norm=None, residual=None, out_type=BF16
):
    row_count, model = values.shape
    source = Source(slots, group, (0, 1))
    width = source.shape[2]
    parts = model // (2 * width)

    def whole(shape):
        return pl.BlockSpec(shape, lambda *_: (0, 0), pipeline_mode=pl.Buffered(1))

    panel = pl.BlockSpec(
        (row_count, width),
        lambda item, place: (0, 2 * (item // 2) + (item % 2 ^ place[0])),
    )
    in_specs = [pl.BlockSpec(memory_space=pl.ANY), whole((VECTOR_ROWS, model))]
    operands = [values, vectors]
    if residual is not None:
        in_specs.append(panel)
        operands.append(residual)
    out_specs = [panel]
    out_shape = [jax.ShapeDtypeStruct((row_count, len(lines) * model), out_type)]
    if norm is not None:
        out_specs.append(pl.BlockSpec((row_count, model), lambda *_: (0, 0)))
        out_shape.append(jax.ShapeDtypeStruct((row_count, model), BF16))
    results = pl.pallas_call(
        functools.partial(
            project_kernel,
            source=source,
            block=block,
            lines=lines,
            norm=norm,
            residual=residual is not None,
        ),
        grid_spec=pltpu.PrefetchScalarGridSpec(
            num_scalar_prefetch=1,
            grid=(2 * parts * len(lines),),
            in_specs=in_specs + source.specs(),
            out_specs=out_specs,
            scratch_shapes=source.scratch()
            + [pltpu.VMEM(values.shape, values.dtype), pltpu.SemaphoreType.DMA],
        ),
        out_shape=out_shape,
        compiler_params=pltpu.CompilerParams(vmem_limit_bytes=60 << 20),
        cost_estimate=SMALL,
    )(place, *operands, *source.operands)
    return results if norm is not None else results[0]


def project_back_kernel(*refs, source, block, count, row):
    refs = list(refs)
    place_ref = refs.pop(0)
    grad_refs = refs[:count]
    refs = refs[count:]
    if row is not None:
        values_hbm, stream_hbm, vectors_ref = refs[:3]
        refs = refs[3:]
    source_refs = refs[: len(source.operands)]
    refs = refs[len(source.operands) :]
    if row is None:
        out_ref, total_ref, buffer, semaphores = refs
    else:
        out_hbm, low_hbm, sums_ref, total_ref, buffer, semaphores = refs[:6]
        values_ref, stream_ref, low_ref, load_semaphores, store_semaphores = refs[6:]
    row_count, model = total_ref.shape
    width = grad_refs[0].shape[1]
    parts = model // (2 * width)
    item = pl.program_id(0)
    steps = 2 * parts * count

    def order(item):
        return item % 2, (block * parts + item // 2) ^ place_ref[1]

    start_fetches(
        source, source_refs, buffer, semaphores, place_ref[PLACE_PLANE], order, item, steps
    )
    if row is not None:
        loads = [
            pltpu.make_async_copy(values_hbm, values_ref, load_semaphores.at[0]),
            pltpu.make_async_copy(stream_hbm, stream_ref, load_semaphores.at[1]),
        ]

    @pl.when(item == 0)
    def _():
        if row is not None:
            for load in loads:
                load.start()
        total_ref[...] = jnp.zeros_like(total_ref)

    columns_ref = fetched(source, source_refs, buffer, semaphores, item)
    for number, grad_ref in enumerate(grad_refs):

        @pl.when(item // (2 * parts) == number)
        def _(grad_ref=grad_ref):
            columns = columns_ref[...]
            size = row_count // 2
            for first in range(0, row_count, size):
                rows = slice(first, first + size)
                total_ref[rows, :] += dot_last(grad_ref[rows, :], columns)

    @pl.when(item == steps - 1)
    def _():
        if row is None:
            out_ref[...] = total_ref[...].astype(out_ref.dtype)
            return
        for load in loads:
            load.wait()
        stores = []
        sums = None
        for number in range(row_count // QUERY_ROWS):
            rows = slice(number * QUERY_ROWS, (number + 1) * QUERY_ROWS)
            grad = total_ref[rows, :]
            stream = stream_ref[rows, :]
            result, normal = norm_back_rows(
                values_ref[rows, :], grad, vectors_ref[row : row + 1, :], stream
            )
            low = result.astype(BF16)
            made = row_sums(grad, normal, low, stream)
            sums = made if sums is None else [a + b for a, b in zip(sums, made, strict=True)]
            total_ref[rows, :] = result
            low_ref[rows, :] = low
            for kind, (held, target) in enumerate(((total_ref, out_hbm), (low_ref, low_hbm))):
                store = pltpu.make_async_copy(
                    held.at[rows, :], target.at[rows, :], store_semaphores.at[kind, number]
                )
                store.start()
                stores.append(store)
        for number, part in enumerate(sums):
            sums_ref[number : number + 1, :] = part
        for store in stores:
            store.wait()


def project_back(place, grads, slots, group, block, out_type, norm=None):
    row_count, model = grads[0].shape
    source = Source(slots, group, (0, 1))
    width = source.shape[2]
    parts = model // (2 * width)

    def grad_panel(number):
        def index(item, place):
            column = 2 * (item // 2 % parts) + (item % 2 ^ place[0])
            last = 2 * (parts - 1) + (1 ^ place[0])
            done = item // (2 * parts) > number
            return 0, jnp.where(item // (2 * parts) == number, column, jnp.where(done, last, place[0]))

        return pl.BlockSpec((row_count, width), index)

    anywhere = pl.BlockSpec(memory_space=pl.ANY)
    in_specs = [grad_panel(number) for number in range(len(grads))]
    operands = list(grads)
    out_specs = [pl.BlockSpec((row_count, model), lambda *_: (0, 0))]
    out_shape = [jax.ShapeDtypeStruct((row_count, model), out_type)]
    scratch = [pltpu.VMEM((row_count, model), F32)] + source.scratch()
    row = None
    if norm is not None:
        values, stream, vectors, row = norm
        in_specs += [
            anywhere,
            anywhere,
            pl.BlockSpec((VECTOR_ROWS, model), lambda *_: (0, 0)),
        ]
        operands += [values, stream, vectors]
        out_specs = [anywhere, anywhere, pl.BlockSpec((8, model), lambda *_: (0, 0))]
        out_shape += [
            jax.ShapeDtypeStruct((row_count, model), BF16),
            jax.ShapeDtypeStruct((8, model), F32),
        ]
        scratch += [
            pltpu.VMEM(values.shape, values.dtype),
            pltpu.VMEM(stream.shape, stream.dtype),
            pltpu.VMEM((row_count, model), BF16),
            pltpu.SemaphoreType.DMA((2,)),
            pltpu.SemaphoreType.DMA((2, row_count // QUERY_ROWS)),
        ]
    results = pl.pallas_call(
        functools.partial(
            project_back_kernel, source=source, block=block, count=len(grads), row=row
        ),
        grid_spec=pltpu.PrefetchScalarGridSpec(
            num_scalar_prefetch=1,
            grid=(2 * parts * len(grads),),
            in_specs=in_specs + source.specs(),
            out_specs=out_specs,
            scratch_shapes=scratch,
        ),
        out_shape=out_shape,
        compiler_params=pltpu.CompilerParams(vmem_limit_bytes=60 << 20),
        cost_estimate=SMALL,
    )(place, *operands, *source.operands)
    return results[0] if norm is None else results


NEAR = ((0, 1), (1, 0), (2, 3), (3, 2))


def pinned(*values):
    return lax.optimization_barrier(values)


def swap_bit(values, device_count, bit):
    return lax.ppermute(values, AXES, [(item, item ^ bit) for item in range(device_count)])


def move_planes(values, moves, plane_size):
    pairs = [
        (source * plane_size + inner, target * plane_size + inner)
        for source, target in moves
        for inner in range(plane_size)
    ]
    return lax.ppermute(values, AXES, pairs)


def by_member(values, member):
    count = values.shape[0]
    bit = 1
    while bit < count:
        pairs = values.reshape((count // (2 * bit), 2, bit) + values.shape[1:])
        turned = jnp.where((member // bit) % 2 == 1, pairs[:, ::-1], pairs)
        values = turned.reshape(values.shape)
        bit *= 2
    return values


def exchange_members(items, device_count):
    return [items[0]] + [swap_bit(item, device_count, k) for k, item in enumerate(items) if k > 0]


def inner_bits(device_count):
    bits = []
    bit = device_count // GROUPS // 2
    while bit > 1:
        bits.append(bit)
        bit //= 2
    return bits


def spread_begin(own):
    rows = own.shape[-2] // 2
    return [own[..., :rows, :], own[..., rows:, :]]


def spread_swaps(parts, stage, device_count):
    bits = inner_bits(device_count)
    return [
        swap_bit(parts[0], device_count, bits[len(bits) - 1 - stage]),
        swap_bit(parts[1], device_count, bits[stage]),
    ]


def spread_on(parts, got, device_count):
    for stage in range(1, len(inner_bits(device_count))):
        parts = [jnp.stack([part, item]) for part, item in zip(parts, got, strict=True)]
        got = spread_swaps(parts, stage, device_count)
    return parts, got


def swap_cores(items, device_count):
    return [swap_bit(item, device_count, 1) for item in items]


def flat_slot(parts, got):
    shape = (-1,) + parts[0].shape[-2:]
    return tuple(item.reshape(shape) for item in (parts[0], got[0], parts[1], got[1]))


class Sum:
    def __init__(self, kept, got, absolute, swaps=()):
        self.kept = kept
        self.got = got
        self.absolute = absolute
        self.swaps = list(swaps)

    def joined(self, got):
        return Sum(self.kept, self.got, self.absolute, self.swaps + [got])


def stage_kernel(*refs, members, terms, parts):
    ins = refs[1:-parts]
    outs = refs[-parts:]
    per_part = 2 * members + terms
    for part, out_ref in enumerate(outs):
        mine = ins[part * per_part : (part + 1) * per_part]
        for member in range(members):
            total = mine[2 * member][0].astype(F32) + mine[2 * member + 1][0].astype(F32)
            for swap_ref in mine[2 * members :]:
                total = total + swap_ref[member, 0].astype(F32)
            out_ref[member, 0] = total.astype(BF16)


def stage_sends(place, pending, device_count):
    levels = len(inner_bits(device_count))
    stage = len(pending.swaps)
    chunks, rows, width = pending.kept[0].shape
    half = rows // 2
    count = chunks >> (stage + 1)
    members = len(pending.kept)

    def relative(part, step):
        if part == 0:
            return count + step
        return (step << (stage + 1)) + (1 << stage)

    def stored(part):
        def index(step, place):
            chunk = relative(part, step)
            return (chunk ^ place[1] if pending.absolute else chunk), part, 0

        return pl.BlockSpec((1, half, width), index)

    def swapped(part, earlier):
        def index(step, place):
            chunk = relative(part, step)
            return 0, (chunk if part == 0 else chunk >> (earlier + 1)), 0, 0

        return pl.BlockSpec((members, 1, half, width), index)

    in_specs = []
    operands = []
    for part in range(2):
        for kept, got in zip(pending.kept, pending.got, strict=True):
            in_specs += [stored(part)] * 2
            operands += [kept, got]
        for earlier, items in enumerate(pending.swaps):
            in_specs.append(swapped(part, earlier))
            operands.append(items[part])
    assert stage < levels
    return pl.pallas_call(
        functools.partial(stage_kernel, members=members, terms=stage, parts=2),
        grid_spec=pltpu.PrefetchScalarGridSpec(
            num_scalar_prefetch=1,
            grid=(count,),
            in_specs=in_specs,
            out_specs=[pl.BlockSpec((members, 1, half, width), lambda step, place: (0, step, 0, 0))]
            * 2,
        ),
        out_shape=[jax.ShapeDtypeStruct((members, count, half, width), BF16)] * 2,
        compiler_params=pltpu.CompilerParams(vmem_limit_bytes=60 << 20),
        cost_estimate=SMALL,
    )(place, *operands)


def stage_swaps(sends, pending, device_count):
    bits = inner_bits(device_count)
    stage = len(pending.swaps)
    return [
        swap_bit(sends[0], device_count, bits[stage]),
        swap_bit(sends[1], device_count, bits[len(bits) - 1 - stage]),
    ]


def finish_stages(place, pending, device_count):
    while len(pending.swaps) < len(inner_bits(device_count)):
        sends = stage_sends(place, pending, device_count)
        pending = pending.joined(stage_swaps(sends, pending, device_count))
    return pending


def total_kernel(*refs, members, stages):
    place_ref = refs[0]
    stored = refs[1 : 1 + 2 * members]
    swaps = refs[1 + 2 * members : 1 + 2 * members + 2 * stages]
    kept_ref, sent_ref = refs[1 + 2 * members + 2 * stages :]

    def total(part, member):
        result = stored[2 * member][0].astype(F32) + stored[2 * member + 1][0].astype(F32)
        for stage in range(stages):
            result = result + swaps[2 * stage + part][member, 0].astype(F32)
        return result

    for part in range(2):

        @pl.when(pl.program_id(0) // 2 == part)
        def _(part=part):
            if members == 1:
                made = total(part, 0)
                kept_ref[...] = made
                sent_ref[...] = made.astype(BF16)
            else:
                low = total(part, 0)
                high = total(part, 1)
                even = place_ref[2] == 0
                kept_ref[...] = jnp.where(even, low, high)
                sent_ref[...] = jnp.where(even, high, low).astype(BF16)


def plane_totals(place, pending):
    chunks, rows, width = pending.kept[0].shape
    quarter = rows // 4
    members = len(pending.kept)

    def stored(step, place):
        return (place[1] if pending.absolute else 0), step, 0

    in_specs = []
    operands = []
    for kept, got in zip(pending.kept, pending.got, strict=True):
        in_specs += [pl.BlockSpec((1, quarter, width), stored)] * 2
        operands += [kept, got]
    for items in pending.swaps:
        for part in range(2):
            in_specs.append(
                pl.BlockSpec(
                    (members, 1, quarter, width),
                    (lambda step, place: (0, 0, jnp.minimum(step, 1), 0))
                    if part == 0
                    else (lambda step, place: (0, 0, jnp.maximum(step - 2, 0), 0)),
                )
            )
            operands.append(items[part])
    panel = pl.BlockSpec((quarter, width), lambda step, place: (step, 0))
    return pl.pallas_call(
        functools.partial(total_kernel, members=members, stages=len(pending.swaps)),
        grid_spec=pltpu.PrefetchScalarGridSpec(
            num_scalar_prefetch=1,
            grid=(4,),
            in_specs=in_specs,
            out_specs=[panel, panel],
        ),
        out_shape=[
            jax.ShapeDtypeStruct((rows, width), F32),
            jax.ShapeDtypeStruct((rows, width), BF16),
        ],
        compiler_params=pltpu.CompilerParams(vmem_limit_bytes=60 << 20),
        cost_estimate=SMALL,
    )(place, *operands)


def column_half(values, half, width):
    rows, columns = values.shape
    if columns == 2 * width:
        return lax.dynamic_slice_in_dim(values, half * width, width, 1)
    pieces = values.reshape(rows, -1, 2, width)
    return lax.dynamic_index_in_dim(pieces, half, 2, keepdims=False).reshape(rows, -1)


def weight_half(pairs, width):
    terms = []
    for left, right in pairs:
        product = dot_rows(left, right).astype(BF16)
        if product.shape[1] == width:
            terms.append(product[None])
        else:
            terms.append(jnp.swapaxes(product.reshape(product.shape[0], -1, width), 0, 1))
    return jnp.concatenate(terms, axis=0)


def dot_high(left, right, dims):
    return lax.dot_general(
        left, right, (dims, ((), ())), precision=HIGHEST, preferred_element_type=F32
    )


def update_kernel(
    place_ref,
    total_ref,
    near_ref,
    far_ref,
    other_ref,
    weight_ref,
    average_ref,
    moment1_ref,
    moment2_ref,
    stats_ref,
    bases_ref,
    grad_ref,
    first_ref,
    second_ref,
    new_ref,
    new_average_ref,
    copy_ref,
    new_stats_ref,
    new_bases_ref,
    state_ref,
    solved_ref,
    *,
    chunks,
):
    blocks = stats_ref.shape[0]
    step = pl.program_id(0)
    rows = weight_ref.shape[0]

    @pl.when(step == 0)
    def _():
        @pl.when(place_ref[PLACE_PLANE] == 0)
        def _():
            grad_ref[...] = total_ref[...] + near_ref[...].astype(F32) + far_ref[...].astype(F32)

        @pl.when(place_ref[PLACE_PLANE] != 0)
        def _():
            grad_ref[...] = other_ref[...]

        for block in range(blocks):
            grad = grad_ref[:, block * BLK : (block + 1) * BLK]
            square = dot_high(grad, grad, ((0,), (0,)))
            renewed = BETA_TWO * stats_ref[block] + (1.0 - BETA_TWO) * square
            new_stats_ref[block] = renewed
            product = dot_high(renewed, bases_ref[block], ((1,), (0,)))
            gram = dot_high(product, product, ((0,), (0,)))
            state_ref[block] = jnp.concatenate([gram, product.T], axis=1)

    def rotate(chunk):
        for block in range(blocks):
            columns = slice(block * BLK, (block + 1) * BLK)
            basis = bases_ref[block]
            turned = dot_high(
                grad_ref[chunk * rows : (chunk + 1) * rows, columns], basis, ((1,), (0,))
            )
            first = BETA_ONE * moment1_ref[:, columns] + (1.0 - BETA_ONE) * turned
            second = BETA_TWO * moment2_ref[:, columns] + (1.0 - BETA_TWO) * turned * turned
            first_ref[:, columns] = first
            second_ref[:, columns] = second
            direction = (
                first
                / (1.0 - BETA_ONE**STEP)
                / (jnp.sqrt(second / (1.0 - BETA_TWO**STEP)) + ADAM_EPS)
            )
            returned = dot_high(direction, basis, ((1,), (1,)))
            weight = weight_ref[:, columns]
            updated = weight - RATE * (returned + DECAY * weight)
            new_ref[:, columns] = updated
            new_average_ref[:, columns] = (
                AVERAGE * average_ref[:, columns] + (1.0 - AVERAGE) * updated
            )
            copy_ref[:, columns] = updated.astype(BF16)

    row_index = lax.broadcasted_iota(jnp.int32, (PANEL, 2 * BLK), 0)
    panels = BLK // PANEL

    def eliminate(panel):
        top_rows = slice(panel * PANEL, (panel + 1) * PANEL)
        tops = [state_ref[block, top_rows, :] for block in range(blocks)]
        for row in range(PANEL):
            lane = panel * PANEL + row
            for block in range(blocks):
                top = tops[block]
                pivot = top[row : row + 1, lane : lane + 1]
                inverse = lax.rsqrt(pivot)
                inverse = inverse * (1.5 - 0.5 * pivot * inverse * inverse)
                scaled = top[row : row + 1] * inverse
                reduced = top - (top[:, lane : lane + 1] * inverse) * scaled
                tops[block] = jnp.where(
                    row_index == row, scaled, jnp.where(row_index > row, reduced, top)
                )
        for block in range(blocks):
            solved_ref[block, top_rows, :] = tops[block][:, BLK:]
            if panel + 1 < panels:
                rest = slice((panel + 1) * PANEL, BLK)
                state_ref[block, rest, :] -= dot_high(
                    tops[block][:, rest], tops[block], ((0,), (0,))
                )

    for chunk in range(chunks):

        @pl.when(step == chunk)
        def _(chunk=chunk):
            rotate(chunk)
            for panel in range(panels * chunk // chunks, panels * (chunk + 1) // chunks):
                eliminate(panel)
            if chunk == chunks - 1:
                for block in range(blocks):
                    new_bases_ref[block] = solved_ref[block].T


def rotated_update(
    place, total, near, far, other, weights, average, moment1, moment2, stats, bases
):
    rows, width = weights.shape
    chunks = rows // QUERY_ROWS
    whole = pl.BlockSpec(
        (rows, width), lambda step, place: (0, 0), pipeline_mode=pl.Buffered(1)
    )
    big = pl.BlockSpec((QUERY_ROWS, width), lambda step, place: (step, 0))
    small = pl.BlockSpec(stats.shape, lambda step, place: (0, 0, 0))
    wide = jax.ShapeDtypeStruct(weights.shape, F32)
    return pl.pallas_call(
        functools.partial(update_kernel, chunks=chunks),
        grid_spec=pltpu.PrefetchScalarGridSpec(
            num_scalar_prefetch=1,
            grid=(chunks,),
            in_specs=[whole] * 4 + [big] * 4 + [small] * 2,
            out_specs=[pl.BlockSpec((rows, width), lambda step, place: (0, 0))]
            + [big] * 5
            + [small] * 2,
            scratch_shapes=[
                pltpu.VMEM(stats.shape[:2] + (2 * BLK,), F32),
                pltpu.VMEM(stats.shape, F32),
            ],
        ),
        out_shape=[wide] * 5
        + [jax.ShapeDtypeStruct(weights.shape, BF16)]
        + [jax.ShapeDtypeStruct(stats.shape, F32)] * 2,
        compiler_params=pltpu.CompilerParams(vmem_limit_bytes=60 << 20),
        cost_estimate=SMALL,
    )(place, total, near, far, other, weights, average, moment1, moment2, stats, bases)


def adam_update(grad, values, moment1, moment2):
    first_moment = BETA_ONE * moment1 + (1.0 - BETA_ONE) * grad
    second_moment = BETA_TWO * moment2 + (1.0 - BETA_TWO) * grad * grad
    updated = values - VECTOR_RATE * (first_moment / (1.0 - BETA_ONE**STEP)) / (
        jnp.sqrt(second_moment / (1.0 - BETA_TWO**STEP)) + ADAM_EPS
    )
    return (first_moment, second_moment, updated)


def exchange_vectors(pieces, rows, width):
    device_count = pieces.shape[0]
    size = rows * width
    padded = pad_vectors(pieces, 16)
    got = lax.all_to_all(padded, AXES, split_axis=0, concat_axis=0, tiled=True)
    return got.reshape(device_count, -1)[:, :size].reshape(device_count, rows, width)


def pad_vectors(pieces, sublanes):
    device_count, size = pieces.shape
    room = sublanes * LANES
    tiles = -(-size // room)
    padded = jnp.pad(pieces, ((0, 0), (0, tiles * room - size)))
    return padded.reshape(device_count, tiles * sublanes, LANES)


def vector_kernel(one_ref, two_ref, three_ref, self_ref, cross_ref, up_ref, out_ref):
    rows = (
        (one_ref, 0),
        (one_ref, 1),
        (two_ref, 0),
        (two_ref, 1),
        (three_ref, 0),
        (three_ref, 1),
        (self_ref, 0),
        (self_ref, 1),
        (two_ref, 2),
        (cross_ref, 0),
        (cross_ref, 1),
        (three_ref, 2),
        (three_ref, 3),
        (up_ref, 0),
        (up_ref, 1),
        (up_ref, 2),
        (up_ref, 3),
    )
    out_ref[...] = jnp.zeros_like(out_ref)
    for number, (source, row) in enumerate(rows):
        out_ref[number : number + 1, :] = source[row : row + 1, :]


def vector_table(sums_one, sums_two, sums_three, self_sums, cross_sums, up_bias):
    return pl.pallas_call(
        vector_kernel,
        out_shape=jax.ShapeDtypeStruct((VECTOR_ROWS, sums_one.shape[1]), F32),
        compiler_params=pltpu.CompilerParams(vmem_limit_bytes=60 << 20),
        cost_estimate=SMALL,
    )(sums_one, sums_two, sums_three, self_sums, cross_sums, up_bias)


def vector_send(terms, device, bit):
    half = terms.shape[1] // 2
    mine = (device // bit) % 2
    kept = lax.dynamic_slice_in_dim(terms, mine * half, half, 1)
    sent = lax.dynamic_slice_in_dim(terms, (1 - mine) * half, half, 1)
    return kept, sent


def local(
    tokens,
    memory,
    page_lengths,
    slot_masks,
    upstream,
    weights,
    weight_average,
    weight_moment1,
    weight_moment2,
    stats,
    bases,
    vectors,
    vector_average,
    vector_moment1,
    vector_moment2,
):
    row_count, model = tokens.shape
    width = weights.shape[1]
    group_size = lax.axis_size("mem")
    device_count = lax.axis_size("seq") * group_size
    device = lax.axis_index(AXES)
    member = lax.axis_index("mem")
    core = device % 2
    quarter = memory.shape[1]
    scale_q = HEAD ** (-0.5)
    plane_size = device_count // GROUPS
    plane = device // plane_size
    inner = (device % plane_size) // 2
    here = jnp.stack([core, inner, plane % 2, plane]).astype(jnp.int32)
    away = jnp.stack([1 - core, inner, plane % 2, plane]).astype(jnp.int32)

    vector_shape = vectors.shape
    own = weights.astype(BF16)
    first = move_planes(own, ((0, 2), (1, 0), (2, 3), (3, 1)), plane_size)
    pieces = jnp.broadcast_to(
        vectors.astype(BF16).reshape(1, -1), (device_count, vectors.size)
    )
    vector_pieces = exchange_vectors(pieces, *vector_shape)
    memory_padded = jnp.pad(memory, ((0, 0), (0, SLOT_PAD - quarter), (0, 0)))
    memory_parts = exchange_members(
        [
            lax.dynamic_index_in_dim(memory_padded, member ^ item, 0, keepdims=False)
            for item in range(group_size)
        ],
        device_count,
    )
    parts = spread_begin(own)
    got = spread_swaps(parts, 0, device_count)
    first, got, vector_pieces, own, memory_parts = pinned(
        first, got, vector_pieces, own, memory_parts
    )
    held = jnp.where((plane == 0) | (plane == 3), own, first)
    near = move_planes(held, NEAR, plane_size)
    middle = move_planes(own, ((1, 2), (2, 1)), plane_size)
    parts, got = spread_on(parts, got, device_count)
    near, middle, first, got = pinned(near, middle, first, got)
    slot_zero = flat_slot(parts, got)
    even = plane % 2 == 0
    parts_one = spread_begin(jnp.where(even, first, near))
    got_one = spread_swaps(parts_one, 0, device_count)
    last = move_planes(middle, ((1, 0), (2, 3)), plane_size)
    zero_away = swap_cores(slot_zero, device_count)
    got_one, zero_away, memory_parts, near, first, upstream, slot_masks = pinned(
        got_one, zero_away, memory_parts, near, first, upstream, slot_masks
    )
    parts_three = spread_begin(jnp.where(even, near, first))
    memory_here = jnp.concatenate(memory_parts, axis=0)
    live_rows = (jnp.arange(row_count) < page_lengths[0]).astype(F32)[:, None]
    slots_here = lax.dynamic_slice_in_dim(slot_masks, member, 1, 0).reshape(group_size, quarter)
    slots_here = by_member(slots_here, member)
    slots_here = jnp.pad(slots_here, ((0, 0), (0, SLOT_PAD - quarter))).reshape(-1, 1)
    slot_bias = jnp.broadcast_to(
        jnp.where(slots_here > 0, 0.0, MASKED).astype(F32), (group_size * SLOT_PAD, LANES)
    )
    grad_low_three = (upstream.astype(F32) * live_rows).astype(BF16)
    vector_rows = jnp.swapaxes(vector_pieces, 0, 1).reshape(vector_shape[0], model).astype(F32)
    table = jnp.pad(vector_rows, ((0, VECTOR_ROWS - vector_shape[0]), (0, 0)))
    parts_one, got_one = spread_on(parts_one, got_one, device_count)
    one_away = swap_cores(parts_one, device_count)
    bias_up = vector_rows[13:17].reshape(-1, 1, width)
    last, table, bias_up, slot_bias, grad_low_three, memory_here, parts_three = pinned(
        last, table, bias_up, slot_bias, grad_low_three, memory_here, parts_three
    )
    parts_two = spread_begin(jnp.where((plane == 1) | (plane == 2), middle, last))
    got_one, one_away, parts_two, table = pinned(got_one, one_away, parts_two, table)
    got_one_away = swap_cores(got_one, device_count)
    got_two = spread_swaps(parts_two, 0, device_count)
    slots = [
        (slot_zero, tuple(zero_away)),
        (flat_slot(parts_one, got_one), flat_slot(one_away, got_one_away)),
    ]

    pairs = HEADS // 2
    self_firsts = (0, pairs, 2 * pairs)
    cross_firsts = (0, 0, pairs)

    self_low, low_one = project(
        here, tokens, table, slots, 0, 0, ((6, scale_q), (None, 1.0), (7, 1.0)), norm=0
    )
    got_two, self_low = pinned(got_two, self_low)
    parts_two, got_two = spread_on(parts_two, got_two, device_count)
    two_away = swap_cores(parts_two, device_count)
    attended, self_log = attention_forward(self_low, self_low, self_low, self_firsts)
    got_two, two_away, attended = pinned(got_two, two_away, attended)
    got_two_away = swap_cores(got_two, device_count)
    got_three = spread_swaps(parts_three, 0, device_count)
    after_self = project(
        here, attended, table, slots, 0, 3, ((8, 1.0),), residual=tokens, out_type=F32
    )
    got_two_away, after_self = pinned(got_two_away, after_self)
    slots.append((flat_slot(parts_two, got_two), flat_slot(two_away, got_two_away)))
    queries_cross, low_two = project(
        here, after_self, table, slots, 1, 0, ((9, scale_q),), norm=2
    )
    got_three, queries_cross, memory_here = pinned(got_three, queries_cross, memory_here)
    parts_three, got_three = spread_on(parts_three, got_three, device_count)
    three_away = swap_cores(parts_three, device_count)
    cross_low = project(here, memory_here, table, slots, 1, 1, ((None, 1.0), (10, 1.0)))
    merged, cross_log = attention_forward(
        queries_cross, cross_low, cross_low, cross_firsts, slot_bias
    )
    got_three, three_away, merged = pinned(got_three, three_away, merged)
    got_three_away = swap_cores(got_three, device_count)
    after_cross = project(
        here, merged, table, slots, 1, 3, ((11, 1.0),), residual=after_self, out_type=F32
    )
    got_three_away, after_cross, grad_low_three = pinned(
        got_three_away, after_cross, grad_low_three
    )
    slots.append((flat_slot(parts_three, got_three), flat_slot(three_away, got_three_away)))

    out_a, back_a, up_sent, down_sent, bias_sent, low_three = feed_half(
        away, after_cross, grad_low_three, table, bias_up, slots, 1, True
    )
    up_got = swap_bit(up_sent, device_count, 1)
    down_got = swap_bit(down_sent, device_count, 1)
    low_three, up_sent, down_sent = pinned(low_three, up_sent, down_sent)
    out_b, back_b, up_kept, down_kept, bias_kept = feed_half(
        here, low_three, grad_low_three, table, bias_up, slots, 0, False
    )
    up_got, down_got, out_b, back_b, up_kept, down_kept = pinned(
        up_got, down_got, out_b, back_b, up_kept, down_kept
    )
    feed_sum = Sum((up_kept, down_kept), (up_got, down_got), False)
    feed_sends = stage_sends(here, feed_sum, device_count)
    feed_sends, back_b = pinned(feed_sends, back_b)
    feed_swaps = stage_swaps(feed_sends, feed_sum, device_count)

    bias_even = jnp.where(core == 0, bias_kept, bias_sent)
    bias_odd = jnp.where(core == 0, bias_sent, bias_kept)
    grad_bias_up = jnp.concatenate([bias_even, bias_odd], axis=1).reshape(4, model)

    grad_two, grad_low_two, sums_three = norm_back(
        after_cross, table, 4, grad_low_three, (back_a, back_b)
    )
    grad_merged = project_back(here, (grad_low_two,), slots, 1, 3, BF16)
    cross_operands = (
        queries_cross,
        cross_low,
        cross_low,
        cross_firsts,
        grad_merged,
        merged,
        cross_log,
        slot_bias,
    )
    cross_whole, (queries_part, keys_part, values_part) = attention_backward(
        away, width, *cross_operands, None
    )
    cross_whole, (queries_own, keys_own, values_own) = attention_backward(
        here, width, *cross_operands, cross_whole
    )
    grad_queries_cross, grad_keys_cross, grad_values_cross, cross_sums = cross_whole
    feed_swaps, queries_part, queries_own, grad_queries_cross = pinned(
        feed_swaps, queries_part, queries_own, grad_queries_cross
    )
    feed_sum = feed_sum.joined(feed_swaps)
    feed_sends = stage_sends(here, feed_sum, device_count)
    feed_sends, queries_part, queries_own, grad_queries_cross = pinned(
        feed_sends, queries_part, queries_own, grad_queries_cross
    )
    feed_swaps = stage_swaps(feed_sends, feed_sum, device_count)
    cross_sent = weight_half(
        (
            (low_two, queries_part),
            (memory_here, keys_part),
            (memory_here, values_part),
            (merged, column_half(grad_low_two, 1 - core, width)),
        ),
        width,
    )
    cross_sent, queries_own, grad_queries_cross = pinned(
        cross_sent, queries_own, grad_queries_cross
    )
    cross_got = swap_bit(cross_sent, device_count, 1)
    cross_kept = weight_half(
        (
            (low_two, queries_own),
            (memory_here, keys_own),
            (memory_here, values_own),
            (merged, column_half(grad_low_two, core, width)),
        ),
        width,
    )

    grad_one, grad_low_one, sums_two = project_back(
        here, (grad_queries_cross,), slots, 1, 0, F32, (after_self, grad_two, table, 2)
    )
    grad_attended = project_back(here, (grad_low_one,), slots, 0, 3, BF16)
    memory_back = project_back(here, (grad_keys_cross, grad_values_cross), slots, 1, 1, BF16)
    memory_back = memory_back.reshape(group_size, SLOT_PAD, model)
    memory_back = exchange_members([memory_back[item] for item in range(group_size)], device_count)
    feed_swaps, cross_got, cross_kept, grad_attended = pinned(
        feed_swaps, cross_got, cross_kept, grad_attended
    )
    feed_sum = finish_stages(here, feed_sum.joined(feed_swaps), device_count)
    feed_kept, feed_sent = plane_totals(here, feed_sum)
    cross_sum = Sum((cross_kept,), (cross_got,), True)
    cross_sends = stage_sends(here, cross_sum, device_count)
    feed_sent, cross_sends, grad_attended = pinned(feed_sent, cross_sends, grad_attended)
    feed_got = move_planes(feed_sent, NEAR, plane_size)
    cross_swaps = stage_swaps(cross_sends, cross_sum, device_count)
    self_operands = (
        self_low,
        self_low,
        self_low,
        self_firsts,
        grad_attended,
        attended,
        self_log,
        None,
    )
    self_whole, (queries_part, keys_part, values_part) = attention_backward(
        away, width, *self_operands, None
    )
    self_sent = weight_half(
        (
            (low_one, queries_part),
            (low_one, keys_part),
            (low_one, values_part),
            (attended, column_half(grad_low_one, 1 - core, width)),
        ),
        width,
    )
    feed_got, cross_swaps, self_sent, self_whole = pinned(
        feed_got, cross_swaps, self_sent, self_whole
    )
    self_got = swap_bit(self_sent, device_count, 1)
    feed_kept = feed_kept + feed_got.astype(F32)
    cross_sum = cross_sum.joined(cross_swaps)
    cross_sends = stage_sends(here, cross_sum, device_count)
    feed_sent, cross_sends, self_whole = pinned(
        feed_kept.astype(BF16), cross_sends, self_whole
    )
    feed_middle = model // 2
    feed_upper = move_planes(feed_sent[:feed_middle], ((0, 2), (1, 3)), plane_size)
    cross_swaps = stage_swaps(cross_sends, cross_sum, device_count)
    self_whole, (queries_own, keys_own, values_own) = attention_backward(
        here, width, *self_operands, self_whole
    )
    grad_queries_self, grad_keys_self, grad_values_self, self_sums = self_whole
    self_kept = weight_half(
        (
            (low_one, queries_own),
            (low_one, keys_own),
            (low_one, values_own),
            (attended, column_half(grad_low_one, core, width)),
        ),
        width,
    )
    self_got, cross_swaps, self_kept = pinned(self_got, cross_swaps, self_kept)
    self_sum = Sum((self_kept,), (self_got,), True)
    self_sends = stage_sends(here, self_sum, device_count)
    self_sends, grad_queries_self, cross_swaps = pinned(
        self_sends, grad_queries_self, cross_swaps
    )
    self_swaps = stage_swaps(self_sends, self_sum, device_count)
    cross_sum = finish_stages(here, cross_sum.joined(cross_swaps), device_count)
    input_grad, _, sums_one = project_back(
        here,
        (grad_queries_self, grad_keys_self, grad_values_self),
        slots,
        0,
        0,
        F32,
        (tokens, grad_one, table, 0),
    )
    sums_one, cross_swaps = pinned(sums_one, cross_sum.swaps)
    cross_sum.swaps = list(cross_swaps)
    cross_total, cross_sent = plane_totals(here, cross_sum)
    self_swaps, cross_sent, sums_one, feed_upper, feed_sent, memory_back = pinned(
        self_swaps, cross_sent, sums_one, feed_upper, feed_sent, memory_back
    )
    feed_lower = move_planes(feed_sent[feed_middle:], ((0, 2), (1, 3)), plane_size)
    self_sum = self_sum.joined(self_swaps)
    self_sends = stage_sends(here, self_sum, device_count)
    self_sends, sums_one, cross_sent = pinned(self_sends, sums_one, cross_sent)
    self_swaps = stage_swaps(self_sends, self_sum, device_count)
    cross_got = move_planes(cross_sent, ((0, 1), (3, 2)), plane_size)
    vector_terms = vector_table(
        sums_one, sums_two, sums_three, self_sums, cross_sums, grad_bias_up
    )
    vector_bits = [1 << number for number in reversed(range(device_count.bit_length() - 1))]
    vector_kept, vector_sent = vector_send(vector_terms, device, vector_bits[0])
    vector_got = swap_bit(vector_sent, device_count, vector_bits[0])

    def vector_next(kept, got, number):
        kept, sent = vector_send(kept + got, device, vector_bits[number])
        return kept, swap_bit(sent, device_count, vector_bits[number])

    self_swaps, vector_sent = pinned(self_swaps, vector_sent)
    self_sum = finish_stages(here, self_sum.joined(self_swaps), device_count)
    self_total, self_sent = plane_totals(here, self_sum)
    self_got = move_planes(self_sent, ((1, 0), (3, 2)), plane_size)
    vector_kept, vector_got = vector_next(vector_kept, vector_got, 1)
    branch = out_a.astype(F32) + out_b.astype(F32)
    result = (after_cross + branch + vector_rows[12]) * live_rows
    mixed = result.astype(BF16)
    mixed, vector_got = pinned(mixed, vector_got)
    vector_kept, vector_got = vector_next(vector_kept, vector_got, 2)
    cross_total = cross_total + cross_got.astype(F32)
    cross_got = move_planes(cross_total.astype(BF16), ((2, 1),), plane_size)

    self_got, cross_got, feed_lower, vector_got = pinned(
        self_got, cross_got, feed_lower, vector_got
    )
    feed_got = jnp.concatenate([feed_upper, feed_lower], axis=0)
    self_sent = (self_total + self_got.astype(F32)).astype(BF16)
    self_sent, cross_got, feed_got, memory_back, vector_got = pinned(
        self_sent, cross_got, feed_got, memory_back, vector_got
    )
    self_far = move_planes(self_sent, ((2, 0),), plane_size)
    group_other = jnp.where(
        plane < 2,
        cross_total + cross_got.astype(F32),
        feed_kept + feed_got.astype(F32),
    )
    memory_back = jnp.stack([item[:quarter] for item in memory_back])
    memory_back = by_member(memory_back, member).astype(F32)
    vector_kept, vector_got = vector_next(vector_kept, vector_got, 3)
    group_other, vector_got = pinned(group_other, vector_got)
    for number in range(4, len(vector_bits)):
        vector_kept, vector_got = vector_next(vector_kept, vector_got, number)
    group_other, self_far, vector_got = pinned(group_other, self_far, vector_got)
    vector_grad = (vector_kept + vector_got)[: vector_shape[0]]
    (
        weight_grad,
        weight_first,
        weight_second,
        new_weights,
        new_average,
        weights_copy,
        new_stats,
        new_bases,
    ) = rotated_update(
        here,
        self_total,
        self_got,
        self_far,
        group_other,
        weights,
        weight_average,
        weight_moment1,
        weight_moment2,
        stats,
        bases,
    )
    vector_first, vector_second, new_vectors = adam_update(
        vector_grad, vectors, vector_moment1, vector_moment2
    )
    new_vector_average = AVERAGE * vector_average + (1.0 - AVERAGE) * new_vectors
    return (
        mixed,
        input_grad,
        memory_back,
        weight_grad,
        weight_first,
        weight_second,
        new_weights,
        new_average,
        weights_copy,
        new_stats,
        new_bases,
        vector_grad,
        vector_first,
        vector_second,
        new_vectors,
        new_vector_average,
        new_vectors.astype(BF16),
        vector_grad[12],
    )


def solution(mesh):
    return jax.shard_map(
        local,
        mesh=mesh,
        in_specs=(
            P(("seq", "mem"), None),
            P("seq", "mem", None),
            P(("seq", "mem")),
            P("seq", None),
            P(("seq", "mem"), None),
            P(None, ("seq", "mem")),
            P(None, ("seq", "mem")),
            P(None, ("seq", "mem")),
            P(None, ("seq", "mem")),
            P(("seq", "mem"), None, None),
            P(("seq", "mem"), None, None),
            P(None, ("seq", "mem")),
            P(None, ("seq", "mem")),
            P(None, ("seq", "mem")),
            P(None, ("seq", "mem")),
        ),
        out_specs=(
            P(("seq", "mem"), None),
            P(("seq", "mem"), None),
            P("seq", "mem", None),
            P(None, ("seq", "mem")),
            P(None, ("seq", "mem")),
            P(None, ("seq", "mem")),
            P(None, ("seq", "mem")),
            P(None, ("seq", "mem")),
            P(None, ("seq", "mem")),
            P(("seq", "mem"), None, None),
            P(("seq", "mem"), None, None),
            P(None, ("seq", "mem")),
            P(None, ("seq", "mem")),
            P(None, ("seq", "mem")),
            P(None, ("seq", "mem")),
            P(None, ("seq", "mem")),
            P(None, ("seq", "mem")),
            P(("seq", "mem")),
        ),
        check_vma=False,
    )
```
